32 devices in a mesh: freq: 2 (over core), tm: 4 (over y, x), clip: 4 (over z).
Axes of the slice: x: 2, y: 2, z: 4, core: 2. Of those that a mesh axis runs over, the one named last changes fastest.
Arguments:
- patches: bfloat16 [12, 128, 8, 768], P('freq', 'tm', 'clip'), may hold values from -6 to 6
- lead_tokens: bfloat16 [8, 2, 768], P('clip'), may hold values from -6 to 6
- lengths: int32 [8], P('clip'), may hold values from 1 to 101, as said below
- input_weight: bfloat16 [768, 2304], replicated, may hold values from -0.21875 to 0.21875
- input_bias: bfloat16 [1536], replicated, may hold values from -4 to 4
- output_weight: bfloat16 [768, 768], replicated, may hold values from -0.875 to 0.875
- output_bias: bfloat16 [768], replicated, may hold values from -4 to 4
- first_gain: bfloat16 [768], replicated, may hold values from 0.5 to 1.5
- first_shift: bfloat16 [768], replicated, may hold values from -4 to 4
- second_gain: bfloat16 [768], replicated, may hold values from 0.5 to 1.5
- second_shift: bfloat16 [768], replicated, may hold values from -4 to 4
- expand_weight: bfloat16 [768, 3072], replicated, may hold values from -0.21875 to 0.21875
- expand_bias: bfloat16 [3072], replicated, may hold values from -4 to 4
- reduce_weight: bfloat16 [3072, 768], replicated, may hold values from -0.109375 to 0.109375
- reduce_bias: bfloat16 [768], replicated, may hold values from -4 to 4
- cot_patches: bfloat16 [12, 128, 8, 768], P('freq', 'tm', 'clip'), may hold values from -6 to 6
- cot_lead: bfloat16 [8, 2, 768], P('clip'), may hold values from -6 to 6
Outputs:
- layer_out: bfloat16 [12, 128, 8, 768], P('freq', 'tm', 'clip')
- lead_out: bfloat16 [8, 2, 768], P('clip')
- patch_grad: bfloat16 [12, 128, 8, 768], P('freq', 'tm', 'clip')
- lead_grad: bfloat16 [8, 2, 768], P('clip')
- input_weight_grad: float32 [768, 2304], P('clip')
- input_bias_grad: float32 [1536], P('clip')
- output_weight_grad: float32 [768, 768], P('clip')
- output_bias_grad: float32 [768], P('clip')
- first_gain_grad: float32 [768], P('clip')
- first_shift_grad: float32 [768], P('clip')
- second_gain_grad: float32 [768], P('clip')
- second_shift_grad: float32 [768], P('clip')
- expand_weight_grad: float32 [768, 3072], P('clip')
- expand_bias_grad: float32 [3072], P('clip')
- reduce_weight_grad: float32 [3072, 768], P('clip')
- reduce_bias_grad: float32 [768], P('clip')
The draws below stay inside these ranges and needn't reach their ends.
Inputs may be any that keep to these rules, and one draw needn't show every extreme that they name: `lengths`: in every aligned block of 2 clips one clip has exactly 101 live time columns.
All inputs are finite; a program needn't handle non-finite values.
Results may differ from the reference program's by a relative error of at most 0.02.
Values may be sent and summed in bfloat16 or wider, within the bound.
No kernel may reach another device: no remote copies, remote signals or barrier semaphores. Data moves between devices by JAX's collectives and lax.ppermute only.
A program may use at most 320 MiB of HBM per device.

```python
import jax
import jax.numpy as jnp
from jax import lax

D = 768
HEADS = 12
FF = 3072
FROWS = 12
TCOLS = 128
CLIP_DEV = 2
CLIPS = 8


def draw_lengths(key, part):
    key = jax.random.fold_in(key, 11)
    first_key, second_key = jax.random.split(key)
    drawn_lengths = jax.random.randint(first_key, (CLIPS // CLIP_DEV, CLIP_DEV), 1, 102)
    chosen = jax.random.randint(second_key, (CLIPS // CLIP_DEV, 1), 0, CLIP_DEV)
    slot_index = jnp.arange(CLIP_DEV)[None, :]
    return jnp.where(slot_index == chosen, 101, drawn_lengths).reshape(CLIPS).astype(jnp.int32)


def levels(own_key, dims, shards, low, high):
    factor_of, own = 1.0, jax.random.fold_in(own_key, 6)
    for position, shards_of in shards:
        draws = jnp.exp(jax.random.uniform(jax.random.fold_in(own, position), (shards_of,), jnp.float32, low / len(shards), high / len(shards)))
        factor_of = factor_of * jnp.repeat(draws, dims[position] // shards_of).reshape([-1 if axis == position else 1 for axis in range(len(dims))])
    return factor_of


def scatter_about(own_key, shape, spread, bound, pieces=(), kind=jnp.bfloat16):
    array = jax.random.normal(own_key, shape, jnp.float32) * spread
    if len(pieces) > 0:
        array = levels(own_key, shape, pieces, -0.22, 0.18) * array
    return jnp.clip(array, min=-bound, max=bound).astype(kind)


def setup_inputs(seed: int = 0) -> dict:
    keys = jax.random.split(jax.random.key(seed), 18)
    patches = scatter_about(keys[0], (FROWS, TCOLS, CLIPS, D), 1.0, 6.0, ((0, 2), (1, 4), (2, 4)))
    lead_tokens = scatter_about(keys[1], (CLIPS, 2, D), 1.0, 6.0, ((0, 4),))
    lengths = draw_lengths(jax.random.fold_in(keys[17], 71), 0)
    input_weight = scatter_about(keys[3], (D, 3 * D), D ** -0.5, 0.21875)
    input_bias = scatter_about(keys[4], (2 * D,), 0.3, 4.0)
    output_weight = scatter_about(keys[5], (D, D), (D // 16) ** -0.5, 0.875)
    output_bias = scatter_about(keys[6], (D,), 0.3, 4.0)
    first_gain = jnp.clip(1.0 + 0.1 * jax.random.normal(keys[7], (D,), jnp.float32), 0.5, 1.5).astype(jnp.bfloat16)
    first_shift = scatter_about(keys[8], (D,), 0.3, 4.0)
    second_gain = jnp.clip(1.0 + 0.1 * jax.random.normal(keys[9], (D,), jnp.float32), 0.5, 1.5).astype(jnp.bfloat16)
    second_shift = scatter_about(keys[10], (D,), 0.3, 4.0)
    expand_weight = scatter_about(keys[11], (D, FF), D ** -0.5, 0.21875)
    expand_bias = scatter_about(keys[12], (FF,), 0.3, 4.0)
    reduce_weight = scatter_about(keys[13], (FF, D), FF ** -0.5, 0.109375)
    reduce_bias = scatter_about(keys[14], (D,), 0.3, 4.0)
    cot_patches = scatter_about(keys[15], (FROWS, TCOLS, CLIPS, D), 1.0, 6.0, ((0, 2), (1, 4), (2, 4)))
    cot_lead = scatter_about(keys[16], (CLIPS, 2, D), 1.0, 6.0, ((0, 4),))
    return dict(patches=patches, lead_tokens=lead_tokens, lengths=lengths, input_weight=input_weight, input_bias=input_bias, output_weight=output_weight, output_bias=output_bias, first_gain=first_gain, first_shift=first_shift, second_gain=second_gain, second_shift=second_shift, expand_weight=expand_weight, expand_bias=expand_bias, reduce_weight=reduce_weight, reduce_bias=reduce_bias, cot_patches=cot_patches, cot_lead=cot_lead)


@jax.custom_vjp
def low(v):
    return lax.optimization_barrier(v.astype(jnp.bfloat16)).astype(jnp.float32)

@jax.custom_vjp
def low_back(v):
    return v

def low_keep(v):
    return (low(v), None)

def low_pass(kept, grad):
    return (grad,)

def back_keep(v):
    return (v, None)

def back_low(kept, grad):
    return (low(grad),)
low.defvjp(low_keep, low_pass)
low_back.defvjp(back_keep, back_low)
PRECISE = lax.Precision.HIGHEST
EPSILON = 1e-06

def product_of(left, right):
    return jnp.dot(left, right, precision=PRECISE, preferred_element_type=jnp.float32)

def layer_norm(inputs, gain_row, shift_row):
    center = inputs - lax.optimization_barrier(jnp.mean(inputs, -1, keepdims=True))
    variance = lax.optimization_barrier(jnp.mean(center * center, -1, keepdims=True))
    return center * lax.rsqrt(variance + EPSILON) * gain_row + shift_row

def clip_forward(params, lead_rows, grid, length):
    input_weight, input_bias, output_weight, output_bias, first_gain, first_shift, second_gain, second_shift, expand_weight, expand_bias, reduce_weight, reduce_bias = params
    head_width = D // HEADS
    all_rows = jnp.concatenate([lead_rows, grid.reshape(FROWS * TCOLS, D)], 0)
    seq_len = all_rows.shape[0]
    hidden_one = low(layer_norm(all_rows, first_gain, first_shift))
    bias_full = jnp.concatenate([input_bias[:D], jnp.zeros((D,), jnp.float32), input_bias[D:]])
    projected = product_of(hidden_one, input_weight) + bias_full
    queries = low(low_back(projected[:, :D])).reshape(seq_len, HEADS, head_width)
    key_heads = low(low_back(projected[:, D:2 * D])).reshape(seq_len, HEADS, head_width)
    values = low(low_back(projected[:, 2 * D:])).reshape(seq_len, HEADS, head_width)
    scores = jnp.einsum('qhd,khd->hqk', queries, key_heads, precision=PRECISE) * head_width ** (-0.5)
    columns = jnp.concatenate([jnp.full((2,), -1, jnp.int32), jnp.tile(jnp.arange(TCOLS, dtype=jnp.int32), FROWS)])
    live_keys = columns < length
    scores = low_back(jnp.where(live_keys[None, None, :], scores, -1e+30))
    probabilities = low(jax.nn.softmax(scores, axis=-1))
    mixed_heads = jnp.einsum('hqk,khd->qhd', probabilities, values, precision=PRECISE).reshape(seq_len, D)
    mixed_heads = low(low_back(mixed_heads))
    first_sum = all_rows + low_back(product_of(mixed_heads, output_weight) + output_bias)
    hidden_two = low(layer_norm(first_sum, second_gain, second_shift))
    expanded = low_back(product_of(hidden_two, expand_weight) + expand_bias)
    activated = low(jax.nn.gelu(expanded, approximate=False))
    return first_sum + low_back(product_of(activated, reduce_weight) + reduce_bias)

def reference(patches, lead_tokens, lengths, input_weight, input_bias, output_weight, output_bias, first_gain, first_shift, second_gain, second_shift, expand_weight, expand_bias, reduce_weight, reduce_bias, cot_patches, cot_lead):
    params = tuple((weight_arg.astype(jnp.float32) for weight_arg in (input_weight, input_bias, output_weight, output_bias, first_gain, first_shift, second_gain, second_shift, expand_weight, expand_bias, reduce_weight, reduce_bias)))

    def forward(weights, lead_all, patch_all):
        clip_grids = jnp.transpose(patch_all, (2, 0, 1, 3))
        clip_step = jax.checkpoint(clip_forward)
        return lax.map(lambda clip_item: clip_step(weights, clip_item[0], clip_item[1], clip_item[2]), (lead_all, clip_grids, lengths))
    result, pullback = jax.vjp(forward, params, lead_tokens.astype(jnp.float32), patches.astype(jnp.float32))
    patch_cot = jnp.transpose(cot_patches.astype(jnp.float32), (2, 0, 1, 3)).reshape(CLIPS, FROWS * TCOLS, D)
    cotangent = jnp.concatenate([cot_lead.astype(jnp.float32), patch_cot], 1)
    weight_grads, lead_gradient, patch_gradient = pullback(cotangent)
    layer_out = result[:, 2:].reshape(CLIPS, FROWS, TCOLS, D).transpose(1, 2, 0, 3).astype(jnp.bfloat16)
    lead_out = result[:, :2].astype(jnp.bfloat16)
    return (layer_out, lead_out, patch_gradient.astype(jnp.bfloat16), lead_gradient.astype(jnp.bfloat16), weight_grads[0], weight_grads[1], weight_grads[2], weight_grads[3], weight_grads[4], weight_grads[5], weight_grads[6], weight_grads[7], weight_grads[8], weight_grads[9], weight_grads[10], weight_grads[11])
```

```python
import functools
import math

import jax
import jax.numpy as jnp
import numpy as np
from jax import lax
from jax.experimental import pallas as pl
from jax.experimental.pallas import tpu as pltpu
from jax.sharding import PartitionSpec as P

HEADS = 12
EPSILON = 1e-06
NEG_FILL = -1e30
MAX_LENGTH = 101
LEADS = 2
LEAD_ROWS = 16
BLOCK_COLS = 8
GROUP = 4
FF_PARTS = 8
bf16 = jnp.bfloat16
f32 = jnp.float32
VMEM_LIMIT = 56 * 1024 * 1024


def mm(a, b):
    return lax.dot_general(a, b, (((1,), (0,)), ((), ())), preferred_element_type=f32)


def mm_nt(a, b):
    return lax.dot_general(a, b, (((1,), (1,)), ((), ())), preferred_element_type=f32)


def standardize(rows):
    center = rows - jnp.mean(rows, -1, keepdims=True)
    scale_inv = lax.rsqrt(jnp.mean(center * center, -1, keepdims=True) + EPSILON)
    return center * scale_inv, scale_inv


def norm_backward(grad_out, gain_row, normed, scale_inv):
    scaled = grad_out * gain_row
    return scale_inv * (
        scaled
        - jnp.mean(scaled, -1, keepdims=True)
        - normed * jnp.mean(scaled * normed, -1, keepdims=True)
    )


def head_mask(head, width, head_width):
    lane_head = lax.broadcasted_iota(jnp.int32, (1, width), 1) // head_width
    return (lane_head == head).astype(f32)


class Sizes:
    def __init__(self, patches_shape, tm_count):
        fr_local, tc_local, clips, feat = patches_shape
        self.fr, self.tc, self.clips, self.feat = fr_local, tc_local, clips, feat
        self.tm = tm_count
        self.blocks = tc_local // BLOCK_COLS
        self.half_block = fr_local * BLOCK_COLS
        self.block = 2 * self.half_block
        self.half = self.blocks * self.half_block
        self.rows = 2 * self.half
        self.query_rows = self.rows + LEAD_ROWS
        self.key_blocks = -(-MAX_LENGTH // BLOCK_COLS)
        self.keys = LEAD_ROWS + self.key_blocks * self.block
        self.head_width = feat // HEADS
        self.width = GROUP * self.head_width
        self.steps = HEADS // GROUP
        self.lanes = GROUP * self.rows + 128


def call(kernel, grid, in_specs, out_specs, out_shape, scratch, args, prefetch, flops, moved):
    return pl.pallas_call(
        kernel,
        out_shape=out_shape,
        grid_spec=pltpu.PrefetchScalarGridSpec(
            num_scalar_prefetch=1,
            grid=grid,
            in_specs=in_specs,
            out_specs=out_specs,
            scratch_shapes=scratch,
        ),
        compiler_params=pltpu.CompilerParams(
            dimension_semantics=("arbitrary",), vmem_limit_bytes=VMEM_LIMIT
        ),
        cost_estimate=pl.CostEstimate(flops=flops, bytes_accessed=moved, transcendentals=0),
    )(prefetch, *args)


def whole(shape):
    return pl.BlockSpec(shape, lambda i, info: (0,) * len(shape))


def chunks_of(z):
    full = z.lanes // 256
    spans = [(c * 256, 256) for c in range(full)]
    if z.lanes % 256:
        spans.append((full * 256, z.lanes % 256))
    return spans


def spread_heads(z, rows, out_ref):
    for head in range(GROUP):
        mask = head_mask(head, z.width, z.head_width)
        part = (rows * mask).astype(bf16)
        out_ref[head * z.rows : (head + 1) * z.rows, :] = part[: z.rows]
        at = GROUP * z.rows + head * LEAD_ROWS
        out_ref[at : at + LEAD_ROWS, :] = part[z.rows :]
    at = GROUP * (z.rows + LEAD_ROWS)
    out_ref[at:, :] = jnp.zeros((z.lanes - at, z.width), bf16)


def join_heads(z, spread):
    patch_part, lead_part = None, None
    for head in range(GROUP):
        mask = head_mask(head, z.width, z.head_width)
        at = GROUP * z.rows + head * LEAD_ROWS
        one = spread[head * z.rows : (head + 1) * z.rows] * mask
        two = spread[at : at + LEAD_ROWS] * mask
        patch_part = one if patch_part is None else patch_part + one
        lead_part = two if lead_part is None else lead_part + two
    return jnp.concatenate([patch_part, lead_part], 0)


def attend_kernel(z, info, *refs):
    pieces = refs[: 2 * z.tm]
    (lead, wq, wk, wv, bq, bv, gain, shift, live) = refs[2 * z.tm : 2 * z.tm + 9]
    (q_out, k_out, v_out, mixed_out, p_out, inv_out, hk, uk, hq, uq) = refs[
        2 * z.tm + 9 : 2 * z.tm + 19
    ]
    spread, total = refs[2 * z.tm + 19 :]
    step = pl.program_id(0)
    me = info[0]

    @pl.when(step == 0)
    def _():
        gain_row, shift_row = gain[...], shift[...]

        def hidden(rows):
            unit, _ = standardize(rows.astype(f32))
            return unit.astype(bf16), (unit * gain_row + shift_row).astype(bf16)

        unit, low = hidden(lead[...])
        uk[0:LEAD_ROWS, :] = unit
        hk[0:LEAD_ROWS, :] = low
        hq[z.rows :, :] = low
        uq[z.rows :, :] = unit
        hb = z.half_block
        for k in range(z.tm):
            source = jnp.bitwise_xor(me, k)
            for half in range(2):
                piece = pieces[2 * k + half]
                for b in range(z.blocks):
                    spot = source * z.blocks + b

                    def place(spot=spot, piece=piece, b=b, half=half, k=k):
                        unit, low = hidden(piece[b * hb : (b + 1) * hb, :])
                        if k == 0:
                            at = half * z.half + b * hb
                            hq[at : at + hb, :] = low
                            uq[at : at + hb, :] = unit

                        @pl.when(spot < z.key_blocks)
                        def _():
                            at = pl.multiple_of(LEAD_ROWS + spot * z.block + half * hb, 16)
                            uk[pl.ds(at, hb), :] = unit
                            hk[pl.ds(at, hb), :] = low

                    place()

    hk_all = hk[...]
    q = (mm(hq[...], wq[...]) + bq[...]).astype(bf16)
    q_out[...] = q
    spread_heads(z, q.astype(f32) * (z.head_width**-0.5), spread)
    k = mm(hk_all, wk[...]).astype(bf16)
    k_out[...] = k
    v = (mm(hk_all, wv[...]) + bv[...]).astype(bf16)
    v_out[...] = v
    live_col = live[...]
    for at, size in chunks_of(z):
        scores = mm_nt(k, spread[at : at + size, :])
        scores = scores + jnp.concatenate([live_col] * (size // 128), 1)
        peak = jnp.max(scores, 0, keepdims=True)
        weights = jnp.exp(scores - peak)
        total[0:1, at : at + size] = jnp.sum(weights, 0, keepdims=True)
        p_out[0, :, at : at + size] = weights.astype(bf16)
    inverse = 1.0 / total[0:1, :]
    inv_out[0] = jnp.broadcast_to(inverse, (8, z.lanes))
    mixed = mm(jnp.transpose(v), p_out[0]) * inverse
    mixed_out[...] = join_heads(z, jnp.transpose(mixed))


def attend(z, me_info, pieces, lead, weight, bias_q, bias_v, gain, shift, live):
    feat, width, nk, nq, nl = z.feat, z.width, z.keys, z.query_rows, z.lanes
    col = lambda offset: pl.BlockSpec((feat, width), lambda i, info: (0, offset * z.steps + i))
    in_specs = (
        [whole((z.half, feat))] * (2 * z.tm)
        + [whole((LEAD_ROWS, feat)), col(0), col(1), col(2)]
        + [pl.BlockSpec((1, width), lambda i, info: (0, i))] * 2
        + [whole((1, feat))] * 2
        + [whole((nk, 128))]
    )
    by_col = lambda rows: pl.BlockSpec((rows, width), lambda i, info: (0, i))
    out_specs = [
        by_col(nq),
        by_col(nk),
        by_col(nk),
        by_col(nq),
        pl.BlockSpec((1, nk, nl), lambda i, info: (i, 0, 0)),
        pl.BlockSpec((1, 8, nl), lambda i, info: (i, 0, 0)),
        whole((nk, feat)),
        whole((nk, feat)),
        whole((nq, feat)),
        whole((nq, feat)),
    ]
    out_shape = [
        jax.ShapeDtypeStruct((nq, feat), bf16),
        jax.ShapeDtypeStruct((nk, feat), bf16),
        jax.ShapeDtypeStruct((nk, feat), bf16),
        jax.ShapeDtypeStruct((nq, feat), f32),
        jax.ShapeDtypeStruct((z.steps, nk, nl), bf16),
        jax.ShapeDtypeStruct((z.steps, 8, nl), f32),
        jax.ShapeDtypeStruct((nk, feat), bf16),
        jax.ShapeDtypeStruct((nk, feat), bf16),
        jax.ShapeDtypeStruct((nq, feat), bf16),
        jax.ShapeDtypeStruct((nq, feat), bf16),
    ]
    return call(
        functools.partial(attend_kernel, z),
        (z.steps,),
        in_specs,
        out_specs,
        out_shape,
        [pltpu.VMEM((nl, width), bf16), pltpu.VMEM((8, nl), f32)],
        (*pieces, lead, weight, weight, weight, bias_q, bias_v, gain, shift, live),
        me_info,
        2 * feat * feat * (nq + 2 * nk) + 4 * z.steps * nk * nl * width,
        z.steps * nk * nl * 2,
    )


def feed_kernel(z, first, last, info, *refs):
    refs = list(refs)
    take = lambda n: [refs.pop(0) for _ in range(n)]
    if first:
        mixed, rows, wo, bo, rb = take(5)
    else:
        (mixed, wo, sum_in, out_in, grad_in) = take(5)
    cot, gain, shift, we, be, wr = take(6)
    dwr, dwe, dbe = take(3)
    if last:
        block_out, grad_first, grad_low, dwo, small = take(5)
    else:
        sum_out, acc_out, grad_out = take(3)
    unit, inv, low, low_t, acc, grad = take(6)
    step = pl.program_id(0)
    gain_row = gain[...]

    @pl.when(step == 0)
    def _():
        if first:
            total = rows[...].astype(f32) + mm(mixed[...].astype(bf16), wo[...]) + bo[...]
            sum_out[...] = total
            acc[...] = total + rb[...]
            grad[...] = jnp.zeros_like(grad)
        else:
            total = sum_in[...]
            acc[...] = out_in[...]
            grad[...] = grad_in[...]
        normed, scale_inv = standardize(total)
        unit[...] = normed
        inv[...] = jnp.broadcast_to(scale_inv, inv.shape)
        hidden = (normed * gain_row + shift[...]).astype(bf16)
        low[...] = hidden
        low_t[...] = jnp.transpose(hidden)

    cot_low = cot[...]
    expand, reduce = we[...], wr[...]
    expanded = mm(low[...], expand) + be[...]
    cdf = 0.5 * (1.0 + lax.erf(expanded * math.sqrt(0.5)))
    pdf = jnp.exp(-0.5 * expanded * expanded) * (1.0 / math.sqrt(2.0 * math.pi))
    activated = (expanded * cdf).astype(bf16)
    acc[...] += mm(activated, reduce)
    dwr[0] = mm(jnp.transpose(activated), cot_low).astype(bf16)
    grad_expanded = (mm_nt(cot_low, reduce) * (cdf + expanded * pdf)).astype(bf16)
    dwe[0] = mm(low_t[...], grad_expanded).astype(bf16)
    dbe[0] = jnp.broadcast_to(
        jnp.sum(grad_expanded.astype(f32), 0, keepdims=True), dbe.shape[1:]
    )
    grad[...] += mm_nt(grad_expanded, expand)

    @pl.when(step == pl.num_programs(0) - 1)
    def _():
        if last:
            block_out[...] = acc[...].astype(bf16)
            rows_grad = cot_low.astype(f32)
            normed, hidden_grad = unit[...], grad[...]
            back = rows_grad + norm_backward(hidden_grad, gain_row, normed, inv[:, 0:1])
            grad_first[...] = back
            back_low = back.astype(bf16)
            grad_low[...] = back_low
            dwo[...] = mm(jnp.transpose(mixed[...].astype(bf16)), back_low).astype(bf16)
            small[...] = jnp.zeros_like(small)
            small[0:1, :] = jnp.sum(back_low.astype(f32), 0, keepdims=True)
            small[1:2, :] = jnp.sum(hidden_grad * normed, 0, keepdims=True)
            small[2:3, :] = jnp.sum(hidden_grad, 0, keepdims=True)
            small[3:4, :] = jnp.sum(rows_grad, 0, keepdims=True)
        else:
            acc_out[...] = acc[...]
            grad_out[...] = grad[...]


def feed(z, info, part, paired, mixed, given, cot, gain, shift, expand, expand_bias, reduce, wo):
    first, last = part == 0, part == 1
    feat, ff = expand.shape
    size = ff // FF_PARTS
    steps = FF_PARTS // 2
    nq = z.query_rows

    def chunk(i, info):
        half = 1 - info[1] if first else info[1]
        return 2 * i + half if paired else steps * half + i

    rows_spec = whole((nq, feat))
    if first:
        head_specs = [rows_spec, rows_spec, whole((feat, feat)), whole((1, feat)), whole((1, feat))]
        head_args = (mixed, given[0], wo, given[1], given[2])
    else:
        head_specs = [rows_spec, whole((feat, feat)), rows_spec, rows_spec, rows_spec]
        head_args = (mixed, wo, *given)
    in_specs = head_specs + [
        rows_spec,
        whole((1, feat)),
        whole((1, feat)),
        pl.BlockSpec((feat, size), lambda i, info: (0, chunk(i, info))),
        pl.BlockSpec((1, size), lambda i, info: (0, chunk(i, info))),
        pl.BlockSpec((size, feat), lambda i, info: (chunk(i, info), 0)),
    ]
    out_specs = [
        pl.BlockSpec((1, size, feat), lambda i, info: (i, 0, 0)),
        pl.BlockSpec((1, feat, size), lambda i, info: (i, 0, 0)),
        pl.BlockSpec((1, 8, size), lambda i, info: (i, 0, 0)),
    ]
    out_shape = [
        jax.ShapeDtypeStruct((steps, size, feat), bf16),
        jax.ShapeDtypeStruct((steps, feat, size), bf16),
        jax.ShapeDtypeStruct((steps, 8, size), f32),
    ]
    wide = jax.ShapeDtypeStruct((nq, feat), f32)
    narrow = jax.ShapeDtypeStruct((nq, feat), bf16)
    if last:
        out_specs += [rows_spec, rows_spec, rows_spec, whole((feat, feat)), whole((8, feat))]
        out_shape += [
            narrow,
            wide,
            narrow,
            jax.ShapeDtypeStruct((feat, feat), bf16),
            jax.ShapeDtypeStruct((8, feat), f32),
        ]
    else:
        out_specs += [rows_spec] * 3
        out_shape += [wide] * 3
    return call(
        functools.partial(feed_kernel, z, first, last),
        (steps,),
        in_specs,
        out_specs,
        out_shape,
        [
            pltpu.VMEM((nq, feat), f32),
            pltpu.VMEM((nq, 128), f32),
            pltpu.VMEM((nq, feat), bf16),
            pltpu.VMEM((feat, nq), bf16),
            pltpu.VMEM((nq, feat), f32),
            pltpu.VMEM((nq, feat), f32),
        ],
        (*head_args, cot, gain, shift, expand, expand_bias, reduce),
        info,
        2 * nq * feat * (ff * 3 + feat),
        4 * feat * ff,
    )


def attend_back_kernel(z, info, *refs):
    refs = list(refs)
    take = lambda n: [refs.pop(0) for _ in range(n)]
    ga, wo, q, k, v, mixed, p, inv, hk, uk, hq, uq, wq, wk, wv, first_lead = take(16)
    dw, db, gain_sums, own = take(4)
    sends = take(z.tm - 1)
    hk_t, hq_t, q_spread, g_spread, ds, keys_acc, query_acc = take(7)
    step = pl.program_id(0)
    me = info[0]
    scale = z.head_width**-0.5

    @pl.when(step == 0)
    def _():
        hk_t[...] = jnp.transpose(hk[...])
        hq_t[...] = jnp.transpose(hq[...])
        keys_acc[...] = jnp.zeros_like(keys_acc)
        query_acc[...] = jnp.zeros_like(query_acc)

    spread_heads(z, q[...].astype(f32) * scale, q_spread)
    grad = mm_nt(ga[...], wo[...]).astype(bf16).astype(f32)
    inverse = inv[0, 0:1, :]
    inverse_col = jnp.transpose(jnp.broadcast_to(inverse, (128, z.lanes)))[:, 0:1]
    product = grad * mixed[...]
    dots = []
    for head in range(GROUP):
        mask = head_mask(head, z.width, z.head_width)
        at = GROUP * z.rows + head * LEAD_ROWS
        part = grad * mask
        low = (part[: z.rows] * inverse_col[head * z.rows : (head + 1) * z.rows]).astype(bf16)
        g_spread[head * z.rows : (head + 1) * z.rows, :] = low
        low = (part[z.rows :] * inverse_col[at : at + LEAD_ROWS]).astype(bf16)
        g_spread[at : at + LEAD_ROWS, :] = low
        dots.append(jnp.sum(product * mask, 1, keepdims=True))
    end = GROUP * (z.rows + LEAD_ROWS)
    g_spread[end:, :] = jnp.zeros((z.lanes - end, z.width), bf16)
    dot_col = jnp.concatenate(
        [d[: z.rows] for d in dots]
        + [d[z.rows :] for d in dots]
        + [jnp.zeros((z.lanes - end, 1), f32)],
        0,
    )
    dot_row = jnp.transpose(jnp.broadcast_to(dot_col, (z.lanes, 128)))[0:1, :] * inverse
    v_all, k_all = v[...], k[...]
    for at, size in chunks_of(z):
        grad_weights = mm_nt(v_all, g_spread[at : at + size, :])
        weights = p[0, :, at : at + size].astype(f32)
        ds[:, at : at + size] = (weights * (grad_weights - dot_row[:, at : at + size])).astype(bf16)
    ds_all = ds[...]
    grad_v = mm(p[0], g_spread[...])
    grad_k = mm(ds_all, q_spread[...])
    grad_q = mm(jnp.transpose(k_all), ds_all)
    grad_q = (join_heads(z, jnp.transpose(grad_q)) * scale).astype(bf16)
    grad_v = grad_v.astype(bf16)
    grad_k = grad_k.astype(bf16)
    db[0] = jnp.concatenate(
        [
            jnp.sum(grad_q.astype(f32), 0, keepdims=True),
            jnp.sum(grad_v.astype(f32), 0, keepdims=True),
            jnp.zeros((6, z.width), f32),
        ],
        0,
    )
    keys_acc[...] += mm_nt(grad_k, wk[...]) + mm_nt(grad_v, wv[...])
    query_acc[...] += mm_nt(grad_q, wq[...])
    dw[0, 0] = mm(hq_t[...], grad_q).astype(bf16)
    dw[0, 1] = mm(hk_t[...], grad_k).astype(bf16)
    dw[0, 2] = mm(hk_t[...], grad_v).astype(bf16)

    @pl.when(step == pl.num_programs(0) - 1)
    def _():
        keys_grad = keys_acc[...]
        gain_sums[...] = jnp.zeros_like(gain_sums)
        gain_sums[0:1, :] = jnp.sum(keys_grad * uk[...].astype(f32), 0, keepdims=True) + jnp.sum(
            query_acc[...] * uq[...].astype(f32), 0, keepdims=True
        )
        gain_sums[1:2, :] = jnp.sum(keys_grad, 0, keepdims=True) + jnp.sum(
            query_acc[...], 0, keepdims=True
        )
        lead = keys_acc[0:LEAD_ROWS, :] + query_acc[z.rows :, :]
        high = first_lead[...].astype(bf16)
        rest = (first_lead[...] - high.astype(f32)).astype(bf16)
        pair = lambda a: a[0:LEADS]
        packed = jnp.concatenate(
            [pair(lead), pair(high.astype(f32)), pair(rest.astype(f32)), jnp.zeros((10, z.feat), f32)],
            0,
        )
        own[z.rows :, :] = packed
        for send in sends:
            send[z.rows :, :] = packed.astype(bf16)
        hb = z.half_block
        for k_ in range(z.tm):
            source = jnp.bitwise_xor(me, k_)
            for b in range(z.blocks):
                spot = source * z.blocks + b
                for half in range(2):
                    to = half * z.half + b * hb
                    at = pl.multiple_of(
                        LEAD_ROWS + jnp.minimum(spot, z.key_blocks - 1) * z.block + half * hb, 16
                    )
                    keep = (spot < z.key_blocks).astype(f32)
                    rows = keys_acc[pl.ds(at, hb), :] * keep
                    if k_ == 0:
                        own[to : to + hb, :] = rows + query_acc[to : to + hb, :]
                    else:
                        sends[k_ - 1][to : to + hb, :] = rows.astype(bf16)


def attend_back(z, info, ga, wo, saved, weight, first_lead):
    q, k, v, mixed, p, inv, hk, uk, hq, uq = saved
    feat, width, nk, nq, nl = z.feat, z.width, z.keys, z.query_rows, z.lanes
    by_col = lambda rows: pl.BlockSpec((rows, width), lambda i, info: (0, i))
    col = lambda offset: pl.BlockSpec((feat, width), lambda i, info: (0, offset * z.steps + i))
    in_specs = [
        whole((nq, feat)),
        pl.BlockSpec((width, feat), lambda i, info: (i, 0)),
        by_col(nq),
        by_col(nk),
        by_col(nk),
        by_col(nq),
        pl.BlockSpec((1, nk, nl), lambda i, info: (i, 0, 0)),
        pl.BlockSpec((1, 8, nl), lambda i, info: (i, 0, 0)),
        whole((nk, feat)),
        whole((nk, feat)),
        whole((nq, feat)),
        whole((nq, feat)),
        col(0),
        col(1),
        col(2),
        whole((LEAD_ROWS, feat)),
    ]
    out_specs = [
        pl.BlockSpec((1, 3, feat, width), lambda i, info: (i, 0, 0, 0)),
        pl.BlockSpec((1, 8, width), lambda i, info: (i, 0, 0)),
        whole((8, feat)),
        whole((nq, feat)),
    ] + [whole((nq, feat))] * (z.tm - 1)
    out_shape = [
        jax.ShapeDtypeStruct((z.steps, 3, feat, width), bf16),
        jax.ShapeDtypeStruct((z.steps, 8, width), f32),
        jax.ShapeDtypeStruct((8, feat), f32),
        jax.ShapeDtypeStruct((nq, feat), f32),
    ] + [jax.ShapeDtypeStruct((nq, feat), bf16)] * (z.tm - 1)
    return call(
        functools.partial(attend_back_kernel, z),
        (z.steps,),
        in_specs,
        out_specs,
        out_shape,
        [
            pltpu.VMEM((feat, nk), bf16),
            pltpu.VMEM((feat, nq), bf16),
            pltpu.VMEM((nl, width), bf16),
            pltpu.VMEM((nl, width), bf16),
            pltpu.VMEM((nk, nl), bf16),
            pltpu.VMEM((nk, feat), f32),
            pltpu.VMEM((nq, feat), f32),
        ],
        (ga, wo, q, k, v, mixed, p, inv, hk, uk, hq, uq, weight, weight, weight, first_lead),
        info,
        4 * feat * feat * (nq + 2 * nk) + 8 * z.steps * nk * nl * width,
        z.steps * nk * nl * 2,
    )


def finish_kernel(z, info, *refs):
    own = refs[0]
    received = refs[1 : z.tm]
    rows, gain, grad_first, out = refs[z.tm :]
    terms = [own[...]] + [one[...].astype(f32) for one in received]
    lead_terms = [terms[0][z.rows :].astype(bf16).astype(f32)] + [t[z.rows :] for t in terms[1:]]
    while len(lead_terms) > 1:
        lead_terms = [a + b for a, b in zip(lead_terms[::2], lead_terms[1::2])]
    total = jnp.concatenate([sum(t[: z.rows] for t in terms), lead_terms[0]], 0)
    normed, scale_inv = standardize(rows[...].astype(f32))
    back = norm_backward(total, gain[...], normed, scale_inv)
    out[0 : z.rows, :] = (back[: z.rows] + grad_first[0 : z.rows, :]).astype(bf16)
    lead = total[z.rows :]
    lead_first = lead[LEADS : 2 * LEADS] + lead[2 * LEADS : 3 * LEADS]
    out[z.rows :, :] = jnp.concatenate(
        [back[z.rows : z.rows + LEADS] + lead_first, jnp.zeros((LEAD_ROWS - LEADS, z.feat), f32)], 0
    ).astype(bf16)


def finish(z, info, own, received, rows, gain, grad_first):
    feat, nq = z.feat, z.query_rows
    return call(
        functools.partial(finish_kernel, z),
        (1,),
        [whole((nq, feat))] * (z.tm + 1) + [whole((1, feat)), whole((nq, feat))],
        whole((nq, feat)),
        jax.ShapeDtypeStruct((nq, feat), bf16),
        [],
        (own, *received, rows, gain, grad_first),
        info,
        nq * feat * 20,
        nq * feat * 20,
    )


def flip(count, k):
    return [(i, i ^ k) for i in range(count)]


def bit_of(index, bit):
    return (index >> bit) & 1


def halve(x, dim, axis, bit):
    mine = bit_of(lax.axis_index(axis), bit)
    sent = lax.dynamic_index_in_dim(x, 1 - mine, dim, keepdims=False)
    got = lax.ppermute(sent, axis, flip(lax.axis_size(axis), 1 << bit))
    kept = lax.dynamic_index_in_dim(x, mine, dim, keepdims=False)
    return (kept.astype(f32) + got.astype(f32)).astype(bf16)


def scatter_tm(x, dim, upward):
    count = lax.axis_size("tm")
    bits = count.bit_length() - 1
    x = x.reshape(x.shape[:dim] + (2,) * bits + x.shape[dim + 1 :])
    left = list(range(bits))[::-1]
    for bit in range(bits) if upward else range(bits)[::-1]:
        x = halve(x, dim + left.index(bit), "tm", bit)
        left.remove(bit)
    return x


def scatter_clip(x):
    count, me = lax.axis_size("clip"), lax.axis_index("clip")
    total = lax.dynamic_index_in_dim(x, me, 0, keepdims=False).astype(f32)
    for k in range(1, count):
        sent = lax.dynamic_index_in_dim(x, me ^ k, 0, keepdims=False)
        total = total + lax.ppermute(sent, "clip", flip(count, k)).astype(f32)
    return total.astype(bf16)


def gather(x, axis):
    count, me = lax.axis_size(axis), lax.axis_index(axis)
    out = jnp.zeros((count,) + x.shape, x.dtype)
    out = lax.dynamic_update_index_in_dim(out, x, me, 0)
    for k in range(1, count):
        out = lax.dynamic_update_index_in_dim(out, lax.ppermute(x, axis, flip(count, k)), me ^ k, 0)
    return out


def sum_all(x):
    for axis in ("freq", "tm"):
        for bit in range(lax.axis_size(axis).bit_length() - 1):
            x = x + lax.ppermute(x, axis, flip(lax.axis_size(axis), 1 << bit))
    total = x
    for k in range(1, lax.axis_size("clip")):
        total = total + lax.ppermute(x, "clip", flip(lax.axis_size("clip"), k))
    return total


def per_device(
    patches,
    lead_tokens,
    lengths,
    input_weight,
    input_bias,
    output_weight,
    output_bias,
    first_gain,
    first_shift,
    second_gain,
    second_shift,
    expand_weight,
    expand_bias,
    reduce_weight,
    reduce_bias,
    cot_patches,
    cot_lead,
):
    tm_count = lax.axis_size("tm")
    clip_count = lax.axis_size("clip")
    z = Sizes(patches.shape, tm_count)
    feat, ff = expand_weight.shape
    core, place = lax.axis_index("freq"), lax.axis_index("tm")
    info = jnp.stack([place, core]).astype(jnp.int32)
    row = lambda vector: vector.astype(f32)[None, :]

    def by_clip(array):
        parts = array.reshape(z.fr, z.blocks, BLOCK_COLS, z.clips, feat)
        parts = parts.transpose(3, 1, 0, 2, 4).reshape(z.clips, z.half, feat)
        return (
            lax.dynamic_index_in_dim(parts, core, 0, keepdims=False),
            lax.dynamic_index_in_dim(parts, 1 - core, 0, keepdims=False),
        )

    def lead_of(array):
        mine = lax.dynamic_index_in_dim(array, core, 0, keepdims=False)
        return jnp.pad(mine, ((0, LEAD_ROWS - LEADS), (0, 0)))

    own_half, other_half = by_clip(patches)
    pieces = []
    for k in range(tm_count):
        pieces.append(lax.ppermute(own_half, "tm", flip(tm_count, k)) if k else own_half)
        pieces.append(
            lax.ppermute(other_half, ("freq", "tm"), flip(2 * tm_count, tm_count | k))
        )
    lead = lead_of(lead_tokens)
    rows = jnp.concatenate([pieces[0], pieces[1], lead], 0)
    own_cot, other_cot = by_clip(cot_patches)
    lead_cot = lead_of(cot_lead) * (place == 0).astype(bf16)
    cot = jnp.concatenate([own_cot, lax.ppermute(other_cot, "freq", flip(2, 1)), lead_cot], 0)

    length = lax.dynamic_index_in_dim(lengths, core, 0, keepdims=False)
    spots = np.arange(z.keys) - LEAD_ROWS
    columns = np.where(spots < 0, 1 << 20, spots // z.block * BLOCK_COLS + spots % BLOCK_COLS)
    columns[:LEADS] = -1
    live = jnp.where(jnp.asarray(columns, jnp.int32)[:, None] < length, 0.0, NEG_FILL)
    live = jnp.broadcast_to(live.astype(f32), (z.keys, 128))

    saved = attend(
        z,
        info,
        pieces,
        lead,
        input_weight,
        row(input_bias[:feat]),
        row(input_bias[feat:]),
        row(first_gain),
        row(first_shift),
        live,
    )
    mixed = saved[3]
    paired = clip_count == FF_PARTS // 2
    if not paired:
        share = (clip_count, 2, ff // (2 * clip_count))
        expand_weight = expand_weight.reshape(feat, *share).swapaxes(1, 2).reshape(feat, ff)
        expand_bias = expand_bias.reshape(share).swapaxes(0, 1).reshape(ff)
        reduce_weight = reduce_weight.reshape(*share, feat).swapaxes(0, 1).reshape(ff, feat)
    gain_two, shift_two, wide_bias = row(second_gain), row(second_shift), row(expand_bias)
    ff_args = (cot, gain_two, shift_two, expand_weight, wide_bias, reduce_weight, output_weight)
    sent_r, sent_e, sent_b, *partial = feed(
        z, info, 0, paired, mixed, (rows, row(output_bias), row(reduce_bias)), *ff_args
    )
    kept_r, kept_e, kept_b, block_out, grad_first, grad_low, dwo, small_two = feed(
        z, info, 1, paired, mixed, partial, *ff_args
    )
    swap = lambda x: lax.ppermute(x, "freq", flip(2, 1))
    both = lambda kept, sent: (kept.astype(f32) + swap(sent).astype(f32)).astype(bf16)

    size = ff // FF_PARTS
    ff_half = ff // 2
    reduce_part = both(kept_r, sent_r).reshape(
        clip_count, tm_count, ff_half // (clip_count * tm_count), feat
    )
    reduce_part = scatter_clip(scatter_tm(reduce_part, 1, True))
    split = max(1, tm_count // (FF_PARTS // 2))
    expand_part = both(kept_e, sent_e).reshape(
        FF_PARTS // 2, clip_count, split, feat // (clip_count * split), size
    )
    expand_part = expand_part.transpose(0, 2, 1, 3, 4).reshape(
        tm_count, clip_count, feat // (clip_count * split), size
    )
    expand_part = scatter_clip(scatter_tm(expand_part, 0, False))

    dw, db, gain_sums, own, *sends = attend_back(
        z, info, grad_low, output_weight, saved, input_weight, grad_first[z.rows :]
    )
    received = [
        lax.ppermute(one, "tm", flip(tm_count, k)) for k, one in enumerate(sends, start=1)
    ]
    grad_all = finish(z, info, own, received, rows, row(first_gain), grad_first)

    part_rows = feat // (clip_count * 2 * tm_count)
    attn = jnp.concatenate(
        [
            dw.reshape(3 * z.steps, feat, z.width),
            dwo.reshape(feat, z.steps, z.width).transpose(1, 0, 2),
        ],
        0,
    ).reshape(4 * z.steps, clip_count, 2, tm_count, part_rows, z.width)
    attn = halve(attn, 2, "freq", 0)
    half_count = 2 * z.steps
    attn = jnp.concatenate(
        [scatter_tm(attn[:half_count], 2, True), scatter_tm(attn[half_count:], 2, False)], 0
    )
    attn = scatter_clip(attn.transpose(1, 0, 2, 3))

    flat = lambda x: x[:, 0, :].reshape(-1, feat)
    if paired:
        all_rows = jnp.zeros((FF_PARTS // 2, 2, size), f32)
        all_rows = lax.dynamic_update_slice(all_rows, kept_b[:, 0:1, :], (0, core, 0))
        all_rows = lax.dynamic_update_slice(all_rows, sent_b[:, 0:1, :], (0, 1 - core, 0))
    else:
        all_rows = jnp.where(core == 0, jnp.stack([kept_b[:, 0], sent_b[:, 0]]), jnp.stack([sent_b[:, 0], kept_b[:, 0]]))
        all_rows = all_rows.reshape(2, clip_count, -1).swapaxes(0, 1)
    small = jnp.concatenate(
        [
            db[:, 0, :].reshape(1, feat),
            db[:, 1, :].reshape(1, feat),
            small_two[0:1],
            gain_sums[0:2],
            small_two[1:4],
            all_rows.reshape(-1, feat),
        ],
        0,
    )
    small = sum_all(small)
    here = lax.axis_index("clip")

    def shard(vector):
        count = vector.shape[0] // clip_count
        return lax.dynamic_slice_in_dim(vector, here * count, count, 0)

    input_bias_grad = shard(small[0:2].reshape(-1))
    output_bias_grad, gain_one_grad, shift_one_grad, gain_two_grad, shift_two_grad = (
        shard(small[i]) for i in range(2, 7)
    )
    reduce_bias_grad = shard(small[7])
    expand_bias_grad = shard(small[8:].reshape(-1))

    round_up = lambda x: gather(gather(x, "tm"), "freq").astype(f32)
    reduce_all = round_up(reduce_part)
    reduce_weight_grad = reduce_all.reshape(ff // clip_count, feat)
    expand_all = round_up(expand_part).reshape(
        2, FF_PARTS // 2, split, feat // (clip_count * split), size
    )
    expand_all = expand_all.transpose(2, 3, 1, 0, 4)
    if not paired:
        expand_all = expand_all.swapaxes(2, 3).reshape(feat // clip_count, 2, clip_count, -1)
        expand_all = expand_all.swapaxes(1, 2)
    expand_weight_grad = expand_all.reshape(feat // clip_count, ff)
    attn_all = round_up(attn).transpose(0, 1, 3, 2, 4)
    attn_all = attn_all.reshape(feat // clip_count, 4 * z.steps, z.width)
    input_all = attn_all[:, : 3 * z.steps].reshape(-1, z.steps, 3, z.width)
    input_weight_grad = input_all.transpose(0, 2, 1, 3).reshape(-1, 3 * feat)
    output_weight_grad = attn_all[:, 3 * z.steps :].reshape(-1, feat)

    def by_row(mine):
        theirs = swap(mine)
        first = jnp.where(core == 0, mine, theirs)
        second = jnp.where(core == 0, theirs, mine)
        pair = jnp.stack([first, second], 0).reshape(
            z.clips, z.blocks, z.fr, BLOCK_COLS, feat
        )
        return pair.transpose(2, 1, 3, 0, 4).reshape(z.fr, z.tc, z.clips, feat)

    def patches_of(array):
        mine, other = array[: z.half], array[z.half : z.rows]
        theirs = swap(other)
        first = jnp.where(core == 0, mine, theirs)
        second = jnp.where(core == 0, theirs, mine)
        pair = jnp.stack([first, second], 0).reshape(
            z.clips, z.blocks, z.fr, BLOCK_COLS, feat
        )
        return pair.transpose(2, 1, 3, 0, 4).reshape(z.fr, z.tc, z.clips, feat)

    def leads_of(array):
        mine = array[z.rows : z.rows + LEADS]
        theirs = swap(mine)
        first = jnp.where(core == 0, mine, theirs)
        second = jnp.where(core == 0, theirs, mine)
        return jnp.stack([first, second], 0)

    return (
        patches_of(block_out),
        leads_of(block_out),
        patches_of(grad_all),
        leads_of(grad_all),
        input_weight_grad,
        input_bias_grad,
        output_weight_grad,
        output_bias_grad,
        gain_one_grad,
        shift_one_grad,
        gain_two_grad,
        shift_two_grad,
        expand_weight_grad,
        expand_bias_grad,
        reduce_weight_grad,
        reduce_bias_grad,
    )


def solution(mesh):
    rows = P("freq", "tm", "clip", None)
    lead = P("clip", None, None)
    in_specs = (rows, lead, P("clip")) + (P(),) * 12 + (rows, lead)
    matrix, vector = P("clip", None), P("clip")
    out_specs = (rows, lead, rows, lead) + (matrix, vector) * 2 + (vector,) * 4 + (matrix, vector) * 2
    return jax.shard_map(
        per_device, mesh=mesh, in_specs=in_specs, out_specs=out_specs, check_vma=False
    )
```

```python
import functools
import math

import jax
import jax.numpy as jnp
import numpy as np
from jax import lax
from jax.experimental import pallas as pl
from jax.experimental.pallas import tpu as pltpu
from jax.sharding import PartitionSpec as P

HEADS = 12
EPSILON = 1e-06
NEG_FILL = -1e30
MAX_LENGTH = 101
LEADS = 2
LEAD_ROWS = 16
BLOCK_COLS = 8
GROUP = 4
FF_PARTS = 8
bf16 = jnp.bfloat16
f32 = jnp.float32
VMEM_LIMIT = 56 * 1024 * 1024


def mm(a, b):
    return lax.dot_general(a, b, (((1,), (0,)), ((), ())), preferred_element_type=f32)


def mm_nt(a, b):
    return lax.dot_general(a, b, (((1,), (1,)), ((), ())), preferred_element_type=f32)


def standardize(rows):
    center = rows - jnp.mean(rows, -1, keepdims=True)
    scale_inv = lax.rsqrt(jnp.mean(center * center, -1, keepdims=True) + EPSILON)
    return center * scale_inv, scale_inv


def norm_backward(grad_out, gain_row, normed, scale_inv):
    scaled = grad_out * gain_row
    return scale_inv * (
        scaled
        - jnp.mean(scaled, -1, keepdims=True)
        - normed * jnp.mean(scaled * normed, -1, keepdims=True)
    )


def head_mask(head, width, head_width):
    lane_head = lax.broadcasted_iota(jnp.int32, (1, width), 1) // head_width
    return (lane_head == head).astype(f32)


class Sizes:
    def __init__(self, patches_shape, tm_count, clip_count):
        fr_local, tc_local, clips, feat = patches_shape
        self.fr, self.tc, self.clips, self.feat = fr_local, tc_local, clips, feat
        self.tm, self.clip = tm_count, clip_count
        self.tape = clip_count == 4 and tm_count == 4
        self.tape_rows = 3 * feat * 2 // (2 * clip_count * tm_count)
        self.blocks = tc_local // BLOCK_COLS
        self.half_block = fr_local * BLOCK_COLS
        self.block = 2 * self.half_block
        self.half = self.blocks * self.half_block
        self.rows = 2 * self.half
        self.query_rows = self.rows + LEAD_ROWS
        self.key_blocks = -(-MAX_LENGTH // BLOCK_COLS)
        self.keys = LEAD_ROWS + self.key_blocks * self.block
        self.head_width = feat // HEADS
        self.width = GROUP * self.head_width
        self.steps = HEADS // GROUP
        self.lanes = GROUP * self.rows + 128


def call(kernel, grid, in_specs, out_specs, out_shape, scratch, args, prefetch, flops, moved):
    return pl.pallas_call(
        kernel,
        out_shape=out_shape,
        grid_spec=pltpu.PrefetchScalarGridSpec(
            num_scalar_prefetch=1,
            grid=grid,
            in_specs=in_specs,
            out_specs=out_specs,
            scratch_shapes=scratch,
        ),
        compiler_params=pltpu.CompilerParams(
            dimension_semantics=("arbitrary",), vmem_limit_bytes=VMEM_LIMIT
        ),
        cost_estimate=pl.CostEstimate(flops=flops, bytes_accessed=moved, transcendentals=0),
    )(prefetch, *args)


def whole(shape):
    return pl.BlockSpec(shape, lambda i, info: (0,) * len(shape))


def chunks_of(z):
    full = z.lanes // 256
    spans = [(c * 256, 256) for c in range(full)]
    if z.lanes % 256:
        spans.append((full * 256, z.lanes % 256))
    return spans


def spread_heads(z, rows, out_ref):
    for head in range(GROUP):
        mask = head_mask(head, z.width, z.head_width)
        part = (rows * mask).astype(bf16)
        out_ref[head * z.rows : (head + 1) * z.rows, :] = part[: z.rows]
        at = GROUP * z.rows + head * LEAD_ROWS
        out_ref[at : at + LEAD_ROWS, :] = part[z.rows :]
    at = GROUP * (z.rows + LEAD_ROWS)
    out_ref[at:, :] = jnp.zeros((z.lanes - at, z.width), bf16)


def join_heads(z, spread):
    patch_part, lead_part = None, None
    for head in range(GROUP):
        mask = head_mask(head, z.width, z.head_width)
        at = GROUP * z.rows + head * LEAD_ROWS
        one = spread[head * z.rows : (head + 1) * z.rows] * mask
        two = spread[at : at + LEAD_ROWS] * mask
        patch_part = one if patch_part is None else patch_part + one
        lead_part = two if lead_part is None else lead_part + two
    return jnp.concatenate([patch_part, lead_part], 0)


def attend_kernel(z, info, *refs):
    pieces = refs[: 2 * z.tm]
    (lead, wq, wk, wv, bq, bv, gain, shift, live) = refs[2 * z.tm : 2 * z.tm + 9]
    (q_out, k_out, v_out, mixed_out, p_out, inv_out, hk_t, hq_t, uk, uq) = refs[
        2 * z.tm + 9 : 2 * z.tm + 19
    ]
    spread, total, hk, hq = refs[2 * z.tm + 19 :]
    step = pl.program_id(0)
    me = info[0]

    @pl.when(step == 0)
    def _():
        gain_row, shift_row = gain[...], shift[...]

        def hidden(rows):
            unit, _ = standardize(rows.astype(f32))
            return unit.astype(bf16), (unit * gain_row + shift_row).astype(bf16)

        unit, low = hidden(lead[...])
        uk[0:LEAD_ROWS, :] = unit
        hk[0:LEAD_ROWS, :] = low
        hq[z.rows :, :] = low
        uq[z.rows :, :] = unit
        hb = z.half_block
        for k in range(z.tm):
            source = jnp.bitwise_xor(me, k)
            for half in range(2):
                piece = pieces[2 * k + half]
                for b in range(z.blocks):
                    spot = source * z.blocks + b

                    def place(spot=spot, piece=piece, b=b, half=half, k=k):
                        unit, low = hidden(piece[b * hb : (b + 1) * hb, :])
                        if k == 0:
                            at = half * z.half + b * hb
                            hq[at : at + hb, :] = low
                            uq[at : at + hb, :] = unit

                        @pl.when(spot < z.key_blocks)
                        def _():
                            at = pl.multiple_of(LEAD_ROWS + spot * z.block + half * hb, 16)
                            uk[pl.ds(at, hb), :] = unit
                            hk[pl.ds(at, hb), :] = low

                    place()
        hk_t[...] = jnp.transpose(hk[...])
        hq_t[...] = jnp.transpose(hq[...])

    hk_all = hk[...]
    q = (mm(hq[...], wq[...]) + bq[...]).astype(bf16)
    q_out[...] = q
    spread_heads(z, q.astype(f32) * (z.head_width**-0.5), spread)
    k = mm(hk_all, wk[...]).astype(bf16)
    k_out[...] = k
    v = (mm(hk_all, wv[...]) + bv[...]).astype(bf16)
    v_out[...] = v
    live_col = live[...]
    for at, size in chunks_of(z):
        scores = mm_nt(k, spread[at : at + size, :])
        scores = scores + jnp.concatenate([live_col] * (size // 128), 1)
        peak = jnp.max(scores, 0, keepdims=True)
        weights = jnp.exp(scores - peak)
        total[0:1, at : at + size] = jnp.sum(weights, 0, keepdims=True)
        p_out[0, :, at : at + size] = weights.astype(bf16)
    inverse = 1.0 / total[0:1, :]
    inv_out[0] = jnp.broadcast_to(inverse, (8, z.lanes))
    mixed = mm(jnp.transpose(v), p_out[0]) * inverse
    mixed_out[...] = join_heads(z, jnp.transpose(mixed))


def attend(z, me_info, pieces, lead, weight, bias_q, bias_v, gain, shift, live):
    feat, width, nk, nq, nl = z.feat, z.width, z.keys, z.query_rows, z.lanes
    col = lambda offset: pl.BlockSpec((feat, width), lambda i, info: (0, offset * z.steps + i))
    in_specs = (
        [whole((z.half, feat))] * (2 * z.tm)
        + [whole((LEAD_ROWS, feat)), col(0), col(1), col(2)]
        + [pl.BlockSpec((1, width), lambda i, info: (0, i))] * 2
        + [whole((1, feat))] * 2
        + [whole((nk, 128))]
    )
    by_col = lambda rows: pl.BlockSpec((rows, width), lambda i, info: (0, i))
    out_specs = [
        by_col(nq),
        by_col(nk),
        by_col(nk),
        by_col(nq),
        pl.BlockSpec((1, nk, nl), lambda i, info: (i, 0, 0)),
        pl.BlockSpec((1, 8, nl), lambda i, info: (i, 0, 0)),
        whole((feat, nk)),
        whole((feat, nq)),
        whole((nk, feat)),
        whole((nq, feat)),
    ]
    out_shape = [
        jax.ShapeDtypeStruct((nq, feat), bf16),
        jax.ShapeDtypeStruct((nk, feat), bf16),
        jax.ShapeDtypeStruct((nk, feat), bf16),
        jax.ShapeDtypeStruct((nq, feat), f32),
        jax.ShapeDtypeStruct((z.steps, nk, nl), bf16),
        jax.ShapeDtypeStruct((z.steps, 8, nl), f32),
        jax.ShapeDtypeStruct((feat, nk), bf16),
        jax.ShapeDtypeStruct((feat, nq), bf16),
        jax.ShapeDtypeStruct((nk, feat), bf16),
        jax.ShapeDtypeStruct((nq, feat), bf16),
    ]
    return call(
        functools.partial(attend_kernel, z),
        (z.steps,),
        in_specs,
        out_specs,
        out_shape,
        [
            pltpu.VMEM((nl, width), bf16),
            pltpu.VMEM((8, nl), f32),
            pltpu.VMEM((nk, feat), bf16),
            pltpu.VMEM((nq, feat), bf16),
        ],
        (*pieces, lead, weight, weight, weight, bias_q, bias_v, gain, shift, live),
        me_info,
        2 * feat * feat * (nq + 2 * nk) + 4 * z.steps * nk * nl * width,
        z.steps * nk * nl * 2,
    )


def feed_kernel(z, first, last, info, *refs):
    refs = list(refs)
    take = lambda n: [refs.pop(0) for _ in range(n)]
    if first:
        mixed, rows, wo, bo, rb = take(5)
    else:
        (mixed, wo, sum_in, out_in, grad_in) = take(5)
    cot, gain, shift, we, be, wr = take(6)
    dwr, dwe, dbe = take(3)
    if last:
        block_mine, block_send, grad_first, grad_low, dwo_send, dwo_keep, small = take(7)
    else:
        sum_out, acc_out, grad_out = take(3)
    unit, inv, low, low_t, acc, grad = take(6)
    hold = take(1)[0] if last else None
    step = pl.program_id(0)
    gain_row = gain[...]

    @pl.when(step == 0)
    def _():
        if first:
            total = rows[...].astype(f32) + mm(mixed[...].astype(bf16), wo[...]) + bo[...]
            sum_out[...] = total
            acc[...] = total + rb[...]
            grad[...] = jnp.zeros_like(grad)
        else:
            total = sum_in[...]
            acc[...] = out_in[...]
            grad[...] = grad_in[...]
        normed, scale_inv = standardize(total)
        unit[...] = normed
        inv[...] = jnp.broadcast_to(scale_inv, inv.shape)
        hidden = (normed * gain_row + shift[...]).astype(bf16)
        low[...] = hidden
        low_t[...] = jnp.transpose(hidden)

    cot_low = cot[...]
    expand, reduce = we[...], wr[...]
    expanded = mm(low[...], expand) + be[...]
    cdf = 0.5 * (1.0 + lax.erf(expanded * math.sqrt(0.5)))
    pdf = jnp.exp(-0.5 * expanded * expanded) * (1.0 / math.sqrt(2.0 * math.pi))
    activated = (expanded * cdf).astype(bf16)
    acc[...] += mm(activated, reduce)
    reduce_grad = mm(jnp.transpose(activated), cot_low).astype(bf16)
    if z.tape:
        part = reduce_grad.shape[0] // z.tm
        for t in range(z.tm):
            for lane in range(z.feat // 128):
                dwr[0, t, lane * part : (lane + 1) * part, :] = reduce_grad[
                    t * part : (t + 1) * part, lane * 128 : (lane + 1) * 128
                ]
    else:
        dwr[0] = reduce_grad
    grad_expanded = (mm_nt(cot_low, reduce) * (cdf + expanded * pdf)).astype(bf16)
    expand_grad = mm(low_t[...], grad_expanded).astype(bf16)
    if z.tape:
        part = z.feat // z.clip
        for c in range(z.clip):
            for lane in range(expand_grad.shape[1] // 128):
                dwe[0, c, lane * part : (lane + 1) * part, :] = expand_grad[
                    c * part : (c + 1) * part, lane * 128 : (lane + 1) * 128
                ]
    else:
        dwe[0] = expand_grad
    dbe[0] = jnp.broadcast_to(
        jnp.sum(grad_expanded.astype(f32), 0, keepdims=True), dbe.shape[1:]
    )
    grad[...] += mm_nt(grad_expanded, expand)

    @pl.when(step == pl.num_programs(0) - 1)
    def _():
        if last:
            block_mine[...] = acc[: z.half, :].astype(bf16)
            block_send[...] = acc[z.half :, :].astype(bf16)
            rows_grad = cot_low.astype(f32)
            normed, hidden_grad = unit[...], grad[...]
            back = rows_grad + norm_backward(hidden_grad, gain_row, normed, inv[:, 0:1])
            grad_first[...] = back
            back_low = back.astype(bf16)
            grad_low[...] = back_low
            dwo = mm(jnp.transpose(mixed[...].astype(bf16)), back_low)
            for j in range(z.steps):
                block = dwo[:, j * z.width : (j + 1) * z.width]
                if z.tape:
                    store_split(z, info[1], block, hold, dwo_send, dwo_keep, j)
                else:
                    dwo_keep[j] = block.astype(bf16)
            small[...] = jnp.zeros_like(small)
            small[0:1, :] = jnp.sum(back_low.astype(f32), 0, keepdims=True)
            small[1:2, :] = jnp.sum(hidden_grad * normed, 0, keepdims=True)
            small[2:3, :] = jnp.sum(hidden_grad, 0, keepdims=True)
            small[3:4, :] = jnp.sum(rows_grad, 0, keepdims=True)
        else:
            acc_out[...] = acc[...]
            grad_out[...] = grad[...]


def feed(z, info, part, paired, mixed, given, cot, gain, shift, expand, expand_bias, reduce, wo):
    first, last = part == 0, part == 1
    feat, ff = expand.shape
    size = ff // FF_PARTS
    steps = FF_PARTS // 2
    nq = z.query_rows

    def chunk(i, info):
        half = 1 - info[1] if first else info[1]
        return 2 * i + half if paired else steps * half + i

    rows_spec = whole((nq, feat))
    if first:
        head_specs = [rows_spec, rows_spec, whole((feat, feat)), whole((1, feat)), whole((1, feat))]
        head_args = (mixed, given[0], wo, given[1], given[2])
    else:
        head_specs = [rows_spec, whole((feat, feat)), rows_spec, rows_spec, rows_spec]
        head_args = (mixed, wo, *given)
    in_specs = head_specs + [
        rows_spec,
        whole((1, feat)),
        whole((1, feat)),
        pl.BlockSpec((feat, size), lambda i, info: (0, chunk(i, info))),
        pl.BlockSpec((1, size), lambda i, info: (0, chunk(i, info))),
        pl.BlockSpec((size, feat), lambda i, info: (chunk(i, info), 0)),
    ]
    if z.tape:
        shapes = [(z.tm, size * feat // (128 * z.tm), 128), (z.clip, size * feat // (128 * z.clip), 128)]
    else:
        shapes = [(size, feat), (feat, size)]
    out_specs = [
        pl.BlockSpec((1, *shape), lambda i, info, n=len(shape): (i,) + (0,) * n) for shape in shapes
    ] + [
        pl.BlockSpec((1, 8, size), lambda i, info: (i, 0, 0)),
    ]
    out_shape = [
        jax.ShapeDtypeStruct((steps, *shapes[0]), bf16),
        jax.ShapeDtypeStruct((steps, *shapes[1]), bf16),
        jax.ShapeDtypeStruct((steps, 8, size), f32),
    ]
    wide = jax.ShapeDtypeStruct((nq, feat), f32)
    narrow = jax.ShapeDtypeStruct((nq, feat), bf16)
    if last:
        split = (z.clip, z.tm, z.tape_rows, 128) if z.tape else (3, feat, z.width)
        parts = [(z.half, feat), (nq - z.half, feat)]
        out_specs += [whole(part) for part in parts]
        out_specs += [rows_spec, rows_spec, whole(split), whole(split), whole((8, feat))]
        out_shape += [jax.ShapeDtypeStruct(part, bf16) for part in parts]
        out_shape += [
            wide,
            narrow,
            jax.ShapeDtypeStruct(split, bf16),
            jax.ShapeDtypeStruct(split, bf16),
            jax.ShapeDtypeStruct((8, feat), f32),
        ]
    else:
        out_specs += [rows_spec] * 3
        out_shape += [wide] * 3
    return call(
        functools.partial(feed_kernel, z, first, last),
        (steps,),
        in_specs,
        out_specs,
        out_shape,
        [
            pltpu.VMEM((nq, feat), f32),
            pltpu.VMEM((nq, 128), f32),
            pltpu.VMEM((nq, feat), bf16),
            pltpu.VMEM((feat, nq), bf16),
            pltpu.VMEM((nq, feat), f32),
            pltpu.VMEM((nq, feat), f32),
        ]
        + [pltpu.VMEM((feat, z.width), f32)] * last,
        (*head_args, cot, gain, shift, expand, expand_bias, reduce),
        info,
        2 * nq * feat * (ff * 3 + feat),
        4 * feat * ff,
    )


def store_split(z, core, value, hold, sent, kept, j):
    hold[...] = value
    half = z.feat // (2 * z.clip)
    part = half // 2
    for c in range(z.clip):
        for out, whose in ((kept, core), (sent, 1 - core)):
            for t in range(z.tm):
                at = pl.multiple_of((2 * c + whose) * half + (t // 2) * part, 16)
                lanes = slice((t % 2) * 128, (t % 2) * 128 + 128)
                out[c, t, j * part : (j + 1) * part, :] = hold[pl.ds(at, part), lanes].astype(bf16)


def plain_to_tape(z, blocks, core):
    lanes = z.width // 128
    x = blocks.reshape(3, z.clip, 2, z.tm // lanes, -1, lanes, 128)
    x = x.transpose(2, 1, 3, 5, 0, 4, 6).reshape(2, z.clip, z.tm, -1, 128)
    return pick(x, 0, 1 - core), pick(x, 0, core)


def attend_back_kernel(z, info, *refs):
    refs = list(refs)
    take = lambda n: [refs.pop(0) for _ in range(n)]
    ga, wo, q, k, v, mixed, p, inv, hk_t, hq_t = take(10)
    sent, kept, db, kv_out, q_grad_out = take(5)
    q_spread, g_spread, ds, hold = take(4)
    core = info[1]
    scale = z.head_width**-0.5

    spread_heads(z, q[...].astype(f32) * scale, q_spread)
    grad = mm_nt(ga[...], wo[...]).astype(bf16).astype(f32)
    inverse = inv[0, 0:1, :]
    inverse_col = jnp.transpose(jnp.broadcast_to(inverse, (128, z.lanes)))[:, 0:1]
    product = grad * mixed[...]
    dots = []
    for head in range(GROUP):
        mask = head_mask(head, z.width, z.head_width)
        at = GROUP * z.rows + head * LEAD_ROWS
        part = grad * mask
        low = (part[: z.rows] * inverse_col[head * z.rows : (head + 1) * z.rows]).astype(bf16)
        g_spread[head * z.rows : (head + 1) * z.rows, :] = low
        low = (part[z.rows :] * inverse_col[at : at + LEAD_ROWS]).astype(bf16)
        g_spread[at : at + LEAD_ROWS, :] = low
        dots.append(jnp.sum(product * mask, 1, keepdims=True))
    end = GROUP * (z.rows + LEAD_ROWS)
    g_spread[end:, :] = jnp.zeros((z.lanes - end, z.width), bf16)
    dot_col = jnp.concatenate(
        [d[: z.rows] for d in dots]
        + [d[z.rows :] for d in dots]
        + [jnp.zeros((z.lanes - end, 1), f32)],
        0,
    )
    dot_row = jnp.transpose(jnp.broadcast_to(dot_col, (z.lanes, 128)))[0:1, :] * inverse
    v_all, k_all = v[...], k[...]
    for at, size in chunks_of(z):
        grad_weights = mm_nt(v_all, g_spread[at : at + size, :])
        weights = p[0, :, at : at + size].astype(f32)
        ds[:, at : at + size] = (weights * (grad_weights - dot_row[:, at : at + size])).astype(bf16)
    ds_all = ds[...]
    grad_v = mm(p[0], g_spread[...])
    grad_k = mm(ds_all, q_spread[...])
    grad_q = mm(jnp.transpose(k_all), ds_all)
    grad_q = (join_heads(z, jnp.transpose(grad_q)) * scale).astype(bf16)
    grad_v = grad_v.astype(bf16)
    grad_k = grad_k.astype(bf16)
    db[...] = jnp.concatenate(
        [
            jnp.sum(grad_q.astype(f32), 0, keepdims=True),
            jnp.sum(grad_v.astype(f32), 0, keepdims=True),
            jnp.zeros((6, z.width), f32),
        ],
        0,
    )
    for j, grad in enumerate((mm(hq_t[...], grad_q), mm(hk_t[...], grad_k), mm(hk_t[...], grad_v))):
        if z.tape:
            store_split(z, core, grad, hold, sent, kept, j)
        else:
            kept[j] = grad.astype(bf16)
    kv_out[:, : z.width] = grad_k
    kv_out[:, z.width :] = grad_v
    q_grad_out[...] = grad_q


def keys_back_kernel(z, info, *refs):
    refs = list(refs)
    take = lambda n: [refs.pop(0) for _ in range(n)]
    uk, uq, weight, first_lead, feed_small = take(5)
    db, grad_kv, grad_q = take(z.steps), take(z.steps), take(z.steps)
    own, small_out = take(2)
    sends = take(4 if z.tape else z.tm - 1)
    keys_acc, query_acc, small = take(3)
    me = info[0]
    keys_grad, query_grad = 0.0, 0.0
    for i in range(z.steps):
        block = lambda part: weight[
            :, (part * z.steps + i) * z.width : (part * z.steps + i + 1) * z.width
        ]
        query_grad += mm_nt(grad_q[i][...], block(0))
        keys_grad += mm_nt(grad_kv[i][:, : z.width], block(1))
        keys_grad += mm_nt(grad_kv[i][:, z.width :], block(2))
    keys_acc[...] = keys_grad
    query_acc[...] = query_grad
    small[...] = jnp.zeros_like(small)
    for i in range(z.steps):
        small[0:2, i * z.width : (i + 1) * z.width] = db[i][0:2, :]
    small[2:3, :] = jnp.sum(keys_grad * uk[...].astype(f32), 0, keepdims=True) + jnp.sum(
        query_grad * uq[...].astype(f32), 0, keepdims=True
    )
    small[3:4, :] = jnp.sum(keys_grad, 0, keepdims=True) + jnp.sum(query_grad, 0, keepdims=True)
    small[4:12, :] = feed_small[...]
    if z.tape:
        for lane in range(z.feat // 128):
            small_out[lane * 16 : lane * 16 + 16, :] = small[
                :, lane * 128 : lane * 128 + 128
            ].astype(bf16)
    else:
        small_out[...] = small[...]
    lead = keys_acc[0:LEAD_ROWS, :] + query_acc[z.rows :, :]
    high = first_lead[...].astype(bf16)
    rest = (first_lead[...] - high.astype(f32)).astype(bf16)
    pair = lambda a: a[0:LEADS]
    packed = jnp.concatenate(
        [pair(lead), pair(high.astype(f32)), pair(rest.astype(f32)), jnp.zeros((10, z.feat), f32)], 0
    )
    small_high = small[...].astype(bf16)
    small_low = (small[...] - small_high.astype(f32)).astype(bf16)
    own[z.rows :, :] = packed
    packed = packed.astype(bf16)
    hb = z.half_block

    def chunk(k, half, out, at):
        source = jnp.bitwise_xor(me, k)
        for b in range(z.blocks):
            spot = source * z.blocks + b
            from_ = pl.multiple_of(
                LEAD_ROWS + jnp.minimum(spot, z.key_blocks - 1) * z.block + half * hb, 16
            )
            rows = keys_acc[pl.ds(from_, hb), :] * (spot < z.key_blocks).astype(f32)
            to = at + b * hb
            if k == 0:
                queries = half * z.half + b * hb
                rows = rows + query_acc[queries : queries + hb, :]
            out[to : to + hb, :] = rows.astype(out.dtype)

    chunk(0, 0, own, 0)
    chunk(0, 1, own, z.half)
    if z.tape:
        along_x, along_y, mid_x, mid_y = sends
        chunk(1, 0, along_x, 0)
        chunk(3, 0, along_x, z.half)
        along_x[z.rows :, :] = packed
        chunk(2, 1, along_y, 0)
        chunk(3, 1, along_y, z.half)
        chunk(2, 0, mid_x, 0)
        chunk(1, 1, mid_y, 0)
    else:
        for k, one in enumerate(sends, start=1):
            chunk(k, 0, one, 0)
            chunk(k, 1, one, z.half)
            one[z.rows :, :] = packed


def attend_back(z, info, i, ga, wo, saved):
    q, k, v, mixed, p, inv, hk_t, hq_t = saved[:8]
    feat, width, nk, nq, nl = z.feat, z.width, z.keys, z.query_rows, z.lanes
    by_col = lambda rows: pl.BlockSpec((rows, width), lambda _, info: (0, i))
    in_specs = [
        whole((nq, feat)),
        pl.BlockSpec((width, feat), lambda _, info: (i, 0)),
        by_col(nq),
        by_col(nk),
        by_col(nk),
        by_col(nq),
        pl.BlockSpec((1, nk, nl), lambda _, info: (i, 0, 0)),
        pl.BlockSpec((1, 8, nl), lambda _, info: (i, 0, 0)),
        whole((feat, nk)),
        whole((feat, nq)),
    ]
    if z.tape:
        part = (z.clip, z.tm, z.tape_rows, 128)
    else:
        part = (3, feat, width)
    sent, kept, *rest = call(
        functools.partial(attend_back_kernel, z),
        (1,),
        in_specs,
        [whole(part), whole(part), whole((8, width)), whole((nk, 2 * width)), whole((nq, width))],
        [
            jax.ShapeDtypeStruct(part, bf16),
            jax.ShapeDtypeStruct(part, bf16),
            jax.ShapeDtypeStruct((8, width), f32),
            jax.ShapeDtypeStruct((nk, 2 * width), bf16),
            jax.ShapeDtypeStruct((nq, width), bf16),
        ],
        [
            pltpu.VMEM((nl, width), bf16),
            pltpu.VMEM((nl, width), bf16),
            pltpu.VMEM((nk, nl), bf16),
            pltpu.VMEM((feat, width), f32),
        ],
        [ga, wo, q, k, v, mixed, p, inv, hk_t, hq_t],
        info,
        16 * nk * nl * width,
        nk * nl * 2,
    )
    if not z.tape:
        sent, kept = plain_to_tape(z, kept, info[1])
    return sent, kept, rest


def keys_back(z, info, saved, weight, first_lead, feed_small, steps):
    feat, width, nk, nq = z.feat, z.width, z.keys, z.query_rows
    uk, uq = saved[8:]
    in_specs = [whole((nk, feat)), whole((nq, feat)), whole(weight.shape)]
    in_specs += [pl.BlockSpec((LEAD_ROWS, feat), lambda _, info: (z.rows // LEAD_ROWS, 0))]
    in_specs += [whole((8, feat))]
    in_specs += [whole((8, width))] * z.steps
    in_specs += [whole((nk, 2 * width))] * z.steps + [whole((nq, width))] * z.steps
    if z.tape:
        sends = [(nq, feat), (z.rows, feat), (z.half, feat), (z.half, feat)]
    else:
        sends = [(nq, feat)] * (z.tm - 1)
    small = (16 * feat // 128, 128) if z.tape else (16, feat)
    return call(
        functools.partial(keys_back_kernel, z),
        (1,),
        in_specs,
        [whole((nq, feat)), whole(small)] + [whole(shape) for shape in sends],
        [
            jax.ShapeDtypeStruct((nq, feat), f32),
            jax.ShapeDtypeStruct(small, bf16 if z.tape else f32),
        ]
        + [jax.ShapeDtypeStruct(shape, bf16) for shape in sends],
        [pltpu.VMEM((nk, feat), f32), pltpu.VMEM((nq, feat), f32), pltpu.VMEM((16, feat), f32)],
        (uk, uq, weight, first_lead, feed_small)
        + tuple(step[j] for j in range(3) for step in steps),
        info,
        4 * feat * feat * (nq + 2 * nk),
        nk * feat * 4,
    )


def finish_kernel(z, info, *refs):
    *received, rows, gain, grad_first, out_mine, out_send = refs[1:]
    own = refs[0]
    mine = own[z.rows :].astype(bf16).astype(f32)
    if z.tape:
        got_x, got_y, got_xy, got_yx = (one[...].astype(f32) for one in received)
        first = own[: z.half] + got_x[: z.half] + got_xy[: z.half]
        second = own[z.half : z.rows] + got_y[: z.half] + got_yx
        lead = (mine + got_x[z.rows :]).astype(bf16).astype(f32) + got_xy[z.half :]
        total = jnp.concatenate([first, second, lead], 0)
    else:
        terms = [one[...].astype(f32) for one in received]
        leads = [mine] + [one[z.rows :] for one in terms]
        while len(leads) > 1:
            leads = [a + b for a, b in zip(leads[::2], leads[1::2])]
        total = jnp.concatenate([own[: z.rows] + sum(t[: z.rows] for t in terms), leads[0]], 0)
    normed, scale_inv = standardize(rows[...].astype(f32))
    back = norm_backward(total, gain[...], normed, scale_inv)
    rows_grad = (back[: z.rows] + grad_first[0 : z.rows, :]).astype(bf16)
    out_mine[...] = rows_grad[: z.half]
    out_send[0 : z.half, :] = rows_grad[z.half :]
    lead = total[z.rows :]
    lead_first = lead[LEADS : 2 * LEADS] + lead[2 * LEADS : 3 * LEADS]
    out_send[z.half :, :] = jnp.concatenate(
        [back[z.rows : z.rows + LEADS] + lead_first, jnp.zeros((LEAD_ROWS - LEADS, z.feat), f32)], 0
    ).astype(bf16)


def finish(z, info, own, received, rows, gain, grad_first):
    feat, nq = z.feat, z.query_rows
    return call(
        functools.partial(finish_kernel, z),
        (1,),
        [whole(one.shape) for one in (own, *received)]
        + [whole((nq, feat)), whole((1, feat)), whole((nq, feat))],
        [whole((z.half, feat)), whole((nq - z.half, feat))],
        [
            jax.ShapeDtypeStruct((z.half, feat), bf16),
            jax.ShapeDtypeStruct((nq - z.half, feat), bf16),
        ],
        [],
        (own, *received, rows, gain, grad_first),
        info,
        nq * feat * 20,
        nq * feat * 20,
    )


def place_blocks(z, t, whose, tape, row, out, lane_at):
    half = z.feat // (2 * z.clip)
    part = half // 2
    at = pl.multiple_of(whose * half + (t // 2) * part, 16)
    for j in range(3):
        block = tape[row + j * part : row + (j + 1) * part, :].astype(f32)
        lane = pl.multiple_of(lane_at(j) + (t % 2) * 128, 128)
        out[pl.ds(at, part), pl.ds(lane, 128)] = block


def assemble_feed_kernel(z, ff, info, *refs):
    me, core = info[0], info[1]
    expand_out, reduce_out, output_out = refs[8:]
    size = ff // FF_PARTS
    count = size * z.feat // (128 * z.tm)
    step = count + z.tape_rows
    part_r, part_e = size // z.tm, z.feat // z.clip
    for whose, (p_0, q_0, p_1, q_1) in ((core, refs[:4]), (1 - core, refs[4:8])):
        for k, tape, base in ((0, p_0, 0), (1, p_0, step), (2, p_1, 0), (3, p_1, step)):
            t = jnp.bitwise_xor(me, k)
            at = pl.multiple_of(whose * size + t * part_r, 16)
            for lane in range(z.feat // 128):
                block = tape[base + lane * part_r : base + (lane + 1) * part_r, :]
                reduce_out[pl.ds(at, part_r), lane * 128 : (lane + 1) * 128] = block.astype(f32)
            place_blocks(z, t, whose, tape, base + count, output_out, lambda j: j * z.width)
        for k, tape, base in ((0, q_0, 0), (2, q_0, step), (1, q_1, 0), (3, q_1, step)):
            at = (2 * jnp.bitwise_xor(me, k) + whose) * size
            for lane in range(size // 128):
                block = tape[base + lane * part_e : base + (lane + 1) * part_e, :]
                to = pl.multiple_of(at + lane * 128, 128)
                expand_out[:, pl.ds(to, 128)] = block.astype(f32)


def assemble_input_kernel(z, info, *refs):
    me, core = info[0], info[1]
    first, late, input_out = refs[:8], refs[8:16], refs[16]
    for core_of, whose in ((0, core), (1, 1 - core)):
        for n, k in enumerate((0, 2, 1, 3)):
            t = jnp.bitwise_xor(me, k)
            tape = late[core_of * 4 + k]
            parts = ((0, first[core_of * 4 + n], 0), (1, tape, 0), (2, tape, z.tape_rows))
            for i, tape, row in parts:
                lane_at = lambda j: j * z.feat + i * z.width
                place_blocks(z, t, whose, tape, row, input_out, lane_at)


def assemble(z, info, tapes, late, ff):
    rows = z.feat // z.clip
    shapes = [(rows, ff), (ff // z.clip, z.feat), (rows, z.feat)]
    feed_grads = call(
        functools.partial(assemble_feed_kernel, z, ff),
        (1,),
        [whole(tapes[0].shape)] * 8,
        [whole(shape) for shape in shapes],
        [jax.ShapeDtypeStruct(shape, f32) for shape in shapes],
        [],
        tapes,
        info,
        1000,
        32 * tapes[0].size,
    )
    last = tapes[0].shape[0] // z.tape_rows - 1
    at = lambda n: pl.BlockSpec((z.tape_rows, 128), lambda i, info: (n, 0))
    first_specs = [at(last // 2), at(last)] * 4
    first = [tapes[1], tapes[1], tapes[3], tapes[3], tapes[5], tapes[5], tapes[7], tapes[7]]
    input_grad = call(
        functools.partial(assemble_input_kernel, z),
        (1,),
        first_specs + [whole((2 * z.tape_rows, 128))] * 8,
        whole((rows, 3 * z.feat)),
        jax.ShapeDtypeStruct((rows, 3 * z.feat), f32),
        [],
        (*first, *late),
        info,
        1000,
        64 * late[0].size,
    )
    return (*feed_grads, input_grad)


def flip(count, k):
    return [(i, i ^ k) for i in range(count)]


def bit_of(index, bit):
    return (index >> bit) & 1


def bits_of(count):
    return count.bit_length() - 1


def pick(x, dim, index):
    return lax.dynamic_index_in_dim(x, index, dim, keepdims=False)


def add(kept, got):
    return (kept.astype(f32) + got.astype(f32)).astype(bf16)


def by_bits(x, dim, count):
    return x.reshape(x.shape[:dim] + (2,) * bits_of(count) + x.shape[dim + 1 :])


def halves(x, dim, axis, bit):
    mine = bit_of(lax.axis_index(axis), bit)
    return pick(x, dim, 1 - mine), pick(x, dim, mine)


def across(x, axis, bit):
    return lax.ppermute(x, axis, flip(lax.axis_size(axis), 1 << bit))


def scatter(x, dim, axis, bits):
    for bit in bits:
        sent, kept = halves(x, dim, axis, bit)
        x = add(kept, across(sent, axis, bit))
    return x


def scatter_up(x, dim, axis, bits):
    for bit in bits:
        at = dim + bits_of(lax.axis_size(axis)) - 1 - bit
        sent, kept = halves(x, at, axis, bit)
        x = add(kept, across(sent, axis, bit))
    return x


def peers(x, dim, axis):
    me = lax.axis_index(axis)
    return [pick(x, dim, me ^ k) for k in range(1, lax.axis_size(axis))]


def to_peers(sent, axis):
    count = lax.axis_size(axis)
    return [lax.ppermute(one, axis, flip(count, k)) for k, one in enumerate(sent, start=1)]


def add_all(own, got):
    total = own.astype(f32)
    for one in got:
        total = total + one.astype(f32)
    return total.astype(bf16)


def in_order(x, got, axis):
    me = lax.axis_index(axis)
    out = jnp.zeros((1 + len(got),) + x.shape, x.dtype)
    for k, one in enumerate([x, *got]):
        out = lax.dynamic_update_index_in_dim(out, one, me ^ k, 0)
    return out


def tie(*values):
    return lax.optimization_barrier(values)


def per_device(
    patches,
    lead_tokens,
    lengths,
    input_weight,
    input_bias,
    output_weight,
    output_bias,
    first_gain,
    first_shift,
    second_gain,
    second_shift,
    expand_weight,
    expand_bias,
    reduce_weight,
    reduce_bias,
    cot_patches,
    cot_lead,
):
    tm_count = lax.axis_size("tm")
    clip_count = lax.axis_size("clip")
    z = Sizes(patches.shape, tm_count, clip_count)
    feat, ff = expand_weight.shape
    core, place = lax.axis_index("freq"), lax.axis_index("tm")
    info = jnp.stack([place, core]).astype(jnp.int32)
    row = lambda vector: vector.astype(f32)[None, :]

    def by_clip(array):
        parts = array.reshape(z.fr, z.blocks, BLOCK_COLS, z.clips, feat)
        parts = parts.transpose(3, 1, 0, 2, 4).reshape(z.clips, z.half, feat)
        return (
            lax.dynamic_index_in_dim(parts, core, 0, keepdims=False),
            lax.dynamic_index_in_dim(parts, 1 - core, 0, keepdims=False),
        )

    def lead_of(array):
        mine = lax.dynamic_index_in_dim(array, core, 0, keepdims=False)
        return jnp.pad(mine, ((0, LEAD_ROWS - LEADS), (0, 0)))

    own_half, other_half = by_clip(patches)
    pieces = []
    for k in range(tm_count):
        pieces.append(lax.ppermute(own_half, "tm", flip(tm_count, k)) if k else own_half)
        pieces.append(
            lax.ppermute(other_half, ("freq", "tm"), flip(2 * tm_count, tm_count | k))
        )
    lead = lead_of(lead_tokens)
    rows = jnp.concatenate([pieces[0], pieces[1], lead], 0)
    own_cot, other_cot = by_clip(cot_patches)
    lead_cot = lead_of(cot_lead) * (place == 0).astype(bf16)
    cot = jnp.concatenate([own_cot, lax.ppermute(other_cot, "freq", flip(2, 1)), lead_cot], 0)

    length = lax.dynamic_index_in_dim(lengths, core, 0, keepdims=False)
    spots = np.arange(z.keys) - LEAD_ROWS
    columns = np.where(spots < 0, 1 << 20, spots // z.block * BLOCK_COLS + spots % BLOCK_COLS)
    columns[:LEADS] = -1
    live = jnp.where(jnp.asarray(columns, jnp.int32)[:, None] < length, 0.0, NEG_FILL)
    live = jnp.broadcast_to(live.astype(f32), (z.keys, 128))

    saved = attend(
        z,
        info,
        pieces,
        lead,
        input_weight,
        row(input_bias[:feat]),
        row(input_bias[feat:]),
        row(first_gain),
        row(first_shift),
        live,
    )
    mixed = saved[3]
    paired = clip_count == FF_PARTS // 2
    if not paired:
        share = (clip_count, 2, ff // (2 * clip_count))
        expand_weight = expand_weight.reshape(feat, *share).swapaxes(1, 2).reshape(feat, ff)
        expand_bias = expand_bias.reshape(share).swapaxes(0, 1).reshape(ff)
        reduce_weight = reduce_weight.reshape(*share, feat).swapaxes(0, 1).reshape(ff, feat)
    gain_two, shift_two, wide_bias = row(second_gain), row(second_shift), row(expand_bias)
    ff_args = (cot, gain_two, shift_two, expand_weight, wide_bias, reduce_weight, output_weight)
    swap = lambda x: across(x, "freq", 0)
    size = ff // FF_PARTS
    half = clip_count // 2
    tm_bits, clip_bits = bits_of(tm_count), bits_of(clip_count)
    low_bits, high_bits = list(range(tm_bits)), list(range(tm_bits))[::-1]
    split = max(1, tm_count // (FF_PARTS // 2))

    sent_r, sent_e, sent_b, *partial = feed(
        z, info, 0, paired, mixed, (rows, row(output_bias), row(reduce_bias)), *ff_args
    )
    sent_r, sent_e, *partial = tie(sent_r, sent_e, *partial)
    got_r, got_e = swap(sent_r), swap(sent_e)
    kept_r, kept_e, kept_b, *given = feed(z, info, 1, paired, mixed, partial, *ff_args)
    block_mine, block_send, grad_first, grad_low, sent_o, kept_o, small_two = given
    kept_r, kept_e, got_r, got_e, grad_low = tie(kept_r, kept_e, got_r, got_e, grad_low)
    sum_r, sum_e = add(kept_r, got_r), add(kept_e, got_e)
    if not z.tape:
        rows_r, rows_e = ff // (2 * clip_count * tm_count), feat // (clip_count * split)
        sum_r = sum_r.reshape(clip_count, tm_count, rows_r, feat // 128, 128).swapaxes(2, 3)
        sum_e = sum_e.reshape(-1, clip_count, split, rows_e, size // 128, 128)
        sum_e = sum_e.transpose(0, 2, 1, 4, 3, 5)
        sent_o, kept_o = plain_to_tape(z, kept_o, core)
    sum_r = sum_r.reshape(clip_count, tm_count, -1, 128)
    sum_e = sum_e.reshape(tm_count, clip_count, -1, 128).swapaxes(0, 1)
    out_r, own_r = halves(by_bits(sum_r, 1, tm_count), 1 + tm_bits - 1, "tm", 0)
    out_e, own_e = halves(by_bits(sum_e, 1, tm_count), 1, "tm", tm_bits - 1)
    grad_low, sent_o, block_send, out_ra, out_ea, out_rb, out_eb = tie(
        grad_low, sent_o, block_send, out_r[:half], out_e[:half], out_r[half:], out_e[half:]
    )
    across_r = lambda x: across(x, "tm", 0)
    across_e = lambda x: across(x, "tm", tm_bits - 1)
    across_z = lambda x: across(x, "clip", clip_bits - 1)
    halves_z = lambda x: halves(by_bits(x, 0, clip_count), 0, "clip", clip_bits - 1)
    rest_z = lambda x: scatter(x, 0, "clip", range(clip_bits - 1)[::-1])

    got_ra, got_ea, got_o = across_r(out_ra), across_e(out_ea), swap(sent_o)
    block_got = swap(block_send)
    sent_0, kept_0, rest_0 = attend_back(z, info, 0, grad_low, output_weight, saved)
    grad_low, got_ra, got_ea, got_o, block_got, sent_0, out_rb, out_eb = tie(
        grad_low, got_ra, got_ea, got_o, block_got, sent_0, out_rb, out_eb
    )
    out_o, own_o = halves_z(add(kept_o, got_o))
    grad_low, out_o = tie(grad_low, out_o)
    got_rb, got_eb, got_0, got_oz = across_r(out_rb), across_e(out_eb), swap(sent_0), across_z(out_o)
    sent_1, kept_1, rest_1 = attend_back(z, info, 1, grad_low, output_weight, saved)
    grad_low, got_rb, got_eb, got_0, got_oz, sent_1 = tie(
        grad_low, got_rb, got_eb, got_0, got_oz, sent_1
    )
    sum_r = add(own_r, jnp.concatenate([got_ra, got_rb], 0))
    sum_e = add(own_e, jnp.concatenate([got_ea, got_eb], 0))
    sum_r = scatter_up(sum_r, 1, "tm", low_bits[1:-1])
    sum_e = scatter(sum_e, 1, "tm", high_bits[1:-1])
    out_r, own_r = halves(sum_r, 1, "tm", low_bits[-1])
    out_e, own_e = halves(sum_e, 1, "tm", high_bits[-1])
    sum_o = add(own_o, got_oz)
    out_0, own_0 = halves_z(add(kept_0, got_0))
    grad_low, out_r, out_e, sum_o, out_0 = tie(grad_low, out_r, out_e, sum_o, out_0)
    got_r, got_e = across(out_r, "tm", low_bits[-1]), across(out_e, "tm", high_bits[-1])
    got_0z, got_1 = across_z(out_0), swap(sent_1)
    sum_o = rest_z(sum_o)

    def split_tm(x, *more):
        x = by_bits(x, 1, tm_count)
        parts = [x[:half], x[half:]]
        if more:
            parts = [jnp.concatenate([p, by_bits(m, 1, tm_count)], 0) for p, m in zip(parts, more)]
        return (
            *halves(parts[0], tm_bits, "tm", 0),
            *halves(parts[1], 1, "tm", tm_bits - 1),
        )

    sent_2, kept_2, rest_2 = attend_back(z, info, 2, grad_low, output_weight, saved)
    sent_2, got_r, got_e, got_0z, got_1, sum_o, *rest_2 = tie(
        sent_2, got_r, got_e, got_0z, got_1, sum_o, *rest_2
    )
    sum_r, sum_e = add(own_r, got_r), add(own_e, got_e)
    out_r, own_r = halves_z(sum_r)
    sum_0 = add(own_0, got_0z)
    out_1x, own_1x, out_1y, own_1y = split_tm(add(kept_1, got_1))
    feed_bias = jnp.stack([kept_b[:, 0], sent_b[:, 0]], 1)
    feed_bias = jnp.where(core == 0, feed_bias, feed_bias[:, ::-1])
    if not paired:
        feed_bias = feed_bias.swapaxes(0, 1).reshape(2, clip_count, -1).swapaxes(0, 1)
    feed_small = jnp.concatenate([small_two[:4], feed_bias.reshape(-1, feat)], 0)
    out_e, own_e = halves_z(sum_e)
    out_r, out_e, sum_0, out_1x, out_1y, sent_2, *rest_2 = tie(
        out_r, out_e, sum_0, out_1x, out_1y, sent_2, *rest_2
    )
    got_r, got_2, got_1x, got_1y = across_z(out_r), swap(sent_2), across_r(out_1x), across_e(out_1y)
    got_e = across_z(out_e)
    sum_0 = rest_z(sum_0)
    own, small, *sends = keys_back(
        z, info, saved, input_weight, grad_first, feed_small, (rest_0, rest_1, rest_2)
    )
    got_2, got_1x, got_1y, sum_0, own, small, *sends = tie(
        got_2, got_1x, got_1y, sum_0, own, small, *sends
    )
    out_2x, own_2x, out_2y, own_2y = split_tm(add(kept_2, got_2), sum_o[None], sum_0[None])
    finish_args = (rows, row(first_gain), grad_first)
    if z.tape:
        flat = lambda *parts: jnp.concatenate([part.reshape(-1, 128) for part in parts], 0)
        count = small.shape[0]
        unpack = lambda got, like: (got[:-count].reshape(like.shape), got[-count:])
        across_x, across_y = lambda x: across(x, "tm", 0), lambda x: across(x, "tm", 1)
        across_zz = lambda x: across(x, "clip", 0)
        along_x, along_y, mid_x, mid_y = sends
        msg_x, out_2y, along_x, along_y = tie(flat(out_2x, small), out_2y, along_x, along_y)
        msg_x, out_2y = across_x(msg_x), across_y(out_2y)
        got_x, got_y = across_x(along_x), across_y(along_y)
        msg_x, got_2y = tie(msg_x, out_2y)
        got_2x, got_small = unpack(msg_x, own_2x)
        small = add(small, got_small)
        sum_x = jnp.concatenate([add(own_1x, got_1x), add(own_2x, got_2x)], 0)
        sum_y = jnp.concatenate([add(own_1y, got_1y), add(own_2y, got_2y)], 0)
        out_x, own_x = halves(sum_x, 1, "tm", 1)
        out_y, own_y = halves(sum_y, 1, "tm", 0)
        small, = tie(small)
        msg_x, out_y = tie(flat(out_x, small), out_y)
        msg_x, got_y2, got_r, got_e = tie(across_y(msg_x), across_x(out_y), got_r, got_e)
        got_x2, got_small = unpack(msg_x, own_x)
        small = add(small, got_small)
        sum_x, sum_y = add(own_x, got_x2), add(own_y, got_y2)
        late = jnp.concatenate(
            [jnp.concatenate([one[:2], one[2:4]], 1) for one in (sum_x, sum_y)], 0
        )
        out_l, own_l = halves_z(late)
        out_r, own_r = halves(add(own_r, got_r), 0, "clip", 0)
        out_e, own_e = halves(add(own_e, got_e), 0, "clip", 0)
        small, = tie(small)
        msg_l, msg_f = tie(flat(out_l, small), flat(out_r, out_e))
        msg_l, got_f, got_x, got_y = tie(across_z(msg_l), across_zz(msg_f), got_x, got_y)
        got_l, got_small = unpack(msg_l, own_l)
        small = add(small, got_small)
        out_l, own_l = halves(add(own_l, got_l), 0, "clip", 0)
        n = out_r.shape[0]
        ready_p = flat(add(own_r, got_f[:n]), sum_x[4])
        ready_q = flat(add(own_e, got_f[n:]), sum_y[4])
        lead = add(along_x[z.rows :], got_x[z.rows :])
        out_xy = jnp.concatenate([add(mid_x, got_x[z.half : z.rows]), lead], 0)
        out_yx = add(mid_y, got_y[z.half :])
        small, = tie(small)
        msg_l, ready_p, ready_q, out_xy, out_yx = tie(
            flat(out_l, small), ready_p, ready_q, out_xy, out_yx
        )
        msg_l, got_p, got_q, got_xy, got_yx = tie(
            across_zz(msg_l),
            across_x(ready_p),
            across_y(ready_q),
            across_y(out_xy),
            across_x(out_yx),
        )
        got_l, got_small = unpack(msg_l, own_l)
        small, late = add(small, got_small), add(own_l, got_l)
        near_p, near_q = flat(ready_p, got_p), flat(ready_q, got_q)
        near_p, near_q, late, small = tie(near_p, near_q, late, small)
        far_p, far_q = across_y(near_p), across_x(near_q)
        late_all = [late] + to_peers([late] * 3, "tm")
        small = small.astype(f32) + swap(small).astype(f32)
        small = small.reshape(-1, 16, 128).swapaxes(0, 1).reshape(16, feat)
        received = [got_x, got_y, got_xy, got_yx]
        grad_mine, grad_send = finish(z, info, own, received, *finish_args)
        grad_send, far_p, far_q, *late_all = tie(grad_send, far_p, far_q, *late_all)
    else:
        received = to_peers(sends, "tm")
        got_2x, got_2y, got_e = across_r(out_2x), across_e(out_2y), across_z(out_e)
        sum_x = jnp.concatenate([add(own_1x, got_1x), add(own_2x, got_2x)], 0)
        sum_y = jnp.concatenate([add(own_1y, got_1y), add(own_2y, got_2y)], 0)
        sum_x = scatter_up(sum_x, 1, "tm", low_bits[1:])
        sum_y = scatter(sum_y, 1, "tm", high_bits[1:])
        sum_r, sum_e = rest_z(add(own_r, got_r)), rest_z(add(own_e, got_e))
        ready = jnp.concatenate([sum_r, sum_e, sum_x[2 * half], sum_y[2 * half]], 0)
        late = jnp.concatenate(
            [
                jnp.concatenate([one[:half], one[half : 2 * half]], 1)
                for one in (sum_x, sum_y)
            ],
            0,
        )
        late = scatter(by_bits(late, 0, clip_count), 0, "clip", range(clip_bits)[::-1])
        ready = jnp.concatenate([ready, late], 0)
        ready_all = [ready] + to_peers([ready] * (tm_count - 1), "tm")
        small = small + swap(small)
        for axis, bits in (("tm", tm_bits), ("clip", clip_bits)):
            for bit in range(bits):
                small = small + across(small, axis, bit)
        grad_mine, grad_send = finish(z, info, own, received, *finish_args)

    here = lax.axis_index("clip")

    def shard(vector):
        count = vector.shape[0] // clip_count
        return lax.dynamic_slice_in_dim(vector, here * count, count, 0)

    input_bias_grad = shard(small[0:2].reshape(-1))
    gain_one_grad, shift_one_grad, output_bias_grad, gain_two_grad, shift_two_grad = (
        shard(small[i]) for i in range(2, 7)
    )
    reduce_bias_grad = shard(small[7])
    expand_bias_grad = shard(small[8:12].reshape(-1))

    count_f = feat * ff // (2 * clip_count * tm_count * 128)
    if z.tape:
        tapes = [near_p, near_q, far_p, far_q]
        tapes, late_all = tapes + [swap(one) for one in tapes], late_all + [swap(one) for one in late_all]
        expand_weight_grad, reduce_weight_grad, output_weight_grad, input_weight_grad = assemble(
            z, info, tapes, late_all, ff
        )
    else:
        tapes = jnp.stack(ready_all)
        other_tapes = swap(tapes)
        both = in_order(tapes, [other_tapes], "freq")
        both = pick(jnp.stack([both[:, np.arange(tm_count) ^ t] for t in range(tm_count)]), 0, place)
        part_r, part_e = both[:, :, :count_f], both[:, :, count_f : 2 * count_f]
        rows_r, rows_e = ff // (2 * clip_count * tm_count), feat // (clip_count * split)
        part_r = part_r.reshape(2, tm_count, feat // 128, rows_r, 128).swapaxes(2, 3)
        reduce_weight_grad = part_r.reshape(ff // clip_count, feat).astype(f32)
        part_e = part_e.reshape(2, FF_PARTS // 2, split, size // 128, rows_e, 128)
        part_e = part_e.transpose(2, 4, 1, 0, 3, 5)
        if not paired:
            part_e = part_e.swapaxes(2, 3).reshape(feat // clip_count, 2, clip_count, -1)
            part_e = part_e.swapaxes(1, 2)
        expand_weight_grad = part_e.reshape(feat // clip_count, ff).astype(f32)
        lanes = z.width // 128
        part_a = both[:, :, 2 * count_f :].reshape(2, tm_count // lanes, lanes, 4, 3, -1, 128)
        part_a = part_a.transpose(0, 1, 5, 3, 4, 2, 6)
        part_a = part_a.reshape(feat // clip_count, 4, 3, z.width).astype(f32)
        output_weight_grad = part_a[:, 0].reshape(-1, feat)
        input_weight_grad = part_a[:, 1:].swapaxes(1, 2).reshape(-1, 3 * feat)

    def patches_of(mine, theirs):
        first = jnp.where(core == 0, mine, theirs[: z.half])
        second = jnp.where(core == 0, theirs[: z.half], mine)
        pair = jnp.stack([first, second], 0).reshape(
            z.clips, z.blocks, z.fr, BLOCK_COLS, feat
        )
        return pair.transpose(2, 1, 3, 0, 4).reshape(z.fr, z.tc, z.clips, feat)

    def leads_of(sent, got):
        mine, theirs = sent[z.half : z.half + LEADS], got[z.half : z.half + LEADS]
        first = jnp.where(core == 0, mine, theirs)
        second = jnp.where(core == 0, theirs, mine)
        return jnp.stack([first, second], 0)

    grad_got = swap(grad_send)
    return (
        patches_of(block_mine, block_got),
        leads_of(block_send, block_got),
        patches_of(grad_mine, grad_got),
        leads_of(grad_send, grad_got),
        input_weight_grad,
        input_bias_grad,
        output_weight_grad,
        output_bias_grad,
        gain_one_grad,
        shift_one_grad,
        gain_two_grad,
        shift_two_grad,
        expand_weight_grad,
        expand_bias_grad,
        reduce_weight_grad,
        reduce_bias_grad,
    )


def solution(mesh):
    rows = P("freq", "tm", "clip", None)
    lead = P("clip", None, None)
    in_specs = (rows, lead, P("clip")) + (P(),) * 12 + (rows, lead)
    matrix, vector = P("clip", None), P("clip")
    out_specs = (rows, lead, rows, lead) + (matrix, vector) * 2 + (vector,) * 4 + (matrix, vector) * 2
    return jax.shard_map(
        per_device, mesh=mesh, in_specs=in_specs, out_specs=out_specs, check_vma=False
    )
```

```python
import functools
import math

import jax
import jax.numpy as jnp
import numpy as np
from jax import lax
from jax.experimental import pallas as pl
from jax.experimental.pallas import tpu as pltpu
from jax.sharding import PartitionSpec as P

HEADS = 12
EPSILON = 1e-06
NEG_FILL = -1e30
MAX_LENGTH = 101
LEADS = 2
LEAD_ROWS = 16
BLOCK_COLS = 8
GROUP = 4
FF_PARTS = 8
bf16 = jnp.bfloat16
f32 = jnp.float32


def mm(a, b):
    return lax.dot_general(a, b, (((1,), (0,)), ((), ())), preferred_element_type=f32)


def mm_nt(a, b):
    return lax.dot_general(a, b, (((1,), (1,)), ((), ())), preferred_element_type=f32)


def standardize(rows):
    center = rows - jnp.mean(rows, -1, keepdims=True)
    scale_inv = lax.rsqrt(jnp.mean(center * center, -1, keepdims=True) + EPSILON)
    return center * scale_inv, scale_inv


def norm_backward(grad_out, gain_row, normed, scale_inv):
    scaled = grad_out * gain_row
    return scale_inv * (
        scaled
        - jnp.mean(scaled, -1, keepdims=True)
        - normed * jnp.mean(scaled * normed, -1, keepdims=True)
    )


def head_mask(head, width, head_width):
    lane_head = lax.broadcasted_iota(jnp.int32, (1, width), 1) // head_width
    return (lane_head == head).astype(f32)


class Sizes:
    def __init__(self, patches_shape, tm_count, clip_count):
        fr_local, tc_local, clips, feat = patches_shape
        self.fr, self.tc, self.clips, self.feat = fr_local, tc_local, clips, feat
        self.tm, self.clip = tm_count, clip_count
        self.tape = clip_count == 4 and tm_count == 4
        self.tape_rows = 3 * feat * 2 // (2 * clip_count * tm_count)
        self.blocks = tc_local // BLOCK_COLS
        self.half_block = fr_local * BLOCK_COLS
        self.block = 2 * self.half_block
        self.half = self.blocks * self.half_block
        self.rows = 2 * self.half
        self.query_rows = self.rows + LEAD_ROWS
        self.key_blocks = -(-MAX_LENGTH // BLOCK_COLS)
        self.keys = LEAD_ROWS + self.key_blocks * self.block
        self.head_width = feat // HEADS
        self.width = GROUP * self.head_width
        self.steps = HEADS // GROUP
        self.lanes = GROUP * self.rows + 128


def call(kernel, room, in_specs, out_specs, out_shape, scratch, args, info, flops, moved):
    return pl.pallas_call(
        kernel,
        out_shape=out_shape,
        in_specs=[pl.BlockSpec(memory_space=pltpu.SMEM), *in_specs],
        out_specs=out_specs,
        scratch_shapes=scratch,
        compiler_params=pltpu.CompilerParams(vmem_limit_bytes=room * 1024 * 1024),
        cost_estimate=pl.CostEstimate(flops=flops, bytes_accessed=moved, transcendentals=0),
    )(info, *args)


def in_vmem(x):
    return pltpu.with_memory_space_constraint(x, pltpu.VMEM)


def in_hbm(x):
    return pltpu.with_memory_space_constraint(x, pltpu.HBM)


def whole(shape):
    return pl.BlockSpec(memory_space=pltpu.VMEM)


def chunks_of(z):
    full = z.lanes // 256
    spans = [(c * 256, 256) for c in range(full)]
    if z.lanes % 256:
        spans.append((full * 256, z.lanes % 256))
    return spans


def spread_heads(z, rows, out_ref):
    for head in range(GROUP):
        mask = head_mask(head, z.width, z.head_width)
        part = (rows * mask).astype(bf16)
        out_ref[head * z.rows : (head + 1) * z.rows, :] = part[: z.rows]
        at = GROUP * z.rows + head * LEAD_ROWS
        out_ref[at : at + LEAD_ROWS, :] = part[z.rows :]
    at = GROUP * (z.rows + LEAD_ROWS)
    out_ref[at:, :] = jnp.zeros((z.lanes - at, z.width), bf16)


def join_heads(z, spread):
    patch_part, lead_part = None, None
    for head in range(GROUP):
        mask = head_mask(head, z.width, z.head_width)
        at = GROUP * z.rows + head * LEAD_ROWS
        one = spread[head * z.rows : (head + 1) * z.rows] * mask
        two = spread[at : at + LEAD_ROWS] * mask
        patch_part = one if patch_part is None else patch_part + one
        lead_part = two if lead_part is None else lead_part + two
    return jnp.concatenate([patch_part, lead_part], 0)


class Copies:
    def __init__(self, sems):
        self.sems, self.going = sems, {}

    def start(self, name, source, to):
        copy = pltpu.make_async_copy(source, to, self.sems.at[len(self.going)])
        copy.start()
        self.going[name] = copy

    def wait(self, *names):
        for name in names:
            self.going[name].wait()


def attend_kernel(z, info, *refs):
    refs = list(refs)
    take = lambda n: [refs.pop(0) for _ in range(n)]
    pieces = take(2 * z.tm)
    lead, weight, bias_q, bias_v, gain, shift, live = take(7)
    low_out, inv_out, uq, q_out, k_out, v_out, mixed_out, hk_t_out, hq_t_out, p_out, uk_out = take(11)
    spread, total, hk, hq, uk, w, p, q_all, k_all, v_all, mixed_all, hk_t, hq_t, sems = take(14)
    me = info[0]
    copies = Copies(sems)
    span = lambda part, i: slice((part * z.steps + i) * z.width, (part * z.steps + i + 1) * z.width)
    copies.start("w", weight, w)
    gain_row, shift_row = gain[...], shift[...]

    def hidden(rows):
        unit, _ = standardize(rows.astype(f32))
        return unit.astype(bf16), (unit * gain_row + shift_row).astype(bf16)

    unit, low = hidden(lead[...])
    uk[0:LEAD_ROWS, :] = unit
    hk[0:LEAD_ROWS, :] = low
    hq[z.rows :, :] = low
    uq[z.rows :, :] = unit
    hb = z.half_block
    for k in range(z.tm):
        source = jnp.bitwise_xor(me, k)
        for half in range(2):
            unit, low = hidden(pieces[2 * k + half][...])
            if k == 0:
                hq[half * z.half : (half + 1) * z.half, :] = low
                uq[half * z.half : (half + 1) * z.half, :] = unit
            for b in range(z.blocks):
                at = LEAD_ROWS + (source * z.blocks + b) * z.block + half * hb
                at = pl.multiple_of(at, 16)
                uk[pl.ds(at, hb), :] = unit[b * hb : (b + 1) * hb]
                hk[pl.ds(at, hb), :] = low[b * hb : (b + 1) * hb]
    copies.start("uk", uk.at[0 : z.keys, :], uk_out)
    hk_all, hq_all = hk[0 : z.keys, :], hq[...]
    hk_t[...] = jnp.transpose(hk_all)
    hq_t[...] = jnp.transpose(hq_all)
    copies.start("hk_t", hk_t, hk_t_out)
    copies.start("hq_t", hq_t, hq_t_out)
    live_col = live[...]
    for i in range(z.steps):
        columns = slice(i * z.width, (i + 1) * z.width)
        slot = i % 2
        if i == 0:
            copies.wait("w")
        if i >= 2:
            copies.wait(f"p{i - 2}")
        q = (mm(hq_all, w[:, span(0, i)]) + bias_q[:, columns]).astype(bf16)
        q_all[i] = q
        spread_heads(z, q.astype(f32) * (z.head_width**-0.5), spread.at[slot])
        k = mm(hk_all, w[:, span(1, i)]).astype(bf16)
        k_all[i] = k
        v = (mm(hk_all, w[:, span(2, i)]) + bias_v[:, columns]).astype(bf16)
        v_all[i] = v
        for name, source, to in (("q", q_all, q_out), ("k", k_all, k_out), ("v", v_all, v_out)):
            copies.start(f"{name}{i}", source.at[i], to.at[i])
        for at, size in chunks_of(z):
            scores = mm_nt(k, spread[slot, at : at + size, :])
            scores = scores + jnp.concatenate([live_col] * (size // 128), 1)
            peak = jnp.max(scores, 0, keepdims=True)
            weights = jnp.exp(scores - peak)
            total[i, 0:1, at : at + size] = jnp.sum(weights, 0, keepdims=True)
            p[slot, :, at : at + size] = weights.astype(bf16)
        copies.start(f"p{i}", p.at[slot], p_out.at[i])
        inverse = 1.0 / total[i, 0:1, :]
        inv_out[i] = jnp.broadcast_to(inverse, (8, z.lanes))
        mixed = mm(jnp.transpose(v), p[slot]) * inverse
        mixed = join_heads(z, jnp.transpose(mixed))
        mixed_all[i] = mixed
        copies.start(f"mixed{i}", mixed_all.at[i], mixed_out.at[i])
        low_out[:, columns] = mixed.astype(bf16)
    for i in range(max(0, z.steps - 2), z.steps):
        copies.wait(f"p{i}")
    copies.wait("uk", "hk_t", "hq_t")
    for i in range(z.steps):
        copies.wait(f"q{i}", f"k{i}", f"v{i}", f"mixed{i}")


def attend(z, me_info, pieces, lead, weight, bias_q, bias_v, gain, shift, live):
    feat, width, nk, nq, nl = z.feat, z.width, z.keys, z.query_rows, z.lanes
    there = pl.BlockSpec(memory_space=pl.ANY)
    in_specs = [whole((z.half, feat))] * (2 * z.tm) + [whole((LEAD_ROWS, feat)), there]
    in_specs += [whole((1, feat))] * 4 + [whole((nk, 128))]
    shapes = [((nq, feat), bf16), ((z.steps, 8, nl), f32), ((nq, feat), bf16)]
    heads = lambda rows, kind: ((z.steps, rows, width), kind)
    far = [heads(nq, bf16), heads(nk, bf16), heads(nk, bf16), heads(nq, f32)]
    far += [((feat, nk), bf16), ((feat, nq), bf16), ((z.steps, nk, nl), bf16), ((nk, feat), bf16)]
    return call(
        functools.partial(attend_kernel, z),
        34,
        in_specs,
        [whole(None)] * 3 + [there] * 8,
        [jax.ShapeDtypeStruct(*one) for one in shapes] + [pltpu.HBM(*one) for one in far],
        [
            pltpu.VMEM((2, nl, width), bf16),
            pltpu.VMEM((z.steps, 8, nl), f32),
            pltpu.VMEM((LEAD_ROWS + z.tm * z.rows, feat), bf16),
            pltpu.VMEM((nq, feat), bf16),
            pltpu.VMEM((LEAD_ROWS + z.tm * z.rows, feat), bf16),
            pltpu.VMEM((feat, 3 * feat), bf16),
            pltpu.VMEM((2, nk, nl), bf16),
            *[pltpu.VMEM(*one) for one in far[:6]],
            pltpu.SemaphoreType.DMA((32,)),
        ],
        (*pieces, lead, in_hbm(weight), bias_q, bias_v, gain, shift, live),
        me_info,
        2 * feat * feat * (nq + 2 * nk) + 4 * z.steps * nk * nl * width,
        z.steps * nk * nl * 2,
    )


def blend_kernel(z, info, mixed, rows, wo, bo, gain, shift, sum_out, unit, inv, low):
    total = rows[...].astype(f32) + mm(mixed[...], wo[...]) + bo[...]
    sum_out[...] = total
    normed, scale_inv = standardize(total)
    unit[...] = normed
    inv[...] = jnp.broadcast_to(scale_inv, inv.shape)
    low[...] = (normed * gain[...] + shift[...]).astype(bf16)


def blend(z, info, mixed, rows, wo, bo, gain, shift):
    wide, narrow = ((z.query_rows, z.feat), f32), ((z.query_rows, z.feat), bf16)
    shapes = [wide, wide, ((z.query_rows, 128), f32), narrow]
    return call(
        functools.partial(blend_kernel, z),
        12,
        [whole(None)] * 6,
        [whole(None)] * 4,
        [jax.ShapeDtypeStruct(*one) for one in shapes],
        [],
        (mixed, rows, wo, bo, gain, shift),
        info,
        2 * z.query_rows * z.feat * z.feat,
        z.query_rows * z.feat * 14,
    )


def feed_kernel(z, paired, info, *refs):
    refs = list(refs)
    take = lambda n: [refs.pop(0) for _ in range(n)]
    low, low_other, cot, cot_other, be, we_in, wr_in = take(7)
    dbe, acc, acc_other, grad, grad_other = take(5)
    outs = take(6 if z.tape else 2)
    we, wr, dwr, dwe, low_t, cot_all, acc_sum, grad_sum, sems = take(9)
    steps = FF_PARTS // 2
    size = we.shape[2] // 2
    nq = z.query_rows
    core = info[1]
    col, line = info[0] % 2, info[0] // 2
    place = lambda i: jnp.bitwise_xor(i, 2 * (1 - line)) if z.tape else i
    at = lambda i: pl.multiple_of(
        (2 * place(i) + core if paired else steps * core + i) * size, size
    )
    copies = Copies(sems)
    names = []

    def leave(name, source, to):
        copies.start(name, source, to)
        names.append(name)

    for i in range(steps):
        pair, span = i // 2, slice(i % 2 * size, (i % 2 + 1) * size)
        copies.start(f"we{i}", we_in.at[:, pl.ds(at(i), size)], we.at[pair, :, span])
        copies.start(f"wr{i}", wr_in.at[pl.ds(at(i), size), :], wr.at[pair, span, :])
    cot_all[:nq, :] = cot[...]
    cot_all[nq:, :] = cot_other[...]
    low_all = jnp.concatenate([low[...], low_other[...]], 0)
    low_t[...] = jnp.transpose(low_all)
    for pair in range(steps // 2):
        both = (2 * pair, 2 * pair + 1)
        copies.wait(*[f"w{which}{i}" for i in both for which in "er"])
        cot_low = cot_all[...]
        expand, reduce = we[pair], wr[pair]
        bias = jnp.concatenate([be[:, pl.ds(at(i), size)] for i in both], 1)
        expanded = mm(low_all, expand) + bias
        grad_activated = mm_nt(cot_low, reduce)
        cdf = 0.5 * (1.0 + lax.erf(expanded * math.sqrt(0.5)))
        pdf = jnp.exp(-0.5 * expanded * expanded) * (1.0 / math.sqrt(2.0 * math.pi))
        activated = (expanded * cdf).astype(bf16)
        reduce_grad = mm(jnp.transpose(activated), cot_low).astype(bf16)
        for n, i in enumerate(both):
            if z.tape:
                part = size // z.tm
                for t in range(z.tm):
                    for lane in range(z.feat // 128):
                        rows = slice(n * size + t * part, n * size + (t + 1) * part)
                        dwr[i, t, lane * part : (lane + 1) * part, :] = reduce_grad[
                            rows, lane * 128 : (lane + 1) * 128
                        ]
                out_ra, out_rb, own_r, out_ea, out_eb, own_e = outs
                for y in range(2):
                    out = (out_ra, out_rb)[pair].at[n, y]
                    leave(f"out_r{i}{y}", dwr.at[i, 2 * y + 1 - col], out)
                    leave(f"own_r{i}{y}", dwr.at[i, 2 * y + col], own_r.at[i, y])
            else:
                dwr[i] = reduce_grad[n * size : (n + 1) * size]
                leave(f"dwr{i}", dwr.at[i], outs[0].at[i])
        grad_expanded = (grad_activated * (cdf + expanded * pdf)).astype(bf16)
        expand_grad = mm(low_t[...], grad_expanded).astype(bf16)
        bias_grad = jnp.sum(grad_expanded.astype(f32), 0, keepdims=True)
        for n, i in enumerate(both):
            span = slice(n * size, (n + 1) * size)
            if z.tape:
                part = z.feat // z.clip
                for c in range(z.clip):
                    for lane in range(size // 128):
                        lanes = slice(n * size + lane * 128, n * size + (lane + 1) * 128)
                        dwe[i, c, lane * part : (lane + 1) * part, :] = expand_grad[
                            c * part : (c + 1) * part, lanes
                        ]
                    out = (out_ea, out_eb)[c // 2].at[c % 2, n] if pair == 0 else own_e.at[c, n]
                    leave(f"e{i}{c}", dwe.at[i, c], out)
            else:
                dwe[i] = expand_grad[:, span]
                leave(f"dwe{i}", dwe.at[i], outs[1].at[i])
            dbe[place(i)] = jnp.broadcast_to(bias_grad[:, span], dbe.shape[1:])
        acc_new, grad_new = mm(activated, reduce), mm_nt(grad_expanded, expand)
        if pair == 0:
            acc_sum[...] = acc_new
            grad_sum[...] = grad_new
        else:
            acc_new, grad_new = acc_sum[...] + acc_new, grad_sum[...] + grad_new
            acc[...] = acc_new[:nq]
            acc_other[...] = acc_new[nq:].astype(bf16)
            grad[...] = grad_new[:nq]
            grad_other[...] = grad_new[nq:].astype(bf16)
    copies.wait(*names)


def feed(z, info, paired, low, low_other, cot, cot_other, expand, expand_bias, reduce):
    feat, ff = expand.shape
    size = ff // FF_PARTS
    steps = FF_PARTS // 2
    nq = z.query_rows
    there, here = pl.BlockSpec(memory_space=pl.ANY), whole(None)
    if z.tape:
        shapes = [(z.tm, size * feat // (128 * z.tm), 128), (z.clip, size * feat // (128 * z.clip), 128)]
    else:
        shapes = [(size, feat), (feat, size)]
    shapes = [(steps, *shape) for shape in shapes]
    wide, narrow = ((nq, feat), f32), ((nq, feat), bf16)
    outs = [((steps, 8, size), f32), wide, narrow, wide, narrow]
    far = shapes
    if z.tape:
        part = lambda n: (n, 2, *shapes[0][2:])
        far = [part(2), part(2), part(4)] * 2
    return call(
        functools.partial(feed_kernel, z, paired),
        44,
        [here] * 5 + [there] * 2,
        [here] * 5 + [there] * len(far),
        [jax.ShapeDtypeStruct(*one) for one in outs] + [pltpu.HBM(shape, bf16) for shape in far],
        [
            pltpu.VMEM((steps // 2, feat, 2 * size), bf16),
            pltpu.VMEM((steps // 2, 2 * size, feat), bf16),
            pltpu.VMEM(shapes[0], bf16),
            pltpu.VMEM(shapes[1], bf16),
            pltpu.VMEM((feat, 2 * nq), bf16),
            pltpu.VMEM((2 * nq, feat), bf16),
            pltpu.VMEM((2 * nq, feat), f32),
            pltpu.VMEM((2 * nq, feat), f32),
            pltpu.SemaphoreType.DMA((48,)),
        ],
        (low, low_other, cot, cot_other, expand_bias, in_hbm(expand), in_hbm(reduce)),
        info,
        6 * nq * feat * ff * 2,
        4 * feat * ff,
    )


def blend_back_kernel(z, info, *refs):
    refs = list(refs)
    take = lambda n: [refs.pop(0) for _ in range(n)]
    grad, grad_got, unit, inv, cot, mixed, gain = take(7)
    first_out, low_grad, send, keep, small, hold = take(6)
    rows_grad = cot[...].astype(f32)
    normed, hidden_grad = unit[...], grad[...] + grad_got[...].astype(f32)
    back = rows_grad + norm_backward(hidden_grad, gain[...], normed, inv[:, 0:1])
    first_out[...] = back
    back_low = back.astype(bf16)
    low_grad[...] = back_low
    dwo = mm(jnp.transpose(mixed[...]), back_low)
    for j in range(z.steps):
        block = dwo[:, j * z.width : (j + 1) * z.width]
        if z.tape:
            store_split(z, info[1], block, hold, send, keep, j)
        else:
            keep[j] = block.astype(bf16)
    small[...] = jnp.zeros_like(small)
    small[0:1, :] = jnp.sum(back_low.astype(f32), 0, keepdims=True)
    small[1:2, :] = jnp.sum(hidden_grad * normed, 0, keepdims=True)
    small[2:3, :] = jnp.sum(hidden_grad, 0, keepdims=True)
    small[3:4, :] = jnp.sum(rows_grad, 0, keepdims=True)


def blend_back(z, info, *args):
    feat, nq = z.feat, z.query_rows
    split = ((z.clip, z.tm, z.tape_rows, 128) if z.tape else (3, feat, z.width), bf16)
    shapes = [((nq, feat), f32), ((nq, feat), bf16), split, split, ((8, feat), f32)]
    return call(
        functools.partial(blend_back_kernel, z),
        20,
        [whole(None)] * len(args),
        [whole(None)] * len(shapes),
        [jax.ShapeDtypeStruct(*one) for one in shapes],
        [pltpu.VMEM((feat, z.width), f32)],
        args,
        info,
        2 * nq * feat * feat,
        nq * feat * 20,
    )


def store_split(z, core, value, hold, sent, kept, j):
    hold[...] = value
    half = z.feat // (2 * z.clip)
    part = half // 2
    for c in range(z.clip):
        for out, whose in ((kept, core), (sent, 1 - core)):
            for t in range(z.tm):
                at = pl.multiple_of((2 * c + whose) * half + (t // 2) * part, 16)
                lanes = slice((t % 2) * 128, (t % 2) * 128 + 128)
                out[c, t, j * part : (j + 1) * part, :] = hold[pl.ds(at, part), lanes].astype(bf16)


def plain_to_tape(z, blocks, core):
    lanes = z.width // 128
    x = blocks.reshape(3, z.clip, 2, z.tm // lanes, -1, lanes, 128)
    x = x.transpose(2, 1, 3, 5, 0, 4, 6).reshape(2, z.clip, z.tm, -1, 128)
    return pick(x, 0, 1 - core), pick(x, 0, core)


def attend_back_kernel(z, i, info, *refs):
    refs = list(refs)
    take = lambda n: [refs.pop(0) for _ in range(n)]
    ga, wo, inv, *far = take(10)
    span = slice(i * z.width, (i + 1) * z.width)
    sent, kept, db, kv_out, q_grad_out = take(5)
    q_spread, g_spread, ds, hold, q, k, v, mixed, hk_t, hq_t, p, sems = take(12)
    core = info[1]
    copies = Copies(sems)
    q_in, k_in, v_in, mixed_in, hk_t_in, hq_t_in, p_in = far
    for name, source, to in (
        ("q", q_in.at[i], q),
        ("mixed", mixed_in.at[i], mixed),
        ("v", v_in.at[i], v),
        ("p", p_in.at[i], p),
        ("k", k_in.at[i], k),
        ("hq_t", hq_t_in, hq_t),
        ("hk_t", hk_t_in, hk_t),
    ):
        copies.start(name, source, to)
    scale = z.head_width**-0.5

    grad = mm_nt(ga[...], wo[span, :]).astype(bf16).astype(f32)
    inverse = inv[i, 0:1, :]
    inverse_col = jnp.transpose(jnp.broadcast_to(inverse, (128, z.lanes)))[:, 0:1]
    copies.wait("q", "mixed")
    spread_heads(z, q[...].astype(f32) * scale, q_spread)
    product = grad * mixed[...]
    dots = []
    for head in range(GROUP):
        mask = head_mask(head, z.width, z.head_width)
        at = GROUP * z.rows + head * LEAD_ROWS
        part = grad * mask
        low = (part[: z.rows] * inverse_col[head * z.rows : (head + 1) * z.rows]).astype(bf16)
        g_spread[head * z.rows : (head + 1) * z.rows, :] = low
        low = (part[z.rows :] * inverse_col[at : at + LEAD_ROWS]).astype(bf16)
        g_spread[at : at + LEAD_ROWS, :] = low
        dots.append(jnp.sum(product * mask, 1, keepdims=True))
    end = GROUP * (z.rows + LEAD_ROWS)
    g_spread[end:, :] = jnp.zeros((z.lanes - end, z.width), bf16)
    dot_col = jnp.concatenate(
        [d[: z.rows] for d in dots]
        + [d[z.rows :] for d in dots]
        + [jnp.zeros((z.lanes - end, 1), f32)],
        0,
    )
    dot_row = jnp.transpose(jnp.broadcast_to(dot_col, (z.lanes, 128)))[0:1, :] * inverse
    copies.wait("v", "p")
    v_all = v[...]
    for at, size in chunks_of(z):
        grad_weights = mm_nt(v_all, g_spread[at : at + size, :])
        weights = p[:, at : at + size].astype(f32)
        ds[:, at : at + size] = (weights * (grad_weights - dot_row[:, at : at + size])).astype(bf16)
    ds_all = ds[...]
    copies.wait("k", "hq_t", "hk_t")
    k_all = k[...]
    grad_v = mm(p[...], g_spread[...])
    grad_k = mm(ds_all, q_spread[...])
    grad_q = mm(jnp.transpose(k_all), ds_all)
    grad_q = (join_heads(z, jnp.transpose(grad_q)) * scale).astype(bf16)
    grad_v = grad_v.astype(bf16)
    grad_k = grad_k.astype(bf16)
    db[...] = jnp.concatenate(
        [
            jnp.sum(grad_q.astype(f32), 0, keepdims=True),
            jnp.sum(grad_v.astype(f32), 0, keepdims=True),
            jnp.zeros((6, z.width), f32),
        ],
        0,
    )
    for j, grad in enumerate((mm(hq_t[...], grad_q), mm(hk_t[...], grad_k), mm(hk_t[...], grad_v))):
        if z.tape:
            store_split(z, core, grad, hold, sent, kept, j)
        else:
            kept[j] = grad.astype(bf16)
    kv_out[:, : z.width] = grad_k
    kv_out[:, z.width :] = grad_v
    q_grad_out[...] = grad_q


def keys_back_kernel(z, info, *refs):
    refs = list(refs)
    take = lambda n: [refs.pop(0) for _ in range(n)]
    uk_in, uq, weight_in, first, feed_small = take(5)
    db, grad_kv, grad_q = take(z.steps), take(z.steps), take(z.steps)
    own, small_out = take(2)
    sends = take(4 if z.tape else z.tm - 1)
    keys_acc, query_acc, small, uk, weight, sems = take(6)
    me = info[0]
    copies = Copies(sems)
    span = lambda part, i: slice((part * z.steps + i) * z.width, (part * z.steps + i + 1) * z.width)
    spans = [slice(r * z.width, (r + 1) * z.width) for r in range(z.steps)]
    for r, span in enumerate(spans):
        copies.start(r, weight_in.at[span, :], weight.at[span, :])
    copies.start("uk", uk_in, uk)
    all_kv = [one[:, : z.width] for one in grad_kv] + [one[:, z.width :] for one in grad_kv]
    all_kv, all_q = jnp.concatenate(all_kv, 1), jnp.concatenate([one[...] for one in grad_q], 1)
    for r, span in enumerate(spans):
        copies.wait(r)
        query_acc[:, span] = mm_nt(all_q, weight[span, : z.feat])
        keys_acc[:, span] = mm_nt(all_kv, weight[span, z.feat :])
    copies.wait("uk")
    keys_grad, query_grad = keys_acc[...], query_acc[...]
    small[...] = jnp.zeros_like(small)
    for i in range(z.steps):
        small[0:2, i * z.width : (i + 1) * z.width] = db[i][0:2, :]
    small[2:3, :] = jnp.sum(keys_grad * uk[...].astype(f32), 0, keepdims=True) + jnp.sum(
        query_grad * uq[...].astype(f32), 0, keepdims=True
    )
    small[3:4, :] = jnp.sum(keys_grad, 0, keepdims=True) + jnp.sum(query_grad, 0, keepdims=True)
    small[4:12, :] = feed_small[...]
    if z.tape:
        for lane in range(z.feat // 128):
            small_out[lane * 16 : lane * 16 + 16, :] = small[
                :, lane * 128 : lane * 128 + 128
            ].astype(bf16)
    else:
        small_out[...] = small[...]
    lead = keys_acc[0:LEAD_ROWS, :] + query_acc[z.rows :, :]
    first_lead = first[z.rows :, :]
    high = first_lead.astype(bf16)
    rest = (first_lead - high.astype(f32)).astype(bf16)
    pair = lambda a: a[0:LEADS]
    packed = jnp.concatenate(
        [pair(lead), pair(high.astype(f32)), pair(rest.astype(f32)), jnp.zeros((10, z.feat), f32)], 0
    )
    small_high = small[...].astype(bf16)
    small_low = (small[...] - small_high.astype(f32)).astype(bf16)
    own[z.rows :, :] = packed
    packed = packed.astype(bf16)
    hb = z.half_block

    def chunk(k, half, out, at):
        source = jnp.bitwise_xor(me, k)
        for b in range(z.blocks):
            spot = source * z.blocks + b
            from_ = pl.multiple_of(
                LEAD_ROWS + jnp.minimum(spot, z.key_blocks - 1) * z.block + half * hb, 16
            )
            rows = keys_acc[pl.ds(from_, hb), :] * (spot < z.key_blocks).astype(f32)
            to = at + b * hb
            if k == 0:
                queries = half * z.half + b * hb
                rows = rows + query_acc[queries : queries + hb, :]
            out[to : to + hb, :] = rows.astype(out.dtype)

    chunk(0, 0, own, 0)
    chunk(0, 1, own, z.half)
    if z.tape:
        along_x, along_y, mid_x, mid_y = sends
        chunk(1, 0, along_x, 0)
        chunk(3, 0, along_x, z.half)
        along_x[z.rows :, :] = packed
        chunk(2, 1, along_y, 0)
        chunk(3, 1, along_y, z.half)
        chunk(2, 0, mid_x, 0)
        chunk(1, 1, mid_y, 0)
    else:
        for k, one in enumerate(sends, start=1):
            chunk(k, 0, one, 0)
            chunk(k, 1, one, z.half)
            one[z.rows :, :] = packed


def attend_back(z, info, i, ga, wo, saved):
    _, inv, _, *far, _ = saved
    feat, width, nk, nq, nl = z.feat, z.width, z.keys, z.query_rows, z.lanes
    in_specs = [whole(None)] * 3 + [pl.BlockSpec(memory_space=pl.ANY)] * 7
    if z.tape:
        part = (z.clip, z.tm, z.tape_rows, 128)
    else:
        part = (3, feat, width)
    sent, kept, *rest = call(
        functools.partial(attend_back_kernel, z, i),
        24,
        in_specs,
        [whole(part), whole(part), whole((8, width)), whole((nk, 2 * width)), whole((nq, width))],
        [
            jax.ShapeDtypeStruct(part, bf16),
            jax.ShapeDtypeStruct(part, bf16),
            jax.ShapeDtypeStruct((8, width), f32),
            jax.ShapeDtypeStruct((nk, 2 * width), bf16),
            jax.ShapeDtypeStruct((nq, width), bf16),
        ],
        [
            pltpu.VMEM((nl, width), bf16),
            pltpu.VMEM((nl, width), bf16),
            pltpu.VMEM((nk, nl), bf16),
            pltpu.VMEM((feat, width), f32),
            pltpu.VMEM((nq, width), bf16),
            pltpu.VMEM((nk, width), bf16),
            pltpu.VMEM((nk, width), bf16),
            pltpu.VMEM((nq, width), f32),
            pltpu.VMEM((feat, nk), bf16),
            pltpu.VMEM((feat, nq), bf16),
            pltpu.VMEM((nk, nl), bf16),
            pltpu.SemaphoreType.DMA((8,)),
        ],
        [ga, wo, inv, *[in_hbm(one) for one in far]],
        info,
        16 * nk * nl * width,
        nk * nl * 2,
    )
    if not z.tape:
        sent, kept = plain_to_tape(z, kept, info[1])
    return sent, kept, rest


def keys_back(z, info, saved, weight, first_lead, feed_small, steps):
    feat, width, nk, nq = z.feat, z.width, z.keys, z.query_rows
    uq, uk = saved[2], saved[10]
    there = pl.BlockSpec(memory_space=pl.ANY)
    in_specs = [there, whole((nq, feat)), there]
    in_specs += [whole(None)]
    in_specs += [whole((8, feat))]
    in_specs += [whole((8, width))] * z.steps
    in_specs += [whole((nk, 2 * width))] * z.steps + [whole((nq, width))] * z.steps
    if z.tape:
        sends = [(nq, feat), (z.rows, feat), (z.half, feat), (z.half, feat)]
    else:
        sends = [(nq, feat)] * (z.tm - 1)
    small = (16 * feat // 128, 128) if z.tape else (16, feat)
    return call(
        functools.partial(keys_back_kernel, z),
        24,
        in_specs,
        [whole((nq, feat)), whole(small)] + [whole(shape) for shape in sends],
        [
            jax.ShapeDtypeStruct((nq, feat), f32),
            jax.ShapeDtypeStruct(small, bf16 if z.tape else f32),
        ]
        + [jax.ShapeDtypeStruct(shape, bf16) for shape in sends],
        [
            pltpu.VMEM((nk, feat), f32),
            pltpu.VMEM((nq, feat), f32),
            pltpu.VMEM((16, feat), f32),
            pltpu.VMEM((nk, feat), bf16),
            pltpu.VMEM(weight.shape, bf16),
            pltpu.SemaphoreType.DMA((16,)),
        ],
        (in_hbm(uk), uq, in_hbm(weight), first_lead, feed_small)
        + tuple(step[j] for j in range(3) for step in steps),
        info,
        4 * feat * feat * (nq + 2 * nk),
        nk * feat * 4,
    )


def finish_kernel(z, info, *refs):
    *received, rows, gain, grad_first, out_mine, out_send = refs[1:]
    own = refs[0]
    mine = own[z.rows :].astype(bf16).astype(f32)
    if z.tape:
        got_x, got_y, got_xy, got_yx = (one[...].astype(f32) for one in received)
        first = own[: z.half] + got_x[: z.half] + got_xy[: z.half]
        second = own[z.half : z.rows] + got_y[: z.half] + got_yx
        lead = (mine + got_x[z.rows :]).astype(bf16).astype(f32) + got_xy[z.half :]
        total = jnp.concatenate([first, second, lead], 0)
    else:
        terms = [one[...].astype(f32) for one in received]
        leads = [mine] + [one[z.rows :] for one in terms]
        while len(leads) > 1:
            leads = [a + b for a, b in zip(leads[::2], leads[1::2])]
        total = jnp.concatenate([own[: z.rows] + sum(t[: z.rows] for t in terms), leads[0]], 0)
    normed, scale_inv = standardize(rows[...].astype(f32))
    back = norm_backward(total, gain[...], normed, scale_inv)
    rows_grad = (back[: z.rows] + grad_first[0 : z.rows, :]).astype(bf16)
    out_mine[...] = rows_grad[: z.half]
    out_send[0 : z.half, :] = rows_grad[z.half :]
    lead = total[z.rows :]
    lead_first = lead[LEADS : 2 * LEADS] + lead[2 * LEADS : 3 * LEADS]
    out_send[z.half :, :] = jnp.concatenate(
        [back[z.rows : z.rows + LEADS] + lead_first, jnp.zeros((LEAD_ROWS - LEADS, z.feat), f32)], 0
    ).astype(bf16)


def finish(z, info, own, received, rows, gain, grad_first):
    feat, nq = z.feat, z.query_rows
    return call(
        functools.partial(finish_kernel, z),
        16,
        [whole(one.shape) for one in (own, *received)]
        + [whole((nq, feat)), whole((1, feat)), whole((nq, feat))],
        [whole((z.half, feat)), whole((nq - z.half, feat))],
        [
            jax.ShapeDtypeStruct((z.half, feat), bf16),
            jax.ShapeDtypeStruct((nq - z.half, feat), bf16),
        ],
        [],
        (own, *received, rows, gain, grad_first),
        info,
        nq * feat * 20,
        nq * feat * 20,
    )


def place_blocks(z, t, whose, tape, row, out, lane_at):
    half = z.feat // (2 * z.clip)
    part = half // 2
    at = pl.multiple_of(whose * half + (t // 2) * part, 16)
    for j in range(3):
        block = tape[row + j * part : row + (j + 1) * part, :].astype(f32)
        lane = pl.multiple_of(lane_at(j) + (t % 2) * 128, 128)
        out[pl.ds(at, part), pl.ds(lane, 128)] = block


def assemble_feed_kernel(z, ff, info, *refs):
    me, core = info[0], info[1]
    expand_out, reduce_out, output_out = refs[8:]
    size = ff // FF_PARTS
    count = size * z.feat // (128 * z.tm)
    step = count + z.tape_rows
    part_r, part_e = size // z.tm, z.feat // z.clip
    for whose, (p_0, q_0, p_1, q_1) in ((core, refs[:4]), (1 - core, refs[4:8])):
        for k, tape, base in ((0, p_0, 0), (1, p_0, step), (2, p_1, 0), (3, p_1, step)):
            t = jnp.bitwise_xor(me, k)
            at = pl.multiple_of(whose * size + t * part_r, 16)
            for lane in range(z.feat // 128):
                block = tape[base + lane * part_r : base + (lane + 1) * part_r, :]
                reduce_out[pl.ds(at, part_r), lane * 128 : (lane + 1) * 128] = block.astype(f32)
            place_blocks(z, t, whose, tape, base + count, output_out, lambda j: j * z.width)
        for k, tape, base in ((0, q_0, 0), (2, q_0, step), (1, q_1, 0), (3, q_1, step)):
            at = (2 * jnp.bitwise_xor(me, k) + whose) * size
            for lane in range(size // 128):
                block = tape[base + lane * part_e : base + (lane + 1) * part_e, :]
                to = pl.multiple_of(at + lane * 128, 128)
                expand_out[:, pl.ds(to, 128)] = block.astype(f32)


def assemble_input_kernel(z, last, info, *refs):
    me, core = info[0], info[1]
    first, late, input_out = refs[:8], refs[8:16], refs[16]
    for core_of, whose in ((0, core), (1, 1 - core)):
        for n, k in enumerate((0, 2, 1, 3)):
            t = jnp.bitwise_xor(me, k)
            tape = late[core_of * 4 + k]
            row = (last if n % 2 else last // 2) * z.tape_rows
            parts = ((0, first[core_of * 4 + n], row), (1, tape, 0), (2, tape, z.tape_rows))
            for i, tape, row in parts:
                lane_at = lambda j: j * z.feat + i * z.width
                place_blocks(z, t, whose, tape, row, input_out, lane_at)


def assemble(z, info, tapes, late, ff):
    rows = z.feat // z.clip
    shapes = [(rows, ff), (ff // z.clip, z.feat), (rows, z.feat)]
    feed_grads = call(
        functools.partial(assemble_feed_kernel, z, ff),
        24,
        [whole(tapes[0].shape)] * 8,
        [whole(shape) for shape in shapes],
        [jax.ShapeDtypeStruct(shape, f32) for shape in shapes],
        [],
        tapes,
        info,
        1000,
        32 * tapes[0].size,
    )
    last = tapes[0].shape[0] // z.tape_rows - 1
    first_specs = [whole(None)] * 8
    first = [tapes[1], tapes[1], tapes[3], tapes[3], tapes[5], tapes[5], tapes[7], tapes[7]]
    input_grad = call(
        functools.partial(assemble_input_kernel, z, last),
        24,
        first_specs + [whole((2 * z.tape_rows, 128))] * 8,
        whole((rows, 3 * z.feat)),
        jax.ShapeDtypeStruct((rows, 3 * z.feat), f32),
        [],
        (*first, *late),
        info,
        1000,
        64 * late[0].size,
    )
    return (*feed_grads, input_grad)


def flip(count, k):
    return [(i, i ^ k) for i in range(count)]


def bit_of(index, bit):
    return (index >> bit) & 1


def bits_of(count):
    return count.bit_length() - 1


def pick(x, dim, index):
    return lax.dynamic_index_in_dim(x, index, dim, keepdims=False)


def add(kept, got):
    return (kept.astype(f32) + got.astype(f32)).astype(bf16)


def by_bits(x, dim, count):
    return x.reshape(x.shape[:dim] + (2,) * bits_of(count) + x.shape[dim + 1 :])


def halves(x, dim, axis, bit):
    mine = bit_of(lax.axis_index(axis), bit)
    return pick(x, dim, 1 - mine), pick(x, dim, mine)


def across(x, axis, bit):
    return lax.ppermute(x, axis, flip(lax.axis_size(axis), 1 << bit))


def scatter(x, dim, axis, bits):
    for bit in bits:
        sent, kept = halves(x, dim, axis, bit)
        x = add(kept, across(sent, axis, bit))
    return x


def scatter_up(x, dim, axis, bits):
    for bit in bits:
        at = dim + bits_of(lax.axis_size(axis)) - 1 - bit
        sent, kept = halves(x, at, axis, bit)
        x = add(kept, across(sent, axis, bit))
    return x


def peers(x, dim, axis):
    me = lax.axis_index(axis)
    return [pick(x, dim, me ^ k) for k in range(1, lax.axis_size(axis))]


def to_peers(sent, axis):
    count = lax.axis_size(axis)
    return [lax.ppermute(one, axis, flip(count, k)) for k, one in enumerate(sent, start=1)]


def add_all(own, got):
    total = own.astype(f32)
    for one in got:
        total = total + one.astype(f32)
    return total.astype(bf16)


def in_order(x, got, axis):
    me = lax.axis_index(axis)
    out = jnp.zeros((1 + len(got),) + x.shape, x.dtype)
    for k, one in enumerate([x, *got]):
        out = lax.dynamic_update_index_in_dim(out, one, me ^ k, 0)
    return out


def tie(*values):
    return lax.optimization_barrier(values)


def per_device(
    patches,
    lead_tokens,
    lengths,
    input_weight,
    input_bias,
    output_weight,
    output_bias,
    first_gain,
    first_shift,
    second_gain,
    second_shift,
    expand_weight,
    expand_bias,
    reduce_weight,
    reduce_bias,
    cot_patches,
    cot_lead,
):
    tm_count = lax.axis_size("tm")
    clip_count = lax.axis_size("clip")
    z = Sizes(patches.shape, tm_count, clip_count)
    feat, ff = expand_weight.shape
    core, place = lax.axis_index("freq"), lax.axis_index("tm")
    info = jnp.stack([place, core]).astype(jnp.int32)
    row = lambda vector: vector.astype(f32)[None, :]

    def by_clip(array):
        parts = array.reshape(z.fr, z.blocks, BLOCK_COLS, z.clips, feat)
        parts = parts.transpose(3, 1, 0, 2, 4).reshape(z.clips, z.half, feat)
        return (
            lax.dynamic_index_in_dim(parts, core, 0, keepdims=False),
            lax.dynamic_index_in_dim(parts, 1 - core, 0, keepdims=False),
        )

    def lead_of(array):
        mine = lax.dynamic_index_in_dim(array, core, 0, keepdims=False)
        return jnp.pad(mine, ((0, LEAD_ROWS - LEADS), (0, 0)))

    own_half, other_half = by_clip(patches)
    pieces = []
    for k in range(tm_count):
        pieces.append(lax.ppermute(own_half, "tm", flip(tm_count, k)) if k else own_half)
        pieces.append(
            lax.ppermute(other_half, ("freq", "tm"), flip(2 * tm_count, tm_count | k))
        )
    lead = lead_of(lead_tokens)
    rows = jnp.concatenate([pieces[0], pieces[1], lead], 0)
    own_cot, other_cot = by_clip(cot_patches)
    lead_cot = lead_of(cot_lead) * (place == 0).astype(bf16)
    cot = jnp.concatenate([own_cot, lax.ppermute(other_cot, "freq", flip(2, 1)), lead_cot], 0)
    cot_got = lax.ppermute(cot, "freq", flip(2, 1))

    length = lax.dynamic_index_in_dim(lengths, core, 0, keepdims=False)
    spots = np.arange(z.keys) - LEAD_ROWS
    columns = np.where(spots < 0, 1 << 20, spots // z.block * BLOCK_COLS + spots % BLOCK_COLS)
    columns[:LEADS] = -1
    live = jnp.where(jnp.asarray(columns, jnp.int32)[:, None] < length, 0.0, NEG_FILL)
    live = jnp.broadcast_to(live.astype(f32), (z.keys, 128))

    saved = attend(
        z,
        info,
        pieces,
        lead,
        input_weight,
        row(input_bias[:feat]),
        row(input_bias[feat:]),
        row(first_gain),
        row(first_shift),
        live,
    )
    mixed_low = saved[0]
    paired = clip_count == FF_PARTS // 2
    if not paired:
        share = (clip_count, 2, ff // (2 * clip_count))
        expand_weight = expand_weight.reshape(feat, *share).swapaxes(1, 2).reshape(feat, ff)
        expand_bias = expand_bias.reshape(share).swapaxes(0, 1).reshape(ff)
        reduce_weight = reduce_weight.reshape(*share, feat).swapaxes(0, 1).reshape(ff, feat)
    gain_two, shift_two = row(second_gain), row(second_shift)
    swap = lambda x: across(x, "freq", 0)
    size = ff // FF_PARTS
    half = clip_count // 2
    tm_bits, clip_bits = bits_of(tm_count), bits_of(clip_count)
    low_bits, high_bits = list(range(tm_bits)), list(range(tm_bits))[::-1]
    split = max(1, tm_count // (FF_PARTS // 2))

    total, unit, inv, low = blend(
        z, info, mixed_low, rows, output_weight, row(output_bias), gain_two, shift_two
    )
    feed_bias, acc, acc_send, grad, grad_send, *sums = feed(
        z, info, paired, low, swap(low), cot, cot_got, expand_weight, row(expand_bias), reduce_weight
    )
    if z.tape:
        out_ra, out_rb, own_r, out_ea, out_eb, own_e = sums
    else:
        sum_r, sum_e = sums
        rows_r, rows_e = ff // (2 * clip_count * tm_count), feat // (clip_count * split)
        sum_r = sum_r.reshape(clip_count, tm_count, rows_r, feat // 128, 128).swapaxes(2, 3)
        sum_e = sum_e.reshape(-1, clip_count, split, rows_e, size // 128, 128)
        sum_e = sum_e.transpose(0, 2, 1, 4, 3, 5)
        sum_r = sum_r.reshape(clip_count, tm_count, -1, 128)
        sum_e = sum_e.reshape(tm_count, clip_count, -1, 128).swapaxes(0, 1)
        out_r, own_r = halves(by_bits(sum_r, 1, tm_count), 1 + tm_bits - 1, "tm", 0)
        out_e, own_e = halves(by_bits(sum_e, 1, tm_count), 1, "tm", tm_bits - 1)
        out_ra, out_rb, out_ea, out_eb = out_r[:half], out_r[half:], out_e[:half], out_e[half:]
    grad, grad_send, acc_send, out_ra, out_ea, out_rb, out_eb = tie(
        grad, grad_send, acc_send, out_ra, out_ea, out_rb, out_eb
    )
    across_r = lambda x: across(x, "tm", 0)
    across_e = lambda x: across(x, "tm", tm_bits - 1)
    across_z = lambda x: across(x, "clip", clip_bits - 1)
    halves_z = lambda x: halves(by_bits(x, 0, clip_count), 0, "clip", clip_bits - 1)
    rest_z = lambda x: scatter(x, 0, "clip", range(clip_bits - 1)[::-1])

    got_ra, got_ea = across_r(out_ra), across_e(out_ea)
    acc_got = swap(acc_send)
    grad_first, grad_low, sent_o, kept_o, small_two = blend_back(
        z, info, grad, swap(grad_send), unit, inv, cot, mixed_low, gain_two
    )
    if not z.tape:
        sent_o, kept_o = plain_to_tape(z, kept_o, core)
    got_o = swap(sent_o)
    sent_0, kept_0, rest_0 = attend_back(z, info, 0, grad_low, output_weight, saved)
    grad_low, got_ra, got_ea, got_o, acc_got, sent_0, out_rb, out_eb = tie(
        grad_low, got_ra, got_ea, got_o, acc_got, sent_0, out_rb, out_eb
    )
    block = (total + acc + acc_got.astype(f32) + row(reduce_bias)).astype(bf16)
    block_mine, block_send = block[: z.half], block[z.half :]
    out_o, own_o = halves_z(add(kept_o, got_o))
    grad_low, out_o = tie(grad_low, out_o)
    got_rb, got_eb, got_0, got_oz = across_r(out_rb), across_e(out_eb), swap(sent_0), across_z(out_o)
    block_got = swap(block_send)
    sent_1, kept_1, rest_1 = attend_back(z, info, 1, grad_low, output_weight, saved)
    grad_low, got_rb, got_eb, got_0, got_oz, block_got, sent_1 = tie(
        grad_low, got_rb, got_eb, got_0, got_oz, block_got, sent_1
    )
    sum_ra, sum_rb = add(own_r[:half], got_ra), add(own_r[half:], got_rb)
    if z.tape:
        first_line = place // 2 == 0
        sum_ra, sum_rb = (
            jnp.where(first_line, sum_rb, sum_ra),
            jnp.where(first_line, sum_ra, sum_rb),
        )
    sum_r = jnp.concatenate([sum_ra, sum_rb], 0)
    sum_e = add(own_e, jnp.concatenate([got_ea, got_eb], 0))
    sum_r = scatter_up(sum_r, 1, "tm", low_bits[1:-1])
    sum_e = scatter(sum_e, 1, "tm", high_bits[1:-1])
    out_r, own_r = halves(sum_r, 1, "tm", low_bits[-1])
    out_e, own_e = halves(sum_e, 1, "tm", high_bits[-1])
    sum_o = add(own_o, got_oz)
    out_0, own_0 = halves_z(add(kept_0, got_0))
    grad_low, out_r, out_e, sum_o, out_0 = tie(grad_low, out_r, out_e, sum_o, out_0)
    got_r, got_e = across(out_r, "tm", low_bits[-1]), across(out_e, "tm", high_bits[-1])
    got_0z, got_1 = across_z(out_0), swap(sent_1)
    sum_o = rest_z(sum_o)

    def split_tm(x, *more):
        x = by_bits(x, 1, tm_count)
        parts = [x[:half], x[half:]]
        if more:
            parts = [jnp.concatenate([p, by_bits(m, 1, tm_count)], 0) for p, m in zip(parts, more)]
        return (
            *halves(parts[0], tm_bits, "tm", 0),
            *halves(parts[1], 1, "tm", tm_bits - 1),
        )

    sent_2, kept_2, rest_2 = attend_back(z, info, 2, grad_low, output_weight, saved)
    sent_2, got_r, got_e, got_0z, got_1, sum_o, *rest_2 = tie(
        sent_2, got_r, got_e, got_0z, got_1, sum_o, *rest_2
    )
    sum_r, sum_e = add(own_r, got_r), add(own_e, got_e)
    out_r, own_r = halves_z(sum_r)
    sum_0 = add(own_0, got_0z)
    out_1x, own_1x, out_1y, own_1y = split_tm(add(kept_1, got_1))
    feed_bias = feed_bias[:, 0:1] * (jnp.arange(2) == core).astype(f32)[:, None]
    if not paired:
        feed_bias = feed_bias.swapaxes(0, 1).reshape(2, clip_count, -1).swapaxes(0, 1)
    feed_small = jnp.concatenate([small_two[:4], feed_bias.reshape(-1, feat)], 0)
    out_e, own_e = halves_z(sum_e)
    out_r, out_e, sum_0, out_1x, out_1y, sent_2, *rest_2 = tie(
        out_r, out_e, sum_0, out_1x, out_1y, sent_2, *rest_2
    )
    got_r, got_2, got_1x, got_1y = across_z(out_r), swap(sent_2), across_r(out_1x), across_e(out_1y)
    got_e = across_z(out_e)
    sum_0 = rest_z(sum_0)
    own, small, *sends = keys_back(
        z, info, saved, input_weight, grad_first, feed_small, (rest_0, rest_1, rest_2)
    )
    got_2, got_1x, got_1y, sum_0, own, small, *sends = tie(
        got_2, got_1x, got_1y, sum_0, own, small, *sends
    )
    out_2x, own_2x, out_2y, own_2y = split_tm(add(kept_2, got_2), sum_o[None], sum_0[None])
    finish_args = (rows, row(first_gain), grad_first)
    if z.tape:
        flat = lambda *parts: jnp.concatenate([part.reshape(-1, 128) for part in parts], 0)
        count = small.shape[0]
        unpack = lambda got, like: (got[:-count].reshape(like.shape), got[-count:])
        across_x, across_y = lambda x: across(x, "tm", 0), lambda x: across(x, "tm", 1)
        across_zz = lambda x: across(x, "clip", 0)
        along_x, along_y, mid_x, mid_y = sends
        msg_x, out_2y, along_x, along_y = tie(flat(out_2x, small), out_2y, along_x, along_y)
        msg_x, out_2y = across_x(msg_x), across_y(out_2y)
        got_x, got_y = across_x(along_x), across_y(along_y)
        msg_x, got_2y = tie(msg_x, out_2y)
        got_2x, got_small = unpack(msg_x, own_2x)
        small = add(small, got_small)
        sum_x = jnp.concatenate([add(own_1x, got_1x), add(own_2x, got_2x)], 0)
        sum_y = jnp.concatenate([add(own_1y, got_1y), add(own_2y, got_2y)], 0)
        out_x, own_x = halves(sum_x, 1, "tm", 1)
        out_y, own_y = halves(sum_y, 1, "tm", 0)
        small, = tie(small)
        msg_x, out_y = tie(flat(out_x, small), out_y)
        msg_x, got_y2, got_r, got_e = tie(across_y(msg_x), across_x(out_y), got_r, got_e)
        got_x2, got_small = unpack(msg_x, own_x)
        small = add(small, got_small)
        sum_x, sum_y = add(own_x, got_x2), add(own_y, got_y2)
        late = jnp.concatenate(
            [jnp.concatenate([one[:2], one[2:4]], 1) for one in (sum_x, sum_y)], 0
        )
        out_l, own_l = halves_z(late)
        out_r, own_r = halves(add(own_r, got_r), 0, "clip", 0)
        out_e, own_e = halves(add(own_e, got_e), 0, "clip", 0)
        small, = tie(small)
        msg_l, msg_f = tie(flat(out_l, small), flat(out_r, out_e))
        msg_l, got_f, got_x, got_y = tie(across_z(msg_l), across_zz(msg_f), got_x, got_y)
        got_l, got_small = unpack(msg_l, own_l)
        small = add(small, got_small)
        out_l, own_l = halves(add(own_l, got_l), 0, "clip", 0)
        n = out_r.shape[0]
        ready_p = flat(add(own_r, got_f[:n]), sum_x[4])
        ready_q = flat(add(own_e, got_f[n:]), sum_y[4])
        lead = add(along_x[z.rows :], got_x[z.rows :])
        out_xy = jnp.concatenate([add(mid_x, got_x[z.half : z.rows]), lead], 0)
        out_yx = add(mid_y, got_y[z.half :])
        small, = tie(small)
        msg_l, ready_p, ready_q, out_xy, out_yx = tie(
            flat(out_l, small), ready_p, ready_q, out_xy, out_yx
        )
        msg_l, got_p, got_q, got_xy, got_yx = tie(
            across_zz(msg_l),
            across_x(ready_p),
            across_y(ready_q),
            across_y(out_xy),
            across_x(out_yx),
        )
        got_l, got_small = unpack(msg_l, own_l)
        small, late = add(small, got_small), add(own_l, got_l)
        near_p, near_q = flat(ready_p, got_p), flat(ready_q, got_q)
        near_p, near_q, late, small = tie(near_p, near_q, late, small)
        far_p, far_q = across_y(near_p), across_x(near_q)
        late_all = [late] + to_peers([late] * 3, "tm")
        small = small.astype(f32) + swap(small).astype(f32)
        small = small.reshape(-1, 16, 128).swapaxes(0, 1).reshape(16, feat)
        received = [got_x, got_y, got_xy, got_yx]
        grad_mine, grad_send = finish(z, info, own, received, *finish_args)
        grad_send, far_p, far_q, *late_all = tie(grad_send, far_p, far_q, *late_all)
    else:
        received = to_peers(sends, "tm")
        got_2x, got_2y, got_e = across_r(out_2x), across_e(out_2y), across_z(out_e)
        sum_x = jnp.concatenate([add(own_1x, got_1x), add(own_2x, got_2x)], 0)
        sum_y = jnp.concatenate([add(own_1y, got_1y), add(own_2y, got_2y)], 0)
        sum_x = scatter_up(sum_x, 1, "tm", low_bits[1:])
        sum_y = scatter(sum_y, 1, "tm", high_bits[1:])
        sum_r, sum_e = rest_z(add(own_r, got_r)), rest_z(add(own_e, got_e))
        ready = jnp.concatenate([sum_r, sum_e, sum_x[2 * half], sum_y[2 * half]], 0)
        late = jnp.concatenate(
            [
                jnp.concatenate([one[:half], one[half : 2 * half]], 1)
                for one in (sum_x, sum_y)
            ],
            0,
        )
        late = scatter(by_bits(late, 0, clip_count), 0, "clip", range(clip_bits)[::-1])
        ready = jnp.concatenate([ready, late], 0)
        ready_all = [ready] + to_peers([ready] * (tm_count - 1), "tm")
        small = small + swap(small)
        for axis, bits in (("tm", tm_bits), ("clip", clip_bits)):
            for bit in range(bits):
                small = small + across(small, axis, bit)
        grad_mine, grad_send = finish(z, info, own, received, *finish_args)

    here = lax.axis_index("clip")

    def shard(vector):
        count = vector.shape[0] // clip_count
        return lax.dynamic_slice_in_dim(vector, here * count, count, 0)

    input_bias_grad = shard(small[0:2].reshape(-1))
    gain_one_grad, shift_one_grad, output_bias_grad, gain_two_grad, shift_two_grad = (
        shard(small[i]) for i in range(2, 7)
    )
    reduce_bias_grad = shard(small[7])
    expand_bias_grad = shard(small[8:12].reshape(-1))

    count_f = feat * ff // (2 * clip_count * tm_count * 128)
    if z.tape:
        tapes = [near_p, near_q, far_p, far_q]
        tapes, late_all = tapes + [swap(one) for one in tapes], late_all + [swap(one) for one in late_all]
        expand_weight_grad, reduce_weight_grad, output_weight_grad, input_weight_grad = assemble(
            z, info, tapes, late_all, ff
        )
    else:
        tapes = jnp.stack(ready_all)
        other_tapes = swap(tapes)
        both = in_order(tapes, [other_tapes], "freq")
        both = pick(jnp.stack([both[:, np.arange(tm_count) ^ t] for t in range(tm_count)]), 0, place)
        part_r, part_e = both[:, :, :count_f], both[:, :, count_f : 2 * count_f]
        rows_r, rows_e = ff // (2 * clip_count * tm_count), feat // (clip_count * split)
        part_r = part_r.reshape(2, tm_count, feat // 128, rows_r, 128).swapaxes(2, 3)
        reduce_weight_grad = part_r.reshape(ff // clip_count, feat).astype(f32)
        part_e = part_e.reshape(2, FF_PARTS // 2, split, size // 128, rows_e, 128)
        part_e = part_e.transpose(2, 4, 1, 0, 3, 5)
        if not paired:
            part_e = part_e.swapaxes(2, 3).reshape(feat // clip_count, 2, clip_count, -1)
            part_e = part_e.swapaxes(1, 2)
        expand_weight_grad = part_e.reshape(feat // clip_count, ff).astype(f32)
        lanes = z.width // 128
        part_a = both[:, :, 2 * count_f :].reshape(2, tm_count // lanes, lanes, 4, 3, -1, 128)
        part_a = part_a.transpose(0, 1, 5, 3, 4, 2, 6)
        part_a = part_a.reshape(feat // clip_count, 4, 3, z.width).astype(f32)
        output_weight_grad = part_a[:, 0].reshape(-1, feat)
        input_weight_grad = part_a[:, 1:].swapaxes(1, 2).reshape(-1, 3 * feat)

    def patches_of(mine, theirs):
        first = jnp.where(core == 0, mine, theirs[: z.half])
        second = jnp.where(core == 0, theirs[: z.half], mine)
        pair = jnp.stack([first, second], 0).reshape(
            z.clips, z.blocks, z.fr, BLOCK_COLS, feat
        )
        return pair.transpose(2, 1, 3, 0, 4).reshape(z.fr, z.tc, z.clips, feat)

    def leads_of(sent, got):
        mine, theirs = sent[z.half : z.half + LEADS], got[z.half : z.half + LEADS]
        first = jnp.where(core == 0, mine, theirs)
        second = jnp.where(core == 0, theirs, mine)
        return jnp.stack([first, second], 0)

    grad_got = swap(grad_send)
    return (
        patches_of(block_mine, block_got),
        leads_of(block_send, block_got),
        patches_of(grad_mine, grad_got),
        leads_of(grad_send, grad_got),
        input_weight_grad,
        input_bias_grad,
        output_weight_grad,
        output_bias_grad,
        gain_one_grad,
        shift_one_grad,
        gain_two_grad,
        shift_two_grad,
        expand_weight_grad,
        expand_bias_grad,
        reduce_weight_grad,
        reduce_bias_grad,
    )


def solution(mesh):
    rows = P("freq", "tm", "clip", None)
    lead = P("clip", None, None)
    in_specs = (rows, lead, P("clip")) + (P(),) * 12 + (rows, lead)
    matrix, vector = P("clip", None), P("clip")
    out_specs = (rows, lead, rows, lead) + (matrix, vector) * 2 + (vector,) * 4 + (matrix, vector) * 2
    return jax.shard_map(
        per_device, mesh=mesh, in_specs=in_specs, out_specs=out_specs, check_vma=False
    )
```

```python
import functools
import math

import jax
import jax.numpy as jnp
import numpy as np
from jax import lax
from jax.experimental import pallas as pl
from jax.experimental.pallas import tpu as pltpu
from jax.sharding import PartitionSpec as P

HEADS = 12
EPSILON = 1e-06
NEG_FILL = -1e30
MAX_LENGTH = 101
LEADS = 2
LEAD_ROWS = 16
BLOCK_COLS = 8
GROUP = 4
FF_PARTS = 8
bf16 = jnp.bfloat16
f32 = jnp.float32


def mm(a, b):
    return lax.dot_general(a, b, (((1,), (0,)), ((), ())), preferred_element_type=f32)


def mm_nt(a, b):
    return lax.dot_general(a, b, (((1,), (1,)), ((), ())), preferred_element_type=f32)


def standardize(rows):
    center = rows - jnp.mean(rows, -1, keepdims=True)
    scale_inv = lax.rsqrt(jnp.mean(center * center, -1, keepdims=True) + EPSILON)
    return center * scale_inv, scale_inv


def norm_backward(grad_out, gain_row, normed, scale_inv):
    scaled = grad_out * gain_row
    return scale_inv * (
        scaled
        - jnp.mean(scaled, -1, keepdims=True)
        - normed * jnp.mean(scaled * normed, -1, keepdims=True)
    )


def head_mask(head, width, head_width):
    lane_head = lax.broadcasted_iota(jnp.int32, (1, width), 1) // head_width
    return (lane_head == head).astype(f32)


class Sizes:
    def __init__(self, patches_shape, tm_count, clip_count):
        fr_local, tc_local, clips, feat = patches_shape
        self.fr, self.tc, self.clips, self.feat = fr_local, tc_local, clips, feat
        self.tm, self.clip = tm_count, clip_count
        self.tape = clip_count == 4 and tm_count == 4
        self.tape_rows = 3 * feat * 2 // (2 * clip_count * tm_count)
        self.blocks = tc_local // BLOCK_COLS
        self.half_block = fr_local * BLOCK_COLS
        self.block = 2 * self.half_block
        self.half = self.blocks * self.half_block
        self.rows = 2 * self.half
        self.query_rows = self.rows + LEAD_ROWS
        self.key_blocks = -(-MAX_LENGTH // BLOCK_COLS)
        self.keys = LEAD_ROWS + self.key_blocks * self.block
        self.head_width = feat // HEADS
        self.width = GROUP * self.head_width
        self.steps = HEADS // GROUP
        self.lanes = GROUP * self.rows + 128


def call(kernel, room, in_specs, out_specs, out_shape, scratch, args, info, flops, moved, aliases={}):
    return pl.pallas_call(
        kernel,
        out_shape=out_shape,
        in_specs=[pl.BlockSpec(memory_space=pltpu.SMEM), *in_specs],
        out_specs=out_specs,
        scratch_shapes=scratch,
        input_output_aliases=aliases,
        compiler_params=pltpu.CompilerParams(vmem_limit_bytes=room * 1024 * 1024),
        cost_estimate=pl.CostEstimate(flops=flops, bytes_accessed=moved, transcendentals=0),
    )(info, *args)


def in_vmem(x):
    return pltpu.with_memory_space_constraint(x, pltpu.VMEM)


def in_hbm(x):
    return pltpu.with_memory_space_constraint(x, pltpu.HBM)


def whole(shape):
    return pl.BlockSpec(memory_space=pltpu.VMEM)


def chunks_of(z):
    full = z.lanes // 256
    spans = [(c * 256, 256) for c in range(full)]
    if z.lanes % 256:
        spans.append((full * 256, z.lanes % 256))
    return spans


def spread_heads(z, rows, out_ref):
    for head in range(GROUP):
        mask = head_mask(head, z.width, z.head_width)
        part = (rows * mask).astype(bf16)
        out_ref[head * z.rows : (head + 1) * z.rows, :] = part[: z.rows]
        at = GROUP * z.rows + head * LEAD_ROWS
        out_ref[at : at + LEAD_ROWS, :] = part[z.rows :]
    at = GROUP * (z.rows + LEAD_ROWS)
    out_ref[at:, :] = jnp.zeros((z.lanes - at, z.width), bf16)


def join_heads(z, spread):
    patch_part, lead_part = None, None
    for head in range(GROUP):
        mask = head_mask(head, z.width, z.head_width)
        at = GROUP * z.rows + head * LEAD_ROWS
        one = spread[head * z.rows : (head + 1) * z.rows] * mask
        two = spread[at : at + LEAD_ROWS] * mask
        patch_part = one if patch_part is None else patch_part + one
        lead_part = two if lead_part is None else lead_part + two
    return jnp.concatenate([patch_part, lead_part], 0)


class Copies:
    def __init__(self, sems):
        self.sems, self.going = sems, {}

    def start(self, name, source, to):
        copy = pltpu.make_async_copy(source, to, self.sems.at[len(self.going)])
        copy.start()
        self.going[name] = copy

    def wait(self, *names):
        for name in names:
            self.going[name].wait()


def attend_kernel(z, info, *refs):
    refs = list(refs)
    take = lambda n: [refs.pop(0) for _ in range(n)]
    pieces = take(2 * z.tm)
    lead, weight, bias_q, bias_v, gain, shift, live = take(7)
    low_out, inv_out, uq, q_out, k_out, v_out, mixed_out, hk_t_out, hq_t_out, p_out, uk_out = take(11)
    spread, total, hk, hq, uk, w, p, q_all, k_all, v_all, mixed_all, hk_t, hq_t, sems = take(14)
    me = info[0]
    copies = Copies(sems)
    span = lambda part, i: slice((part * z.steps + i) * z.width, (part * z.steps + i + 1) * z.width)
    copies.start("w", weight, w)
    gain_row, shift_row = gain[...], shift[...]

    def hidden(rows):
        unit, _ = standardize(rows.astype(f32))
        return unit.astype(bf16), (unit * gain_row + shift_row).astype(bf16)

    unit, low = hidden(lead[...])
    uk[0:LEAD_ROWS, :] = unit
    hk[0:LEAD_ROWS, :] = low
    hq[z.rows :, :] = low
    uq[z.rows :, :] = unit
    hb = z.half_block
    for k in range(z.tm):
        source = jnp.bitwise_xor(me, k)
        for half in range(2):
            unit, low = hidden(pieces[2 * k + half][...])
            if k == 0:
                hq[half * z.half : (half + 1) * z.half, :] = low
                uq[half * z.half : (half + 1) * z.half, :] = unit
            for b in range(z.blocks):
                at = LEAD_ROWS + (source * z.blocks + b) * z.block + half * hb
                at = pl.multiple_of(at, 16)
                uk[pl.ds(at, hb), :] = unit[b * hb : (b + 1) * hb]
                hk[pl.ds(at, hb), :] = low[b * hb : (b + 1) * hb]
    copies.start("uk", uk.at[0 : z.keys, :], uk_out)
    hk_all, hq_all = hk[0 : z.keys, :], hq[...]
    hk_t[...] = jnp.transpose(hk_all)
    hq_t[...] = jnp.transpose(hq_all)
    copies.start("hk_t", hk_t, hk_t_out)
    copies.start("hq_t", hq_t, hq_t_out)
    copies.wait("w")
    outs = ((q_all, q_out), (k_all, k_out), (v_all, v_out), (mixed_all, mixed_out))

    def group_copies(i):
        pairs = [(source.at[i], to.at[i]) for source, to in outs] + [(p.at[i % 2], p_out.at[i])]
        return [
            pltpu.make_async_copy(source, to, sems.at[8 + i * len(pairs) + n])
            for n, (source, to) in enumerate(pairs)
        ]

    def group(i, carry):
        columns = lambda part: pl.ds(pl.multiple_of((part * z.steps + i) * z.width, z.width), z.width)
        slot = i % 2
        q_copy, k_copy, v_copy, mixed_copy, p_copy = group_copies(i)

        @pl.when(i >= 2)
        def _():
            group_copies(i - 2)[-1].wait()

        q = (mm(hq[...], w[:, columns(0)]) + bias_q[:, columns(0)]).astype(bf16)
        q_all[i] = q
        spread_heads(z, q.astype(f32) * (z.head_width**-0.5), spread)
        k = mm(hk[0 : z.keys, :], w[:, columns(1)]).astype(bf16)
        k_all[i] = k
        v = (mm(hk[0 : z.keys, :], w[:, columns(2)]) + bias_v[:, columns(0)]).astype(bf16)
        v_all[i] = v
        q_copy.start()
        k_copy.start()
        v_copy.start()
        for at, size in chunks_of(z):
            scores = mm_nt(k, spread[at : at + size, :])
            scores = scores + jnp.concatenate([live[...]] * (size // 128), 1)
            peak = jnp.max(scores, 0, keepdims=True)
            weights = jnp.exp(scores - peak)
            total[i, 0:1, at : at + size] = jnp.sum(weights, 0, keepdims=True)
            p[slot, :, at : at + size] = weights.astype(bf16)
        p_copy.start()
        inverse = 1.0 / total[i, 0:1, :]
        inv_out[i] = jnp.broadcast_to(inverse, (8, z.lanes))
        mixed = mm(jnp.transpose(v), p[slot]) * inverse
        mixed = join_heads(z, jnp.transpose(mixed))
        mixed_all[i] = mixed
        mixed_copy.start()
        low_out[:, columns(0)] = mixed.astype(bf16)
        return carry

    lax.fori_loop(0, z.steps, group, 0)
    for i in range(z.steps):
        *near, p_copy = group_copies(i)
        for copy in near:
            copy.wait()
        if i >= z.steps - 2:
            p_copy.wait()
    copies.wait("uk", "hk_t", "hq_t")


def attend(z, me_info, pieces, lead, weight, bias_q, bias_v, gain, shift, live):
    feat, width, nk, nq, nl = z.feat, z.width, z.keys, z.query_rows, z.lanes
    there = pl.BlockSpec(memory_space=pl.ANY)
    in_specs = [whole((z.half, feat))] * (2 * z.tm) + [whole((LEAD_ROWS, feat)), there]
    in_specs += [whole((1, feat))] * 4 + [whole((nk, 128))]
    shapes = [((nq, feat), bf16), ((z.steps, 8, nl), f32), ((nq, feat), bf16)]
    heads = lambda rows, kind: ((z.steps, rows, width), kind)
    far = [heads(nq, bf16), heads(nk, bf16), heads(nk, bf16), heads(nq, f32)]
    far += [((feat, nk), bf16), ((feat, nq), bf16), ((z.steps, nk, nl), bf16), ((nk, feat), bf16)]
    return call(
        functools.partial(attend_kernel, z),
        38,
        in_specs,
        [whole(None)] * 3 + [there] * 8,
        [jax.ShapeDtypeStruct(*one) for one in shapes] + [pltpu.HBM(*one) for one in far],
        [
            pltpu.VMEM((nl, width), bf16),
            pltpu.VMEM((z.steps, 8, nl), f32),
            pltpu.VMEM((LEAD_ROWS + z.tm * z.rows, feat), bf16),
            pltpu.VMEM((nq, feat), bf16),
            pltpu.VMEM((LEAD_ROWS + z.tm * z.rows, feat), bf16),
            pltpu.VMEM((feat, 3 * feat), bf16),
            pltpu.VMEM((2, nk, nl), bf16),
            *[pltpu.VMEM(*one) for one in far[:6]],
            pltpu.SemaphoreType.DMA((32,)),
        ],
        (*pieces, lead, in_hbm(weight), bias_q, bias_v, gain, shift, live),
        me_info,
        2 * feat * feat * (nq + 2 * nk) + 4 * z.steps * nk * nl * width,
        z.steps * nk * nl * 2,
    )


def blend_kernel(z, info, mixed, rows, wo, bo, gain, shift, sum_out, unit, inv, low):
    total = rows[...].astype(f32) + mm(mixed[...], wo[...]) + bo[...]
    sum_out[...] = total
    normed, scale_inv = standardize(total)
    unit[...] = normed
    inv[...] = jnp.broadcast_to(scale_inv, inv.shape)
    low[...] = (normed * gain[...] + shift[...]).astype(bf16)


def blend(z, info, mixed, rows, wo, bo, gain, shift):
    wide, narrow = ((z.query_rows, z.feat), f32), ((z.query_rows, z.feat), bf16)
    shapes = [wide, wide, ((z.query_rows, 128), f32), narrow]
    return call(
        functools.partial(blend_kernel, z),
        12,
        [whole(None)] * 6,
        [whole(None)] * 4,
        [jax.ShapeDtypeStruct(*one) for one in shapes],
        [],
        (mixed, rows, wo, bo, gain, shift),
        info,
        2 * z.query_rows * z.feat * z.feat,
        z.query_rows * z.feat * 14,
    )


def feed_kernel(z, paired, info, *refs):
    refs = list(refs)
    take = lambda n: [refs.pop(0) for _ in range(n)]
    low, low_other, cot, cot_other, be, we_in, wr_in = take(7)
    dbe, acc, acc_other, grad, grad_other = take(5)
    outs = take(4 if z.tape else 2)
    we, wr, dwr, dwe, low_t, cot_all, acc_sum, grad_sum, sems = take(9)
    steps = FF_PARTS // 2
    size = we.shape[2] // 2
    nq = z.query_rows
    core = info[1]
    col, line = info[0] % 2, info[0] // 2
    place = lambda i: jnp.bitwise_xor(i, 2 * (1 - line)) if z.tape else i
    at = lambda i: pl.multiple_of(
        (2 * place(i) + core if paired else steps * core + i) * size, size
    )
    copies = Copies(sems)
    names = []

    def leave(name, source, to):
        copies.start(name, source, to)
        names.append(name)

    for i in range(steps):
        pair, span = i // 2, slice(i % 2 * size, (i % 2 + 1) * size)
        copies.start(f"we{i}", we_in.at[:, pl.ds(at(i), size)], we.at[pair, :, span])
        copies.start(f"wr{i}", wr_in.at[pl.ds(at(i), size), :], wr.at[pair, span, :])
    cot_all[:nq, :] = cot[...]
    cot_all[nq:, :] = cot_other[...]
    low_all = jnp.concatenate([low[...], low_other[...]], 0)
    low_t[...] = jnp.transpose(low_all)
    for pair in range(steps // 2):
        both = (2 * pair, 2 * pair + 1)
        copies.wait(*[f"w{which}{i}" for i in both for which in "er"])
        cot_low = cot_all[...]
        expand, reduce = we[pair], wr[pair]
        bias = jnp.concatenate([be[:, pl.ds(at(i), size)] for i in both], 1)
        expanded = mm(low_all, expand) + bias
        grad_activated = mm_nt(cot_low, reduce)
        cdf = 0.5 * (1.0 + lax.erf(expanded * math.sqrt(0.5)))
        pdf = jnp.exp(-0.5 * expanded * expanded) * (1.0 / math.sqrt(2.0 * math.pi))
        activated = (expanded * cdf).astype(bf16)
        reduce_grad = mm(jnp.transpose(activated), cot_low).astype(bf16)
        for n, i in enumerate(both):
            if z.tape:
                part = size // z.tm
                for t in range(z.tm):
                    for lane in range(z.feat // 128):
                        rows = slice(n * size + t * part, n * size + (t + 1) * part)
                        dwr[i, t, lane * part : (lane + 1) * part, :] = reduce_grad[
                            rows, lane * 128 : (lane + 1) * 128
                        ]
                out_r, own_r, out_e, own_e = outs
                for y in range(2):
                    leave(f"out_r{i}{y}", dwr.at[i, 2 * y + 1 - col], out_r.at[y, i])
                    leave(f"own_r{i}{y}", dwr.at[i, 2 * y + col], own_r.at[y, i])
            else:
                dwr[i] = reduce_grad[n * size : (n + 1) * size]
                leave(f"dwr{i}", dwr.at[i], outs[0].at[i])
        grad_expanded = (grad_activated * (cdf + expanded * pdf)).astype(bf16)
        expand_grad = mm(low_t[...], grad_expanded).astype(bf16)
        bias_grad = jnp.sum(grad_expanded.astype(f32), 0, keepdims=True)
        for n, i in enumerate(both):
            span = slice(n * size, (n + 1) * size)
            if z.tape:
                part = z.feat // z.clip
                for c in range(z.clip):
                    for lane in range(size // 128):
                        lanes = slice(n * size + lane * 128, n * size + (lane + 1) * 128)
                        dwe[i, c, lane * part : (lane + 1) * part, :] = expand_grad[
                            c * part : (c + 1) * part, lanes
                        ]
                    leave(f"e{i}{c}", dwe.at[i, c], (out_e, own_e)[pair].at[n, c])
            else:
                dwe[i] = expand_grad[:, span]
                leave(f"dwe{i}", dwe.at[i], outs[1].at[i])
            dbe[place(i)] = jnp.broadcast_to(bias_grad[:, span], dbe.shape[1:])
        acc_new, grad_new = mm(activated, reduce), mm_nt(grad_expanded, expand)
        if pair == 0:
            acc_sum[...] = acc_new
            grad_sum[...] = grad_new
        else:
            acc_new, grad_new = acc_sum[...] + acc_new, grad_sum[...] + grad_new
            acc[...] = acc_new[:nq]
            acc_other[...] = acc_new[nq:].astype(bf16)
            grad[...] = grad_new[:nq]
            grad_other[...] = grad_new[nq:].astype(bf16)
    copies.wait(*names)


def feed(z, info, paired, low, low_other, cot, cot_other, expand, expand_bias, reduce):
    feat, ff = expand.shape
    size = ff // FF_PARTS
    steps = FF_PARTS // 2
    nq = z.query_rows
    there, here = pl.BlockSpec(memory_space=pl.ANY), whole(None)
    if z.tape:
        shapes = [(z.tm, size * feat // (128 * z.tm), 128), (z.clip, size * feat // (128 * z.clip), 128)]
    else:
        shapes = [(size, feat), (feat, size)]
    shapes = [(steps, *shape) for shape in shapes]
    wide, narrow = ((nq, feat), f32), ((nq, feat), bf16)
    outs = [((steps, 8, size), f32), wide, narrow, wide, narrow]
    far = shapes
    if z.tape:
        far = [(2, 4, *shapes[0][2:])] * 4
    return call(
        functools.partial(feed_kernel, z, paired),
        44,
        [here] * 5 + [there] * 2,
        [here] * 5 + [there] * len(far),
        [jax.ShapeDtypeStruct(*one) for one in outs] + [pltpu.HBM(shape, bf16) for shape in far],
        [
            pltpu.VMEM((steps // 2, feat, 2 * size), bf16),
            pltpu.VMEM((steps // 2, 2 * size, feat), bf16),
            pltpu.VMEM(shapes[0], bf16),
            pltpu.VMEM(shapes[1], bf16),
            pltpu.VMEM((feat, 2 * nq), bf16),
            pltpu.VMEM((2 * nq, feat), bf16),
            pltpu.VMEM((2 * nq, feat), f32),
            pltpu.VMEM((2 * nq, feat), f32),
            pltpu.SemaphoreType.DMA((48,)),
        ],
        (low, low_other, cot, cot_other, expand_bias, in_hbm(expand), in_hbm(reduce)),
        info,
        6 * nq * feat * ff * 2,
        4 * feat * ff,
    )


def blend_back_kernel(z, info, *refs):
    refs = list(refs)
    take = lambda n: [refs.pop(0) for _ in range(n)]
    grad, grad_got, unit, inv, cot, mixed, gain = take(7)
    first_out, low_grad, send, keep, small, hold = take(6)
    rows_grad = cot[...].astype(f32)
    normed, hidden_grad = unit[...], grad[...] + grad_got[...].astype(f32)
    back = rows_grad + norm_backward(hidden_grad, gain[...], normed, inv[:, 0:1])
    first_out[...] = back
    back_low = back.astype(bf16)
    low_grad[...] = back_low
    dwo = mm(jnp.transpose(mixed[...]), back_low)
    for j in range(z.steps):
        block = dwo[:, j * z.width : (j + 1) * z.width]
        if z.tape:
            store_split(z, info[1], block, hold, send, keep, j)
        else:
            keep[j] = block.astype(bf16)
    small[...] = jnp.zeros_like(small)
    small[0:1, :] = jnp.sum(back_low.astype(f32), 0, keepdims=True)
    small[1:2, :] = jnp.sum(hidden_grad * normed, 0, keepdims=True)
    small[2:3, :] = jnp.sum(hidden_grad, 0, keepdims=True)
    small[3:4, :] = jnp.sum(rows_grad, 0, keepdims=True)


def blend_back(z, info, *args):
    feat, nq = z.feat, z.query_rows
    split = ((z.clip, z.tm, z.tape_rows, 128) if z.tape else (3, feat, z.width), bf16)
    shapes = [((nq, feat), f32), ((nq, feat), bf16), split, split, ((8, feat), f32)]
    return call(
        functools.partial(blend_back_kernel, z),
        20,
        [whole(None)] * len(args),
        [whole(None)] * len(shapes),
        [jax.ShapeDtypeStruct(*one) for one in shapes],
        [pltpu.VMEM((feat, z.width), f32)],
        args,
        info,
        2 * nq * feat * feat,
        nq * feat * 20,
    )


def store_split(z, core, value, hold, sent, kept, j):
    hold[...] = value
    half = z.feat // (2 * z.clip)
    part = half // 2
    for c in range(z.clip):
        for out, whose in ((kept, core), (sent, 1 - core)):
            for t in range(z.tm):
                at = pl.multiple_of((2 * c + whose) * half + (t // 2) * part, 16)
                lanes = slice((t % 2) * 128, (t % 2) * 128 + 128)
                out[c, t, j * part : (j + 1) * part, :] = hold[pl.ds(at, part), lanes].astype(bf16)


def plain_to_tape(z, blocks, core):
    lanes = z.width // 128
    x = blocks.reshape(3, z.clip, 2, z.tm // lanes, -1, lanes, 128)
    x = x.transpose(2, 1, 3, 5, 0, 4, 6).reshape(2, z.clip, z.tm, -1, 128)
    return pick(x, 0, 1 - core), pick(x, 0, core)


def attend_back_kernel(z, i, info, *refs):
    refs = list(refs)
    take = lambda n: [refs.pop(0) for _ in range(n)]
    ga, wo, inv, *far = take(10)
    span = slice(i * z.width, (i + 1) * z.width)
    sent, kept, db, kv_out, q_grad_out = take(5)
    q_spread, g_spread, ds, hold, q, k, v, mixed, hk_t, hq_t, p, sems = take(12)
    core = info[1]
    copies = Copies(sems)
    q_in, k_in, v_in, mixed_in, hk_t_in, hq_t_in, p_in = far
    for name, source, to in (
        ("q", q_in.at[i], q),
        ("mixed", mixed_in.at[i], mixed),
        ("v", v_in.at[i], v),
        ("p", p_in.at[i], p),
        ("k", k_in.at[i], k),
        ("hq_t", hq_t_in, hq_t),
        ("hk_t", hk_t_in, hk_t),
    ):
        copies.start(name, source, to)
    scale = z.head_width**-0.5

    grad = mm_nt(ga[...], wo[span, :]).astype(bf16).astype(f32)
    inverse = inv[i, 0:1, :]
    inverse_col = jnp.transpose(jnp.broadcast_to(inverse, (128, z.lanes)))[:, 0:1]
    copies.wait("q", "mixed")
    spread_heads(z, q[...].astype(f32) * scale, q_spread)
    product = grad * mixed[...]
    dots = []
    for head in range(GROUP):
        mask = head_mask(head, z.width, z.head_width)
        at = GROUP * z.rows + head * LEAD_ROWS
        part = grad * mask
        low = (part[: z.rows] * inverse_col[head * z.rows : (head + 1) * z.rows]).astype(bf16)
        g_spread[head * z.rows : (head + 1) * z.rows, :] = low
        low = (part[z.rows :] * inverse_col[at : at + LEAD_ROWS]).astype(bf16)
        g_spread[at : at + LEAD_ROWS, :] = low
        dots.append(jnp.sum(product * mask, 1, keepdims=True))
    end = GROUP * (z.rows + LEAD_ROWS)
    g_spread[end:, :] = jnp.zeros((z.lanes - end, z.width), bf16)
    dot_col = jnp.concatenate(
        [d[: z.rows] for d in dots]
        + [d[z.rows :] for d in dots]
        + [jnp.zeros((z.lanes - end, 1), f32)],
        0,
    )
    dot_row = jnp.transpose(jnp.broadcast_to(dot_col, (z.lanes, 128)))[0:1, :] * inverse
    copies.wait("v", "p")
    v_all = v[...]
    for at, size in chunks_of(z):
        grad_weights = mm_nt(v_all, g_spread[at : at + size, :])
        weights = p[:, at : at + size].astype(f32)
        ds[:, at : at + size] = (weights * (grad_weights - dot_row[:, at : at + size])).astype(bf16)
    ds_all = ds[...]
    copies.wait("k", "hq_t", "hk_t")
    k_all = k[...]
    grad_v = mm(p[...], g_spread[...])
    grad_k = mm(ds_all, q_spread[...])
    grad_q = mm(jnp.transpose(k_all), ds_all)
    grad_q = (join_heads(z, jnp.transpose(grad_q)) * scale).astype(bf16)
    grad_v = grad_v.astype(bf16)
    grad_k = grad_k.astype(bf16)
    db[...] = jnp.concatenate(
        [
            jnp.sum(grad_q.astype(f32), 0, keepdims=True),
            jnp.sum(grad_v.astype(f32), 0, keepdims=True),
            jnp.zeros((6, z.width), f32),
        ],
        0,
    )
    for j, grad in enumerate((mm(hq_t[...], grad_q), mm(hk_t[...], grad_k), mm(hk_t[...], grad_v))):
        if z.tape:
            store_split(z, core, grad, hold, sent, kept, j)
        else:
            kept[j] = grad.astype(bf16)
    kv_out[:, : z.width] = grad_k
    kv_out[:, z.width :] = grad_v
    q_grad_out[...] = grad_q


def keys_back_kernel(z, info, *refs):
    refs = list(refs)
    take = lambda n: [refs.pop(0) for _ in range(n)]
    uk_in, uq, weight_in, first, feed_small = take(5)
    db, grad_kv, grad_q = take(z.steps), take(z.steps), take(z.steps)
    own, small_out = take(2)
    sends = take(4 if z.tape else z.tm - 1)
    keys_acc, query_acc, small, uk, weight, sems = take(6)
    me = info[0]
    copies = Copies(sems)
    span = lambda part, i: slice((part * z.steps + i) * z.width, (part * z.steps + i + 1) * z.width)
    spans = [slice(r * z.width, (r + 1) * z.width) for r in range(z.steps)]
    for r, span in enumerate(spans):
        copies.start(r, weight_in.at[span, :], weight.at[span, :])
    copies.start("uk", uk_in, uk)
    all_kv = [one[:, : z.width] for one in grad_kv] + [one[:, z.width :] for one in grad_kv]
    all_kv, all_q = jnp.concatenate(all_kv, 1), jnp.concatenate([one[...] for one in grad_q], 1)
    for r, span in enumerate(spans):
        copies.wait(r)
        query_acc[:, span] = mm_nt(all_q, weight[span, : z.feat])
        keys_acc[:, span] = mm_nt(all_kv, weight[span, z.feat :])
    copies.wait("uk")
    keys_grad, query_grad = keys_acc[...], query_acc[...]
    small[...] = jnp.zeros_like(small)
    for i in range(z.steps):
        small[0:2, i * z.width : (i + 1) * z.width] = db[i][0:2, :]
    small[2:3, :] = jnp.sum(keys_grad * uk[...].astype(f32), 0, keepdims=True) + jnp.sum(
        query_grad * uq[...].astype(f32), 0, keepdims=True
    )
    small[3:4, :] = jnp.sum(keys_grad, 0, keepdims=True) + jnp.sum(query_grad, 0, keepdims=True)
    small[4:12, :] = feed_small[...]
    if z.tape:
        for lane in range(z.feat // 128):
            small_out[lane * 16 : lane * 16 + 16, :] = small[
                :, lane * 128 : lane * 128 + 128
            ].astype(bf16)
    else:
        small_out[...] = small[...]
    lead = keys_acc[0:LEAD_ROWS, :] + query_acc[z.rows :, :]
    first_lead = first[z.rows :, :]
    high = first_lead.astype(bf16)
    rest = (first_lead - high.astype(f32)).astype(bf16)
    pair = lambda a: a[0:LEADS]
    packed = jnp.concatenate(
        [pair(lead), pair(high.astype(f32)), pair(rest.astype(f32)), jnp.zeros((10, z.feat), f32)], 0
    )
    small_high = small[...].astype(bf16)
    small_low = (small[...] - small_high.astype(f32)).astype(bf16)
    own[z.rows :, :] = packed
    packed = packed.astype(bf16)
    hb = z.half_block

    def chunk(k, half, out, at):
        source = jnp.bitwise_xor(me, k)
        for b in range(z.blocks):
            spot = source * z.blocks + b
            from_ = pl.multiple_of(
                LEAD_ROWS + jnp.minimum(spot, z.key_blocks - 1) * z.block + half * hb, 16
            )
            rows = keys_acc[pl.ds(from_, hb), :] * (spot < z.key_blocks).astype(f32)
            to = at + b * hb
            if k == 0:
                queries = half * z.half + b * hb
                rows = rows + query_acc[queries : queries + hb, :]
            out[to : to + hb, :] = rows.astype(out.dtype)

    chunk(0, 0, own, 0)
    chunk(0, 1, own, z.half)
    if z.tape:
        along_x, along_y, mid_x, mid_y = sends
        chunk(1, 0, along_x, 0)
        chunk(3, 0, along_x, z.half)
        along_x[z.rows :, :] = packed
        chunk(2, 1, along_y, 0)
        chunk(3, 1, along_y, z.half)
        chunk(2, 0, mid_x, 0)
        chunk(1, 1, mid_y, 0)
    else:
        for k, one in enumerate(sends, start=1):
            chunk(k, 0, one, 0)
            chunk(k, 1, one, z.half)
            one[z.rows :, :] = packed


def attend_back(z, info, i, ga, wo, saved):
    _, inv, _, *far, _ = saved
    feat, width, nk, nq, nl = z.feat, z.width, z.keys, z.query_rows, z.lanes
    in_specs = [whole(None)] * 3 + [pl.BlockSpec(memory_space=pl.ANY)] * 7
    if z.tape:
        part = (z.clip, z.tm, z.tape_rows, 128)
    else:
        part = (3, feat, width)
    sent, kept, *rest = call(
        functools.partial(attend_back_kernel, z, i),
        24,
        in_specs,
        [whole(part), whole(part), whole((8, width)), whole((nk, 2 * width)), whole((nq, width))],
        [
            jax.ShapeDtypeStruct(part, bf16),
            jax.ShapeDtypeStruct(part, bf16),
            jax.ShapeDtypeStruct((8, width), f32),
            jax.ShapeDtypeStruct((nk, 2 * width), bf16),
            jax.ShapeDtypeStruct((nq, width), bf16),
        ],
        [
            pltpu.VMEM((nl, width), bf16),
            pltpu.VMEM((nl, width), bf16),
            pltpu.VMEM((nk, nl), bf16),
            pltpu.VMEM((feat, width), f32),
            pltpu.VMEM((nq, width), bf16),
            pltpu.VMEM((nk, width), bf16),
            pltpu.VMEM((nk, width), bf16),
            pltpu.VMEM((nq, width), f32),
            pltpu.VMEM((feat, nk), bf16),
            pltpu.VMEM((feat, nq), bf16),
            pltpu.VMEM((nk, nl), bf16),
            pltpu.SemaphoreType.DMA((8,)),
        ],
        [ga, wo, inv, *[in_hbm(one) for one in far]],
        info,
        1000,
        1000,
    )
    if not z.tape:
        sent, kept = plain_to_tape(z, kept, info[1])
    return sent, kept, rest


def keys_back(z, info, saved, weight, first_lead, feed_small, steps):
    feat, width, nk, nq = z.feat, z.width, z.keys, z.query_rows
    uq, uk = saved[2], saved[10]
    there = pl.BlockSpec(memory_space=pl.ANY)
    in_specs = [there, whole((nq, feat)), there]
    in_specs += [whole(None)]
    in_specs += [whole((8, feat))]
    in_specs += [whole((8, width))] * z.steps
    in_specs += [whole((nk, 2 * width))] * z.steps + [whole((nq, width))] * z.steps
    if z.tape:
        sends = [(nq, feat), (z.rows, feat), (z.half, feat), (z.half, feat)]
    else:
        sends = [(nq, feat)] * (z.tm - 1)
    small = (16 * feat // 128, 128) if z.tape else (16, feat)
    return call(
        functools.partial(keys_back_kernel, z),
        24,
        in_specs,
        [whole((nq, feat)), whole(small)] + [whole(shape) for shape in sends],
        [
            jax.ShapeDtypeStruct((nq, feat), f32),
            jax.ShapeDtypeStruct(small, bf16 if z.tape else f32),
        ]
        + [jax.ShapeDtypeStruct(shape, bf16) for shape in sends],
        [
            pltpu.VMEM((nk, feat), f32),
            pltpu.VMEM((nq, feat), f32),
            pltpu.VMEM((16, feat), f32),
            pltpu.VMEM((nk, feat), bf16),
            pltpu.VMEM(weight.shape, bf16),
            pltpu.SemaphoreType.DMA((16,)),
        ],
        (in_hbm(uk), uq, in_hbm(weight), first_lead, feed_small)
        + tuple(step[j] for j in range(3) for step in steps),
        info,
        4 * feat * feat * (nq + 2 * nk),
        nk * feat * 4,
    )


def finish_kernel(z, info, *refs):
    *received, rows, gain, grad_first, out_mine, out_send = refs[1:]
    own = refs[0]
    mine = own[z.rows :].astype(bf16).astype(f32)
    if z.tape:
        got_x, got_y, got_xy, got_yx = (one[...].astype(f32) for one in received)
        first = own[: z.half] + got_x[: z.half] + got_xy[: z.half]
        second = own[z.half : z.rows] + got_y[: z.half] + got_yx
        lead = (mine + got_x[z.rows :]).astype(bf16).astype(f32) + got_xy[z.half :]
        total = jnp.concatenate([first, second, lead], 0)
    else:
        terms = [one[...].astype(f32) for one in received]
        leads = [mine] + [one[z.rows :] for one in terms]
        while len(leads) > 1:
            leads = [a + b for a, b in zip(leads[::2], leads[1::2])]
        total = jnp.concatenate([own[: z.rows] + sum(t[: z.rows] for t in terms), leads[0]], 0)
    normed, scale_inv = standardize(rows[...].astype(f32))
    back = norm_backward(total, gain[...], normed, scale_inv)
    rows_grad = (back[: z.rows] + grad_first[0 : z.rows, :]).astype(bf16)
    out_mine[...] = rows_grad[: z.half]
    out_send[0 : z.half, :] = rows_grad[z.half :]
    lead = total[z.rows :]
    lead_first = lead[LEADS : 2 * LEADS] + lead[2 * LEADS : 3 * LEADS]
    out_send[z.half :, :] = jnp.concatenate(
        [back[z.rows : z.rows + LEADS] + lead_first, jnp.zeros((LEAD_ROWS - LEADS, z.feat), f32)], 0
    ).astype(bf16)


def finish(z, info, own, received, rows, gain, grad_first):
    feat, nq = z.feat, z.query_rows
    return call(
        functools.partial(finish_kernel, z),
        16,
        [whole(one.shape) for one in (own, *received)]
        + [whole((nq, feat)), whole((1, feat)), whole((nq, feat))],
        [whole((z.half, feat)), whole((nq - z.half, feat))],
        [
            jax.ShapeDtypeStruct((z.half, feat), bf16),
            jax.ShapeDtypeStruct((nq - z.half, feat), bf16),
        ],
        [],
        (own, *received, rows, gain, grad_first),
        info,
        nq * feat * 20,
        nq * feat * 20,
    )


def place_blocks(z, t, whose, tape, row, out, lane_at):
    half = z.feat // (2 * z.clip)
    part = half // 2
    at = pl.multiple_of(whose * half + (t // 2) * part, 16)
    for j in range(3):
        block = tape[row + j * part : row + (j + 1) * part, :].astype(f32)
        lane = pl.multiple_of(lane_at(j) + (t % 2) * 128, 128)
        out[pl.ds(at, part), pl.ds(lane, 128)] = block


def assemble_feed_kernel(z, ff, far, info, *refs):
    me, core = info[0], info[1]
    expand_out, reduce_out, expand, reduce, sems = refs[-5:]
    p_mine, q_mine, p_other, q_other = refs[:4]
    size = ff // FF_PARTS
    step = size * z.feat // (128 * z.tm) + z.tape_rows
    part_r, part_e = size // z.tm, z.feat // z.clip
    copies = Copies(sems)
    names = []
    for whose, p, q in ((core, p_mine, q_mine), (1 - core, p_other, q_other)):
        for j, (k_p, k_q) in enumerate(((2, 1), (3, 3)) if far else ((0, 0), (1, 2))):
            n = len(names)
            for lane in range(z.feat // 128):
                block = p[j * step + lane * part_r : j * step + (lane + 1) * part_r, :]
                reduce[n, :, lane * 128 : (lane + 1) * 128] = block.astype(f32)
            at = pl.multiple_of(whose * size + jnp.bitwise_xor(me, k_p) * part_r, 16)
            copies.start((n, 0), reduce.at[n], reduce_out.at[pl.ds(at, part_r), :])
            for lane in range(size // 128):
                block = q[j * step + lane * part_e : j * step + (lane + 1) * part_e, :]
                expand[n, :, lane * 128 : (lane + 1) * 128] = block.astype(f32)
            at = pl.multiple_of((2 * jnp.bitwise_xor(me, k_q) + whose) * size, 128)
            copies.start((n, 1), expand.at[n], expand_out.at[:, pl.ds(at, size)])
            names.append(n)
    copies.wait(*[(n, i) for n in names for i in range(2)])


def assemble_feed(z, info, ff, far, tapes, before):
    rows, size = z.feat // z.clip, ff // FF_PARTS
    there = pl.BlockSpec(memory_space=pl.ANY)
    return call(
        functools.partial(assemble_feed_kernel, z, ff, far),
        16,
        [whole(None)] * 4 + [there] * len(before),
        [there] * 2,
        [pltpu.HBM((rows, ff), f32), pltpu.HBM((ff // z.clip, z.feat), f32)],
        [
            pltpu.VMEM((4, rows, size), f32),
            pltpu.VMEM((4, size // z.tm, z.feat), f32),
            pltpu.SemaphoreType.DMA((8,)),
        ],
        (*tapes, *before),
        info,
        1000,
        24 * tapes[0].size,
        {5: 0, 6: 1} if before else {},
    )


def assemble_input_kernel(z, step, info, *refs):
    me, core = info[0], info[1]
    near, far, (late, late_other), (output_out, input_out) = refs[:4], refs[4:8], refs[8:10], refs[10:]
    last = step - z.tape_rows
    for whose, m, late_tape in ((core, 0, late), (1 - core, 2, late_other)):
        for k in range(z.tm):
            t = jnp.bitwise_xor(me, k)
            tape, at = (near[m], far[m])[k // 2], k % 2 * step + last
            place_blocks(z, t, whose, tape, at, output_out, lambda j: j * z.width)
            tape, at = (near[m + 1], far[m + 1])[k % 2], k // 2 * step + last
            place_blocks(z, t, whose, tape, at, input_out, lambda j: j * z.feat)
            for i in (1, 2):
                row = (2 * k + i - 1) * z.tape_rows
                lane_at = lambda j: j * z.feat + i * z.width
                place_blocks(z, t, whose, late_tape, row, input_out, lane_at)


def assemble_input(z, info, near, far, late):
    rows = z.feat // z.clip
    shapes = [(rows, z.feat), (rows, 3 * z.feat)]
    return call(
        functools.partial(assemble_input_kernel, z, near[0].shape[0] // 2),
        20,
        [whole(None)] * 10,
        [whole(None)] * 2,
        [jax.ShapeDtypeStruct(shape, f32) for shape in shapes],
        [],
        (*near, *far, *late),
        info,
        1000,
        16 * late[0].size,
    )


def small_kernel(z, info, mine, other, *outs):
    total = mine[...].astype(f32) + other[...].astype(f32)
    lanes = z.feat // 128

    def row(i):
        return jnp.concatenate([total[n * 16 + i : n * 16 + i + 1, :] for n in range(lanes)], 1)

    rows = [row(i) for i in range(12)]
    biases = jnp.concatenate(rows[:2], 1)
    count = z.feat // z.clip
    for c in range(z.clip):

        @pl.when(info[2] == c)
        def _(c=c):
            outs[0][...] = biases[0, 2 * count * c : 2 * count * (c + 1)]
            for i in range(2, 8):
                outs[i - 1][...] = rows[i][0, count * c : count * (c + 1)]
            outs[7][...] = rows[8 + c][0, :]


def small_grads(z, info, mine, other):
    count = z.feat // z.clip
    sizes = [2 * count] + [count] * 6 + [4 * count]
    return call(
        functools.partial(small_kernel, z),
        4,
        [whole(None)] * 2,
        [whole(None)] * 8,
        [jax.ShapeDtypeStruct((size,), f32) for size in sizes],
        [],
        (mine, other),
        info,
        1000,
        1000,
    )


def flip(count, k):
    return [(i, i ^ k) for i in range(count)]


def bit_of(index, bit):
    return (index >> bit) & 1


def bits_of(count):
    return count.bit_length() - 1


def pick(x, dim, index):
    return lax.dynamic_index_in_dim(x, index, dim, keepdims=False)


def add(kept, got):
    return (kept.astype(f32) + got.astype(f32)).astype(bf16)


def by_bits(x, dim, count):
    return x.reshape(x.shape[:dim] + (2,) * bits_of(count) + x.shape[dim + 1 :])


def halves(x, dim, axis, bit):
    mine = bit_of(lax.axis_index(axis), bit)
    return pick(x, dim, 1 - mine), pick(x, dim, mine)


def across(x, axis, bit):
    return lax.ppermute(x, axis, flip(lax.axis_size(axis), 1 << bit))


def scatter(x, dim, axis, bits):
    for bit in bits:
        sent, kept = halves(x, dim, axis, bit)
        x = add(kept, across(sent, axis, bit))
    return x


def scatter_up(x, dim, axis, bits):
    for bit in bits:
        at = dim + bits_of(lax.axis_size(axis)) - 1 - bit
        sent, kept = halves(x, at, axis, bit)
        x = add(kept, across(sent, axis, bit))
    return x


def peers(x, dim, axis):
    me = lax.axis_index(axis)
    return [pick(x, dim, me ^ k) for k in range(1, lax.axis_size(axis))]


def to_peers(sent, axis):
    count = lax.axis_size(axis)
    return [lax.ppermute(one, axis, flip(count, k)) for k, one in enumerate(sent, start=1)]


def add_all(own, got):
    total = own.astype(f32)
    for one in got:
        total = total + one.astype(f32)
    return total.astype(bf16)


def in_order(x, got, axis):
    me = lax.axis_index(axis)
    out = jnp.zeros((1 + len(got),) + x.shape, x.dtype)
    for k, one in enumerate([x, *got]):
        out = lax.dynamic_update_index_in_dim(out, one, me ^ k, 0)
    return out


def tie(*values):
    return lax.optimization_barrier(values)


def per_device(
    patches,
    lead_tokens,
    lengths,
    input_weight,
    input_bias,
    output_weight,
    output_bias,
    first_gain,
    first_shift,
    second_gain,
    second_shift,
    expand_weight,
    expand_bias,
    reduce_weight,
    reduce_bias,
    cot_patches,
    cot_lead,
):
    tm_count = lax.axis_size("tm")
    clip_count = lax.axis_size("clip")
    z = Sizes(patches.shape, tm_count, clip_count)
    feat, ff = expand_weight.shape
    core, place = lax.axis_index("freq"), lax.axis_index("tm")
    info = jnp.stack([place, core, lax.axis_index("clip")]).astype(jnp.int32)
    row = lambda vector: vector.astype(f32)[None, :]

    def by_clip(array):
        parts = array.reshape(z.fr, z.blocks, BLOCK_COLS, z.clips, feat)
        parts = parts.transpose(3, 1, 0, 2, 4).reshape(z.clips, z.half, feat)
        return (
            lax.dynamic_index_in_dim(parts, core, 0, keepdims=False),
            lax.dynamic_index_in_dim(parts, 1 - core, 0, keepdims=False),
        )

    def lead_of(array):
        mine = lax.dynamic_index_in_dim(array, core, 0, keepdims=False)
        return jnp.pad(mine, ((0, LEAD_ROWS - LEADS), (0, 0)))

    own_half, other_half = by_clip(patches)
    pieces = []
    for k in range(tm_count):
        pieces.append(lax.ppermute(own_half, "tm", flip(tm_count, k)) if k else own_half)
        pieces.append(
            lax.ppermute(other_half, ("freq", "tm"), flip(2 * tm_count, tm_count | k))
        )
    lead = lead_of(lead_tokens)
    rows = jnp.concatenate([pieces[0], pieces[1], lead], 0)
    own_cot, other_cot = by_clip(cot_patches)
    lead_cot = lead_of(cot_lead) * (place == 0).astype(bf16)
    cot = jnp.concatenate([own_cot, lax.ppermute(other_cot, "freq", flip(2, 1)), lead_cot], 0)
    cot_got = lax.ppermute(cot, "freq", flip(2, 1))

    length = lax.dynamic_index_in_dim(lengths, core, 0, keepdims=False)
    spots = np.arange(z.keys) - LEAD_ROWS
    columns = np.where(spots < 0, 1 << 20, spots // z.block * BLOCK_COLS + spots % BLOCK_COLS)
    columns[:LEADS] = -1
    live = jnp.where(jnp.asarray(columns, jnp.int32)[:, None] < length, 0.0, NEG_FILL)
    live = jnp.broadcast_to(live.astype(f32), (z.keys, 128))

    saved = attend(
        z,
        info,
        pieces,
        lead,
        input_weight,
        row(input_bias[:feat]),
        row(input_bias[feat:]),
        row(first_gain),
        row(first_shift),
        live,
    )
    mixed_low = saved[0]
    paired = clip_count == FF_PARTS // 2
    if not paired:
        share = (clip_count, 2, ff // (2 * clip_count))
        expand_weight = expand_weight.reshape(feat, *share).swapaxes(1, 2).reshape(feat, ff)
        expand_bias = expand_bias.reshape(share).swapaxes(0, 1).reshape(ff)
        reduce_weight = reduce_weight.reshape(*share, feat).swapaxes(0, 1).reshape(ff, feat)
    gain_two, shift_two = row(second_gain), row(second_shift)
    swap = lambda x: across(x, "freq", 0)
    size = ff // FF_PARTS
    half = clip_count // 2
    tm_bits, clip_bits = bits_of(tm_count), bits_of(clip_count)
    low_bits, high_bits = list(range(tm_bits)), list(range(tm_bits))[::-1]
    split = max(1, tm_count // (FF_PARTS // 2))

    total, unit, inv, low = blend(
        z, info, mixed_low, rows, output_weight, row(output_bias), gain_two, shift_two
    )
    feed_bias, acc, acc_send, grad, grad_send, *sums = feed(
        z, info, paired, low, swap(low), cot, cot_got, expand_weight, row(expand_bias), reduce_weight
    )
    if z.tape:
        out_r, own_r, out_e, own_e = sums
    else:
        sum_r, sum_e = sums
        rows_r, rows_e = ff // (2 * clip_count * tm_count), feat // (clip_count * split)
        sum_r = sum_r.reshape(clip_count, tm_count, rows_r, feat // 128, 128).swapaxes(2, 3)
        sum_e = sum_e.reshape(-1, clip_count, split, rows_e, size // 128, 128)
        sum_e = sum_e.transpose(0, 2, 1, 4, 3, 5)
        sum_r = sum_r.reshape(clip_count, tm_count, -1, 128)
        sum_e = sum_e.reshape(tm_count, clip_count, -1, 128).swapaxes(0, 1)
        out_r, own_r = halves(by_bits(sum_r, 1, tm_count), 1 + tm_bits - 1, "tm", 0)
        out_e, own_e = halves(by_bits(sum_e, 1, tm_count), 1, "tm", tm_bits - 1)
    grad, grad_send, acc_send, out_r, out_e = tie(grad, grad_send, acc_send, out_r, out_e)
    across_r = lambda x: across(x, "tm", 0)
    across_e = lambda x: across(x, "tm", tm_bits - 1)
    across_z = lambda x: across(x, "clip", 0)
    halves_z = lambda x: halves(by_bits(x, 0, clip_count), clip_bits - 1, "clip", 0)
    rest_z = lambda x: scatter_up(x, 0, "clip", range(1, clip_bits))

    got_r, got_e = across_r(out_r), across_e(out_e)
    acc_got = swap(acc_send)
    grad_first, grad_low, sent_o, kept_o, small_two = blend_back(
        z, info, grad, swap(grad_send), unit, inv, cot, mixed_low, gain_two
    )
    if not z.tape:
        sent_o, kept_o = plain_to_tape(z, kept_o, core)
    got_o = swap(sent_o)
    sent_0, kept_0, rest_0 = attend_back(z, info, 0, grad_low, output_weight, saved)
    grad_low, got_o, acc_got, sent_0 = tie(grad_low, got_o, acc_got, sent_0)
    out_o, own_o = halves_z(add(kept_o, got_o))
    grad_low, out_o = tie(grad_low, out_o)
    got_0, got_oz = swap(sent_0), across_z(out_o)
    sent_1, kept_1, rest_1 = attend_back(z, info, 1, grad_low, output_weight, saved)
    grad_low, got_r, got_e, got_0, got_oz, sent_1 = tie(
        grad_low, got_r, got_e, got_0, got_oz, sent_1
    )
    sum_r, sum_e = add(own_r, got_r), add(own_e, got_e)
    if z.tape:
        out_r, own_r = halves(sum_r, 0, "tm", 1)
        out_e, own_e = halves(sum_e, 0, "tm", 0)
        ordered = lambda x: jnp.where(place // 2 == 0, jnp.concatenate([x[half:], x[:half]], 0), x)
        out_r, own_r = ordered(out_r), ordered(own_r)
    else:
        sum_r = scatter_up(sum_r, 1, "tm", low_bits[1:-1])
        sum_e = scatter(sum_e, 1, "tm", high_bits[1:-1])
        out_r, own_r = halves(sum_r, 1, "tm", low_bits[-1])
        out_e, own_e = halves(sum_e, 1, "tm", high_bits[-1])
    sum_o = add(own_o, got_oz)
    out_0, own_0 = halves_z(add(kept_0, got_0))
    grad_low, out_r, out_e, sum_o, out_0 = tie(grad_low, out_r, out_e, sum_o, out_0)
    got_r, got_e = across(out_r, "tm", low_bits[-1]), across(out_e, "tm", high_bits[-1])
    got_0z, got_1 = across_z(out_0), swap(sent_1)
    sum_o = rest_z(sum_o)

    def split_tm(x, *more):
        x = by_bits(x, 1, tm_count)
        parts = [x[:half], x[half:]]
        if more:
            parts = [jnp.concatenate([p, by_bits(m, 1, tm_count)], 0) for p, m in zip(parts, more)]
        return (
            *halves(parts[0], tm_bits, "tm", 0),
            *halves(parts[1], 1, "tm", tm_bits - 1),
        )

    sent_2, kept_2, rest_2 = attend_back(z, info, 2, grad_low, output_weight, saved)
    sent_2, got_r, got_e, got_0z, got_1, sum_o, *rest_2 = tie(
        sent_2, got_r, got_e, got_0z, got_1, sum_o, *rest_2
    )
    sum_r, sum_e = add(own_r, got_r), add(own_e, got_e)
    out_f, own_f = halves_z(jnp.concatenate([sum_r, sum_e], 1))
    count_f = sum_r.shape[1]
    sum_0 = add(own_0, got_0z)
    out_1x, own_1x, out_1y, own_1y = split_tm(add(kept_1, got_1))
    feed_bias = feed_bias[:, 0:1] * (jnp.arange(2) == core).astype(f32)[:, None]
    if not paired:
        feed_bias = feed_bias.swapaxes(0, 1).reshape(2, clip_count, -1).swapaxes(0, 1)
    feed_small = jnp.concatenate([small_two[:4], feed_bias.reshape(-1, feat)], 0)
    out_f, sum_0, out_1x, out_1y, sent_2, *rest_2 = tie(
        out_f, sum_0, out_1x, out_1y, sent_2, *rest_2
    )
    got_f, got_2, got_1x, got_1y = across_z(out_f), swap(sent_2), across_r(out_1x), across_e(out_1y)
    sum_0 = rest_z(sum_0)
    own, small, *sends = keys_back(
        z, info, saved, input_weight, grad_first, feed_small, (rest_0, rest_1, rest_2)
    )
    got_f, got_2, got_1x, got_1y, sum_0, own, small, *sends = tie(
        got_f, got_2, got_1x, got_1y, sum_0, own, small, *sends
    )
    out_2x, own_2x, out_2y, own_2y = split_tm(add(kept_2, got_2), sum_o[None], sum_0[None])
    def patches_of(mine, theirs):
        first = jnp.where(core == 0, mine, theirs[: z.half])
        second = jnp.where(core == 0, theirs[: z.half], mine)
        pair = jnp.stack([first, second], 0).reshape(
            z.clips, z.blocks, z.fr, BLOCK_COLS, feat
        )
        return pair.transpose(2, 1, 3, 0, 4).reshape(z.fr, z.tc, z.clips, feat)

    finish_args = (rows, row(first_gain), grad_first)
    block_of = lambda total: (total + acc + acc_got.astype(f32) + row(reduce_bias)).astype(bf16)
    if z.tape:
        flat = lambda *parts: jnp.concatenate([part.reshape(-1, 128) for part in parts], 0)
        count = small.shape[0]
        unpack = lambda got, like: (got[:-count].reshape(like.shape), got[-count:])
        across_x, across_y = lambda x: across(x, "tm", 0), lambda x: across(x, "tm", 1)
        across_zz = lambda x: across(x, "clip", 1)
        along_x, along_y, mid_x, mid_y = sends
        out_f, own_f = halves(add(own_f, got_f), 0, "clip", 1)
        token, msg_x, out_2y, along_x, along_y, out_f = tie(
            info, flat(out_2x, small), out_2y, along_x, along_y, out_f
        )
        got_f = across_zz(out_f)
        msg_x, got_2y = across_x(msg_x), across_y(out_2y)
        got_x, got_y = across_x(along_x), across_y(along_y)
        token, msg_x, got_2y = tie(token, msg_x, got_2y)
        got_2x, got_small = unpack(msg_x, own_2x)
        small = add(small, got_small)
        sum_x = jnp.concatenate([add(own_1x, got_1x), add(own_2x, got_2x)], 0)
        sum_y = jnp.concatenate([add(own_1y, got_1y), add(own_2y, got_2y)], 0)
        out_x, own_x = halves(sum_x, 1, "tm", 1)
        out_y, own_y = halves(sum_y, 1, "tm", 0)
        token, small = tie(token, small)
        token, msg_x, out_y = tie(token, flat(out_x, small), out_y)
        msg_x, got_y2 = across_y(msg_x), across_x(out_y)
        token, msg_x, got_y2 = tie(token, msg_x, got_y2)
        got_x2, got_small = unpack(msg_x, own_x)
        small = add(small, got_small)
        sum_x, sum_y = add(own_x, got_x2), add(own_y, got_y2)
        late = [jnp.concatenate([one[:2], one[2:4]], 1) for one in (sum_x, sum_y)]
        out_l, own_l = halves_z(jnp.concatenate(late, 0))
        token, small = tie(token, small)
        token, msg_l = tie(token, flat(out_l, small))
        msg_l = across_z(msg_l)
        token, got_f = tie(token, got_f)
        sum_f = add(own_f, got_f)
        token, ready_p, ready_q = tie(
            token, flat(sum_f[:count_f], sum_x[4]), flat(sum_f[count_f:], sum_y[4])
        )
        got_p, got_q = across_x(ready_p), across_y(ready_q)
        token, total_now, got_x, got_y = tie(token, total, got_x, got_y)
        block = block_of(total_now)
        block_mine, block_send = block[: z.half], block[z.half :]
        lead = add(along_x[z.rows :], got_x[z.rows :])
        out_xy = jnp.concatenate([add(mid_x, got_x[z.half : z.rows]), lead], 0)
        out_yx = add(mid_y, got_y[z.half :])
        token, out_xy, out_yx = tie(token, out_xy, out_yx)
        got_xy, got_yx = across_y(out_xy), across_x(out_yx)
        token, msg_l, block_mine, block_send = tie(token, msg_l, block_mine, block_send)
        got_l, got_small = unpack(msg_l, own_l)
        small = add(small, got_small)
        out_l, own_l = halves(add(own_l, got_l), 0, "clip", 1)
        token, small = tie(token, small)
        token, msg_l = tie(token, flat(out_l, small))
        msg_l = across_zz(msg_l)
        token, got_xy, got_yx = tie(token, got_xy, got_yx)
        received = [got_x, got_y, got_xy, got_yx]
        grad_mine, grad_send = finish(z, token, own, received, *finish_args)
        token, grad_send = tie(token, grad_send)
        grad_got, block_got = swap(grad_send), swap(block_send)
        token, got_p, got_q, grad_got, block_got = tie(token, got_p, got_q, grad_got, block_got)
        token, near_p, near_q = tie(token, flat(ready_p, got_p), flat(ready_q, got_q))
        far_p, far_q = across_y(near_p), across_x(near_q)
        other_p, other_q = swap(near_p), swap(near_q)
        token, msg_l, other_p, other_q = tie(token, msg_l, other_p, other_q)
        got_l, got_small = unpack(msg_l, own_l)
        small, late = add(small, got_small), add(own_l, got_l)
        token, small, late = tie(token, small, late)
        late_all = to_peers([late] * 3, "tm")
        feed_grads = assemble_feed(z, token, ff, 0, (near_p, near_q, other_p, other_q), ())
        patch_outs = (patches_of(block_mine, block_got), patches_of(grad_mine, grad_got))
        token, far_p, far_q, *rest = tie(token, far_p, far_q, *feed_grads, *patch_outs)
        feed_grads, patch_outs = rest[:2], rest[2:]
        other_far = (swap(far_p), swap(far_q))
        token, *late_all = tie(token, *late_all)
        token, late, small = tie(token, flat(late, *late_all), small)
        late_got, small_got = swap(late), swap(small)
        vectors = small_grads(z, token, small, small_got)
    else:
        received = to_peers(sends, "tm")
        got_2x, got_2y = across_r(out_2x), across_e(out_2y)
        sum_x = jnp.concatenate([add(own_1x, got_1x), add(own_2x, got_2x)], 0)
        sum_y = jnp.concatenate([add(own_1y, got_1y), add(own_2y, got_2y)], 0)
        sum_x = scatter_up(sum_x, 1, "tm", low_bits[1:])
        sum_y = scatter(sum_y, 1, "tm", high_bits[1:])
        sum_f = rest_z(add(own_f, got_f))
        ready = jnp.concatenate([sum_f, sum_x[2 * half], sum_y[2 * half]], 0)
        late = jnp.concatenate(
            [
                jnp.concatenate([one[:half], one[half : 2 * half]], 1)
                for one in (sum_x, sum_y)
            ],
            0,
        )
        late = scatter(by_bits(late, 0, clip_count), 0, "clip", range(clip_bits)[::-1])
        ready = jnp.concatenate([ready, late], 0)
        ready_all = [ready] + to_peers([ready] * (tm_count - 1), "tm")
        small = small + swap(small)
        for axis, bits in (("tm", tm_bits), ("clip", clip_bits)):
            for bit in range(bits):
                small = small + across(small, axis, bit)
        grad_mine, grad_send = finish(z, info, own, received, *finish_args)

    here = lax.axis_index("clip")

    def shard(vector):
        count = vector.shape[0] // clip_count
        return lax.dynamic_slice_in_dim(vector, here * count, count, 0)

    if not z.tape:
        vectors = [shard(small[0:2].reshape(-1)), *[shard(small[i]) for i in range(2, 8)]]
        vectors.append(shard(small[8:12].reshape(-1)))
    input_bias_grad, gain_one_grad, shift_one_grad, output_bias_grad = vectors[:4]
    gain_two_grad, shift_two_grad, reduce_bias_grad, expand_bias_grad = vectors[4:]

    if z.tape:
        far = (far_p, far_q, *other_far)
        expand_weight_grad, reduce_weight_grad = assemble_feed(z, token, ff, 1, far, feed_grads)
        output_weight_grad, input_weight_grad = assemble_input(
            z, token, (near_p, near_q, other_p, other_q), far, (late, late_got)
        )
    else:
        block = block_of(total)
        block_mine, block_send = block[: z.half], block[z.half :]
        grad_got, block_got = swap(grad_send), swap(block_send)
        patch_outs = (patches_of(block_mine, block_got), patches_of(grad_mine, grad_got))
        tapes = jnp.stack(ready_all)
        other_tapes = swap(tapes)
        both = in_order(tapes, [other_tapes], "freq")
        both = pick(jnp.stack([both[:, np.arange(tm_count) ^ t] for t in range(tm_count)]), 0, place)
        part_r, part_e = both[:, :, :count_f], both[:, :, count_f : 2 * count_f]
        rows_r, rows_e = ff // (2 * clip_count * tm_count), feat // (clip_count * split)
        part_r = part_r.reshape(2, tm_count, feat // 128, rows_r, 128).swapaxes(2, 3)
        reduce_weight_grad = part_r.reshape(ff // clip_count, feat).astype(f32)
        part_e = part_e.reshape(2, FF_PARTS // 2, split, size // 128, rows_e, 128)
        part_e = part_e.transpose(2, 4, 1, 0, 3, 5)
        if not paired:
            part_e = part_e.swapaxes(2, 3).reshape(feat // clip_count, 2, clip_count, -1)
            part_e = part_e.swapaxes(1, 2)
        expand_weight_grad = part_e.reshape(feat // clip_count, ff).astype(f32)
        lanes = z.width // 128
        part_a = both[:, :, 2 * count_f :].reshape(2, tm_count // lanes, lanes, 4, 3, -1, 128)
        part_a = part_a.transpose(0, 1, 5, 3, 4, 2, 6)
        part_a = part_a.reshape(feat // clip_count, 4, 3, z.width).astype(f32)
        output_weight_grad = part_a[:, 0].reshape(-1, feat)
        input_weight_grad = part_a[:, 1:].swapaxes(1, 2).reshape(-1, 3 * feat)

    def leads_of(sent, got):
        mine, theirs = sent[z.half : z.half + LEADS], got[z.half : z.half + LEADS]
        first = jnp.where(core == 0, mine, theirs)
        second = jnp.where(core == 0, theirs, mine)
        return jnp.stack([first, second], 0)

    return (
        patch_outs[0],
        leads_of(block_send, block_got),
        patch_outs[1],
        leads_of(grad_send, grad_got),
        input_weight_grad,
        input_bias_grad,
        output_weight_grad,
        output_bias_grad,
        gain_one_grad,
        shift_one_grad,
        gain_two_grad,
        shift_two_grad,
        expand_weight_grad,
        expand_bias_grad,
        reduce_weight_grad,
        reduce_bias_grad,
    )


def solution(mesh):
    rows = P("freq", "tm", "clip", None)
    lead = P("clip", None, None)
    in_specs = (rows, lead, P("clip")) + (P(),) * 12 + (rows, lead)
    matrix, vector = P("clip", None), P("clip")
    out_specs = (rows, lead, rows, lead) + (matrix, vector) * 2 + (vector,) * 4 + (matrix, vector) * 2
    return jax.shard_map(
        per_device, mesh=mesh, in_specs=in_specs, out_specs=out_specs, check_vma=False
    )
```

```python
import functools
import math

import jax
import jax.numpy as jnp
import numpy as np
from jax import lax
from jax.experimental import pallas as pl
from jax.experimental.pallas import tpu as pltpu
from jax.sharding import PartitionSpec as P

HEADS = 12
EPSILON = 1e-06
NEG_FILL = -1e30
MAX_LENGTH = 101
LEADS = 2
LEAD_ROWS = 16
BLOCK_COLS = 8
GROUP = 4
FF_PARTS = 8
bf16 = jnp.bfloat16
f32 = jnp.float32


def mm(a, b):
    return lax.dot_general(a, b, (((1,), (0,)), ((), ())), preferred_element_type=f32)


def mm_nt(a, b):
    return lax.dot_general(a, b, (((1,), (1,)), ((), ())), preferred_element_type=f32)


def standardize(rows):
    center = rows - jnp.mean(rows, -1, keepdims=True)
    scale_inv = lax.rsqrt(jnp.mean(center * center, -1, keepdims=True) + EPSILON)
    return center * scale_inv, scale_inv


def norm_backward(grad_out, gain_row, normed, scale_inv):
    scaled = grad_out * gain_row
    return scale_inv * (
        scaled
        - jnp.mean(scaled, -1, keepdims=True)
        - normed * jnp.mean(scaled * normed, -1, keepdims=True)
    )


def head_mask(head, width, head_width):
    lane_head = lax.broadcasted_iota(jnp.int32, (1, width), 1) // head_width
    return (lane_head == head).astype(f32)


class Sizes:
    def __init__(self, patches_shape, tm_count, clip_count):
        fr_local, tc_local, clips, feat = patches_shape
        self.fr, self.tc, self.clips, self.feat = fr_local, tc_local, clips, feat
        self.tm, self.clip = tm_count, clip_count
        self.tape = clip_count == 4 and tm_count == 4
        self.tape_rows = 3 * feat * 2 // (2 * clip_count * tm_count)
        self.blocks = tc_local // BLOCK_COLS
        self.half_block = fr_local * BLOCK_COLS
        self.block = 2 * self.half_block
        self.half = self.blocks * self.half_block
        self.rows = 2 * self.half
        self.query_rows = self.rows + LEAD_ROWS
        self.key_blocks = -(-MAX_LENGTH // BLOCK_COLS)
        self.keys = LEAD_ROWS + self.key_blocks * self.block
        self.head_width = feat // HEADS
        self.width = GROUP * self.head_width
        self.steps = HEADS // GROUP
        self.lanes = GROUP * self.rows + 128


def call(kernel, room, in_specs, out_specs, out_shape, scratch, args, info, flops, moved, aliases={}):
    return pl.pallas_call(
        kernel,
        out_shape=out_shape,
        in_specs=[pl.BlockSpec(memory_space=pltpu.SMEM), *in_specs],
        out_specs=out_specs,
        scratch_shapes=scratch,
        input_output_aliases=aliases,
        compiler_params=pltpu.CompilerParams(vmem_limit_bytes=room * 1024 * 1024),
        cost_estimate=pl.CostEstimate(flops=flops, bytes_accessed=moved, transcendentals=0),
    )(info, *args)


def in_vmem(x):
    return pltpu.with_memory_space_constraint(x, pltpu.VMEM)


def in_hbm(x):
    return pltpu.with_memory_space_constraint(x, pltpu.HBM)


def whole(shape):
    return pl.BlockSpec(memory_space=pltpu.VMEM)


def chunks_of(z):
    full = z.lanes // 256
    spans = [(c * 256, 256) for c in range(full)]
    if z.lanes % 256:
        spans.append((full * 256, z.lanes % 256))
    return spans


def spread_heads(z, rows, out_ref):
    for head in range(GROUP):
        mask = head_mask(head, z.width, z.head_width)
        part = (rows * mask).astype(bf16)
        out_ref[head * z.rows : (head + 1) * z.rows, :] = part[: z.rows]
        at = GROUP * z.rows + head * LEAD_ROWS
        out_ref[at : at + LEAD_ROWS, :] = part[z.rows :]
    at = GROUP * (z.rows + LEAD_ROWS)
    out_ref[at:, :] = jnp.zeros((z.lanes - at, z.width), bf16)


def join_heads(z, spread):
    patch_part, lead_part = None, None
    for head in range(GROUP):
        mask = head_mask(head, z.width, z.head_width)
        at = GROUP * z.rows + head * LEAD_ROWS
        one = spread[head * z.rows : (head + 1) * z.rows] * mask
        two = spread[at : at + LEAD_ROWS] * mask
        patch_part = one if patch_part is None else patch_part + one
        lead_part = two if lead_part is None else lead_part + two
    return jnp.concatenate([patch_part, lead_part], 0)


class Copies:
    def __init__(self, sems):
        self.sems, self.going = sems, {}

    def start(self, name, source, to):
        copy = pltpu.make_async_copy(source, to, self.sems.at[len(self.going)])
        copy.start()
        self.going[name] = copy

    def wait(self, *names):
        for name in names:
            self.going[name].wait()


def attend_kernel(z, info, *refs):
    refs = list(refs)
    take = lambda n: [refs.pop(0) for _ in range(n)]
    pieces = take(2 * z.tm)
    lead, weight, bias_q, bias_v, gain, shift, live, wo_in, bo, gain_two, shift_two = take(11)
    low_out, inv_out, uq, unit_out, scale_out, low_two = take(6)
    q_out, k_out, v_out, mixed_out, hk_t_out, hq_t_out, p_out, uk_out, sum_out = take(9)
    spread, total, hk, hq, uk, w, p, q_all, k_all, v_all, mixed_all, hk_t, hq_t, first, wo, sems = take(16)
    me = info[0]
    copies = Copies(sems)
    span = lambda part, i: slice((part * z.steps + i) * z.width, (part * z.steps + i + 1) * z.width)
    copies.start("w", weight, w)
    copies.start("wo", wo_in, wo)
    gain_row, shift_row = gain[...], shift[...]

    def hidden(rows):
        unit, _ = standardize(rows.astype(f32))
        return unit.astype(bf16), (unit * gain_row + shift_row).astype(bf16)

    unit, low = hidden(lead[...])
    uk[0:LEAD_ROWS, :] = unit
    hk[0:LEAD_ROWS, :] = low
    hq[z.rows :, :] = low
    uq[z.rows :, :] = unit
    hb = z.half_block
    for k in range(z.tm):
        source = jnp.bitwise_xor(me, k)
        for half in range(2):
            unit, low = hidden(pieces[2 * k + half][...])
            if k == 0:
                hq[half * z.half : (half + 1) * z.half, :] = low
                uq[half * z.half : (half + 1) * z.half, :] = unit
            for b in range(z.blocks):
                at = LEAD_ROWS + (source * z.blocks + b) * z.block + half * hb
                at = pl.multiple_of(at, 16)
                uk[pl.ds(at, hb), :] = unit[b * hb : (b + 1) * hb]
                hk[pl.ds(at, hb), :] = low[b * hb : (b + 1) * hb]
    copies.start("uk", uk.at[0 : z.keys, :], uk_out)
    hk_all, hq_all = hk[0 : z.keys, :], hq[...]
    hk_t[...] = jnp.transpose(hk_all)
    hq_t[...] = jnp.transpose(hq_all)
    copies.start("hk_t", hk_t, hk_t_out)
    copies.start("hq_t", hq_t, hq_t_out)
    copies.wait("w")
    outs = ((q_all, q_out), (k_all, k_out), (v_all, v_out), (mixed_all, mixed_out))

    def group_copies(i):
        pairs = [(source.at[i], to.at[i]) for source, to in outs] + [(p.at[i % 2], p_out.at[i])]
        return [
            pltpu.make_async_copy(source, to, sems.at[8 + i * len(pairs) + n])
            for n, (source, to) in enumerate(pairs)
        ]

    def group(i, carry):
        columns = lambda part: pl.ds(pl.multiple_of((part * z.steps + i) * z.width, z.width), z.width)
        slot = i % 2
        q_copy, k_copy, v_copy, mixed_copy, p_copy = group_copies(i)

        @pl.when(i >= 2)
        def _():
            group_copies(i - 2)[-1].wait()

        q = (mm(hq[...], w[:, columns(0)]) + bias_q[:, columns(0)]).astype(bf16)
        q_all[i] = q
        spread_heads(z, q.astype(f32) * (z.head_width**-0.5), spread)
        k = mm(hk[0 : z.keys, :], w[:, columns(1)]).astype(bf16)
        k_all[i] = k
        v = (mm(hk[0 : z.keys, :], w[:, columns(2)]) + bias_v[:, columns(0)]).astype(bf16)
        v_all[i] = v
        q_copy.start()
        k_copy.start()
        v_copy.start()
        for at, size in chunks_of(z):
            scores = mm_nt(k, spread[at : at + size, :])
            scores = scores + jnp.concatenate([live[...]] * (size // 128), 1)
            peak = jnp.max(scores, 0, keepdims=True)
            weights = jnp.exp(scores - peak)
            total[i, 0:1, at : at + size] = jnp.sum(weights, 0, keepdims=True)
            p[slot, :, at : at + size] = weights.astype(bf16)
        p_copy.start()
        inverse = 1.0 / total[i, 0:1, :]
        inv_out[i] = jnp.broadcast_to(inverse, (8, z.lanes))
        mixed = mm(jnp.transpose(v), p[slot]) * inverse
        mixed = join_heads(z, jnp.transpose(mixed))
        mixed_all[i] = mixed
        mixed_copy.start()
        low_out[:, columns(0)] = mixed.astype(bf16)
        return carry

    lax.fori_loop(0, z.steps, group, 0)
    copies.wait("wo")
    rows = jnp.concatenate([pieces[0][...], pieces[1][...], lead[...]], 0).astype(f32)
    rows = rows + mm(low_out[...], wo[...]) + bo[...]
    first[...] = rows
    copies.start("sum", first, sum_out)
    normed, scale_inv = standardize(rows)
    unit_out[...] = normed
    scale_out[...] = jnp.broadcast_to(scale_inv, scale_out.shape)
    low_two[...] = (normed * gain_two[...] + shift_two[...]).astype(bf16)
    for i in range(z.steps):
        *near, p_copy = group_copies(i)
        for copy in near:
            copy.wait()
        if i >= z.steps - 2:
            p_copy.wait()
    copies.wait("uk", "hk_t", "hq_t", "sum")


def attend(z, me_info, pieces, lead, weight, bias_q, bias_v, gain, shift, live, wo, *second):
    feat, width, nk, nq, nl = z.feat, z.width, z.keys, z.query_rows, z.lanes
    there = pl.BlockSpec(memory_space=pl.ANY)
    in_specs = [whole((z.half, feat))] * (2 * z.tm) + [whole((LEAD_ROWS, feat)), there]
    in_specs += [whole((1, feat))] * 4 + [whole((nk, 128)), there] + [whole(None)] * 3
    shapes = [((nq, feat), bf16), ((z.steps, 8, nl), f32), ((nq, feat), bf16)]
    shapes += [((nq, feat), f32), ((nq, 128), f32), ((nq, feat), bf16)]
    heads = lambda rows, kind: ((z.steps, rows, width), kind)
    far = [heads(nq, bf16), heads(nk, bf16), heads(nk, bf16), heads(nq, f32)]
    far += [((feat, nk), bf16), ((feat, nq), bf16), ((z.steps, nk, nl), bf16), ((nk, feat), bf16)]
    far.append(((nq, feat), f32))
    return call(
        functools.partial(attend_kernel, z),
        42,
        in_specs,
        [whole(None)] * 6 + [there] * 9,
        [jax.ShapeDtypeStruct(*one) for one in shapes] + [pltpu.HBM(*one) for one in far],
        [
            pltpu.VMEM((nl, width), bf16),
            pltpu.VMEM((z.steps, 8, nl), f32),
            pltpu.VMEM((LEAD_ROWS + z.tm * z.rows, feat), bf16),
            pltpu.VMEM((nq, feat), bf16),
            pltpu.VMEM((LEAD_ROWS + z.tm * z.rows, feat), bf16),
            pltpu.VMEM((feat, 3 * feat), bf16),
            pltpu.VMEM((2, nk, nl), bf16),
            *[pltpu.VMEM(*one) for one in far[:6]],
            pltpu.VMEM((nq, feat), f32),
            pltpu.VMEM((feat, feat), bf16),
            pltpu.SemaphoreType.DMA((32,)),
        ],
        (*pieces, lead, in_hbm(weight), bias_q, bias_v, gain, shift, live, in_hbm(wo), *second),
        me_info,
        2 * feat * feat * (nq + 2 * nk) + 4 * z.steps * nk * nl * width,
        z.steps * nk * nl * 2,
    )


def feed_kernel(z, paired, info, *refs):
    refs = list(refs)
    take = lambda n: [refs.pop(0) for _ in range(n)]
    low, low_other, cot, cot_other, be, we_in, wr_in = take(7)
    dbe, acc, acc_other, grad, grad_other = take(5)
    outs = take(4 if z.tape else 2)
    we, wr, dwr, dwe, low_t, cot_all, acc_sum, grad_sum, sems = take(9)
    steps = FF_PARTS // 2
    size = we.shape[2] // 2
    nq = z.query_rows
    core = info[1]
    col, line = info[0] % 2, info[0] // 2
    place = lambda i: jnp.bitwise_xor(i, 2 * (1 - line)) if z.tape else i
    at = lambda i: pl.multiple_of(
        (2 * place(i) + core if paired else steps * core + i) * size, size
    )
    copies = Copies(sems)
    names = []

    def leave(name, source, to):
        copies.start(name, source, to)
        names.append(name)

    for i in range(steps):
        pair, span = i // 2, slice(i % 2 * size, (i % 2 + 1) * size)
        copies.start(f"we{i}", we_in.at[:, pl.ds(at(i), size)], we.at[pair, :, span])
        copies.start(f"wr{i}", wr_in.at[pl.ds(at(i), size), :], wr.at[pair, span, :])
    cot_all[:nq, :] = cot[...]
    cot_all[nq:, :] = cot_other[...]
    low_all = jnp.concatenate([low[...], low_other[...]], 0)
    low_t[...] = jnp.transpose(low_all)
    for pair in range(steps // 2):
        both = (2 * pair, 2 * pair + 1)
        copies.wait(*[f"w{which}{i}" for i in both for which in "er"])
        cot_low = cot_all[...]
        expand, reduce = we[pair], wr[pair]
        bias = jnp.concatenate([be[:, pl.ds(at(i), size)] for i in both], 1)
        expanded = mm(low_all, expand) + bias
        grad_activated = mm_nt(cot_low, reduce)
        cdf = 0.5 * (1.0 + lax.erf(expanded * math.sqrt(0.5)))
        pdf = jnp.exp(-0.5 * expanded * expanded) * (1.0 / math.sqrt(2.0 * math.pi))
        activated = (expanded * cdf).astype(bf16)
        reduce_grad = mm(jnp.transpose(activated), cot_low).astype(bf16)
        for n, i in enumerate(both):
            if z.tape:
                part = size // z.tm
                for t in range(z.tm):
                    for lane in range(z.feat // 128):
                        rows = slice(n * size + t * part, n * size + (t + 1) * part)
                        dwr[i, t, lane * part : (lane + 1) * part, :] = reduce_grad[
                            rows, lane * 128 : (lane + 1) * 128
                        ]
                out_r, own_r, out_e, own_e = outs
                for y in range(2):
                    leave(f"out_r{i}{y}", dwr.at[i, 2 * y + 1 - col], out_r.at[y, i])
                    leave(f"own_r{i}{y}", dwr.at[i, 2 * y + col], own_r.at[y, i])
            else:
                dwr[i] = reduce_grad[n * size : (n + 1) * size]
                leave(f"dwr{i}", dwr.at[i], outs[0].at[i])
        grad_expanded = (grad_activated * (cdf + expanded * pdf)).astype(bf16)
        expand_grad = mm(low_t[...], grad_expanded).astype(bf16)
        bias_grad = jnp.sum(grad_expanded.astype(f32), 0, keepdims=True)
        for n, i in enumerate(both):
            span = slice(n * size, (n + 1) * size)
            if z.tape:
                part = z.feat // z.clip
                for c in range(z.clip):
                    for lane in range(size // 128):
                        lanes = slice(n * size + lane * 128, n * size + (lane + 1) * 128)
                        dwe[i, c, lane * part : (lane + 1) * part, :] = expand_grad[
                            c * part : (c + 1) * part, lanes
                        ]
                    leave(f"e{i}{c}", dwe.at[i, c], (out_e, own_e)[pair].at[n, c])
            else:
                dwe[i] = expand_grad[:, span]
                leave(f"dwe{i}", dwe.at[i], outs[1].at[i])
            dbe[place(i)] = jnp.broadcast_to(bias_grad[:, span], dbe.shape[1:])
        acc_new, grad_new = mm(activated, reduce), mm_nt(grad_expanded, expand)
        if pair == 0:
            acc_sum[...] = acc_new
            grad_sum[...] = grad_new
        else:
            acc_new, grad_new = acc_sum[...] + acc_new, grad_sum[...] + grad_new
            acc[...] = acc_new[:nq]
            acc_other[...] = acc_new[nq:].astype(bf16)
            grad[...] = grad_new[:nq]
            grad_other[...] = grad_new[nq:].astype(bf16)
    copies.wait(*names)


def feed(z, info, paired, low, low_other, cot, cot_other, expand, expand_bias, reduce):
    feat, ff = expand.shape
    size = ff // FF_PARTS
    steps = FF_PARTS // 2
    nq = z.query_rows
    there, here = pl.BlockSpec(memory_space=pl.ANY), whole(None)
    if z.tape:
        shapes = [(z.tm, size * feat // (128 * z.tm), 128), (z.clip, size * feat // (128 * z.clip), 128)]
    else:
        shapes = [(size, feat), (feat, size)]
    shapes = [(steps, *shape) for shape in shapes]
    wide, narrow = ((nq, feat), f32), ((nq, feat), bf16)
    outs = [((steps, 8, size), f32), wide, narrow, wide, narrow]
    far = shapes
    if z.tape:
        far = [(2, 4, *shapes[0][2:])] * 4
    return call(
        functools.partial(feed_kernel, z, paired),
        44,
        [here] * 5 + [there] * 2,
        [here] * 5 + [there] * len(far),
        [jax.ShapeDtypeStruct(*one) for one in outs] + [pltpu.HBM(shape, bf16) for shape in far],
        [
            pltpu.VMEM((steps // 2, feat, 2 * size), bf16),
            pltpu.VMEM((steps // 2, 2 * size, feat), bf16),
            pltpu.VMEM(shapes[0], bf16),
            pltpu.VMEM(shapes[1], bf16),
            pltpu.VMEM((feat, 2 * nq), bf16),
            pltpu.VMEM((2 * nq, feat), bf16),
            pltpu.VMEM((2 * nq, feat), f32),
            pltpu.VMEM((2 * nq, feat), f32),
            pltpu.SemaphoreType.DMA((48,)),
        ],
        (low, low_other, cot, cot_other, expand_bias, in_hbm(expand), in_hbm(reduce)),
        info,
        6 * nq * feat * ff * 2,
        4 * feat * ff,
    )


def blend_back_kernel(z, info, *refs):
    refs = list(refs)
    take = lambda n: [refs.pop(0) for _ in range(n)]
    grad, grad_got, unit, inv, cot, mixed, gain = take(7)
    first_out, low_grad, send, keep, small, hold = take(6)
    rows_grad = cot[...].astype(f32)
    normed, hidden_grad = unit[...], grad[...] + grad_got[...].astype(f32)
    back = rows_grad + norm_backward(hidden_grad, gain[...], normed, inv[:, 0:1])
    first_out[...] = back
    back_low = back.astype(bf16)
    low_grad[...] = back_low
    dwo = mm(jnp.transpose(mixed[...]), back_low)
    for j in range(z.steps):
        block = dwo[:, j * z.width : (j + 1) * z.width]
        if z.tape:
            store_split(z, info[1], block, hold, send, keep, j)
        else:
            keep[j] = block.astype(bf16)
    small[...] = jnp.zeros_like(small)
    small[0:1, :] = jnp.sum(back_low.astype(f32), 0, keepdims=True)
    small[1:2, :] = jnp.sum(hidden_grad * normed, 0, keepdims=True)
    small[2:3, :] = jnp.sum(hidden_grad, 0, keepdims=True)
    small[3:4, :] = jnp.sum(rows_grad, 0, keepdims=True)


def blend_back(z, info, *args):
    feat, nq = z.feat, z.query_rows
    split = ((z.clip, z.tm, z.tape_rows, 128) if z.tape else (3, feat, z.width), bf16)
    shapes = [((nq, feat), f32), ((nq, feat), bf16), split, split, ((8, feat), f32)]
    return call(
        functools.partial(blend_back_kernel, z),
        20,
        [whole(None)] * len(args),
        [whole(None)] * len(shapes),
        [jax.ShapeDtypeStruct(*one) for one in shapes],
        [pltpu.VMEM((feat, z.width), f32)],
        args,
        info,
        2 * nq * feat * feat,
        nq * feat * 20,
    )


def store_split(z, core, value, hold, sent, kept, j):
    hold[...] = value
    half = z.feat // (2 * z.clip)
    part = half // 2
    for c in range(z.clip):
        for out, whose in ((kept, core), (sent, 1 - core)):
            for t in range(z.tm):
                at = pl.multiple_of((2 * c + whose) * half + (t // 2) * part, 16)
                lanes = slice((t % 2) * 128, (t % 2) * 128 + 128)
                out[c, t, j * part : (j + 1) * part, :] = hold[pl.ds(at, part), lanes].astype(bf16)


def plain_to_tape(z, blocks, core):
    lanes = z.width // 128
    x = blocks.reshape(3, z.clip, 2, z.tm // lanes, -1, lanes, 128)
    x = x.transpose(2, 1, 3, 5, 0, 4, 6).reshape(2, z.clip, z.tm, -1, 128)
    return pick(x, 0, 1 - core), pick(x, 0, core)


def attend_back_kernel(z, i, info, *refs):
    refs = list(refs)
    take = lambda n: [refs.pop(0) for _ in range(n)]
    ga, wo, inv, *far = take(10)
    span = slice(i * z.width, (i + 1) * z.width)
    sent, kept, db, kv_out, q_grad_out = take(5)
    q_spread, g_spread, ds, hold, q, k, v, mixed, hk_t, hq_t, p, sems = take(12)
    core = info[1]
    copies = Copies(sems)
    q_in, k_in, v_in, mixed_in, hk_t_in, hq_t_in, p_in = far
    for name, source, to in (
        ("q", q_in.at[i], q),
        ("mixed", mixed_in.at[i], mixed),
        ("v", v_in.at[i], v),
        ("p", p_in.at[i], p),
        ("k", k_in.at[i], k),
        ("hq_t", hq_t_in, hq_t),
        ("hk_t", hk_t_in, hk_t),
    ):
        copies.start(name, source, to)
    scale = z.head_width**-0.5

    grad = mm_nt(ga[...], wo[span, :]).astype(bf16).astype(f32)
    inverse = inv[i, 0:1, :]
    inverse_col = jnp.transpose(jnp.broadcast_to(inverse, (128, z.lanes)))[:, 0:1]
    copies.wait("q", "mixed")
    spread_heads(z, q[...].astype(f32) * scale, q_spread)
    product = grad * mixed[...]
    dots = []
    for head in range(GROUP):
        mask = head_mask(head, z.width, z.head_width)
        at = GROUP * z.rows + head * LEAD_ROWS
        part = grad * mask
        low = (part[: z.rows] * inverse_col[head * z.rows : (head + 1) * z.rows]).astype(bf16)
        g_spread[head * z.rows : (head + 1) * z.rows, :] = low
        low = (part[z.rows :] * inverse_col[at : at + LEAD_ROWS]).astype(bf16)
        g_spread[at : at + LEAD_ROWS, :] = low
        dots.append(jnp.sum(product * mask, 1, keepdims=True))
    end = GROUP * (z.rows + LEAD_ROWS)
    g_spread[end:, :] = jnp.zeros((z.lanes - end, z.width), bf16)
    dot_col = jnp.concatenate(
        [d[: z.rows] for d in dots]
        + [d[z.rows :] for d in dots]
        + [jnp.zeros((z.lanes - end, 1), f32)],
        0,
    )
    dot_row = jnp.transpose(jnp.broadcast_to(dot_col, (z.lanes, 128)))[0:1, :] * inverse
    copies.wait("v", "p")
    v_all = v[...]
    for at, size in chunks_of(z):
        grad_weights = mm_nt(v_all, g_spread[at : at + size, :])
        weights = p[:, at : at + size].astype(f32)
        ds[:, at : at + size] = (weights * (grad_weights - dot_row[:, at : at + size])).astype(bf16)
    ds_all = ds[...]
    copies.wait("k", "hq_t", "hk_t")
    k_all = k[...]
    grad_v = mm(p[...], g_spread[...])
    grad_k = mm(ds_all, q_spread[...])
    grad_q = mm(jnp.transpose(k_all), ds_all)
    grad_q = (join_heads(z, jnp.transpose(grad_q)) * scale).astype(bf16)
    grad_v = grad_v.astype(bf16)
    grad_k = grad_k.astype(bf16)
    db[...] = jnp.concatenate(
        [
            jnp.sum(grad_q.astype(f32), 0, keepdims=True),
            jnp.sum(grad_v.astype(f32), 0, keepdims=True),
            jnp.zeros((6, z.width), f32),
        ],
        0,
    )
    for j, grad in enumerate((mm(hq_t[...], grad_q), mm(hk_t[...], grad_k), mm(hk_t[...], grad_v))):
        if z.tape:
            store_split(z, core, grad, hold, sent, kept, j)
        else:
            kept[j] = grad.astype(bf16)
    kv_out[:, : z.width] = grad_k
    kv_out[:, z.width :] = grad_v
    q_grad_out[...] = grad_q


def keys_back_kernel(z, info, *refs):
    refs = list(refs)
    take = lambda n: [refs.pop(0) for _ in range(n)]
    uk_in, uq, weight_in, first, feed_small = take(5)
    db, grad_kv, grad_q = take(z.steps), take(z.steps), take(z.steps)
    own, small_out = take(2)
    sends = take(4 if z.tape else z.tm - 1)
    keys_acc, query_acc, small, uk, weight, sems = take(6)
    me = info[0]
    copies = Copies(sems)
    span = lambda part, i: slice((part * z.steps + i) * z.width, (part * z.steps + i + 1) * z.width)
    copies.start("w", weight_in, weight)
    copies.start("uk", uk_in, uk)
    column = lambda part, i: slice((part * z.steps + i) * z.width, (part * z.steps + i + 1) * z.width)
    copies.wait("w")
    query_grad, keys_grad = 0.0, 0.0
    for i in range(z.steps):
        query_grad += mm_nt(grad_q[i][...], weight[:, column(0, i)])
        keys_grad += mm_nt(grad_kv[i][:, : z.width], weight[:, column(1, i)])
        keys_grad += mm_nt(grad_kv[i][:, z.width :], weight[:, column(2, i)])
    keys_acc[...] = keys_grad
    query_acc[...] = query_grad
    copies.wait("uk")
    small[...] = jnp.zeros_like(small)
    for i in range(z.steps):
        small[0:2, i * z.width : (i + 1) * z.width] = db[i][0:2, :]
    small[2:3, :] = jnp.sum(keys_grad * uk[...].astype(f32), 0, keepdims=True) + jnp.sum(
        query_grad * uq[...].astype(f32), 0, keepdims=True
    )
    small[3:4, :] = jnp.sum(keys_grad, 0, keepdims=True) + jnp.sum(query_grad, 0, keepdims=True)
    small[4:12, :] = feed_small[...]
    if z.tape:
        for lane in range(z.feat // 128):
            small_out[lane * 16 : lane * 16 + 16, :] = small[
                :, lane * 128 : lane * 128 + 128
            ].astype(bf16)
    else:
        small_out[...] = small[...]
    lead = keys_acc[0:LEAD_ROWS, :] + query_acc[z.rows :, :]
    first_lead = first[z.rows :, :]
    high = first_lead.astype(bf16)
    rest = (first_lead - high.astype(f32)).astype(bf16)
    pair = lambda a: a[0:LEADS]
    packed = jnp.concatenate(
        [pair(lead), pair(high.astype(f32)), pair(rest.astype(f32)), jnp.zeros((10, z.feat), f32)], 0
    )
    small_high = small[...].astype(bf16)
    small_low = (small[...] - small_high.astype(f32)).astype(bf16)
    own[z.rows :, :] = packed
    packed = packed.astype(bf16)
    hb = z.half_block

    def chunk(k, half, out, at):
        source = jnp.bitwise_xor(me, k)
        for b in range(z.blocks):
            spot = source * z.blocks + b
            from_ = pl.multiple_of(
                LEAD_ROWS + jnp.minimum(spot, z.key_blocks - 1) * z.block + half * hb, 16
            )
            rows = keys_acc[pl.ds(from_, hb), :] * (spot < z.key_blocks).astype(f32)
            to = at + b * hb
            if k == 0:
                queries = half * z.half + b * hb
                rows = rows + query_acc[queries : queries + hb, :]
            out[to : to + hb, :] = rows.astype(out.dtype)

    chunk(0, 0, own, 0)
    chunk(0, 1, own, z.half)
    if z.tape:
        along_x, along_y, mid_x, mid_y = sends
        chunk(1, 0, along_x, 0)
        chunk(3, 0, along_x, z.half)
        along_x[z.rows :, :] = packed
        chunk(2, 1, along_y, 0)
        chunk(3, 1, along_y, z.half)
        chunk(2, 0, mid_x, 0)
        chunk(1, 1, mid_y, 0)
    else:
        for k, one in enumerate(sends, start=1):
            chunk(k, 0, one, 0)
            chunk(k, 1, one, z.half)
            one[z.rows :, :] = packed


def attend_back(z, info, i, ga, wo, saved):
    inv, far = saved[1], saved[6:13]
    feat, width, nk, nq, nl = z.feat, z.width, z.keys, z.query_rows, z.lanes
    in_specs = [whole(None)] * 3 + [pl.BlockSpec(memory_space=pl.ANY)] * 7
    if z.tape:
        part = (z.clip, z.tm, z.tape_rows, 128)
    else:
        part = (3, feat, width)
    sent, kept, *rest = call(
        functools.partial(attend_back_kernel, z, i),
        24,
        in_specs,
        [whole(part), whole(part), whole((8, width)), whole((nk, 2 * width)), whole((nq, width))],
        [
            jax.ShapeDtypeStruct(part, bf16),
            jax.ShapeDtypeStruct(part, bf16),
            jax.ShapeDtypeStruct((8, width), f32),
            jax.ShapeDtypeStruct((nk, 2 * width), bf16),
            jax.ShapeDtypeStruct((nq, width), bf16),
        ],
        [
            pltpu.VMEM((nl, width), bf16),
            pltpu.VMEM((nl, width), bf16),
            pltpu.VMEM((nk, nl), bf16),
            pltpu.VMEM((feat, width), f32),
            pltpu.VMEM((nq, width), bf16),
            pltpu.VMEM((nk, width), bf16),
            pltpu.VMEM((nk, width), bf16),
            pltpu.VMEM((nq, width), f32),
            pltpu.VMEM((feat, nk), bf16),
            pltpu.VMEM((feat, nq), bf16),
            pltpu.VMEM((nk, nl), bf16),
            pltpu.SemaphoreType.DMA((8,)),
        ],
        [ga, wo, inv, *[in_hbm(one) for one in far]],
        info,
        1000,
        1000,
    )
    if not z.tape:
        sent, kept = plain_to_tape(z, kept, info[1])
    return sent, kept, rest


def keys_back(z, info, saved, weight, first_lead, feed_small, steps):
    feat, width, nk, nq = z.feat, z.width, z.keys, z.query_rows
    uq, uk = saved[2], saved[13]
    there = pl.BlockSpec(memory_space=pl.ANY)
    in_specs = [there, whole((nq, feat)), there]
    in_specs += [whole(None)]
    in_specs += [whole((8, feat))]
    in_specs += [whole((8, width))] * z.steps
    in_specs += [whole((nk, 2 * width))] * z.steps + [whole((nq, width))] * z.steps
    if z.tape:
        sends = [(nq, feat), (z.rows, feat), (z.half, feat), (z.half, feat)]
    else:
        sends = [(nq, feat)] * (z.tm - 1)
    small = (16 * feat // 128, 128) if z.tape else (16, feat)
    return call(
        functools.partial(keys_back_kernel, z),
        24,
        in_specs,
        [whole((nq, feat)), whole(small)] + [whole(shape) for shape in sends],
        [
            jax.ShapeDtypeStruct((nq, feat), f32),
            jax.ShapeDtypeStruct(small, bf16 if z.tape else f32),
        ]
        + [jax.ShapeDtypeStruct(shape, bf16) for shape in sends],
        [
            pltpu.VMEM((nk, feat), f32),
            pltpu.VMEM((nq, feat), f32),
            pltpu.VMEM((16, feat), f32),
            pltpu.VMEM((nk, feat), bf16),
            pltpu.VMEM(weight.shape, bf16),
            pltpu.SemaphoreType.DMA((16,)),
        ],
        (in_hbm(uk), uq, in_hbm(weight), first_lead, feed_small)
        + tuple(step[j] for j in range(3) for step in steps),
        info,
        4 * feat * feat * (nq + 2 * nk),
        nk * feat * 4,
    )


def finish_kernel(z, info, *refs):
    *received, rows, gain, grad_first, out_mine, out_send = refs[1:]
    own = refs[0]
    mine = own[z.rows :].astype(bf16).astype(f32)
    if z.tape:
        got_x, got_y, got_xy, got_yx = (one[...].astype(f32) for one in received)
        first = own[: z.half] + got_x[: z.half] + got_xy[: z.half]
        second = own[z.half : z.rows] + got_y[: z.half] + got_yx
        lead = (mine + got_x[z.rows :]).astype(bf16).astype(f32) + got_xy[z.half :]
        total = jnp.concatenate([first, second, lead], 0)
    else:
        terms = [one[...].astype(f32) for one in received]
        leads = [mine] + [one[z.rows :] for one in terms]
        while len(leads) > 1:
            leads = [a + b for a, b in zip(leads[::2], leads[1::2])]
        total = jnp.concatenate([own[: z.rows] + sum(t[: z.rows] for t in terms), leads[0]], 0)
    normed, scale_inv = standardize(rows[...].astype(f32))
    back = norm_backward(total, gain[...], normed, scale_inv)
    rows_grad = (back[: z.rows] + grad_first[0 : z.rows, :]).astype(bf16)
    out_mine[...] = rows_grad[: z.half]
    out_send[0 : z.half, :] = rows_grad[z.half :]
    lead = total[z.rows :]
    lead_first = lead[LEADS : 2 * LEADS] + lead[2 * LEADS : 3 * LEADS]
    out_send[z.half :, :] = jnp.concatenate(
        [back[z.rows : z.rows + LEADS] + lead_first, jnp.zeros((LEAD_ROWS - LEADS, z.feat), f32)], 0
    ).astype(bf16)


def finish(z, info, own, received, rows, gain, grad_first):
    feat, nq = z.feat, z.query_rows
    return call(
        functools.partial(finish_kernel, z),
        16,
        [whole(one.shape) for one in (own, *received)]
        + [whole((nq, feat)), whole((1, feat)), whole((nq, feat))],
        [whole((z.half, feat)), whole((nq - z.half, feat))],
        [
            jax.ShapeDtypeStruct((z.half, feat), bf16),
            jax.ShapeDtypeStruct((nq - z.half, feat), bf16),
        ],
        [],
        (own, *received, rows, gain, grad_first),
        info,
        nq * feat * 20,
        nq * feat * 20,
    )


def place_blocks(z, t, whose, tape, row, out, lane_at):
    half = z.feat // (2 * z.clip)
    part = half // 2
    at = pl.multiple_of(whose * half + (t // 2) * part, 16)
    for j in range(3):
        block = tape[row + j * part : row + (j + 1) * part, :].astype(f32)
        lane = pl.multiple_of(lane_at(j) + (t % 2) * 128, 128)
        out[pl.ds(at, part), pl.ds(lane, 128)] = block


def assemble_feed_kernel(z, ff, far, info, *refs):
    me, core = info[0], info[1]
    expand_out, reduce_out, expand, reduce, sems = refs[-5:]
    p_mine, q_mine, p_other, q_other = refs[:4]
    size = ff // FF_PARTS
    step = size * z.feat // (128 * z.tm) + z.tape_rows
    part_r, part_e = size // z.tm, z.feat // z.clip
    copies = Copies(sems)
    names = []
    for whose, p, q in ((core, p_mine, q_mine), (1 - core, p_other, q_other)):
        for j, (k_p, k_q) in enumerate(((2, 1), (3, 3)) if far else ((0, 0), (1, 2))):
            n = len(names)
            for lane in range(z.feat // 128):
                block = p[j * step + lane * part_r : j * step + (lane + 1) * part_r, :]
                reduce[n, :, lane * 128 : (lane + 1) * 128] = block.astype(f32)
            at = pl.multiple_of(whose * size + jnp.bitwise_xor(me, k_p) * part_r, 16)
            copies.start((n, 0), reduce.at[n], reduce_out.at[pl.ds(at, part_r), :])
            for lane in range(size // 128):
                block = q[j * step + lane * part_e : j * step + (lane + 1) * part_e, :]
                expand[n, :, lane * 128 : (lane + 1) * 128] = block.astype(f32)
            at = pl.multiple_of((2 * jnp.bitwise_xor(me, k_q) + whose) * size, 128)
            copies.start((n, 1), expand.at[n], expand_out.at[:, pl.ds(at, size)])
            names.append(n)
    copies.wait(*[(n, i) for n in names for i in range(2)])


def assemble_feed(z, info, ff, far, tapes, before):
    rows, size = z.feat // z.clip, ff // FF_PARTS
    there = pl.BlockSpec(memory_space=pl.ANY)
    return call(
        functools.partial(assemble_feed_kernel, z, ff, far),
        16,
        [whole(None)] * 4 + [there] * len(before),
        [there] * 2,
        [pltpu.HBM((rows, ff), f32), pltpu.HBM((ff // z.clip, z.feat), f32)],
        [
            pltpu.VMEM((4, rows, size), f32),
            pltpu.VMEM((4, size // z.tm, z.feat), f32),
            pltpu.SemaphoreType.DMA((8,)),
        ],
        (*tapes, *before),
        info,
        1000,
        24 * tapes[0].size,
        {5: 0, 6: 1} if before else {},
    )


def assemble_input_kernel(z, step, info, *refs):
    me, core = info[0], info[1]
    near, far, (late, late_other), (output_out, input_out) = refs[:4], refs[4:8], refs[8:10], refs[10:]
    last = step - z.tape_rows
    for whose, m, late_tape in ((core, 0, late), (1 - core, 2, late_other)):
        for k in range(z.tm):
            t = jnp.bitwise_xor(me, k)
            tape, at = (near[m], far[m])[k // 2], k % 2 * step + last
            place_blocks(z, t, whose, tape, at, output_out, lambda j: j * z.width)
            tape, at = (near[m + 1], far[m + 1])[k % 2], k // 2 * step + last
            place_blocks(z, t, whose, tape, at, input_out, lambda j: j * z.feat)
            for i in (1, 2):
                row = (2 * k + i - 1) * z.tape_rows
                lane_at = lambda j: j * z.feat + i * z.width
                place_blocks(z, t, whose, late_tape, row, input_out, lane_at)


def assemble_input(z, info, near, far, late):
    rows = z.feat // z.clip
    shapes = [(rows, z.feat), (rows, 3 * z.feat)]
    return call(
        functools.partial(assemble_input_kernel, z, near[0].shape[0] // 2),
        20,
        [whole(None)] * 10,
        [whole(None)] * 2,
        [jax.ShapeDtypeStruct(shape, f32) for shape in shapes],
        [],
        (*near, *far, *late),
        info,
        1000,
        16 * late[0].size,
    )


def small_kernel(z, info, mine, other, *outs):
    total = mine[...].astype(f32) + other[...].astype(f32)
    lanes = z.feat // 128

    def row(i):
        return jnp.concatenate([total[n * 16 + i : n * 16 + i + 1, :] for n in range(lanes)], 1)

    rows = [row(i) for i in range(12)]
    biases = jnp.concatenate(rows[:2], 1)
    count = z.feat // z.clip
    for c in range(z.clip):

        @pl.when(info[2] == c)
        def _(c=c):
            outs[0][...] = biases[0, 2 * count * c : 2 * count * (c + 1)]
            for i in range(2, 8):
                outs[i - 1][...] = rows[i][0, count * c : count * (c + 1)]
            outs[7][...] = rows[8 + c][0, :]


def small_grads(z, info, mine, other):
    count = z.feat // z.clip
    sizes = [2 * count] + [count] * 6 + [4 * count]
    return call(
        functools.partial(small_kernel, z),
        4,
        [whole(None)] * 2,
        [whole(None)] * 8,
        [jax.ShapeDtypeStruct((size,), f32) for size in sizes],
        [],
        (mine, other),
        info,
        1000,
        1000,
    )


def flip(count, k):
    return [(i, i ^ k) for i in range(count)]


def bit_of(index, bit):
    return (index >> bit) & 1


def bits_of(count):
    return count.bit_length() - 1


def pick(x, dim, index):
    return lax.dynamic_index_in_dim(x, index, dim, keepdims=False)


def add(kept, got):
    return (kept.astype(f32) + got.astype(f32)).astype(bf16)


def by_bits(x, dim, count):
    return x.reshape(x.shape[:dim] + (2,) * bits_of(count) + x.shape[dim + 1 :])


def halves(x, dim, axis, bit):
    mine = bit_of(lax.axis_index(axis), bit)
    return pick(x, dim, 1 - mine), pick(x, dim, mine)


def across(x, axis, bit):
    return lax.ppermute(x, axis, flip(lax.axis_size(axis), 1 << bit))


def scatter(x, dim, axis, bits):
    for bit in bits:
        sent, kept = halves(x, dim, axis, bit)
        x = add(kept, across(sent, axis, bit))
    return x


def scatter_up(x, dim, axis, bits):
    for bit in bits:
        at = dim + bits_of(lax.axis_size(axis)) - 1 - bit
        sent, kept = halves(x, at, axis, bit)
        x = add(kept, across(sent, axis, bit))
    return x


def peers(x, dim, axis):
    me = lax.axis_index(axis)
    return [pick(x, dim, me ^ k) for k in range(1, lax.axis_size(axis))]


def to_peers(sent, axis):
    count = lax.axis_size(axis)
    return [lax.ppermute(one, axis, flip(count, k)) for k, one in enumerate(sent, start=1)]


def add_all(own, got):
    total = own.astype(f32)
    for one in got:
        total = total + one.astype(f32)
    return total.astype(bf16)


def in_order(x, got, axis):
    me = lax.axis_index(axis)
    out = jnp.zeros((1 + len(got),) + x.shape, x.dtype)
    for k, one in enumerate([x, *got]):
        out = lax.dynamic_update_index_in_dim(out, one, me ^ k, 0)
    return out


def tie(*values):
    return lax.optimization_barrier(values)


def per_device(
    patches,
    lead_tokens,
    lengths,
    input_weight,
    input_bias,
    output_weight,
    output_bias,
    first_gain,
    first_shift,
    second_gain,
    second_shift,
    expand_weight,
    expand_bias,
    reduce_weight,
    reduce_bias,
    cot_patches,
    cot_lead,
):
    tm_count = lax.axis_size("tm")
    clip_count = lax.axis_size("clip")
    z = Sizes(patches.shape, tm_count, clip_count)
    feat, ff = expand_weight.shape
    core, place = lax.axis_index("freq"), lax.axis_index("tm")
    info = jnp.stack([place, core, lax.axis_index("clip")]).astype(jnp.int32)
    row = lambda vector: vector.astype(f32)[None, :]

    def by_clip(array):
        parts = array.reshape(z.fr, z.blocks, BLOCK_COLS, z.clips, feat)
        parts = parts.transpose(3, 1, 0, 2, 4).reshape(z.clips, z.half, feat)
        return (
            lax.dynamic_index_in_dim(parts, core, 0, keepdims=False),
            lax.dynamic_index_in_dim(parts, 1 - core, 0, keepdims=False),
        )

    def lead_of(array):
        mine = lax.dynamic_index_in_dim(array, core, 0, keepdims=False)
        return jnp.pad(mine, ((0, LEAD_ROWS - LEADS), (0, 0)))

    own_half, other_half = by_clip(patches)
    pieces = []
    for k in range(tm_count):
        pieces.append(lax.ppermute(own_half, "tm", flip(tm_count, k)) if k else own_half)
        pieces.append(
            lax.ppermute(other_half, ("freq", "tm"), flip(2 * tm_count, tm_count | k))
        )
    lead = lead_of(lead_tokens)
    rows = jnp.concatenate([pieces[0], pieces[1], lead], 0)
    own_cot, other_cot = by_clip(cot_patches)
    lead_cot = lead_of(cot_lead) * (place == 0).astype(bf16)
    cot = jnp.concatenate([own_cot, lax.ppermute(other_cot, "freq", flip(2, 1)), lead_cot], 0)
    cot_got = lax.ppermute(cot, "freq", flip(2, 1))

    length = lax.dynamic_index_in_dim(lengths, core, 0, keepdims=False)
    spots = np.arange(z.keys) - LEAD_ROWS
    columns = np.where(spots < 0, 1 << 20, spots // z.block * BLOCK_COLS + spots % BLOCK_COLS)
    columns[:LEADS] = -1
    live = jnp.where(jnp.asarray(columns, jnp.int32)[:, None] < length, 0.0, NEG_FILL)
    live = jnp.broadcast_to(live.astype(f32), (z.keys, 128))

    saved = attend(
        z,
        info,
        pieces,
        lead,
        input_weight,
        row(input_bias[:feat]),
        row(input_bias[feat:]),
        row(first_gain),
        row(first_shift),
        live,
        output_weight,
        row(output_bias),
        row(second_gain),
        row(second_shift),
    )
    mixed_low = saved[0]
    paired = clip_count == FF_PARTS // 2
    if not paired:
        share = (clip_count, 2, ff // (2 * clip_count))
        expand_weight = expand_weight.reshape(feat, *share).swapaxes(1, 2).reshape(feat, ff)
        expand_bias = expand_bias.reshape(share).swapaxes(0, 1).reshape(ff)
        reduce_weight = reduce_weight.reshape(*share, feat).swapaxes(0, 1).reshape(ff, feat)
    gain_two = row(second_gain)
    swap = lambda x: across(x, "freq", 0)
    size = ff // FF_PARTS
    half = clip_count // 2
    tm_bits, clip_bits = bits_of(tm_count), bits_of(clip_count)
    low_bits, high_bits = list(range(tm_bits)), list(range(tm_bits))[::-1]
    split = max(1, tm_count // (FF_PARTS // 2))

    unit, inv, low, total = saved[3], saved[4], saved[5], saved[14]
    feed_bias, acc, acc_send, grad, grad_send, *sums = feed(
        z, info, paired, low, swap(low), cot, cot_got, expand_weight, row(expand_bias), reduce_weight
    )
    if z.tape:
        out_r, own_r, out_e, own_e = sums
    else:
        sum_r, sum_e = sums
        rows_r, rows_e = ff // (2 * clip_count * tm_count), feat // (clip_count * split)
        sum_r = sum_r.reshape(clip_count, tm_count, rows_r, feat // 128, 128).swapaxes(2, 3)
        sum_e = sum_e.reshape(-1, clip_count, split, rows_e, size // 128, 128)
        sum_e = sum_e.transpose(0, 2, 1, 4, 3, 5)
        sum_r = sum_r.reshape(clip_count, tm_count, -1, 128)
        sum_e = sum_e.reshape(tm_count, clip_count, -1, 128).swapaxes(0, 1)
        out_r, own_r = halves(by_bits(sum_r, 1, tm_count), 1 + tm_bits - 1, "tm", 0)
        out_e, own_e = halves(by_bits(sum_e, 1, tm_count), 1, "tm", tm_bits - 1)
    grad, grad_send, acc_send, out_r, out_e = tie(grad, grad_send, acc_send, out_r, out_e)
    across_r = lambda x: across(x, "tm", 0)
    across_e = lambda x: across(x, "tm", tm_bits - 1)
    across_z = lambda x: across(x, "clip", 0)
    halves_z = lambda x: halves(by_bits(x, 0, clip_count), clip_bits - 1, "clip", 0)
    rest_z = lambda x: scatter_up(x, 0, "clip", range(1, clip_bits))

    got_r, got_e = across_r(out_r), across_e(out_e)
    acc_got = swap(acc_send)
    grad_first, grad_low, sent_o, kept_o, small_two = blend_back(
        z, info, grad, swap(grad_send), unit, inv, cot, mixed_low, gain_two
    )
    if not z.tape:
        sent_o, kept_o = plain_to_tape(z, kept_o, core)
    got_o = swap(sent_o)
    sent_0, kept_0, rest_0 = attend_back(z, info, 0, grad_low, output_weight, saved)
    grad_low, got_o, acc_got, sent_0 = tie(grad_low, got_o, acc_got, sent_0)
    out_o, own_o = halves_z(add(kept_o, got_o))
    grad_low, out_o = tie(grad_low, out_o)
    got_0, got_oz = swap(sent_0), across_z(out_o)
    sent_1, kept_1, rest_1 = attend_back(z, info, 1, grad_low, output_weight, saved)
    grad_low, got_r, got_e, got_0, got_oz, sent_1 = tie(
        grad_low, got_r, got_e, got_0, got_oz, sent_1
    )
    sum_r, sum_e = add(own_r, got_r), add(own_e, got_e)
    if z.tape:
        out_r, own_r = halves(sum_r, 0, "tm", 1)
        out_e, own_e = halves(sum_e, 0, "tm", 0)
        ordered = lambda x: jnp.where(place // 2 == 0, jnp.concatenate([x[half:], x[:half]], 0), x)
        out_r, own_r = ordered(out_r), ordered(own_r)
    else:
        sum_r = scatter_up(sum_r, 1, "tm", low_bits[1:-1])
        sum_e = scatter(sum_e, 1, "tm", high_bits[1:-1])
        out_r, own_r = halves(sum_r, 1, "tm", low_bits[-1])
        out_e, own_e = halves(sum_e, 1, "tm", high_bits[-1])
    sum_o = add(own_o, got_oz)
    out_0, own_0 = halves_z(add(kept_0, got_0))
    grad_low, out_r, out_e, sum_o, out_0 = tie(grad_low, out_r, out_e, sum_o, out_0)
    got_r, got_e = across(out_r, "tm", low_bits[-1]), across(out_e, "tm", high_bits[-1])
    got_0z, got_1 = across_z(out_0), swap(sent_1)
    sum_o = rest_z(sum_o)

    def split_tm(x, *more):
        x = by_bits(x, 1, tm_count)
        parts = [x[:half], x[half:]]
        if more:
            parts = [jnp.concatenate([p, by_bits(m, 1, tm_count)], 0) for p, m in zip(parts, more)]
        return (
            *halves(parts[0], tm_bits, "tm", 0),
            *halves(parts[1], 1, "tm", tm_bits - 1),
        )

    sent_2, kept_2, rest_2 = attend_back(z, info, 2, grad_low, output_weight, saved)
    sent_2, got_r, got_e, got_0z, got_1, sum_o, *rest_2 = tie(
        sent_2, got_r, got_e, got_0z, got_1, sum_o, *rest_2
    )
    sum_r, sum_e = add(own_r, got_r), add(own_e, got_e)
    out_f, own_f = halves_z(jnp.concatenate([sum_r, sum_e], 1))
    count_f = sum_r.shape[1]
    sum_0 = add(own_0, got_0z)
    out_1x, own_1x, out_1y, own_1y = split_tm(add(kept_1, got_1))
    feed_bias = feed_bias[:, 0:1] * (jnp.arange(2) == core).astype(f32)[:, None]
    if not paired:
        feed_bias = feed_bias.swapaxes(0, 1).reshape(2, clip_count, -1).swapaxes(0, 1)
    feed_small = jnp.concatenate([small_two[:4], feed_bias.reshape(-1, feat)], 0)
    out_f, sum_0, out_1x, out_1y, sent_2, *rest_2 = tie(
        out_f, sum_0, out_1x, out_1y, sent_2, *rest_2
    )
    got_f, got_2, got_1x, got_1y = across_z(out_f), swap(sent_2), across_r(out_1x), across_e(out_1y)
    sum_0 = rest_z(sum_0)
    own, small, *sends = keys_back(
        z, info, saved, input_weight, grad_first, feed_small, (rest_0, rest_1, rest_2)
    )
    got_2, got_1x, got_1y, sum_0, own, small, *sends = tie(
        got_2, got_1x, got_1y, sum_0, own, small, *sends
    )
    out_2x, own_2x, out_2y, own_2y = split_tm(add(kept_2, got_2), sum_o[None], sum_0[None])
    def patches_of(mine, theirs):
        first = jnp.where(core == 0, mine, theirs[: z.half])
        second = jnp.where(core == 0, theirs[: z.half], mine)
        pair = jnp.stack([first, second], 0).reshape(
            z.clips, z.blocks, z.fr, BLOCK_COLS, feat
        )
        return pair.transpose(2, 1, 3, 0, 4).reshape(z.fr, z.tc, z.clips, feat)

    finish_args = (rows, row(first_gain), grad_first)
    block_of = lambda total: (total + acc + acc_got.astype(f32) + row(reduce_bias)).astype(bf16)
    if z.tape:
        flat = lambda *parts: jnp.concatenate([part.reshape(-1, 128) for part in parts], 0)
        count = small.shape[0]
        unpack = lambda got, like: (got[:-count].reshape(like.shape), got[-count:])
        across_x, across_y = lambda x: across(x, "tm", 0), lambda x: across(x, "tm", 1)
        across_zz = lambda x: across(x, "clip", 1)
        along_x, along_y, mid_x, mid_y = sends
        token, msg_x, out_2y, along_x, along_y = tie(
            info, flat(out_2x, small), out_2y, along_x, along_y
        )
        msg_x, got_2y = across_x(msg_x), across_y(out_2y)
        got_x, got_y = across_x(along_x), across_y(along_y)
        token, msg_x, got_2y = tie(token, msg_x, got_2y)
        got_2x, got_small = unpack(msg_x, own_2x)
        small = add(small, got_small)
        sum_x = jnp.concatenate([add(own_1x, got_1x), add(own_2x, got_2x)], 0)
        sum_y = jnp.concatenate([add(own_1y, got_1y), add(own_2y, got_2y)], 0)
        out_x, own_x = halves(sum_x, 1, "tm", 1)
        out_y, own_y = halves(sum_y, 1, "tm", 0)
        token, small = tie(token, small)
        token, msg_x, out_y, got_f = tie(token, flat(out_x, small), out_y, got_f)
        out_f, own_f = halves(add(own_f, got_f), 0, "clip", 1)
        msg_x, got_y2, got_f = across_y(msg_x), across_x(out_y), across_zz(out_f)
        token, msg_x, got_y2 = tie(token, msg_x, got_y2)
        got_x2, got_small = unpack(msg_x, own_x)
        small = add(small, got_small)
        sum_x, sum_y = add(own_x, got_x2), add(own_y, got_y2)
        late = [jnp.concatenate([one[:2], one[2:4]], 1) for one in (sum_x, sum_y)]
        out_l, own_l = halves_z(jnp.concatenate(late, 0))
        token, small = tie(token, small)
        token, msg_l = tie(token, flat(out_l, small))
        msg_l = across_z(msg_l)
        token, got_f = tie(token, got_f)
        sum_f = add(own_f, got_f)
        token, ready_p, ready_q = tie(
            token, flat(sum_f[:count_f], sum_x[4]), flat(sum_f[count_f:], sum_y[4])
        )
        got_p, got_q = across_x(ready_p), across_y(ready_q)
        token, total_now, got_x, got_y = tie(token, total, got_x, got_y)
        block = block_of(total_now)
        block_mine, block_send = block[: z.half], block[z.half :]
        lead = add(along_x[z.rows :], got_x[z.rows :])
        out_xy = jnp.concatenate([add(mid_x, got_x[z.half : z.rows]), lead], 0)
        out_yx = add(mid_y, got_y[z.half :])
        token, out_xy, out_yx = tie(token, out_xy, out_yx)
        got_xy, got_yx = across_y(out_xy), across_x(out_yx)
        token, msg_l, block_mine, block_send = tie(token, msg_l, block_mine, block_send)
        got_l, got_small = unpack(msg_l, own_l)
        small = add(small, got_small)
        out_l, own_l = halves(add(own_l, got_l), 0, "clip", 1)
        token, small = tie(token, small)
        token, msg_l = tie(token, flat(out_l, small))
        msg_l = across_zz(msg_l)
        token, got_xy, got_yx = tie(token, got_xy, got_yx)
        received = [got_x, got_y, got_xy, got_yx]
        grad_mine, grad_send = finish(z, token, own, received, *finish_args)
        token, grad_send = tie(token, grad_send)
        grad_got, block_got = swap(grad_send), swap(block_send)
        token, got_p, got_q, grad_got, block_got = tie(token, got_p, got_q, grad_got, block_got)
        token, near_p, near_q = tie(token, flat(ready_p, got_p), flat(ready_q, got_q))
        far_p, far_q = across_y(near_p), across_x(near_q)
        other_p, other_q = swap(near_p), swap(near_q)
        token, msg_l, other_p, other_q = tie(token, msg_l, other_p, other_q)
        got_l, got_small = unpack(msg_l, own_l)
        small, late = add(small, got_small), add(own_l, got_l)
        token, small, late = tie(token, small, late)
        late_all = to_peers([late] * 3, "tm")
        feed_grads = assemble_feed(z, token, ff, 0, (near_p, near_q, other_p, other_q), ())
        patch_outs = (patches_of(block_mine, block_got), patches_of(grad_mine, grad_got))
        token, far_p, far_q, *rest = tie(token, far_p, far_q, *feed_grads, *patch_outs)
        feed_grads, patch_outs = rest[:2], rest[2:]
        other_far = (swap(far_p), swap(far_q))
        token, *late_all = tie(token, *late_all)
        token, late, small = tie(token, flat(late, *late_all), small)
        late_got, small_got = swap(late), swap(small)
        token, *other_far = tie(token, *other_far)
        far = (far_p, far_q, *other_far)
        feed_grads = assemble_feed(z, token, ff, 1, far, feed_grads)
        token, *feed_grads = tie(token, *feed_grads)
        vectors = small_grads(z, token, small, small_got)
    else:
        received = to_peers(sends, "tm")
        got_2x, got_2y = across_r(out_2x), across_e(out_2y)
        sum_x = jnp.concatenate([add(own_1x, got_1x), add(own_2x, got_2x)], 0)
        sum_y = jnp.concatenate([add(own_1y, got_1y), add(own_2y, got_2y)], 0)
        sum_x = scatter_up(sum_x, 1, "tm", low_bits[1:])
        sum_y = scatter(sum_y, 1, "tm", high_bits[1:])
        sum_f = rest_z(add(own_f, got_f))
        ready = jnp.concatenate([sum_f, sum_x[2 * half], sum_y[2 * half]], 0)
        late = jnp.concatenate(
            [
                jnp.concatenate([one[:half], one[half : 2 * half]], 1)
                for one in (sum_x, sum_y)
            ],
            0,
        )
        late = scatter(by_bits(late, 0, clip_count), 0, "clip", range(clip_bits)[::-1])
        ready = jnp.concatenate([ready, late], 0)
        ready_all = [ready] + to_peers([ready] * (tm_count - 1), "tm")
        small = small + swap(small)
        for axis, bits in (("tm", tm_bits), ("clip", clip_bits)):
            for bit in range(bits):
                small = small + across(small, axis, bit)
        grad_mine, grad_send = finish(z, info, own, received, *finish_args)

    here = lax.axis_index("clip")

    def shard(vector):
        count = vector.shape[0] // clip_count
        return lax.dynamic_slice_in_dim(vector, here * count, count, 0)

    if not z.tape:
        vectors = [shard(small[0:2].reshape(-1)), *[shard(small[i]) for i in range(2, 8)]]
        vectors.append(shard(small[8:12].reshape(-1)))
    input_bias_grad, gain_one_grad, shift_one_grad, output_bias_grad = vectors[:4]
    gain_two_grad, shift_two_grad, reduce_bias_grad, expand_bias_grad = vectors[4:]

    if z.tape:
        expand_weight_grad, reduce_weight_grad = feed_grads
        output_weight_grad, input_weight_grad = assemble_input(
            z, token, (near_p, near_q, other_p, other_q), far, (late, late_got)
        )
    else:
        block = block_of(total)
        block_mine, block_send = block[: z.half], block[z.half :]
        grad_got, block_got = swap(grad_send), swap(block_send)
        patch_outs = (patches_of(block_mine, block_got), patches_of(grad_mine, grad_got))
        tapes = jnp.stack(ready_all)
        other_tapes = swap(tapes)
        both = in_order(tapes, [other_tapes], "freq")
        both = pick(jnp.stack([both[:, np.arange(tm_count) ^ t] for t in range(tm_count)]), 0, place)
        part_r, part_e = both[:, :, :count_f], both[:, :, count_f : 2 * count_f]
        rows_r, rows_e = ff // (2 * clip_count * tm_count), feat // (clip_count * split)
        part_r = part_r.reshape(2, tm_count, feat // 128, rows_r, 128).swapaxes(2, 3)
        reduce_weight_grad = part_r.reshape(ff // clip_count, feat).astype(f32)
        part_e = part_e.reshape(2, FF_PARTS // 2, split, size // 128, rows_e, 128)
        part_e = part_e.transpose(2, 4, 1, 0, 3, 5)
        if not paired:
            part_e = part_e.swapaxes(2, 3).reshape(feat // clip_count, 2, clip_count, -1)
            part_e = part_e.swapaxes(1, 2)
        expand_weight_grad = part_e.reshape(feat // clip_count, ff).astype(f32)
        lanes = z.width // 128
        part_a = both[:, :, 2 * count_f :].reshape(2, tm_count // lanes, lanes, 4, 3, -1, 128)
        part_a = part_a.transpose(0, 1, 5, 3, 4, 2, 6)
        part_a = part_a.reshape(feat // clip_count, 4, 3, z.width).astype(f32)
        output_weight_grad = part_a[:, 0].reshape(-1, feat)
        input_weight_grad = part_a[:, 1:].swapaxes(1, 2).reshape(-1, 3 * feat)

    def leads_of(sent, got):
        mine, theirs = sent[z.half : z.half + LEADS], got[z.half : z.half + LEADS]
        first = jnp.where(core == 0, mine, theirs)
        second = jnp.where(core == 0, theirs, mine)
        return jnp.stack([first, second], 0)

    return (
        patch_outs[0],
        leads_of(block_send, block_got),
        patch_outs[1],
        leads_of(grad_send, grad_got),
        input_weight_grad,
        input_bias_grad,
        output_weight_grad,
        output_bias_grad,
        gain_one_grad,
        shift_one_grad,
        gain_two_grad,
        shift_two_grad,
        expand_weight_grad,
        expand_bias_grad,
        reduce_weight_grad,
        reduce_bias_grad,
    )


def solution(mesh):
    rows = P("freq", "tm", "clip", None)
    lead = P("clip", None, None)
    in_specs = (rows, lead, P("clip")) + (P(),) * 12 + (rows, lead)
    matrix, vector = P("clip", None), P("clip")
    out_specs = (rows, lead, rows, lead) + (matrix, vector) * 2 + (vector,) * 4 + (matrix, vector) * 2
    return jax.shard_map(
        per_device, mesh=mesh, in_specs=in_specs, out_specs=out_specs, check_vma=False
    )
```

```python
import functools
import math

import jax
import jax.numpy as jnp
import numpy as np
from jax import lax
from jax.experimental import pallas as pl
from jax.experimental.pallas import tpu as pltpu
from jax.sharding import PartitionSpec as P

HEADS = 12
EPSILON = 1e-06
NEG_FILL = -1e30
MAX_LENGTH = 101
LEADS = 2
LEAD_ROWS = 16
BLOCK_COLS = 8
GROUP = 4
FF_PARTS = 8
bf16 = jnp.bfloat16
f32 = jnp.float32


def mm(a, b):
    return lax.dot_general(a, b, (((1,), (0,)), ((), ())), preferred_element_type=f32)


def mm_nt(a, b):
    return lax.dot_general(a, b, (((1,), (1,)), ((), ())), preferred_element_type=f32)


def standardize(rows):
    center = rows - jnp.mean(rows, -1, keepdims=True)
    scale_inv = lax.rsqrt(jnp.mean(center * center, -1, keepdims=True) + EPSILON)
    return center * scale_inv, scale_inv


def norm_backward(grad_out, gain_row, normed, scale_inv):
    scaled = grad_out * gain_row
    return scale_inv * (
        scaled
        - jnp.mean(scaled, -1, keepdims=True)
        - normed * jnp.mean(scaled * normed, -1, keepdims=True)
    )


def head_mask(head, width, head_width):
    lane_head = lax.broadcasted_iota(jnp.int32, (1, width), 1) // head_width
    return (lane_head == head).astype(f32)


class Sizes:
    def __init__(self, patches_shape, tm_count, clip_count):
        fr_local, tc_local, clips, feat = patches_shape
        self.fr, self.tc, self.clips, self.feat = fr_local, tc_local, clips, feat
        self.tm, self.clip = tm_count, clip_count
        self.tape = clip_count == 4 and tm_count == 4
        self.tape_rows = 3 * feat * 2 // (2 * clip_count * tm_count)
        self.blocks = tc_local // BLOCK_COLS
        self.half_block = fr_local * BLOCK_COLS
        self.block = 2 * self.half_block
        self.half = self.blocks * self.half_block
        self.rows = 2 * self.half
        self.query_rows = self.rows + LEAD_ROWS
        self.key_blocks = -(-MAX_LENGTH // BLOCK_COLS)
        self.keys = LEAD_ROWS + self.key_blocks * self.block
        self.head_width = feat // HEADS
        self.width = GROUP * self.head_width
        self.steps = HEADS // GROUP
        self.lanes = GROUP * self.rows + 128


def call(kernel, room, in_specs, out_specs, out_shape, scratch, args, info, flops, moved, aliases={}):
    return pl.pallas_call(
        kernel,
        out_shape=out_shape,
        in_specs=[pl.BlockSpec(memory_space=pltpu.SMEM), *in_specs],
        out_specs=out_specs,
        scratch_shapes=scratch,
        input_output_aliases=aliases,
        compiler_params=pltpu.CompilerParams(vmem_limit_bytes=room * 1024 * 1024),
        cost_estimate=pl.CostEstimate(flops=flops, bytes_accessed=moved, transcendentals=0),
    )(info, *args)


def in_vmem(x):
    return pltpu.with_memory_space_constraint(x, pltpu.VMEM)


def in_hbm(x):
    return pltpu.with_memory_space_constraint(x, pltpu.HBM)


def whole(shape):
    return pl.BlockSpec(memory_space=pltpu.VMEM)


def chunks_of(z):
    full = z.lanes // 256
    spans = [(c * 256, 256) for c in range(full)]
    if z.lanes % 256:
        spans.append((full * 256, z.lanes % 256))
    return spans


def spread_heads(z, rows, out_ref):
    for head in range(GROUP):
        mask = head_mask(head, z.width, z.head_width)
        part = (rows * mask).astype(bf16)
        out_ref[head * z.rows : (head + 1) * z.rows, :] = part[: z.rows]
        at = GROUP * z.rows + head * LEAD_ROWS
        out_ref[at : at + LEAD_ROWS, :] = part[z.rows :]
    at = GROUP * (z.rows + LEAD_ROWS)
    out_ref[at:, :] = jnp.zeros((z.lanes - at, z.width), bf16)


def join_heads(z, spread):
    patch_part, lead_part = None, None
    for head in range(GROUP):
        mask = head_mask(head, z.width, z.head_width)
        at = GROUP * z.rows + head * LEAD_ROWS
        one = spread[head * z.rows : (head + 1) * z.rows] * mask
        two = spread[at : at + LEAD_ROWS] * mask
        patch_part = one if patch_part is None else patch_part + one
        lead_part = two if lead_part is None else lead_part + two
    return jnp.concatenate([patch_part, lead_part], 0)


class Copies:
    def __init__(self, sems):
        self.sems, self.going = sems, {}

    def start(self, name, source, to):
        copy = pltpu.make_async_copy(source, to, self.sems.at[len(self.going)])
        copy.start()
        self.going[name] = copy

    def wait(self, *names):
        for name in names:
            self.going[name].wait()


def attend_kernel(z, info, *refs):
    refs = list(refs)
    take = lambda n: [refs.pop(0) for _ in range(n)]
    pieces = take(2 * z.tm)
    lead, weight, bias_q, bias_v, gain, shift, live, wo_in, bo, gain_two, shift_two = take(11)
    low_out, inv_out, uq, unit_out, scale_out, low_two = take(6)
    q_out, k_out, v_out, mixed_out, hk_t_out, hq_t_out, p_out, uk_out, sum_out = take(9)
    spread, total, hk, hq, uk, w, p, q_all, k_all, v_all, mixed_all, hk_t, hq_t, first, wo, sems = take(16)
    me = info[0]
    copies = Copies(sems)
    span = lambda part, i: slice((part * z.steps + i) * z.width, (part * z.steps + i + 1) * z.width)
    copies.start("w", weight, w)
    copies.start("wo", wo_in, wo)
    gain_row, shift_row = gain[...], shift[...]

    def hidden(rows):
        unit, _ = standardize(rows.astype(f32))
        return unit.astype(bf16), (unit * gain_row + shift_row).astype(bf16)

    unit, low = hidden(lead[...])
    uk[0:LEAD_ROWS, :] = unit
    hk[0:LEAD_ROWS, :] = low
    hq[z.rows :, :] = low
    uq[z.rows :, :] = unit
    hb = z.half_block
    for k in range(z.tm):
        source = jnp.bitwise_xor(me, k)
        for half in range(2):
            unit, low = hidden(pieces[2 * k + half][...])
            if k == 0:
                hq[half * z.half : (half + 1) * z.half, :] = low
                uq[half * z.half : (half + 1) * z.half, :] = unit
            for b in range(z.blocks):
                at = LEAD_ROWS + (source * z.blocks + b) * z.block + half * hb
                at = pl.multiple_of(at, 16)
                uk[pl.ds(at, hb), :] = unit[b * hb : (b + 1) * hb]
                hk[pl.ds(at, hb), :] = low[b * hb : (b + 1) * hb]
    copies.start("uk", uk.at[0 : z.keys, :], uk_out)
    hk_all, hq_all = hk[0 : z.keys, :], hq[...]
    hk_t[...] = jnp.transpose(hk_all)
    hq_t[...] = jnp.transpose(hq_all)
    copies.start("hk_t", hk_t, hk_t_out)
    copies.start("hq_t", hq_t, hq_t_out)
    copies.wait("w")
    outs = ((q_all, q_out), (k_all, k_out), (v_all, v_out), (mixed_all, mixed_out))

    def group_copies(i):
        pairs = [(source.at[i], to.at[i]) for source, to in outs] + [(p.at[i % 2], p_out.at[i])]
        return [
            pltpu.make_async_copy(source, to, sems.at[8 + i * len(pairs) + n])
            for n, (source, to) in enumerate(pairs)
        ]

    def group(i, carry):
        columns = lambda part: pl.ds(pl.multiple_of((part * z.steps + i) * z.width, z.width), z.width)
        slot = i % 2
        q_copy, k_copy, v_copy, mixed_copy, p_copy = group_copies(i)

        @pl.when(i >= 2)
        def _():
            group_copies(i - 2)[-1].wait()

        q = (mm(hq[...], w[:, columns(0)]) + bias_q[:, columns(0)]).astype(bf16)
        q_all[i] = q
        spread_heads(z, q.astype(f32) * (z.head_width**-0.5), spread)
        k = mm(hk[0 : z.keys, :], w[:, columns(1)]).astype(bf16)
        k_all[i] = k
        v = (mm(hk[0 : z.keys, :], w[:, columns(2)]) + bias_v[:, columns(0)]).astype(bf16)
        v_all[i] = v
        q_copy.start()
        k_copy.start()
        v_copy.start()
        for at, size in chunks_of(z):
            scores = mm_nt(k, spread[at : at + size, :])
            scores = scores + jnp.concatenate([live[...]] * (size // 128), 1)
            peak = jnp.max(scores, 0, keepdims=True)
            weights = jnp.exp(scores - peak)
            total[i, 0:1, at : at + size] = jnp.sum(weights, 0, keepdims=True)
            p[slot, :, at : at + size] = weights.astype(bf16)
        p_copy.start()
        inverse = 1.0 / total[i, 0:1, :]
        inv_out[i] = jnp.broadcast_to(inverse, (8, z.lanes))
        mixed = mm(jnp.transpose(v), p[slot]) * inverse
        mixed = join_heads(z, jnp.transpose(mixed))
        mixed_all[i] = mixed
        mixed_copy.start()
        low_out[:, columns(0)] = mixed.astype(bf16)
        return carry

    lax.fori_loop(0, z.steps, group, 0)
    copies.wait("wo")
    rows = jnp.concatenate([pieces[0][...], pieces[1][...], lead[...]], 0).astype(f32)
    rows = rows + mm(low_out[...], wo[...]) + bo[...]
    first[...] = rows
    copies.start("sum", first, sum_out)
    normed, scale_inv = standardize(rows)
    unit_out[...] = normed
    scale_out[...] = jnp.broadcast_to(scale_inv, scale_out.shape)
    low_two[...] = (normed * gain_two[...] + shift_two[...]).astype(bf16)
    for i in range(z.steps):
        *near, p_copy = group_copies(i)
        for copy in near:
            copy.wait()
        if i >= z.steps - 2:
            p_copy.wait()
    copies.wait("uk", "hk_t", "hq_t", "sum")


def attend(z, me_info, pieces, lead, weight, bias_q, bias_v, gain, shift, live, wo, *second):
    feat, width, nk, nq, nl = z.feat, z.width, z.keys, z.query_rows, z.lanes
    there = pl.BlockSpec(memory_space=pl.ANY)
    in_specs = [whole((z.half, feat))] * (2 * z.tm) + [whole((LEAD_ROWS, feat)), there]
    in_specs += [whole((1, feat))] * 4 + [whole((nk, 128)), there] + [whole(None)] * 3
    shapes = [((nq, feat), bf16), ((z.steps, 8, nl), f32), ((nq, feat), bf16)]
    shapes += [((nq, feat), f32), ((nq, 128), f32), ((nq, feat), bf16)]
    heads = lambda rows, kind: ((z.steps, rows, width), kind)
    far = [heads(nq, bf16), heads(nk, bf16), heads(nk, bf16), heads(nq, f32)]
    far += [((feat, nk), bf16), ((feat, nq), bf16), ((z.steps, nk, nl), bf16), ((nk, feat), bf16)]
    far.append(((nq, feat), f32))
    return call(
        functools.partial(attend_kernel, z),
        42,
        in_specs,
        [whole(None)] * 6 + [there] * 9,
        [jax.ShapeDtypeStruct(*one) for one in shapes] + [pltpu.HBM(*one) for one in far],
        [
            pltpu.VMEM((nl, width), bf16),
            pltpu.VMEM((z.steps, 8, nl), f32),
            pltpu.VMEM((LEAD_ROWS + z.tm * z.rows, feat), bf16),
            pltpu.VMEM((nq, feat), bf16),
            pltpu.VMEM((LEAD_ROWS + z.tm * z.rows, feat), bf16),
            pltpu.VMEM((feat, 3 * feat), bf16),
            pltpu.VMEM((2, nk, nl), bf16),
            *[pltpu.VMEM(*one) for one in far[:6]],
            pltpu.VMEM((nq, feat), f32),
            pltpu.VMEM((feat, feat), bf16),
            pltpu.SemaphoreType.DMA((32,)),
        ],
        (*pieces, lead, in_hbm(weight), bias_q, bias_v, gain, shift, live, in_hbm(wo), *second),
        me_info,
        2 * feat * feat * (nq + 2 * nk) + 4 * z.steps * nk * nl * width,
        z.steps * nk * nl * 2,
    )


def feed_kernel(z, paired, info, *refs):
    refs = list(refs)
    take = lambda n: [refs.pop(0) for _ in range(n)]
    low, low_other, cot, cot_other, be, we_in, wr_in = take(7)
    dbe, acc, acc_other, grad, grad_other = take(5)
    outs = take(4 if z.tape else 2)
    we, wr, dwr, dwe, low_t, cot_all, acc_sum, grad_sum, sems = take(9)
    steps = FF_PARTS // 2
    size = we.shape[2] // 2
    nq = z.query_rows
    core = info[1]
    col, line = info[0] % 2, info[0] // 2
    place = lambda i: jnp.bitwise_xor(i, 2 * (1 - line)) if z.tape else i
    at = lambda i: pl.multiple_of(
        (2 * place(i) + core if paired else steps * core + i) * size, size
    )
    copies = Copies(sems)
    names = []

    def leave(name, source, to):
        copies.start(name, source, to)
        names.append(name)

    for i in range(steps):
        pair, span = i // 2, slice(i % 2 * size, (i % 2 + 1) * size)
        copies.start(f"we{i}", we_in.at[:, pl.ds(at(i), size)], we.at[pair, :, span])
        copies.start(f"wr{i}", wr_in.at[pl.ds(at(i), size), :], wr.at[pair, span, :])
    cot_all[:nq, :] = cot[...]
    cot_all[nq:, :] = cot_other[...]
    low_all = jnp.concatenate([low[...], low_other[...]], 0)
    low_t[...] = jnp.transpose(low_all)
    for pair in range(steps // 2):
        both = (2 * pair, 2 * pair + 1)
        copies.wait(*[f"w{which}{i}" for i in both for which in "er"])
        cot_low = cot_all[...]
        expand, reduce = we[pair], wr[pair]
        bias = jnp.concatenate([be[:, pl.ds(at(i), size)] for i in both], 1)
        expanded = mm(low_all, expand) + bias
        grad_activated = mm_nt(cot_low, reduce)
        cdf = 0.5 * (1.0 + lax.erf(expanded * math.sqrt(0.5)))
        pdf = jnp.exp(-0.5 * expanded * expanded) * (1.0 / math.sqrt(2.0 * math.pi))
        activated = (expanded * cdf).astype(bf16)
        reduce_grad = mm(jnp.transpose(activated), cot_low).astype(bf16)
        for n, i in enumerate(both):
            if z.tape:
                part = size // z.tm
                for t in range(z.tm):
                    for lane in range(z.feat // 128):
                        rows = slice(n * size + t * part, n * size + (t + 1) * part)
                        dwr[i, t, lane * part : (lane + 1) * part, :] = reduce_grad[
                            rows, lane * 128 : (lane + 1) * 128
                        ]
                out_r, own_r, out_e, own_e = outs
                for y in range(2):
                    leave(f"out_r{i}{y}", dwr.at[i, 2 * y + 1 - col], out_r.at[y, i])
                    leave(f"own_r{i}{y}", dwr.at[i, 2 * y + col], own_r.at[y, i])
            else:
                dwr[i] = reduce_grad[n * size : (n + 1) * size]
                leave(f"dwr{i}", dwr.at[i], outs[0].at[i])
        grad_expanded = (grad_activated * (cdf + expanded * pdf)).astype(bf16)
        expand_grad = mm(low_t[...], grad_expanded).astype(bf16)
        bias_grad = jnp.sum(grad_expanded.astype(f32), 0, keepdims=True)
        for n, i in enumerate(both):
            span = slice(n * size, (n + 1) * size)
            if z.tape:
                part = z.feat // z.clip
                for c in range(z.clip):
                    for lane in range(size // 128):
                        lanes = slice(n * size + lane * 128, n * size + (lane + 1) * 128)
                        dwe[i, c, lane * part : (lane + 1) * part, :] = expand_grad[
                            c * part : (c + 1) * part, lanes
                        ]
                    leave(f"e{i}{c}", dwe.at[i, c], (out_e, own_e)[pair].at[n, c])
            else:
                dwe[i] = expand_grad[:, span]
                leave(f"dwe{i}", dwe.at[i], outs[1].at[i])
            dbe[place(i)] = jnp.broadcast_to(bias_grad[:, span], dbe.shape[1:])
        acc_new, grad_new = mm(activated, reduce), mm_nt(grad_expanded, expand)
        if pair == 0:
            acc_sum[...] = acc_new
            grad_sum[...] = grad_new
        else:
            acc_new, grad_new = acc_sum[...] + acc_new, grad_sum[...] + grad_new
            acc[...] = acc_new[:nq]
            acc_other[...] = acc_new[nq:].astype(bf16)
            grad[...] = grad_new[:nq]
            grad_other[...] = grad_new[nq:].astype(bf16)
    copies.wait(*names)


def feed(z, info, paired, low, low_other, cot, cot_other, expand, expand_bias, reduce):
    feat, ff = expand.shape
    size = ff // FF_PARTS
    steps = FF_PARTS // 2
    nq = z.query_rows
    there, here = pl.BlockSpec(memory_space=pl.ANY), whole(None)
    if z.tape:
        shapes = [(z.tm, size * feat // (128 * z.tm), 128), (z.clip, size * feat // (128 * z.clip), 128)]
    else:
        shapes = [(size, feat), (feat, size)]
    shapes = [(steps, *shape) for shape in shapes]
    wide, narrow = ((nq, feat), f32), ((nq, feat), bf16)
    outs = [((steps, 8, size), f32), wide, narrow, wide, narrow]
    far = shapes
    if z.tape:
        far = [(2, 4, *shapes[0][2:])] * 4
    return call(
        functools.partial(feed_kernel, z, paired),
        44,
        [here] * 5 + [there] * 2,
        [here] * 5 + [there] * len(far),
        [jax.ShapeDtypeStruct(*one) for one in outs] + [pltpu.HBM(shape, bf16) for shape in far],
        [
            pltpu.VMEM((steps // 2, feat, 2 * size), bf16),
            pltpu.VMEM((steps // 2, 2 * size, feat), bf16),
            pltpu.VMEM(shapes[0], bf16),
            pltpu.VMEM(shapes[1], bf16),
            pltpu.VMEM((feat, 2 * nq), bf16),
            pltpu.VMEM((2 * nq, feat), bf16),
            pltpu.VMEM((2 * nq, feat), f32),
            pltpu.VMEM((2 * nq, feat), f32),
            pltpu.SemaphoreType.DMA((48,)),
        ],
        (low, low_other, cot, cot_other, expand_bias, in_hbm(expand), in_hbm(reduce)),
        info,
        6 * nq * feat * ff * 2,
        4 * feat * ff,
    )


def blend_back_kernel(z, info, *refs):
    refs = list(refs)
    take = lambda n: [refs.pop(0) for _ in range(n)]
    grad, grad_got, unit, inv, cot, mixed, gain = take(7)
    first_out, low_grad, send, keep, small, hold = take(6)
    rows_grad = cot[...].astype(f32)
    normed, hidden_grad = unit[...], grad[...] + grad_got[...].astype(f32)
    back = rows_grad + norm_backward(hidden_grad, gain[...], normed, inv[:, 0:1])
    first_out[...] = back
    back_low = back.astype(bf16)
    low_grad[...] = back_low
    dwo = mm(jnp.transpose(mixed[...]), back_low)
    for j in range(z.steps):
        block = dwo[:, j * z.width : (j + 1) * z.width]
        if z.tape:
            store_split(z, info[1], block, hold, send, keep, j)
        else:
            keep[j] = block.astype(bf16)
    small[...] = jnp.zeros_like(small)
    small[0:1, :] = jnp.sum(back_low.astype(f32), 0, keepdims=True)
    small[1:2, :] = jnp.sum(hidden_grad * normed, 0, keepdims=True)
    small[2:3, :] = jnp.sum(hidden_grad, 0, keepdims=True)
    small[3:4, :] = jnp.sum(rows_grad, 0, keepdims=True)


def blend_back(z, info, *args):
    feat, nq = z.feat, z.query_rows
    split = ((z.clip, z.tm, z.tape_rows, 128) if z.tape else (3, feat, z.width), bf16)
    shapes = [((nq, feat), f32), ((nq, feat), bf16), split, split, ((8, feat), f32)]
    return call(
        functools.partial(blend_back_kernel, z),
        20,
        [whole(None)] * len(args),
        [whole(None)] * len(shapes),
        [jax.ShapeDtypeStruct(*one) for one in shapes],
        [pltpu.VMEM((feat, z.width), f32)],
        args,
        info,
        2 * nq * feat * feat,
        nq * feat * 20,
    )


def store_split(z, core, value, hold, sent, kept, j):
    hold[...] = value
    half = z.feat // (2 * z.clip)
    part = half // 2
    for c in range(z.clip):
        for out, whose in ((kept, core), (sent, 1 - core)):
            for t in range(z.tm):
                at = pl.multiple_of((2 * c + whose) * half + (t // 2) * part, 16)
                lanes = slice((t % 2) * 128, (t % 2) * 128 + 128)
                out[c, t, j * part : (j + 1) * part, :] = hold[pl.ds(at, part), lanes].astype(bf16)


def plain_to_tape(z, blocks, core):
    lanes = z.width // 128
    x = blocks.reshape(3, z.clip, 2, z.tm // lanes, -1, lanes, 128)
    x = x.transpose(2, 1, 3, 5, 0, 4, 6).reshape(2, z.clip, z.tm, -1, 128)
    return pick(x, 0, 1 - core), pick(x, 0, core)


def attend_back_kernel(z, i, info, *refs):
    refs = list(refs)
    take = lambda n: [refs.pop(0) for _ in range(n)]
    ga, wo, inv, *far = take(10)
    span = slice(i * z.width, (i + 1) * z.width)
    sent, kept, db, kv_out, q_grad_out = take(5)
    q_spread, g_spread, ds, hold, q, k, v, mixed, hk_t, hq_t, p, sems = take(12)
    core = info[1]
    copies = Copies(sems)
    q_in, k_in, v_in, mixed_in, hk_t_in, hq_t_in, p_in = far
    for name, source, to in (
        ("q", q_in.at[i], q),
        ("mixed", mixed_in.at[i], mixed),
        ("v", v_in.at[i], v),
        ("p", p_in.at[i], p),
        ("k", k_in.at[i], k),
        ("hq_t", hq_t_in, hq_t),
        ("hk_t", hk_t_in, hk_t),
    ):
        copies.start(name, source, to)
    scale = z.head_width**-0.5

    grad = mm_nt(ga[...], wo[span, :]).astype(bf16).astype(f32)
    inverse = inv[i, 0:1, :]
    inverse_col = jnp.transpose(jnp.broadcast_to(inverse, (128, z.lanes)))[:, 0:1]
    copies.wait("q", "mixed")
    spread_heads(z, q[...].astype(f32) * scale, q_spread)
    product = grad * mixed[...]
    dots = []
    for head in range(GROUP):
        mask = head_mask(head, z.width, z.head_width)
        at = GROUP * z.rows + head * LEAD_ROWS
        part = grad * mask
        low = (part[: z.rows] * inverse_col[head * z.rows : (head + 1) * z.rows]).astype(bf16)
        g_spread[head * z.rows : (head + 1) * z.rows, :] = low
        low = (part[z.rows :] * inverse_col[at : at + LEAD_ROWS]).astype(bf16)
        g_spread[at : at + LEAD_ROWS, :] = low
        dots.append(jnp.sum(product * mask, 1, keepdims=True))
    end = GROUP * (z.rows + LEAD_ROWS)
    g_spread[end:, :] = jnp.zeros((z.lanes - end, z.width), bf16)
    dot_col = jnp.concatenate(
        [d[: z.rows] for d in dots]
        + [d[z.rows :] for d in dots]
        + [jnp.zeros((z.lanes - end, 1), f32)],
        0,
    )
    dot_row = jnp.transpose(jnp.broadcast_to(dot_col, (z.lanes, 128)))[0:1, :] * inverse
    copies.wait("v", "p")
    v_all = v[...]
    for at, size in chunks_of(z):
        grad_weights = mm_nt(v_all, g_spread[at : at + size, :])
        weights = p[:, at : at + size].astype(f32)
        ds[:, at : at + size] = (weights * (grad_weights - dot_row[:, at : at + size])).astype(bf16)
    ds_all = ds[...]
    copies.wait("k", "hq_t", "hk_t")
    k_all = k[...]
    grad_v = mm(p[...], g_spread[...])
    grad_k = mm(ds_all, q_spread[...])
    grad_q = mm(jnp.transpose(k_all), ds_all)
    grad_q = (join_heads(z, jnp.transpose(grad_q)) * scale).astype(bf16)
    grad_v = grad_v.astype(bf16)
    grad_k = grad_k.astype(bf16)
    db[...] = jnp.concatenate(
        [
            jnp.sum(grad_q.astype(f32), 0, keepdims=True),
            jnp.sum(grad_v.astype(f32), 0, keepdims=True),
            jnp.zeros((6, z.width), f32),
        ],
        0,
    )
    for j, grad in enumerate((mm(hq_t[...], grad_q), mm(hk_t[...], grad_k), mm(hk_t[...], grad_v))):
        if z.tape:
            store_split(z, core, grad, hold, sent, kept, j)
        else:
            kept[j] = grad.astype(bf16)
    kv_out[:, : z.width] = grad_k
    kv_out[:, z.width :] = grad_v
    q_grad_out[...] = grad_q


def keys_back_kernel(z, info, *refs):
    refs = list(refs)
    take = lambda n: [refs.pop(0) for _ in range(n)]
    uk_in, uq, weight_in, first, feed_small = take(5)
    db, grad_kv, grad_q = take(z.steps), take(z.steps), take(z.steps)
    own, small_out = take(2)
    sends = take(4 if z.tape else z.tm - 1)
    keys_acc, query_acc, small, uk, weight, sems = take(6)
    me = info[0]
    copies = Copies(sems)
    span = lambda part, i: slice((part * z.steps + i) * z.width, (part * z.steps + i + 1) * z.width)
    copies.start("w", weight_in, weight)
    copies.start("uk", uk_in, uk)
    column = lambda part, i: slice((part * z.steps + i) * z.width, (part * z.steps + i + 1) * z.width)
    copies.wait("w")
    query_grad, keys_grad = 0.0, 0.0
    for i in range(z.steps):
        query_grad += mm_nt(grad_q[i][...], weight[:, column(0, i)])
        keys_grad += mm_nt(grad_kv[i][:, : z.width], weight[:, column(1, i)])
        keys_grad += mm_nt(grad_kv[i][:, z.width :], weight[:, column(2, i)])
    keys_acc[...] = keys_grad
    query_acc[...] = query_grad
    copies.wait("uk")
    small[...] = jnp.zeros_like(small)
    for i in range(z.steps):
        small[0:2, i * z.width : (i + 1) * z.width] = db[i][0:2, :]
    small[2:3, :] = jnp.sum(keys_grad * uk[...].astype(f32), 0, keepdims=True) + jnp.sum(
        query_grad * uq[...].astype(f32), 0, keepdims=True
    )
    small[3:4, :] = jnp.sum(keys_grad, 0, keepdims=True) + jnp.sum(query_grad, 0, keepdims=True)
    small[4:12, :] = feed_small[...]
    if z.tape:
        for lane in range(z.feat // 128):
            small_out[lane * 16 : lane * 16 + 16, :] = small[
                :, lane * 128 : lane * 128 + 128
            ].astype(bf16)
    else:
        small_out[...] = small[...]
    lead = keys_acc[0:LEAD_ROWS, :] + query_acc[z.rows :, :]
    first_lead = first[z.rows :, :]
    high = first_lead.astype(bf16)
    rest = (first_lead - high.astype(f32)).astype(bf16)
    pair = lambda a: a[0:LEADS]
    packed = jnp.concatenate(
        [pair(lead), pair(high.astype(f32)), pair(rest.astype(f32)), jnp.zeros((10, z.feat), f32)], 0
    )
    small_high = small[...].astype(bf16)
    small_low = (small[...] - small_high.astype(f32)).astype(bf16)
    own[z.rows :, :] = packed
    packed = packed.astype(bf16)
    hb = z.half_block

    def chunk(k, half, out, at):
        source = jnp.bitwise_xor(me, k)
        for b in range(z.blocks):
            spot = source * z.blocks + b
            from_ = pl.multiple_of(
                LEAD_ROWS + jnp.minimum(spot, z.key_blocks - 1) * z.block + half * hb, 16
            )
            rows = keys_acc[pl.ds(from_, hb), :] * (spot < z.key_blocks).astype(f32)
            to = at + b * hb
            if k == 0:
                queries = half * z.half + b * hb
                rows = rows + query_acc[queries : queries + hb, :]
            out[to : to + hb, :] = rows.astype(out.dtype)

    chunk(0, 0, own, 0)
    chunk(0, 1, own, z.half)
    if z.tape:
        along_x, along_y, mid_x, mid_y = sends
        chunk(1, 0, along_x, 0)
        chunk(3, 0, along_x, z.half)
        along_x[z.rows :, :] = packed
        chunk(2, 1, along_y, 0)
        chunk(3, 1, along_y, z.half)
        chunk(2, 0, mid_x, 0)
        chunk(1, 1, mid_y, 0)
    else:
        for k, one in enumerate(sends, start=1):
            chunk(k, 0, one, 0)
            chunk(k, 1, one, z.half)
            one[z.rows :, :] = packed


def attend_back(z, info, i, ga, wo, saved):
    inv, far = saved[1], saved[6:13]
    feat, width, nk, nq, nl = z.feat, z.width, z.keys, z.query_rows, z.lanes
    in_specs = [whole(None)] * 3 + [pl.BlockSpec(memory_space=pl.ANY)] * 7
    if z.tape:
        part = (z.clip, z.tm, z.tape_rows, 128)
    else:
        part = (3, feat, width)
    sent, kept, *rest = call(
        functools.partial(attend_back_kernel, z, i),
        24,
        in_specs,
        [whole(part), whole(part), whole((8, width)), whole((nk, 2 * width)), whole((nq, width))],
        [
            jax.ShapeDtypeStruct(part, bf16),
            jax.ShapeDtypeStruct(part, bf16),
            jax.ShapeDtypeStruct((8, width), f32),
            jax.ShapeDtypeStruct((nk, 2 * width), bf16),
            jax.ShapeDtypeStruct((nq, width), bf16),
        ],
        [
            pltpu.VMEM((nl, width), bf16),
            pltpu.VMEM((nl, width), bf16),
            pltpu.VMEM((nk, nl), bf16),
            pltpu.VMEM((feat, width), f32),
            pltpu.VMEM((nq, width), bf16),
            pltpu.VMEM((nk, width), bf16),
            pltpu.VMEM((nk, width), bf16),
            pltpu.VMEM((nq, width), f32),
            pltpu.VMEM((feat, nk), bf16),
            pltpu.VMEM((feat, nq), bf16),
            pltpu.VMEM((nk, nl), bf16),
            pltpu.SemaphoreType.DMA((8,)),
        ],
        [ga, wo, inv, *[in_hbm(one) for one in far]],
        info,
        1000,
        1000,
    )
    if not z.tape:
        sent, kept = plain_to_tape(z, kept, info[1])
    return sent, kept, rest


def keys_back(z, info, saved, weight, first_lead, feed_small, steps):
    feat, width, nk, nq = z.feat, z.width, z.keys, z.query_rows
    uq, uk = saved[2], saved[13]
    there = pl.BlockSpec(memory_space=pl.ANY)
    in_specs = [there, whole((nq, feat)), there]
    in_specs += [whole(None)]
    in_specs += [whole((8, feat))]
    in_specs += [whole((8, width))] * z.steps
    in_specs += [whole((nk, 2 * width))] * z.steps + [whole((nq, width))] * z.steps
    if z.tape:
        sends = [(nq, feat), (z.rows, feat), (z.half, feat), (z.half, feat)]
    else:
        sends = [(nq, feat)] * (z.tm - 1)
    small = (16 * feat // 128, 128) if z.tape else (16, feat)
    return call(
        functools.partial(keys_back_kernel, z),
        24,
        in_specs,
        [whole((nq, feat)), whole(small)] + [whole(shape) for shape in sends],
        [
            jax.ShapeDtypeStruct((nq, feat), f32),
            jax.ShapeDtypeStruct(small, bf16 if z.tape else f32),
        ]
        + [jax.ShapeDtypeStruct(shape, bf16) for shape in sends],
        [
            pltpu.VMEM((nk, feat), f32),
            pltpu.VMEM((nq, feat), f32),
            pltpu.VMEM((16, feat), f32),
            pltpu.VMEM((nk, feat), bf16),
            pltpu.VMEM(weight.shape, bf16),
            pltpu.SemaphoreType.DMA((16,)),
        ],
        (in_hbm(uk), uq, in_hbm(weight), first_lead, feed_small)
        + tuple(step[j] for j in range(3) for step in steps),
        info,
        4 * feat * feat * (nq + 2 * nk),
        nk * feat * 4,
    )


def finish_kernel(z, info, *refs):
    *received, rows, gain, grad_first, out_mine, out_send = refs[1:]
    own = refs[0]
    mine = own[z.rows :].astype(bf16).astype(f32)
    if z.tape:
        got_x, got_y, got_xy, got_yx = (one[...].astype(f32) for one in received)
        first = own[: z.half] + got_x[: z.half] + got_xy[: z.half]
        second = own[z.half : z.rows] + got_y[: z.half] + got_yx
        lead = (mine + got_x[z.rows :]).astype(bf16).astype(f32) + got_xy[z.half :]
        total = jnp.concatenate([first, second, lead], 0)
    else:
        terms = [one[...].astype(f32) for one in received]
        leads = [mine] + [one[z.rows :] for one in terms]
        while len(leads) > 1:
            leads = [a + b for a, b in zip(leads[::2], leads[1::2])]
        total = jnp.concatenate([own[: z.rows] + sum(t[: z.rows] for t in terms), leads[0]], 0)
    normed, scale_inv = standardize(rows[...].astype(f32))
    back = norm_backward(total, gain[...], normed, scale_inv)
    rows_grad = (back[: z.rows] + grad_first[0 : z.rows, :]).astype(bf16)
    out_mine[...] = rows_grad[: z.half]
    out_send[0 : z.half, :] = rows_grad[z.half :]
    lead = total[z.rows :]
    lead_first = lead[LEADS : 2 * LEADS] + lead[2 * LEADS : 3 * LEADS]
    out_send[z.half :, :] = jnp.concatenate(
        [back[z.rows : z.rows + LEADS] + lead_first, jnp.zeros((LEAD_ROWS - LEADS, z.feat), f32)], 0
    ).astype(bf16)


def finish(z, info, own, received, rows, gain, grad_first):
    feat, nq = z.feat, z.query_rows
    return call(
        functools.partial(finish_kernel, z),
        16,
        [whole(one.shape) for one in (own, *received)]
        + [whole((nq, feat)), whole((1, feat)), whole((nq, feat))],
        [whole((z.half, feat)), whole((nq - z.half, feat))],
        [
            jax.ShapeDtypeStruct((z.half, feat), bf16),
            jax.ShapeDtypeStruct((nq - z.half, feat), bf16),
        ],
        [],
        (own, *received, rows, gain, grad_first),
        info,
        nq * feat * 20,
        nq * feat * 20,
    )


def place_blocks(z, t, whose, tape, row, out, lane_at):
    half = z.feat // (2 * z.clip)
    part = half // 2
    at = pl.multiple_of(whose * half + (t // 2) * part, 16)
    for j in range(3):
        block = tape[row + j * part : row + (j + 1) * part, :].astype(f32)
        lane = pl.multiple_of(lane_at(j) + (t % 2) * 128, 128)
        out[pl.ds(at, part), pl.ds(lane, 128)] = block


def assemble_feed_kernel(z, ff, far, info, *refs):
    me, core = info[0], info[1]
    expand_out, reduce_out, expand, reduce, sems = refs[-5:]
    p_mine, q_mine, p_other, q_other = refs[:4]
    size = ff // FF_PARTS
    step = size * z.feat // (128 * z.tm) + z.tape_rows
    part_r, part_e = size // z.tm, z.feat // z.clip
    copies = Copies(sems)
    names = []
    for whose, p, q in ((core, p_mine, q_mine), (1 - core, p_other, q_other)):
        for j, (k_p, k_q) in enumerate(((2, 1), (3, 3)) if far else ((0, 0), (1, 2))):
            n = len(names)
            for lane in range(z.feat // 128):
                block = p[j * step + lane * part_r : j * step + (lane + 1) * part_r, :]
                reduce[n, :, lane * 128 : (lane + 1) * 128] = block.astype(f32)
            at = pl.multiple_of(whose * size + jnp.bitwise_xor(me, k_p) * part_r, 16)
            copies.start((n, 0), reduce.at[n], reduce_out.at[pl.ds(at, part_r), :])
            for lane in range(size // 128):
                block = q[j * step + lane * part_e : j * step + (lane + 1) * part_e, :]
                expand[n, :, lane * 128 : (lane + 1) * 128] = block.astype(f32)
            at = pl.multiple_of((2 * jnp.bitwise_xor(me, k_q) + whose) * size, 128)
            copies.start((n, 1), expand.at[n], expand_out.at[:, pl.ds(at, size)])
            names.append(n)
    copies.wait(*[(n, i) for n in names for i in range(2)])


def assemble_feed(z, info, ff, far, tapes, before):
    rows, size = z.feat // z.clip, ff // FF_PARTS
    there = pl.BlockSpec(memory_space=pl.ANY)
    return call(
        functools.partial(assemble_feed_kernel, z, ff, far),
        16,
        [whole(None)] * 4 + [there] * len(before),
        [there] * 2,
        [pltpu.HBM((rows, ff), f32), pltpu.HBM((ff // z.clip, z.feat), f32)],
        [
            pltpu.VMEM((4, rows, size), f32),
            pltpu.VMEM((4, size // z.tm, z.feat), f32),
            pltpu.SemaphoreType.DMA((8,)),
        ],
        (*tapes, *before),
        info,
        1000,
        24 * tapes[0].size,
        {5: 0, 6: 1} if before else {},
    )


def assemble_input_kernel(z, step, info, *refs):
    me, core = info[0], info[1]
    near, far, (late, late_other), (output_out, input_out) = refs[:4], refs[4:8], refs[8:10], refs[10:]
    last = step - z.tape_rows
    for whose, m, late_tape in ((core, 0, late), (1 - core, 2, late_other)):
        for k in range(z.tm):
            t = jnp.bitwise_xor(me, k)
            tape, at = (near[m], far[m])[k // 2], k % 2 * step + last
            place_blocks(z, t, whose, tape, at, output_out, lambda j: j * z.width)
            tape, at = (near[m + 1], far[m + 1])[k % 2], k // 2 * step + last
            place_blocks(z, t, whose, tape, at, input_out, lambda j: j * z.feat)
            for i in (1, 2):
                row = (2 * k + i - 1) * z.tape_rows
                lane_at = lambda j: j * z.feat + i * z.width
                place_blocks(z, t, whose, late_tape, row, input_out, lane_at)


def assemble_input(z, info, near, far, late):
    rows = z.feat // z.clip
    shapes = [(rows, z.feat), (rows, 3 * z.feat)]
    return call(
        functools.partial(assemble_input_kernel, z, near[0].shape[0] // 2),
        20,
        [whole(None)] * 10,
        [whole(None)] * 2,
        [jax.ShapeDtypeStruct(shape, f32) for shape in shapes],
        [],
        (*near, *far, *late),
        info,
        1000,
        16 * late[0].size,
    )


def small_kernel(z, info, mine, other, *outs):
    total = mine[...].astype(f32) + other[...].astype(f32)
    lanes = z.feat // 128

    def row(i):
        return jnp.concatenate([total[n * 16 + i : n * 16 + i + 1, :] for n in range(lanes)], 1)

    rows = [row(i) for i in range(12)]
    biases = jnp.concatenate(rows[:2], 1)
    count = z.feat // z.clip
    for c in range(z.clip):

        @pl.when(info[2] == c)
        def _(c=c):
            outs[0][...] = biases[0, 2 * count * c : 2 * count * (c + 1)]
            for i in range(2, 8):
                outs[i - 1][...] = rows[i][0, count * c : count * (c + 1)]
            outs[7][...] = rows[8 + c][0, :]


def small_grads(z, info, mine, other):
    count = z.feat // z.clip
    sizes = [2 * count] + [count] * 6 + [4 * count]
    return call(
        functools.partial(small_kernel, z),
        4,
        [whole(None)] * 2,
        [whole(None)] * 8,
        [jax.ShapeDtypeStruct((size,), f32) for size in sizes],
        [],
        (mine, other),
        info,
        1000,
        1000,
    )


def flip(count, k):
    return [(i, i ^ k) for i in range(count)]


def bit_of(index, bit):
    return (index >> bit) & 1


def bits_of(count):
    return count.bit_length() - 1


def pick(x, dim, index):
    return lax.dynamic_index_in_dim(x, index, dim, keepdims=False)


def add(kept, got):
    return (kept.astype(f32) + got.astype(f32)).astype(bf16)


def by_bits(x, dim, count):
    return x.reshape(x.shape[:dim] + (2,) * bits_of(count) + x.shape[dim + 1 :])


def halves(x, dim, axis, bit):
    mine = bit_of(lax.axis_index(axis), bit)
    return pick(x, dim, 1 - mine), pick(x, dim, mine)


def across(x, axis, bit):
    return lax.ppermute(x, axis, flip(lax.axis_size(axis), 1 << bit))


def scatter(x, dim, axis, bits):
    for bit in bits:
        sent, kept = halves(x, dim, axis, bit)
        x = add(kept, across(sent, axis, bit))
    return x


def scatter_up(x, dim, axis, bits):
    for bit in bits:
        at = dim + bits_of(lax.axis_size(axis)) - 1 - bit
        sent, kept = halves(x, at, axis, bit)
        x = add(kept, across(sent, axis, bit))
    return x


def peers(x, dim, axis):
    me = lax.axis_index(axis)
    return [pick(x, dim, me ^ k) for k in range(1, lax.axis_size(axis))]


def to_peers(sent, axis):
    count = lax.axis_size(axis)
    return [lax.ppermute(one, axis, flip(count, k)) for k, one in enumerate(sent, start=1)]


def add_all(own, got):
    total = own.astype(f32)
    for one in got:
        total = total + one.astype(f32)
    return total.astype(bf16)


def in_order(x, got, axis):
    me = lax.axis_index(axis)
    out = jnp.zeros((1 + len(got),) + x.shape, x.dtype)
    for k, one in enumerate([x, *got]):
        out = lax.dynamic_update_index_in_dim(out, one, me ^ k, 0)
    return out


def tie(*values):
    return lax.optimization_barrier(values)


def per_device(
    patches,
    lead_tokens,
    lengths,
    input_weight,
    input_bias,
    output_weight,
    output_bias,
    first_gain,
    first_shift,
    second_gain,
    second_shift,
    expand_weight,
    expand_bias,
    reduce_weight,
    reduce_bias,
    cot_patches,
    cot_lead,
):
    tm_count = lax.axis_size("tm")
    clip_count = lax.axis_size("clip")
    z = Sizes(patches.shape, tm_count, clip_count)
    feat, ff = expand_weight.shape
    core, place = lax.axis_index("freq"), lax.axis_index("tm")
    info = jnp.stack([place, core, lax.axis_index("clip")]).astype(jnp.int32)
    row = lambda vector: vector.astype(f32)[None, :]

    def by_clip(array):
        parts = array.reshape(z.fr, z.blocks, BLOCK_COLS, z.clips, feat)
        parts = parts.transpose(3, 1, 0, 2, 4).reshape(z.clips, z.half, feat)
        return (
            lax.dynamic_index_in_dim(parts, core, 0, keepdims=False),
            lax.dynamic_index_in_dim(parts, 1 - core, 0, keepdims=False),
        )

    def lead_of(array):
        mine = lax.dynamic_index_in_dim(array, core, 0, keepdims=False)
        return jnp.pad(mine, ((0, LEAD_ROWS - LEADS), (0, 0)))

    own_half, other_half = by_clip(patches)
    pieces = []
    for k in range(tm_count):
        pieces.append(lax.ppermute(own_half, "tm", flip(tm_count, k)) if k else own_half)
        pieces.append(
            lax.ppermute(other_half, ("freq", "tm"), flip(2 * tm_count, tm_count | k))
        )
    lead = lead_of(lead_tokens)
    rows = jnp.concatenate([pieces[0], pieces[1], lead], 0)
    own_cot, other_cot = by_clip(cot_patches)
    lead_cot = lead_of(cot_lead) * (place == 0).astype(bf16)
    cot = jnp.concatenate([own_cot, lax.ppermute(other_cot, "freq", flip(2, 1)), lead_cot], 0)
    cot_got = lax.ppermute(cot, "freq", flip(2, 1))

    length = lax.dynamic_index_in_dim(lengths, core, 0, keepdims=False)
    spots = np.arange(z.keys) - LEAD_ROWS
    columns = np.where(spots < 0, 1 << 20, spots // z.block * BLOCK_COLS + spots % BLOCK_COLS)
    columns[:LEADS] = -1
    live = jnp.where(jnp.asarray(columns, jnp.int32)[:, None] < length, 0.0, NEG_FILL)
    live = jnp.broadcast_to(live.astype(f32), (z.keys, 128))

    saved = attend(
        z,
        info,
        pieces,
        lead,
        input_weight,
        row(input_bias[:feat]),
        row(input_bias[feat:]),
        row(first_gain),
        row(first_shift),
        live,
        output_weight,
        row(output_bias),
        row(second_gain),
        row(second_shift),
    )
    mixed_low = saved[0]
    paired = clip_count == FF_PARTS // 2
    if not paired:
        share = (clip_count, 2, ff // (2 * clip_count))
        expand_weight = expand_weight.reshape(feat, *share).swapaxes(1, 2).reshape(feat, ff)
        expand_bias = expand_bias.reshape(share).swapaxes(0, 1).reshape(ff)
        reduce_weight = reduce_weight.reshape(*share, feat).swapaxes(0, 1).reshape(ff, feat)
    gain_two = row(second_gain)
    swap = lambda x: across(x, "freq", 0)
    size = ff // FF_PARTS
    half = clip_count // 2
    tm_bits, clip_bits = bits_of(tm_count), bits_of(clip_count)
    low_bits, high_bits = list(range(tm_bits)), list(range(tm_bits))[::-1]
    split = max(1, tm_count // (FF_PARTS // 2))

    unit, inv, low, total = saved[3], saved[4], saved[5], saved[14]
    feed_bias, acc, acc_send, grad, grad_send, *sums = feed(
        z, info, paired, low, swap(low), cot, cot_got, expand_weight, row(expand_bias), reduce_weight
    )
    if z.tape:
        out_r, own_r, out_e, own_e = sums
    else:
        sum_r, sum_e = sums
        rows_r, rows_e = ff // (2 * clip_count * tm_count), feat // (clip_count * split)
        sum_r = sum_r.reshape(clip_count, tm_count, rows_r, feat // 128, 128).swapaxes(2, 3)
        sum_e = sum_e.reshape(-1, clip_count, split, rows_e, size // 128, 128)
        sum_e = sum_e.transpose(0, 2, 1, 4, 3, 5)
        sum_r = sum_r.reshape(clip_count, tm_count, -1, 128)
        sum_e = sum_e.reshape(tm_count, clip_count, -1, 128).swapaxes(0, 1)
        out_r, own_r = halves(by_bits(sum_r, 1, tm_count), 1 + tm_bits - 1, "tm", 0)
        out_e, own_e = halves(by_bits(sum_e, 1, tm_count), 1, "tm", tm_bits - 1)
    grad, grad_send, acc_send, out_r, out_e = tie(grad, grad_send, acc_send, out_r, out_e)
    across_r = lambda x: across(x, "tm", 0)
    across_e = lambda x: across(x, "tm", tm_bits - 1)
    across_z = lambda x: across(x, "clip", 0)
    halves_z = lambda x: halves(by_bits(x, 0, clip_count), clip_bits - 1, "clip", 0)
    rest_z = lambda x: scatter_up(x, 0, "clip", range(1, clip_bits))

    got_r, got_e = across_r(out_r), across_e(out_e)
    acc_got = swap(acc_send)
    grad_first, grad_low, sent_o, kept_o, small_two = blend_back(
        z, info, grad, swap(grad_send), unit, inv, cot, mixed_low, gain_two
    )
    if not z.tape:
        sent_o, kept_o = plain_to_tape(z, kept_o, core)
    got_o = swap(sent_o)
    sent_0, kept_0, rest_0 = attend_back(z, info, 0, grad_low, output_weight, saved)
    grad_low, got_o, acc_got, sent_0 = tie(grad_low, got_o, acc_got, sent_0)
    out_o, own_o = halves_z(add(kept_o, got_o))
    grad_low, out_o = tie(grad_low, out_o)
    got_0, got_oz = swap(sent_0), across_z(out_o)
    sent_1, kept_1, rest_1 = attend_back(z, info, 1, grad_low, output_weight, saved)
    grad_low, got_r, got_e, got_0, got_oz, sent_1 = tie(
        grad_low, got_r, got_e, got_0, got_oz, sent_1
    )
    sum_r, sum_e = add(own_r, got_r), add(own_e, got_e)
    if z.tape:
        out_r, own_r = halves(sum_r, 0, "tm", 1)
        out_e, own_e = halves(sum_e, 0, "tm", 0)
        ordered = lambda x: jnp.where(place // 2 == 0, jnp.concatenate([x[half:], x[:half]], 0), x)
        out_r, own_r = ordered(out_r), ordered(own_r)
    else:
        sum_r = scatter_up(sum_r, 1, "tm", low_bits[1:-1])
        sum_e = scatter(sum_e, 1, "tm", high_bits[1:-1])
        out_r, own_r = halves(sum_r, 1, "tm", low_bits[-1])
        out_e, own_e = halves(sum_e, 1, "tm", high_bits[-1])
    sum_o = add(own_o, got_oz)
    out_0, own_0 = halves_z(add(kept_0, got_0))
    grad_low, out_r, out_e, sum_o, out_0 = tie(grad_low, out_r, out_e, sum_o, out_0)
    got_r, got_e = across(out_r, "tm", low_bits[-1]), across(out_e, "tm", high_bits[-1])
    got_0z, got_1 = across_z(out_0), swap(sent_1)
    sum_o = rest_z(sum_o)

    def split_tm(x, *more):
        x = by_bits(x, 1, tm_count)
        parts = [x[:half], x[half:]]
        if more:
            parts = [jnp.concatenate([p, by_bits(m, 1, tm_count)], 0) for p, m in zip(parts, more)]
        return (
            *halves(parts[0], tm_bits, "tm", 0),
            *halves(parts[1], 1, "tm", tm_bits - 1),
        )

    sent_2, kept_2, rest_2 = attend_back(z, info, 2, grad_low, output_weight, saved)
    sent_2, got_r, got_e, got_0z, got_1, sum_o, *rest_2 = tie(
        sent_2, got_r, got_e, got_0z, got_1, sum_o, *rest_2
    )
    sum_r, sum_e = add(own_r, got_r), add(own_e, got_e)
    out_f, own_f = halves_z(jnp.concatenate([sum_r, sum_e], 1))
    count_f = sum_r.shape[1]
    sum_0 = add(own_0, got_0z)
    out_1x, own_1x, out_1y, own_1y = split_tm(add(kept_1, got_1))
    feed_bias = feed_bias[:, 0:1] * (jnp.arange(2) == core).astype(f32)[:, None]
    if not paired:
        feed_bias = feed_bias.swapaxes(0, 1).reshape(2, clip_count, -1).swapaxes(0, 1)
    feed_small = jnp.concatenate([small_two[:4], feed_bias.reshape(-1, feat)], 0)
    out_f, sum_0, out_1x, out_1y, sent_2, *rest_2 = tie(
        out_f, sum_0, out_1x, out_1y, sent_2, *rest_2
    )
    got_f, got_2, got_1x, got_1y = across_z(out_f), swap(sent_2), across_r(out_1x), across_e(out_1y)
    sum_0 = rest_z(sum_0)
    own, small, *sends = keys_back(
        z, info, saved, input_weight, grad_first, feed_small, (rest_0, rest_1, rest_2)
    )
    got_2, got_1x, got_1y, sum_0, own, small, *sends = tie(
        got_2, got_1x, got_1y, sum_0, own, small, *sends
    )
    out_2x, own_2x, out_2y, own_2y = split_tm(add(kept_2, got_2), sum_o[None], sum_0[None])
    def patches_of(mine, theirs):
        first = jnp.where(core == 0, mine, theirs[: z.half])
        second = jnp.where(core == 0, theirs[: z.half], mine)
        pair = jnp.stack([first, second], 0).reshape(
            z.clips, z.blocks, z.fr, BLOCK_COLS, feat
        )
        return pair.transpose(2, 1, 3, 0, 4).reshape(z.fr, z.tc, z.clips, feat)

    finish_args = (rows, row(first_gain), grad_first)
    block_of = lambda total: (total + acc + acc_got.astype(f32) + row(reduce_bias)).astype(bf16)
    if z.tape:
        flat = lambda *parts: jnp.concatenate([part.reshape(-1, 128) for part in parts], 0)
        count = small.shape[0]
        unpack = lambda got, like: (got[:-count].reshape(like.shape), got[-count:])
        across_x, across_y = lambda x: across(x, "tm", 0), lambda x: across(x, "tm", 1)
        across_zz = lambda x: across(x, "clip", 1)
        along_x, along_y, mid_x, mid_y = sends
        token, msg_x, out_2y, along_x, along_y = tie(
            info, flat(out_2x, small), out_2y, along_x, along_y
        )
        msg_x, got_2y = across_x(msg_x), across_y(out_2y)
        got_x, got_y = across_x(along_x), across_y(along_y)
        token, msg_x, got_2y = tie(token, msg_x, got_2y)
        got_2x, got_small = unpack(msg_x, own_2x)
        small = add(small, got_small)
        sum_x = jnp.concatenate([add(own_1x, got_1x), add(own_2x, got_2x)], 0)
        sum_y = jnp.concatenate([add(own_1y, got_1y), add(own_2y, got_2y)], 0)
        out_x, own_x = halves(sum_x, 1, "tm", 1)
        out_y, own_y = halves(sum_y, 1, "tm", 0)
        token, small = tie(token, small)
        token, msg_x, out_y, got_f = tie(token, flat(out_x, small), out_y, got_f)
        out_f, own_f = halves(add(own_f, got_f), 0, "clip", 1)
        msg_x, got_y2, got_f = across_y(msg_x), across_x(out_y), across_zz(out_f)
        token, msg_x, got_y2 = tie(token, msg_x, got_y2)
        got_x2, got_small = unpack(msg_x, own_x)
        small = add(small, got_small)
        sum_x, sum_y = add(own_x, got_x2), add(own_y, got_y2)
        late = [jnp.concatenate([one[:2], one[2:4]], 1) for one in (sum_x, sum_y)]
        out_l, own_l = halves_z(jnp.concatenate(late, 0))
        token, small = tie(token, small)
        token, msg_l = tie(token, flat(out_l, small))
        msg_l = across_z(msg_l)
        token, got_f = tie(token, got_f)
        sum_f = add(own_f, got_f)
        token, ready_p, ready_q = tie(
            token, flat(sum_f[:count_f], sum_x[4]), flat(sum_f[count_f:], sum_y[4])
        )
        got_p, got_q = across_x(ready_p), across_y(ready_q)
        token, got_x, got_y = tie(token, got_x, got_y)
        lead = add(along_x[z.rows :], got_x[z.rows :])
        out_xy = jnp.concatenate([add(mid_x, got_x[z.half : z.rows]), lead], 0)
        out_yx = add(mid_y, got_y[z.half :])
        token, out_xy, out_yx, total_now = tie(token, out_xy, out_yx, total)
        got_xy, got_yx = across_y(out_xy), across_x(out_yx)
        block = block_of(total_now)
        block_mine, block_send = block[: z.half], block[z.half :]
        token, msg_l, block_mine, block_send = tie(token, msg_l, block_mine, block_send)
        got_l, got_small = unpack(msg_l, own_l)
        small = add(small, got_small)
        out_l, own_l = halves(add(own_l, got_l), 0, "clip", 1)
        token, small = tie(token, small)
        token, msg_l = tie(token, flat(out_l, small))
        msg_l = across_zz(msg_l)
        token, got_xy, got_yx, got_p, got_q = tie(token, got_xy, got_yx, got_p, got_q)
        received = [got_x, got_y, got_xy, got_yx]
        grad_mine, grad_send = finish(z, token, own, received, *finish_args)
        token, grad_send = tie(token, grad_send)
        grad_got, block_got = swap(grad_send), swap(block_send)
        token, grad_got, block_got = tie(token, grad_got, block_got)
        token, near_p, near_q = tie(token, flat(ready_p, got_p), flat(ready_q, got_q))
        far_p, far_q = across_y(near_p), across_x(near_q)
        other_p, other_q = swap(near_p), swap(near_q)
        token, msg_l, other_p, other_q = tie(token, msg_l, other_p, other_q)
        got_l, got_small = unpack(msg_l, own_l)
        small, late = add(small, got_small), add(own_l, got_l)
        token, small, late = tie(token, small, late)
        late_all = to_peers([late] * 3, "tm")
        feed_grads = assemble_feed(z, token, ff, 0, (near_p, near_q, other_p, other_q), ())
        patch_outs = (patches_of(block_mine, block_got), patches_of(grad_mine, grad_got))
        token, far_p, far_q, *rest = tie(token, far_p, far_q, *feed_grads, *patch_outs)
        feed_grads, patch_outs = rest[:2], rest[2:]
        other_far = (swap(far_p), swap(far_q))
        token, *late_all = tie(token, *late_all)
        token, late, small = tie(token, flat(late, *late_all), small)
        late_got, small_got = swap(late), swap(small)
        token, *other_far = tie(token, *other_far)
        far = (far_p, far_q, *other_far)
        feed_grads = assemble_feed(z, token, ff, 1, far, feed_grads)
        token, *feed_grads = tie(token, *feed_grads)
        vectors = small_grads(z, token, small, small_got)
    else:
        received = to_peers(sends, "tm")
        got_2x, got_2y = across_r(out_2x), across_e(out_2y)
        sum_x = jnp.concatenate([add(own_1x, got_1x), add(own_2x, got_2x)], 0)
        sum_y = jnp.concatenate([add(own_1y, got_1y), add(own_2y, got_2y)], 0)
        sum_x = scatter_up(sum_x, 1, "tm", low_bits[1:])
        sum_y = scatter(sum_y, 1, "tm", high_bits[1:])
        sum_f = rest_z(add(own_f, got_f))
        ready = jnp.concatenate([sum_f, sum_x[2 * half], sum_y[2 * half]], 0)
        late = jnp.concatenate(
            [
                jnp.concatenate([one[:half], one[half : 2 * half]], 1)
                for one in (sum_x, sum_y)
            ],
            0,
        )
        late = scatter(by_bits(late, 0, clip_count), 0, "clip", range(clip_bits)[::-1])
        ready = jnp.concatenate([ready, late], 0)
        ready_all = [ready] + to_peers([ready] * (tm_count - 1), "tm")
        small = small + swap(small)
        for axis, bits in (("tm", tm_bits), ("clip", clip_bits)):
            for bit in range(bits):
                small = small + across(small, axis, bit)
        grad_mine, grad_send = finish(z, info, own, received, *finish_args)

    here = lax.axis_index("clip")

    def shard(vector):
        count = vector.shape[0] // clip_count
        return lax.dynamic_slice_in_dim(vector, here * count, count, 0)

    if not z.tape:
        vectors = [shard(small[0:2].reshape(-1)), *[shard(small[i]) for i in range(2, 8)]]
        vectors.append(shard(small[8:12].reshape(-1)))
    input_bias_grad, gain_one_grad, shift_one_grad, output_bias_grad = vectors[:4]
    gain_two_grad, shift_two_grad, reduce_bias_grad, expand_bias_grad = vectors[4:]

    if z.tape:
        expand_weight_grad, reduce_weight_grad = feed_grads
        output_weight_grad, input_weight_grad = assemble_input(
            z, token, (near_p, near_q, other_p, other_q), far, (late, late_got)
        )
    else:
        block = block_of(total)
        block_mine, block_send = block[: z.half], block[z.half :]
        grad_got, block_got = swap(grad_send), swap(block_send)
        patch_outs = (patches_of(block_mine, block_got), patches_of(grad_mine, grad_got))
        tapes = jnp.stack(ready_all)
        other_tapes = swap(tapes)
        both = in_order(tapes, [other_tapes], "freq")
        both = pick(jnp.stack([both[:, np.arange(tm_count) ^ t] for t in range(tm_count)]), 0, place)
        part_r, part_e = both[:, :, :count_f], both[:, :, count_f : 2 * count_f]
        rows_r, rows_e = ff // (2 * clip_count * tm_count), feat // (clip_count * split)
        part_r = part_r.reshape(2, tm_count, feat // 128, rows_r, 128).swapaxes(2, 3)
        reduce_weight_grad = part_r.reshape(ff // clip_count, feat).astype(f32)
        part_e = part_e.reshape(2, FF_PARTS // 2, split, size // 128, rows_e, 128)
        part_e = part_e.transpose(2, 4, 1, 0, 3, 5)
        if not paired:
            part_e = part_e.swapaxes(2, 3).reshape(feat // clip_count, 2, clip_count, -1)
            part_e = part_e.swapaxes(1, 2)
        expand_weight_grad = part_e.reshape(feat // clip_count, ff).astype(f32)
        lanes = z.width // 128
        part_a = both[:, :, 2 * count_f :].reshape(2, tm_count // lanes, lanes, 4, 3, -1, 128)
        part_a = part_a.transpose(0, 1, 5, 3, 4, 2, 6)
        part_a = part_a.reshape(feat // clip_count, 4, 3, z.width).astype(f32)
        output_weight_grad = part_a[:, 0].reshape(-1, feat)
        input_weight_grad = part_a[:, 1:].swapaxes(1, 2).reshape(-1, 3 * feat)

    def leads_of(sent, got):
        mine, theirs = sent[z.half : z.half + LEADS], got[z.half : z.half + LEADS]
        first = jnp.where(core == 0, mine, theirs)
        second = jnp.where(core == 0, theirs, mine)
        return jnp.stack([first, second], 0)

    return (
        patch_outs[0],
        leads_of(block_send, block_got),
        patch_outs[1],
        leads_of(grad_send, grad_got),
        input_weight_grad,
        input_bias_grad,
        output_weight_grad,
        output_bias_grad,
        gain_one_grad,
        shift_one_grad,
        gain_two_grad,
        shift_two_grad,
        expand_weight_grad,
        expand_bias_grad,
        reduce_weight_grad,
        reduce_bias_grad,
    )


def solution(mesh):
    rows = P("freq", "tm", "clip", None)
    lead = P("clip", None, None)
    in_specs = (rows, lead, P("clip")) + (P(),) * 12 + (rows, lead)
    matrix, vector = P("clip", None), P("clip")
    out_specs = (rows, lead, rows, lead) + (matrix, vector) * 2 + (vector,) * 4 + (matrix, vector) * 2
    return jax.shard_map(
        per_device, mesh=mesh, in_specs=in_specs, out_specs=out_specs, check_vma=False
    )
```

```python
import functools
import math

import jax
import jax.numpy as jnp
import numpy as np
from jax import lax
from jax.experimental import pallas as pl
from jax.experimental.pallas import tpu as pltpu
from jax.sharding import PartitionSpec as P

HEADS = 12
EPSILON = 1e-06
NEG_FILL = -1e30
MAX_LENGTH = 101
LEADS = 2
LEAD_ROWS = 16
BLOCK_COLS = 8
GROUP = 4
FF_PARTS = 8
bf16 = jnp.bfloat16
f32 = jnp.float32


def mm(a, b):
    return lax.dot_general(a, b, (((1,), (0,)), ((), ())), preferred_element_type=f32)


def mm_nt(a, b):
    return lax.dot_general(a, b, (((1,), (1,)), ((), ())), preferred_element_type=f32)


def standardize(rows):
    center = rows - jnp.mean(rows, -1, keepdims=True)
    scale_inv = lax.rsqrt(jnp.mean(center * center, -1, keepdims=True) + EPSILON)
    return center * scale_inv, scale_inv


def norm_backward(grad_out, gain_row, normed, scale_inv):
    scaled = grad_out * gain_row
    return scale_inv * (
        scaled
        - jnp.mean(scaled, -1, keepdims=True)
        - normed * jnp.mean(scaled * normed, -1, keepdims=True)
    )


def head_mask(head, width, head_width):
    lane_head = lax.broadcasted_iota(jnp.int32, (1, width), 1) // head_width
    return (lane_head == head).astype(f32)


class Sizes:
    def __init__(self, patches_shape, tm_count, clip_count):
        fr_local, tc_local, clips, feat = patches_shape
        self.fr, self.tc, self.clips, self.feat = fr_local, tc_local, clips, feat
        self.tm, self.clip = tm_count, clip_count
        self.tape = clip_count == 4 and tm_count == 4
        self.tape_rows = 3 * feat * 2 // (2 * clip_count * tm_count)
        self.blocks = tc_local // BLOCK_COLS
        self.half_block = fr_local * BLOCK_COLS
        self.block = 2 * self.half_block
        self.half = self.blocks * self.half_block
        self.rows = 2 * self.half
        self.query_rows = self.rows + LEAD_ROWS
        self.key_blocks = -(-MAX_LENGTH // BLOCK_COLS)
        self.keys = LEAD_ROWS + self.key_blocks * self.block
        self.head_width = feat // HEADS
        self.width = GROUP * self.head_width
        self.steps = HEADS // GROUP
        self.lanes = GROUP * self.rows + 128


def call(kernel, room, in_specs, out_specs, out_shape, scratch, args, info, flops, moved, aliases={}):
    return pl.pallas_call(
        kernel,
        out_shape=out_shape,
        in_specs=[pl.BlockSpec(memory_space=pltpu.SMEM), *in_specs],
        out_specs=out_specs,
        scratch_shapes=scratch,
        input_output_aliases=aliases,
        compiler_params=pltpu.CompilerParams(vmem_limit_bytes=room * 1024 * 1024),
        cost_estimate=pl.CostEstimate(flops=flops, bytes_accessed=moved, transcendentals=0),
    )(info, *args)


def in_vmem(x):
    return pltpu.with_memory_space_constraint(x, pltpu.VMEM)


def in_hbm(x):
    return pltpu.with_memory_space_constraint(x, pltpu.HBM)


def whole(shape):
    return pl.BlockSpec(memory_space=pltpu.VMEM)


def chunks_of(z):
    full = z.lanes // 256
    spans = [(c * 256, 256) for c in range(full)]
    if z.lanes % 256:
        spans.append((full * 256, z.lanes % 256))
    return spans


def spread_heads(z, rows, out_ref):
    for head in range(GROUP):
        mask = head_mask(head, z.width, z.head_width)
        part = (rows * mask).astype(bf16)
        out_ref[head * z.rows : (head + 1) * z.rows, :] = part[: z.rows]
        at = GROUP * z.rows + head * LEAD_ROWS
        out_ref[at : at + LEAD_ROWS, :] = part[z.rows :]
    at = GROUP * (z.rows + LEAD_ROWS)
    out_ref[at:, :] = jnp.zeros((z.lanes - at, z.width), bf16)


def join_heads(z, spread):
    patch_part, lead_part = None, None
    for head in range(GROUP):
        mask = head_mask(head, z.width, z.head_width)
        at = GROUP * z.rows + head * LEAD_ROWS
        one = spread[head * z.rows : (head + 1) * z.rows] * mask
        two = spread[at : at + LEAD_ROWS] * mask
        patch_part = one if patch_part is None else patch_part + one
        lead_part = two if lead_part is None else lead_part + two
    return jnp.concatenate([patch_part, lead_part], 0)


class Copies:
    def __init__(self, sems):
        self.sems, self.going = sems, {}

    def start(self, name, source, to):
        copy = pltpu.make_async_copy(source, to, self.sems.at[len(self.going)])
        copy.start()
        self.going[name] = copy

    def wait(self, *names):
        for name in names:
            self.going[name].wait()


def attend_kernel(z, info, *refs):
    refs = list(refs)
    take = lambda n: [refs.pop(0) for _ in range(n)]
    pieces = take(2 * z.tm)
    lead, weight, bias_q, bias_v, gain, shift, live, wo_in, bo, gain_two, shift_two = take(11)
    low_out, inv_out, uq, unit_out, scale_out, low_two = take(6)
    q_out, k_out, v_out, mixed_out, hk_t_out, hq_t_out, p_out, uk_out, sum_out = take(9)
    spread, total, hk, hq, uk, w, p, q_all, k_all, v_all, mixed_all, hk_t, hq_t, first, wo, sems = take(16)
    me = info[0]
    copies = Copies(sems)
    span = lambda part, i: slice((part * z.steps + i) * z.width, (part * z.steps + i + 1) * z.width)
    copies.start("w", weight, w)
    copies.start("wo", wo_in, wo)
    gain_row, shift_row = gain[...], shift[...]

    def hidden(rows):
        unit, _ = standardize(rows.astype(f32))
        return unit.astype(bf16), (unit * gain_row + shift_row).astype(bf16)

    unit, low = hidden(lead[...])
    uk[0:LEAD_ROWS, :] = unit
    hk[0:LEAD_ROWS, :] = low
    hq[z.rows :, :] = low
    uq[z.rows :, :] = unit
    hb = z.half_block
    for k in range(z.tm):
        source = jnp.bitwise_xor(me, k)
        for half in range(2):
            unit, low = hidden(pieces[2 * k + half][...])
            if k == 0:
                hq[half * z.half : (half + 1) * z.half, :] = low
                uq[half * z.half : (half + 1) * z.half, :] = unit
            for b in range(z.blocks):
                at = LEAD_ROWS + (source * z.blocks + b) * z.block + half * hb
                at = pl.multiple_of(at, 16)
                uk[pl.ds(at, hb), :] = unit[b * hb : (b + 1) * hb]
                hk[pl.ds(at, hb), :] = low[b * hb : (b + 1) * hb]
    copies.start("uk", uk.at[0 : z.keys, :], uk_out)
    hk_all, hq_all = hk[0 : z.keys, :], hq[...]
    hk_t[...] = jnp.transpose(hk_all)
    hq_t[...] = jnp.transpose(hq_all)
    copies.start("hk_t", hk_t, hk_t_out)
    copies.start("hq_t", hq_t, hq_t_out)
    copies.wait("w")
    outs = ((q_all, q_out), (k_all, k_out), (v_all, v_out), (mixed_all, mixed_out))

    def group_copies(i):
        pairs = [(source.at[i], to.at[i]) for source, to in outs] + [(p.at[i % 2], p_out.at[i])]
        return [
            pltpu.make_async_copy(source, to, sems.at[8 + i * len(pairs) + n])
            for n, (source, to) in enumerate(pairs)
        ]

    def group(i, carry):
        columns = lambda part: pl.ds(pl.multiple_of((part * z.steps + i) * z.width, z.width), z.width)
        slot = i % 2
        q_copy, k_copy, v_copy, mixed_copy, p_copy = group_copies(i)

        @pl.when(i >= 2)
        def _():
            group_copies(i - 2)[-1].wait()

        q = (mm(hq[...], w[:, columns(0)]) + bias_q[:, columns(0)]).astype(bf16)
        q_all[i] = q
        spread_heads(z, q.astype(f32) * (z.head_width**-0.5), spread)
        k = mm(hk[0 : z.keys, :], w[:, columns(1)]).astype(bf16)
        k_all[i] = k
        v = (mm(hk[0 : z.keys, :], w[:, columns(2)]) + bias_v[:, columns(0)]).astype(bf16)
        v_all[i] = v
        q_copy.start()
        k_copy.start()
        v_copy.start()
        for at, size in chunks_of(z):
            scores = mm_nt(k, spread[at : at + size, :])
            scores = scores + jnp.concatenate([live[...]] * (size // 128), 1)
            peak = jnp.max(scores, 0, keepdims=True)
            weights = jnp.exp(scores - peak)
            total[i, 0:1, at : at + size] = jnp.sum(weights, 0, keepdims=True)
            p[slot, :, at : at + size] = weights.astype(bf16)
        p_copy.start()
        inverse = 1.0 / total[i, 0:1, :]
        inv_out[i] = jnp.broadcast_to(inverse, (8, z.lanes))
        mixed = mm(jnp.transpose(v), p[slot]) * inverse
        mixed = join_heads(z, jnp.transpose(mixed))
        mixed_all[i] = mixed
        mixed_copy.start()
        low_out[:, columns(0)] = mixed.astype(bf16)
        return carry

    lax.fori_loop(0, z.steps, group, 0)
    copies.wait("wo")
    rows = jnp.concatenate([pieces[0][...], pieces[1][...], lead[...]], 0).astype(f32)
    rows = rows + mm(low_out[...], wo[...]) + bo[...]
    first[...] = rows
    copies.start("sum", first, sum_out)
    normed, scale_inv = standardize(rows)
    unit_out[...] = normed
    scale_out[...] = jnp.broadcast_to(scale_inv, scale_out.shape)
    low_two[...] = (normed * gain_two[...] + shift_two[...]).astype(bf16)
    for i in range(z.steps):
        *near, p_copy = group_copies(i)
        for copy in near:
            copy.wait()
        if i >= z.steps - 2:
            p_copy.wait()
    copies.wait("uk", "hk_t", "hq_t", "sum")


def attend(z, me_info, pieces, lead, weight, bias_q, bias_v, gain, shift, live, wo, *second):
    feat, width, nk, nq, nl = z.feat, z.width, z.keys, z.query_rows, z.lanes
    there = pl.BlockSpec(memory_space=pl.ANY)
    in_specs = [whole((z.half, feat))] * (2 * z.tm) + [whole((LEAD_ROWS, feat)), there]
    in_specs += [whole((1, feat))] * 4 + [whole((nk, 128)), there] + [whole(None)] * 3
    shapes = [((nq, feat), bf16), ((z.steps, 8, nl), f32), ((nq, feat), bf16)]
    shapes += [((nq, feat), f32), ((nq, 128), f32), ((nq, feat), bf16)]
    heads = lambda rows, kind: ((z.steps, rows, width), kind)
    far = [heads(nq, bf16), heads(nk, bf16), heads(nk, bf16), heads(nq, f32)]
    far += [((feat, nk), bf16), ((feat, nq), bf16), ((z.steps, nk, nl), bf16), ((nk, feat), bf16)]
    far.append(((nq, feat), f32))
    return call(
        functools.partial(attend_kernel, z),
        42,
        in_specs,
        [whole(None)] * 6 + [there] * 9,
        [jax.ShapeDtypeStruct(*one) for one in shapes] + [pltpu.HBM(*one) for one in far],
        [
            pltpu.VMEM((nl, width), bf16),
            pltpu.VMEM((z.steps, 8, nl), f32),
            pltpu.VMEM((LEAD_ROWS + z.tm * z.rows, feat), bf16),
            pltpu.VMEM((nq, feat), bf16),
            pltpu.VMEM((LEAD_ROWS + z.tm * z.rows, feat), bf16),
            pltpu.VMEM((feat, 3 * feat), bf16),
            pltpu.VMEM((2, nk, nl), bf16),
            *[pltpu.VMEM(*one) for one in far[:6]],
            pltpu.VMEM((nq, feat), f32),
            pltpu.VMEM((feat, feat), bf16),
            pltpu.SemaphoreType.DMA((32,)),
        ],
        (*pieces, lead, in_hbm(weight), bias_q, bias_v, gain, shift, live, in_hbm(wo), *second),
        me_info,
        2 * feat * feat * (nq + 2 * nk) + 4 * z.steps * nk * nl * width,
        z.steps * nk * nl * 2,
    )


def feed_kernel(z, paired, info, *refs):
    refs = list(refs)
    take = lambda n: [refs.pop(0) for _ in range(n)]
    low, low_other, cot, cot_other, be, we_in, wr_in = take(7)
    dbe, acc, acc_other, grad, grad_other = take(5)
    outs = take(4 if z.tape else 2)
    we, wr, dwr, dwe, low_t, cot_all, acc_sum, grad_sum, sems = take(9)
    steps = FF_PARTS // 2
    size = we.shape[2] // 2
    nq = z.query_rows
    core = info[1]
    col, line = info[0] % 2, info[0] // 2
    place = lambda i: jnp.bitwise_xor(i, 2 * (1 - line)) if z.tape else i
    at = lambda i: pl.multiple_of(
        (2 * place(i) + core if paired else steps * core + i) * size, size
    )
    copies = Copies(sems)
    names = []

    def leave(name, source, to):
        copies.start(name, source, to)
        names.append(name)

    for i in range(steps):
        pair, span = i // 2, slice(i % 2 * size, (i % 2 + 1) * size)
        copies.start(f"we{i}", we_in.at[:, pl.ds(at(i), size)], we.at[pair, :, span])
        copies.start(f"wr{i}", wr_in.at[pl.ds(at(i), size), :], wr.at[pair, span, :])
    cot_all[:nq, :] = cot[...]
    cot_all[nq:, :] = cot_other[...]
    low_all = jnp.concatenate([low[...], low_other[...]], 0)
    low_t[...] = jnp.transpose(low_all)
    for pair in range(steps // 2):
        both = (2 * pair, 2 * pair + 1)
        copies.wait(*[f"w{which}{i}" for i in both for which in "er"])
        cot_low = cot_all[...]
        expand, reduce = we[pair], wr[pair]
        bias = jnp.concatenate([be[:, pl.ds(at(i), size)] for i in both], 1)
        expanded = mm(low_all, expand) + bias
        grad_activated = mm_nt(cot_low, reduce)
        cdf = 0.5 * (1.0 + lax.erf(expanded * math.sqrt(0.5)))
        pdf = jnp.exp(-0.5 * expanded * expanded) * (1.0 / math.sqrt(2.0 * math.pi))
        activated = (expanded * cdf).astype(bf16)
        reduce_grad = mm(jnp.transpose(activated), cot_low).astype(bf16)
        for n, i in enumerate(both):
            if z.tape:
                part = size // z.tm
                for t in range(z.tm):
                    for lane in range(z.feat // 128):
                        rows = slice(n * size + t * part, n * size + (t + 1) * part)
                        dwr[i, t, lane * part : (lane + 1) * part, :] = reduce_grad[
                            rows, lane * 128 : (lane + 1) * 128
                        ]
                out_r, own_r, out_e, own_e = outs
                for y in range(2):
                    leave(f"out_r{i}{y}", dwr.at[i, 2 * y + 1 - col], out_r.at[y, i])
                    leave(f"own_r{i}{y}", dwr.at[i, 2 * y + col], own_r.at[y, i])
            else:
                dwr[i] = reduce_grad[n * size : (n + 1) * size]
                leave(f"dwr{i}", dwr.at[i], outs[0].at[i])
        grad_expanded = (grad_activated * (cdf + expanded * pdf)).astype(bf16)
        expand_grad = mm(low_t[...], grad_expanded).astype(bf16)
        bias_grad = jnp.sum(grad_expanded.astype(f32), 0, keepdims=True)
        for n, i in enumerate(both):
            span = slice(n * size, (n + 1) * size)
            if z.tape:
                part = z.feat // z.clip
                for c in range(z.clip):
                    for lane in range(size // 128):
                        lanes = slice(n * size + lane * 128, n * size + (lane + 1) * 128)
                        dwe[i, c, lane * part : (lane + 1) * part, :] = expand_grad[
                            c * part : (c + 1) * part, lanes
                        ]
                    leave(f"e{i}{c}", dwe.at[i, c], (out_e, own_e)[pair].at[n, c])
            else:
                dwe[i] = expand_grad[:, span]
                leave(f"dwe{i}", dwe.at[i], outs[1].at[i])
            dbe[place(i)] = jnp.broadcast_to(bias_grad[:, span], dbe.shape[1:])
        acc_new, grad_new = mm(activated, reduce), mm_nt(grad_expanded, expand)
        if pair == 0:
            acc_sum[...] = acc_new
            grad_sum[...] = grad_new
        else:
            acc_new, grad_new = acc_sum[...] + acc_new, grad_sum[...] + grad_new
            acc[...] = acc_new[:nq]
            acc_other[...] = acc_new[nq:].astype(bf16)
            grad[...] = grad_new[:nq]
            grad_other[...] = grad_new[nq:].astype(bf16)
    copies.wait(*names)


def feed(z, info, paired, low, low_other, cot, cot_other, expand, expand_bias, reduce):
    feat, ff = expand.shape
    size = ff // FF_PARTS
    steps = FF_PARTS // 2
    nq = z.query_rows
    there, here = pl.BlockSpec(memory_space=pl.ANY), whole(None)
    if z.tape:
        shapes = [(z.tm, size * feat // (128 * z.tm), 128), (z.clip, size * feat // (128 * z.clip), 128)]
    else:
        shapes = [(size, feat), (feat, size)]
    shapes = [(steps, *shape) for shape in shapes]
    wide, narrow = ((nq, feat), f32), ((nq, feat), bf16)
    outs = [((steps, 8, size), f32), wide, narrow, wide, narrow]
    far = shapes
    if z.tape:
        far = [(2, 4, *shapes[0][2:])] * 4
    return call(
        functools.partial(feed_kernel, z, paired),
        44,
        [here] * 5 + [there] * 2,
        [here] * 5 + [there] * len(far),
        [jax.ShapeDtypeStruct(*one) for one in outs] + [pltpu.HBM(shape, bf16) for shape in far],
        [
            pltpu.VMEM((steps // 2, feat, 2 * size), bf16),
            pltpu.VMEM((steps // 2, 2 * size, feat), bf16),
            pltpu.VMEM(shapes[0], bf16),
            pltpu.VMEM(shapes[1], bf16),
            pltpu.VMEM((feat, 2 * nq), bf16),
            pltpu.VMEM((2 * nq, feat), bf16),
            pltpu.VMEM((2 * nq, feat), f32),
            pltpu.VMEM((2 * nq, feat), f32),
            pltpu.SemaphoreType.DMA((48,)),
        ],
        (low, low_other, cot, cot_other, expand_bias, in_hbm(expand), in_hbm(reduce)),
        info,
        6 * nq * feat * ff * 2,
        4 * feat * ff,
    )


def blend_back_kernel(z, info, *refs):
    refs = list(refs)
    take = lambda n: [refs.pop(0) for _ in range(n)]
    grad, grad_got, unit, inv, cot, mixed, gain = take(7)
    first_out, low_grad, send, keep, small, hold = take(6)
    rows_grad = cot[...].astype(f32)
    normed, hidden_grad = unit[...], grad[...] + grad_got[...].astype(f32)
    back = rows_grad + norm_backward(hidden_grad, gain[...], normed, inv[:, 0:1])
    first_out[...] = back
    back_low = back.astype(bf16)
    low_grad[...] = back_low
    dwo = mm(jnp.transpose(mixed[...]), back_low)
    for j in range(z.steps):
        block = dwo[:, j * z.width : (j + 1) * z.width]
        if z.tape:
            store_split(z, info[1], block, hold, send, keep, j)
        else:
            keep[j] = block.astype(bf16)
    small[...] = jnp.zeros_like(small)
    small[0:1, :] = jnp.sum(back_low.astype(f32), 0, keepdims=True)
    small[1:2, :] = jnp.sum(hidden_grad * normed, 0, keepdims=True)
    small[2:3, :] = jnp.sum(hidden_grad, 0, keepdims=True)
    small[3:4, :] = jnp.sum(rows_grad, 0, keepdims=True)


def blend_back(z, info, *args):
    feat, nq = z.feat, z.query_rows
    split = ((z.clip, z.tm, z.tape_rows, 128) if z.tape else (3, feat, z.width), bf16)
    shapes = [((nq, feat), f32), ((nq, feat), bf16), split, split, ((8, feat), f32)]
    return call(
        functools.partial(blend_back_kernel, z),
        20,
        [whole(None)] * len(args),
        [whole(None)] * len(shapes),
        [jax.ShapeDtypeStruct(*one) for one in shapes],
        [pltpu.VMEM((feat, z.width), f32)],
        args,
        info,
        2 * nq * feat * feat,
        nq * feat * 20,
    )


def store_split(z, core, value, hold, sent, kept, j):
    hold[...] = value
    half = z.feat // (2 * z.clip)
    part = half // 2
    for c in range(z.clip):
        for out, whose in ((kept, core), (sent, 1 - core)):
            for t in range(z.tm):
                at = pl.multiple_of((2 * c + whose) * half + (t // 2) * part, 16)
                lanes = slice((t % 2) * 128, (t % 2) * 128 + 128)
                out[c, t, j * part : (j + 1) * part, :] = hold[pl.ds(at, part), lanes].astype(bf16)


def plain_to_tape(z, blocks, core):
    lanes = z.width // 128
    x = blocks.reshape(3, z.clip, 2, z.tm // lanes, -1, lanes, 128)
    x = x.transpose(2, 1, 3, 5, 0, 4, 6).reshape(2, z.clip, z.tm, -1, 128)
    return pick(x, 0, 1 - core), pick(x, 0, core)


def attend_back_kernel(z, i, info, *refs):
    refs = list(refs)
    take = lambda n: [refs.pop(0) for _ in range(n)]
    ga, wo, inv, *far = take(10)
    span = slice(i * z.width, (i + 1) * z.width)
    sent, kept, db, kv_out, q_grad_out = take(5)
    q_spread, g_spread, ds, hold, q, k, v, mixed, hk_t, hq_t, p, sems = take(12)
    core = info[1]
    copies = Copies(sems)
    q_in, k_in, v_in, mixed_in, hk_t_in, hq_t_in, p_in = far
    for name, source, to in (
        ("q", q_in.at[i], q),
        ("mixed", mixed_in.at[i], mixed),
        ("v", v_in.at[i], v),
        ("p", p_in.at[i], p),
        ("k", k_in.at[i], k),
        ("hq_t", hq_t_in, hq_t),
        ("hk_t", hk_t_in, hk_t),
    ):
        copies.start(name, source, to)
    scale = z.head_width**-0.5

    grad = mm_nt(ga[...], wo[span, :]).astype(bf16).astype(f32)
    inverse = inv[i, 0:1, :]
    inverse_col = jnp.transpose(jnp.broadcast_to(inverse, (128, z.lanes)))[:, 0:1]
    copies.wait("q", "mixed")
    spread_heads(z, q[...].astype(f32) * scale, q_spread)
    product = grad * mixed[...]
    dots = []
    for head in range(GROUP):
        mask = head_mask(head, z.width, z.head_width)
        at = GROUP * z.rows + head * LEAD_ROWS
        part = grad * mask
        low = (part[: z.rows] * inverse_col[head * z.rows : (head + 1) * z.rows]).astype(bf16)
        g_spread[head * z.rows : (head + 1) * z.rows, :] = low
        low = (part[z.rows :] * inverse_col[at : at + LEAD_ROWS]).astype(bf16)
        g_spread[at : at + LEAD_ROWS, :] = low
        dots.append(jnp.sum(product * mask, 1, keepdims=True))
    end = GROUP * (z.rows + LEAD_ROWS)
    g_spread[end:, :] = jnp.zeros((z.lanes - end, z.width), bf16)
    dot_col = jnp.concatenate(
        [d[: z.rows] for d in dots]
        + [d[z.rows :] for d in dots]
        + [jnp.zeros((z.lanes - end, 1), f32)],
        0,
    )
    dot_row = jnp.transpose(jnp.broadcast_to(dot_col, (z.lanes, 128)))[0:1, :] * inverse
    copies.wait("v", "p")
    v_all = v[...]
    for at, size in chunks_of(z):
        grad_weights = mm_nt(v_all, g_spread[at : at + size, :])
        weights = p[:, at : at + size].astype(f32)
        ds[:, at : at + size] = (weights * (grad_weights - dot_row[:, at : at + size])).astype(bf16)
    ds_all = ds[...]
    copies.wait("k", "hq_t", "hk_t")
    k_all = k[...]
    grad_v = mm(p[...], g_spread[...])
    grad_k = mm(ds_all, q_spread[...])
    grad_q = mm(jnp.transpose(k_all), ds_all)
    grad_q = (join_heads(z, jnp.transpose(grad_q)) * scale).astype(bf16)
    grad_v = grad_v.astype(bf16)
    grad_k = grad_k.astype(bf16)
    db[...] = jnp.concatenate(
        [
            jnp.sum(grad_q.astype(f32), 0, keepdims=True),
            jnp.sum(grad_v.astype(f32), 0, keepdims=True),
            jnp.zeros((6, z.width), f32),
        ],
        0,
    )
    for j, grad in enumerate((mm(hq_t[...], grad_q), mm(hk_t[...], grad_k), mm(hk_t[...], grad_v))):
        if z.tape:
            store_split(z, core, grad, hold, sent, kept, j)
        else:
            kept[j] = grad.astype(bf16)
    kv_out[:, : z.width] = grad_k
    kv_out[:, z.width :] = grad_v
    q_grad_out[...] = grad_q


def keys_back_kernel(z, info, *refs):
    refs = list(refs)
    take = lambda n: [refs.pop(0) for _ in range(n)]
    uk_in, uq, weight_in, first, feed_small = take(5)
    db, grad_kv, grad_q = take(z.steps), take(z.steps), take(z.steps)
    own, small_out = take(2)
    sends = take(4 if z.tape else z.tm - 1)
    keys_acc, query_acc, small, uk, weight, sems = take(6)
    me = info[0]
    copies = Copies(sems)
    span = lambda part, i: slice((part * z.steps + i) * z.width, (part * z.steps + i + 1) * z.width)
    copies.start("w", weight_in, weight)
    copies.start("uk", uk_in, uk)
    column = lambda part, i: slice((part * z.steps + i) * z.width, (part * z.steps + i + 1) * z.width)
    copies.wait("w")
    query_grad, keys_grad = 0.0, 0.0
    for i in range(z.steps):
        query_grad += mm_nt(grad_q[i][...], weight[:, column(0, i)])
        keys_grad += mm_nt(grad_kv[i][:, : z.width], weight[:, column(1, i)])
        keys_grad += mm_nt(grad_kv[i][:, z.width :], weight[:, column(2, i)])
    keys_acc[...] = keys_grad
    query_acc[...] = query_grad
    copies.wait("uk")
    small[...] = jnp.zeros_like(small)
    for i in range(z.steps):
        small[0:2, i * z.width : (i + 1) * z.width] = db[i][0:2, :]
    small[2:3, :] = jnp.sum(keys_grad * uk[...].astype(f32), 0, keepdims=True) + jnp.sum(
        query_grad * uq[...].astype(f32), 0, keepdims=True
    )
    small[3:4, :] = jnp.sum(keys_grad, 0, keepdims=True) + jnp.sum(query_grad, 0, keepdims=True)
    small[4:12, :] = feed_small[...]
    if z.tape:
        for lane in range(z.feat // 128):
            small_out[lane * 16 : lane * 16 + 16, :] = small[
                :, lane * 128 : lane * 128 + 128
            ].astype(bf16)
    else:
        small_out[...] = small[...]
    lead = keys_acc[0:LEAD_ROWS, :] + query_acc[z.rows :, :]
    first_lead = first[z.rows :, :]
    high = first_lead.astype(bf16)
    rest = (first_lead - high.astype(f32)).astype(bf16)
    pair = lambda a: a[0:LEADS]
    packed = jnp.concatenate(
        [pair(lead), pair(high.astype(f32)), pair(rest.astype(f32)), jnp.zeros((10, z.feat), f32)], 0
    )
    small_high = small[...].astype(bf16)
    small_low = (small[...] - small_high.astype(f32)).astype(bf16)
    own[z.rows :, :] = packed
    packed = packed.astype(bf16)
    hb = z.half_block

    def chunk(k, half, out, at):
        source = jnp.bitwise_xor(me, k)
        for b in range(z.blocks):
            spot = source * z.blocks + b
            from_ = pl.multiple_of(
                LEAD_ROWS + jnp.minimum(spot, z.key_blocks - 1) * z.block + half * hb, 16
            )
            rows = keys_acc[pl.ds(from_, hb), :] * (spot < z.key_blocks).astype(f32)
            to = at + b * hb
            if k == 0:
                queries = half * z.half + b * hb
                rows = rows + query_acc[queries : queries + hb, :]
            out[to : to + hb, :] = rows.astype(out.dtype)

    chunk(0, 0, own, 0)
    chunk(0, 1, own, z.half)
    if z.tape:
        along_x, along_y, mid_x, mid_y = sends
        chunk(1, 0, along_x, 0)
        chunk(3, 0, along_x, z.half)
        along_x[z.rows :, :] = packed
        chunk(2, 1, along_y, 0)
        chunk(3, 1, along_y, z.half)
        chunk(2, 0, mid_x, 0)
        chunk(1, 1, mid_y, 0)
    else:
        for k, one in enumerate(sends, start=1):
            chunk(k, 0, one, 0)
            chunk(k, 1, one, z.half)
            one[z.rows :, :] = packed


def attend_back(z, info, i, ga, wo, saved):
    inv, far = saved[1], saved[6:13]
    feat, width, nk, nq, nl = z.feat, z.width, z.keys, z.query_rows, z.lanes
    in_specs = [whole(None)] * 3 + [pl.BlockSpec(memory_space=pl.ANY)] * 7
    if z.tape:
        part = (z.clip, z.tm, z.tape_rows, 128)
    else:
        part = (3, feat, width)
    sent, kept, *rest = call(
        functools.partial(attend_back_kernel, z, i),
        24,
        in_specs,
        [whole(part), whole(part), whole((8, width)), whole((nk, 2 * width)), whole((nq, width))],
        [
            jax.ShapeDtypeStruct(part, bf16),
            jax.ShapeDtypeStruct(part, bf16),
            jax.ShapeDtypeStruct((8, width), f32),
            jax.ShapeDtypeStruct((nk, 2 * width), bf16),
            jax.ShapeDtypeStruct((nq, width), bf16),
        ],
        [
            pltpu.VMEM((nl, width), bf16),
            pltpu.VMEM((nl, width), bf16),
            pltpu.VMEM((nk, nl), bf16),
            pltpu.VMEM((feat, width), f32),
            pltpu.VMEM((nq, width), bf16),
            pltpu.VMEM((nk, width), bf16),
            pltpu.VMEM((nk, width), bf16),
            pltpu.VMEM((nq, width), f32),
            pltpu.VMEM((feat, nk), bf16),
            pltpu.VMEM((feat, nq), bf16),
            pltpu.VMEM((nk, nl), bf16),
            pltpu.SemaphoreType.DMA((8,)),
        ],
        [ga, wo, inv, *[in_hbm(one) for one in far]],
        info,
        1000,
        1000,
    )
    if not z.tape:
        sent, kept = plain_to_tape(z, kept, info[1])
    return sent, kept, rest


def keys_back(z, info, saved, weight, first_lead, feed_small, steps):
    feat, width, nk, nq = z.feat, z.width, z.keys, z.query_rows
    uq, uk = saved[2], saved[13]
    there = pl.BlockSpec(memory_space=pl.ANY)
    in_specs = [there, whole((nq, feat)), there]
    in_specs += [whole(None)]
    in_specs += [whole((8, feat))]
    in_specs += [whole((8, width))] * z.steps
    in_specs += [whole((nk, 2 * width))] * z.steps + [whole((nq, width))] * z.steps
    if z.tape:
        sends = [(nq, feat), (z.rows, feat), (z.half, feat), (z.half, feat)]
    else:
        sends = [(nq, feat)] * (z.tm - 1)
    small = (16 * feat // 128, 128) if z.tape else (16, feat)
    return call(
        functools.partial(keys_back_kernel, z),
        24,
        in_specs,
        [whole((nq, feat)), whole(small)] + [whole(shape) for shape in sends],
        [
            jax.ShapeDtypeStruct((nq, feat), f32),
            jax.ShapeDtypeStruct(small, bf16 if z.tape else f32),
        ]
        + [jax.ShapeDtypeStruct(shape, bf16) for shape in sends],
        [
            pltpu.VMEM((nk, feat), f32),
            pltpu.VMEM((nq, feat), f32),
            pltpu.VMEM((16, feat), f32),
            pltpu.VMEM((nk, feat), bf16),
            pltpu.VMEM(weight.shape, bf16),
            pltpu.SemaphoreType.DMA((16,)),
        ],
        (in_hbm(uk), uq, in_hbm(weight), first_lead, feed_small)
        + tuple(step[j] for j in range(3) for step in steps),
        info,
        4 * feat * feat * (nq + 2 * nk),
        nk * feat * 4,
    )


def finish_kernel(z, info, *refs):
    *received, rows, gain, grad_first, out_mine, out_send = refs[1:]
    own = refs[0]
    mine = own[z.rows :].astype(bf16).astype(f32)
    if z.tape:
        got_x, got_y, got_xy, got_yx = (one[...].astype(f32) for one in received)
        first = own[: z.half] + got_x[: z.half] + got_xy[: z.half]
        second = own[z.half : z.rows] + got_y[: z.half] + got_yx
        lead = (mine + got_x[z.rows :]).astype(bf16).astype(f32) + got_xy[z.half :]
        total = jnp.concatenate([first, second, lead], 0)
    else:
        terms = [one[...].astype(f32) for one in received]
        leads = [mine] + [one[z.rows :] for one in terms]
        while len(leads) > 1:
            leads = [a + b for a, b in zip(leads[::2], leads[1::2])]
        total = jnp.concatenate([own[: z.rows] + sum(t[: z.rows] for t in terms), leads[0]], 0)
    normed, scale_inv = standardize(rows[...].astype(f32))
    back = norm_backward(total, gain[...], normed, scale_inv)
    rows_grad = (back[: z.rows] + grad_first[0 : z.rows, :]).astype(bf16)
    out_mine[...] = rows_grad[: z.half]
    out_send[0 : z.half, :] = rows_grad[z.half :]
    lead = total[z.rows :]
    lead_first = lead[LEADS : 2 * LEADS] + lead[2 * LEADS : 3 * LEADS]
    out_send[z.half :, :] = jnp.concatenate(
        [back[z.rows : z.rows + LEADS] + lead_first, jnp.zeros((LEAD_ROWS - LEADS, z.feat), f32)], 0
    ).astype(bf16)


def finish(z, info, own, received, rows, gain, grad_first):
    feat, nq = z.feat, z.query_rows
    return call(
        functools.partial(finish_kernel, z),
        16,
        [whole(one.shape) for one in (own, *received)]
        + [whole((nq, feat)), whole((1, feat)), whole((nq, feat))],
        [whole((z.half, feat)), whole((nq - z.half, feat))],
        [
            jax.ShapeDtypeStruct((z.half, feat), bf16),
            jax.ShapeDtypeStruct((nq - z.half, feat), bf16),
        ],
        [],
        (own, *received, rows, gain, grad_first),
        info,
        nq * feat * 20,
        nq * feat * 20,
    )


def place_blocks(z, t, whose, tape, row, out, lane_at):
    half = z.feat // (2 * z.clip)
    part = half // 2
    at = pl.multiple_of(whose * half + (t // 2) * part, 16)
    for j in range(3):
        block = tape[row + j * part : row + (j + 1) * part, :].astype(f32)
        lane = pl.multiple_of(lane_at(j) + (t % 2) * 128, 128)
        out[pl.ds(at, part), pl.ds(lane, 128)] = block


def assemble_feed_kernel(z, ff, far, info, *refs):
    me, core = info[0], info[1]
    expand_out, reduce_out, expand, reduce, sems = refs[-5:]
    p_mine, q_mine, p_other, q_other = refs[:4]
    size = ff // FF_PARTS
    step = size * z.feat // (128 * z.tm) + z.tape_rows
    part_r, part_e = size // z.tm, z.feat // z.clip
    copies = Copies(sems)
    names = []
    for whose, p, q in ((core, p_mine, q_mine), (1 - core, p_other, q_other)):
        for j, (k_p, k_q) in enumerate(((2, 1), (3, 3)) if far else ((0, 0), (1, 2))):
            n = len(names)
            for lane in range(z.feat // 128):
                block = p[j * step + lane * part_r : j * step + (lane + 1) * part_r, :]
                reduce[n, :, lane * 128 : (lane + 1) * 128] = block.astype(f32)
            at = pl.multiple_of(whose * size + jnp.bitwise_xor(me, k_p) * part_r, 16)
            copies.start((n, 0), reduce.at[n], reduce_out.at[pl.ds(at, part_r), :])
            for lane in range(size // 128):
                block = q[j * step + lane * part_e : j * step + (lane + 1) * part_e, :]
                expand[n, :, lane * 128 : (lane + 1) * 128] = block.astype(f32)
            at = pl.multiple_of((2 * jnp.bitwise_xor(me, k_q) + whose) * size, 128)
            copies.start((n, 1), expand.at[n], expand_out.at[:, pl.ds(at, size)])
            names.append(n)
    copies.wait(*[(n, i) for n in names for i in range(2)])


def assemble_feed(z, info, ff, far, tapes, before):
    rows, size = z.feat // z.clip, ff // FF_PARTS
    there = pl.BlockSpec(memory_space=pl.ANY)
    return call(
        functools.partial(assemble_feed_kernel, z, ff, far),
        16,
        [whole(None)] * 4 + [there] * len(before),
        [there] * 2,
        [pltpu.HBM((rows, ff), f32), pltpu.HBM((ff // z.clip, z.feat), f32)],
        [
            pltpu.VMEM((4, rows, size), f32),
            pltpu.VMEM((4, size // z.tm, z.feat), f32),
            pltpu.SemaphoreType.DMA((8,)),
        ],
        (*tapes, *before),
        info,
        1000,
        24 * tapes[0].size,
        {5: 0, 6: 1} if before else {},
    )


def assemble_input_kernel(z, step, info, *refs):
    me, core = info[0], info[1]
    near, far, (late, late_other) = refs[:4], refs[4:8], refs[8:10]
    output_out, input_out = refs[12:14]
    small_kernel(z, info, refs[10], refs[11], *refs[14:])
    last = step - z.tape_rows
    for whose, m, late_tape in ((core, 0, late), (1 - core, 2, late_other)):
        for k in range(z.tm):
            t = jnp.bitwise_xor(me, k)
            tape, at = (near[m], far[m])[k // 2], k % 2 * step + last
            place_blocks(z, t, whose, tape, at, output_out, lambda j: j * z.width)
            tape, at = (near[m + 1], far[m + 1])[k % 2], k // 2 * step + last
            place_blocks(z, t, whose, tape, at, input_out, lambda j: j * z.feat)
            for i in (1, 2):
                row = (2 * k + i - 1) * z.tape_rows
                lane_at = lambda j: j * z.feat + i * z.width
                place_blocks(z, t, whose, late_tape, row, input_out, lane_at)


def assemble_input(z, info, near, far, late, small):
    rows = z.feat // z.clip
    shapes = [(rows, z.feat), (rows, 3 * z.feat), (2 * rows,)] + [(rows,)] * 6 + [(4 * rows,)]
    return call(
        functools.partial(assemble_input_kernel, z, near[0].shape[0] // 2),
        20,
        [whole(None)] * 12,
        [whole(None)] * 10,
        [jax.ShapeDtypeStruct(shape, f32) for shape in shapes],
        [],
        (*near, *far, *late, *small),
        info,
        1000,
        16 * late[0].size,
    )


def small_kernel(z, info, mine, other, *outs):
    total = mine[...].astype(f32) + other[...].astype(f32)
    lanes = z.feat // 128

    def row(i):
        return jnp.concatenate([total[n * 16 + i : n * 16 + i + 1, :] for n in range(lanes)], 1)

    rows = [row(i) for i in range(12)]
    biases = jnp.concatenate(rows[:2], 1)
    count = z.feat // z.clip
    for c in range(z.clip):

        @pl.when(info[2] == c)
        def _(c=c):
            outs[0][...] = biases[0, 2 * count * c : 2 * count * (c + 1)]
            for i in range(2, 8):
                outs[i - 1][...] = rows[i][0, count * c : count * (c + 1)]
            outs[7][...] = rows[8 + c][0, :]


def flip(count, k):
    return [(i, i ^ k) for i in range(count)]


def bit_of(index, bit):
    return (index >> bit) & 1


def bits_of(count):
    return count.bit_length() - 1


def pick(x, dim, index):
    return lax.dynamic_index_in_dim(x, index, dim, keepdims=False)


def add(kept, got):
    return (kept.astype(f32) + got.astype(f32)).astype(bf16)


def by_bits(x, dim, count):
    return x.reshape(x.shape[:dim] + (2,) * bits_of(count) + x.shape[dim + 1 :])


def halves(x, dim, axis, bit):
    mine = bit_of(lax.axis_index(axis), bit)
    return pick(x, dim, 1 - mine), pick(x, dim, mine)


def across(x, axis, bit):
    return lax.ppermute(x, axis, flip(lax.axis_size(axis), 1 << bit))


def scatter(x, dim, axis, bits):
    for bit in bits:
        sent, kept = halves(x, dim, axis, bit)
        x = add(kept, across(sent, axis, bit))
    return x


def scatter_up(x, dim, axis, bits):
    for bit in bits:
        at = dim + bits_of(lax.axis_size(axis)) - 1 - bit
        sent, kept = halves(x, at, axis, bit)
        x = add(kept, across(sent, axis, bit))
    return x


def peers(x, dim, axis):
    me = lax.axis_index(axis)
    return [pick(x, dim, me ^ k) for k in range(1, lax.axis_size(axis))]


def to_peers(sent, axis):
    count = lax.axis_size(axis)
    return [lax.ppermute(one, axis, flip(count, k)) for k, one in enumerate(sent, start=1)]


def add_all(own, got):
    total = own.astype(f32)
    for one in got:
        total = total + one.astype(f32)
    return total.astype(bf16)


def in_order(x, got, axis):
    me = lax.axis_index(axis)
    out = jnp.zeros((1 + len(got),) + x.shape, x.dtype)
    for k, one in enumerate([x, *got]):
        out = lax.dynamic_update_index_in_dim(out, one, me ^ k, 0)
    return out


def tie(*values):
    return lax.optimization_barrier(values)


def per_device(
    patches,
    lead_tokens,
    lengths,
    input_weight,
    input_bias,
    output_weight,
    output_bias,
    first_gain,
    first_shift,
    second_gain,
    second_shift,
    expand_weight,
    expand_bias,
    reduce_weight,
    reduce_bias,
    cot_patches,
    cot_lead,
):
    tm_count = lax.axis_size("tm")
    clip_count = lax.axis_size("clip")
    z = Sizes(patches.shape, tm_count, clip_count)
    feat, ff = expand_weight.shape
    core, place = lax.axis_index("freq"), lax.axis_index("tm")
    info = jnp.stack([place, core, lax.axis_index("clip")]).astype(jnp.int32)
    row = lambda vector: vector.astype(f32)[None, :]

    def by_clip(array):
        parts = array.reshape(z.fr, z.blocks, BLOCK_COLS, z.clips, feat)
        parts = parts.transpose(3, 1, 0, 2, 4).reshape(z.clips, z.half, feat)
        return (
            lax.dynamic_index_in_dim(parts, core, 0, keepdims=False),
            lax.dynamic_index_in_dim(parts, 1 - core, 0, keepdims=False),
        )

    def lead_of(array):
        mine = lax.dynamic_index_in_dim(array, core, 0, keepdims=False)
        return jnp.pad(mine, ((0, LEAD_ROWS - LEADS), (0, 0)))

    own_half, other_half = by_clip(patches)
    pieces = []
    for k in range(tm_count):
        pieces.append(lax.ppermute(own_half, "tm", flip(tm_count, k)) if k else own_half)
        pieces.append(
            lax.ppermute(other_half, ("freq", "tm"), flip(2 * tm_count, tm_count | k))
        )
    lead = lead_of(lead_tokens)
    rows = jnp.concatenate([pieces[0], pieces[1], lead], 0)
    own_cot, other_cot = by_clip(cot_patches)
    lead_cot = lead_of(cot_lead) * (place == 0).astype(bf16)
    cot = jnp.concatenate([own_cot, lax.ppermute(other_cot, "freq", flip(2, 1)), lead_cot], 0)
    cot_got = lax.ppermute(cot, "freq", flip(2, 1))

    length = lax.dynamic_index_in_dim(lengths, core, 0, keepdims=False)
    spots = np.arange(z.keys) - LEAD_ROWS
    columns = np.where(spots < 0, 1 << 20, spots // z.block * BLOCK_COLS + spots % BLOCK_COLS)
    columns[:LEADS] = -1
    live = jnp.where(jnp.asarray(columns, jnp.int32)[:, None] < length, 0.0, NEG_FILL)
    live = jnp.broadcast_to(live.astype(f32), (z.keys, 128))

    saved = attend(
        z,
        info,
        pieces,
        lead,
        input_weight,
        row(input_bias[:feat]),
        row(input_bias[feat:]),
        row(first_gain),
        row(first_shift),
        live,
        output_weight,
        row(output_bias),
        row(second_gain),
        row(second_shift),
    )
    mixed_low = saved[0]
    paired = clip_count == FF_PARTS // 2
    if not paired:
        share = (clip_count, 2, ff // (2 * clip_count))
        expand_weight = expand_weight.reshape(feat, *share).swapaxes(1, 2).reshape(feat, ff)
        expand_bias = expand_bias.reshape(share).swapaxes(0, 1).reshape(ff)
        reduce_weight = reduce_weight.reshape(*share, feat).swapaxes(0, 1).reshape(ff, feat)
    gain_two = row(second_gain)
    swap = lambda x: across(x, "freq", 0)
    size = ff // FF_PARTS
    half = clip_count // 2
    tm_bits, clip_bits = bits_of(tm_count), bits_of(clip_count)
    low_bits, high_bits = list(range(tm_bits)), list(range(tm_bits))[::-1]
    split = max(1, tm_count // (FF_PARTS // 2))

    unit, inv, low, total = saved[3], saved[4], saved[5], saved[14]
    feed_bias, acc, acc_send, grad, grad_send, *sums = feed(
        z, info, paired, low, swap(low), cot, cot_got, expand_weight, row(expand_bias), reduce_weight
    )
    if z.tape:
        out_r, own_r, out_e, own_e = sums
    else:
        sum_r, sum_e = sums
        rows_r, rows_e = ff // (2 * clip_count * tm_count), feat // (clip_count * split)
        sum_r = sum_r.reshape(clip_count, tm_count, rows_r, feat // 128, 128).swapaxes(2, 3)
        sum_e = sum_e.reshape(-1, clip_count, split, rows_e, size // 128, 128)
        sum_e = sum_e.transpose(0, 2, 1, 4, 3, 5)
        sum_r = sum_r.reshape(clip_count, tm_count, -1, 128)
        sum_e = sum_e.reshape(tm_count, clip_count, -1, 128).swapaxes(0, 1)
        out_r, own_r = halves(by_bits(sum_r, 1, tm_count), 1 + tm_bits - 1, "tm", 0)
        out_e, own_e = halves(by_bits(sum_e, 1, tm_count), 1, "tm", tm_bits - 1)
    grad, grad_send, acc_send, out_r, out_e = tie(grad, grad_send, acc_send, out_r, out_e)
    across_r = lambda x: across(x, "tm", 0)
    across_e = lambda x: across(x, "tm", tm_bits - 1)
    across_z = lambda x: across(x, "clip", 0)
    halves_z = lambda x: halves(by_bits(x, 0, clip_count), clip_bits - 1, "clip", 0)
    rest_z = lambda x: scatter_up(x, 0, "clip", range(1, clip_bits))

    got_r, got_e = across_r(out_r), across_e(out_e)
    acc_got = swap(acc_send)
    grad_first, grad_low, sent_o, kept_o, small_two = blend_back(
        z, info, grad, swap(grad_send), unit, inv, cot, mixed_low, gain_two
    )
    if not z.tape:
        sent_o, kept_o = plain_to_tape(z, kept_o, core)
    got_o = swap(sent_o)
    sent_0, kept_0, rest_0 = attend_back(z, info, 0, grad_low, output_weight, saved)
    grad_low, got_o, acc_got, sent_0 = tie(grad_low, got_o, acc_got, sent_0)
    out_o, own_o = halves_z(add(kept_o, got_o))
    grad_low, out_o = tie(grad_low, out_o)
    got_0, got_oz = swap(sent_0), across_z(out_o)
    sent_1, kept_1, rest_1 = attend_back(z, info, 1, grad_low, output_weight, saved)
    grad_low, got_r, got_e, got_0, got_oz, sent_1 = tie(
        grad_low, got_r, got_e, got_0, got_oz, sent_1
    )
    sum_r, sum_e = add(own_r, got_r), add(own_e, got_e)
    if z.tape:
        out_r, own_r = halves(sum_r, 0, "tm", 1)
        out_e, own_e = halves(sum_e, 0, "tm", 0)
        ordered = lambda x: jnp.where(place // 2 == 0, jnp.concatenate([x[half:], x[:half]], 0), x)
        out_r, own_r = ordered(out_r), ordered(own_r)
    else:
        sum_r = scatter_up(sum_r, 1, "tm", low_bits[1:-1])
        sum_e = scatter(sum_e, 1, "tm", high_bits[1:-1])
        out_r, own_r = halves(sum_r, 1, "tm", low_bits[-1])
        out_e, own_e = halves(sum_e, 1, "tm", high_bits[-1])
    sum_o = add(own_o, got_oz)
    out_0, own_0 = halves_z(add(kept_0, got_0))
    grad_low, out_r, out_e, sum_o, out_0 = tie(grad_low, out_r, out_e, sum_o, out_0)
    got_r, got_e = across(out_r, "tm", low_bits[-1]), across(out_e, "tm", high_bits[-1])
    got_0z, got_1 = across_z(out_0), swap(sent_1)
    sum_o = rest_z(sum_o)

    def split_tm(x, *more):
        x = by_bits(x, 1, tm_count)
        parts = [x[:half], x[half:]]
        if more:
            parts = [jnp.concatenate([p, by_bits(m, 1, tm_count)], 0) for p, m in zip(parts, more)]
        return (
            *halves(parts[0], tm_bits, "tm", 0),
            *halves(parts[1], 1, "tm", tm_bits - 1),
        )

    sent_2, kept_2, rest_2 = attend_back(z, info, 2, grad_low, output_weight, saved)
    sent_2, got_r, got_e, got_0z, got_1, sum_o, *rest_2 = tie(
        sent_2, got_r, got_e, got_0z, got_1, sum_o, *rest_2
    )
    sum_r, sum_e = add(own_r, got_r), add(own_e, got_e)
    out_f, own_f = halves_z(jnp.concatenate([sum_r, sum_e], 1))
    count_f = sum_r.shape[1]
    sum_0 = add(own_0, got_0z)
    out_1x, own_1x, out_1y, own_1y = split_tm(add(kept_1, got_1))
    feed_bias = feed_bias[:, 0:1] * (jnp.arange(2) == core).astype(f32)[:, None]
    if not paired:
        feed_bias = feed_bias.swapaxes(0, 1).reshape(2, clip_count, -1).swapaxes(0, 1)
    feed_small = jnp.concatenate([small_two[:4], feed_bias.reshape(-1, feat)], 0)
    out_f, sum_0, out_1x, out_1y, sent_2, *rest_2 = tie(
        out_f, sum_0, out_1x, out_1y, sent_2, *rest_2
    )
    got_f, got_2, got_1x, got_1y = across_z(out_f), swap(sent_2), across_r(out_1x), across_e(out_1y)
    sum_0 = rest_z(sum_0)
    own, small, *sends = keys_back(
        z, info, saved, input_weight, grad_first, feed_small, (rest_0, rest_1, rest_2)
    )
    got_2, got_1x, got_1y, sum_0, own, small, *sends = tie(
        got_2, got_1x, got_1y, sum_0, own, small, *sends
    )
    out_2x, own_2x, out_2y, own_2y = split_tm(add(kept_2, got_2), sum_o[None], sum_0[None])
    def patches_of(mine, theirs):
        first = jnp.where(core == 0, mine, theirs[: z.half])
        second = jnp.where(core == 0, theirs[: z.half], mine)
        pair = jnp.stack([first, second], 0).reshape(
            z.clips, z.blocks, z.fr, BLOCK_COLS, feat
        )
        return pair.transpose(2, 1, 3, 0, 4).reshape(z.fr, z.tc, z.clips, feat)

    finish_args = (rows, row(first_gain), grad_first)
    block_of = lambda total: (total + acc + acc_got.astype(f32) + row(reduce_bias)).astype(bf16)
    if z.tape:
        flat = lambda *parts: jnp.concatenate([part.reshape(-1, 128) for part in parts], 0)
        count = small.shape[0]
        unpack = lambda got, like: (got[:-count].reshape(like.shape), got[-count:])
        across_x, across_y = lambda x: across(x, "tm", 0), lambda x: across(x, "tm", 1)
        across_zz = lambda x: across(x, "clip", 1)
        along_x, along_y, mid_x, mid_y = sends
        token, msg_x, out_2y, along_x, along_y = tie(
            info, flat(out_2x, small), out_2y, along_x, along_y
        )
        msg_x, got_2y = across_x(msg_x), across_y(out_2y)
        got_x, got_y = across_x(along_x), across_y(along_y)
        token, msg_x, got_2y = tie(token, msg_x, got_2y)
        got_2x, got_small = unpack(msg_x, own_2x)
        small = add(small, got_small)
        sum_x = jnp.concatenate([add(own_1x, got_1x), add(own_2x, got_2x)], 0)
        sum_y = jnp.concatenate([add(own_1y, got_1y), add(own_2y, got_2y)], 0)
        out_x, own_x = halves(sum_x, 1, "tm", 1)
        out_y, own_y = halves(sum_y, 1, "tm", 0)
        token, small = tie(token, small)
        token, msg_x, out_y, got_f = tie(token, flat(out_x, small), out_y, got_f)
        out_f, own_f = halves(add(own_f, got_f), 0, "clip", 1)
        msg_x, got_y2, got_f = across_y(msg_x), across_x(out_y), across_zz(out_f)
        token, msg_x, got_y2 = tie(token, msg_x, got_y2)
        got_x2, got_small = unpack(msg_x, own_x)
        small = add(small, got_small)
        sum_x, sum_y = add(own_x, got_x2), add(own_y, got_y2)
        late = [jnp.concatenate([one[:2], one[2:4]], 1) for one in (sum_x, sum_y)]
        out_l, own_l = halves_z(jnp.concatenate(late, 0))
        token, small = tie(token, small)
        token, msg_l = tie(token, flat(out_l, small))
        msg_l = across_z(msg_l)
        token, got_f = tie(token, got_f)
        sum_f = add(own_f, got_f)
        token, ready_p, ready_q = tie(
            token, flat(sum_f[:count_f], sum_x[4]), flat(sum_f[count_f:], sum_y[4])
        )
        got_p, got_q = across_x(ready_p), across_y(ready_q)
        token, got_x, got_y = tie(token, got_x, got_y)
        lead = add(along_x[z.rows :], got_x[z.rows :])
        out_xy = jnp.concatenate([add(mid_x, got_x[z.half : z.rows]), lead], 0)
        out_yx = add(mid_y, got_y[z.half :])
        token, out_xy, out_yx = tie(token, out_xy, out_yx)
        got_xy, got_yx = across_y(out_xy), across_x(out_yx)
        token, msg_l = tie(token, msg_l)
        got_l, got_small = unpack(msg_l, own_l)
        small = add(small, got_small)
        out_l, own_l = halves(add(own_l, got_l), 0, "clip", 1)
        token, small = tie(token, small)
        token, msg_l, total_now = tie(token, flat(out_l, small), total)
        msg_l = across_zz(msg_l)
        block = block_of(total_now)
        block_mine, block_send = block[: z.half], block[z.half :]
        token, got_xy, got_yx, got_p, got_q, block_mine, block_send = tie(
            token, got_xy, got_yx, got_p, got_q, block_mine, block_send
        )
        received = [got_x, got_y, got_xy, got_yx]
        grad_mine, grad_send = finish(z, token, own, received, *finish_args)
        token, grad_send = tie(token, grad_send)
        grad_got, block_got = swap(grad_send), swap(block_send)
        token, grad_got, block_got = tie(token, grad_got, block_got)
        token, near_p, near_q = tie(token, flat(ready_p, got_p), flat(ready_q, got_q))
        far_p, far_q = across_y(near_p), across_x(near_q)
        other_p, other_q = swap(near_p), swap(near_q)
        token, msg_l, other_p, other_q = tie(token, msg_l, other_p, other_q)
        got_l, got_small = unpack(msg_l, own_l)
        small, late = add(small, got_small), add(own_l, got_l)
        token, small, late = tie(token, small, late)
        late_all = to_peers([late] * 3, "tm")
        feed_grads = assemble_feed(z, token, ff, 0, (near_p, near_q, other_p, other_q), ())
        patch_outs = (patches_of(block_mine, block_got), patches_of(grad_mine, grad_got))
        token, far_p, far_q, *rest = tie(token, far_p, far_q, *feed_grads, *patch_outs)
        feed_grads, patch_outs = rest[:2], rest[2:]
        other_far = (swap(far_p), swap(far_q))
        token, *late_all = tie(token, *late_all)
        token, late, small = tie(token, flat(late, *late_all), small)
        late_got, small_got = swap(late), swap(small)
        token, *other_far = tie(token, *other_far)
        far = (far_p, far_q, *other_far)
        feed_grads = assemble_feed(z, token, ff, 1, far, feed_grads)
        token, *feed_grads = tie(token, *feed_grads)
        output_weight_grad, input_weight_grad, *vectors = assemble_input(
            z, token, (near_p, near_q, other_p, other_q), far, (late, late_got), (small, small_got)
        )
    else:
        received = to_peers(sends, "tm")
        got_2x, got_2y = across_r(out_2x), across_e(out_2y)
        sum_x = jnp.concatenate([add(own_1x, got_1x), add(own_2x, got_2x)], 0)
        sum_y = jnp.concatenate([add(own_1y, got_1y), add(own_2y, got_2y)], 0)
        sum_x = scatter_up(sum_x, 1, "tm", low_bits[1:])
        sum_y = scatter(sum_y, 1, "tm", high_bits[1:])
        sum_f = rest_z(add(own_f, got_f))
        ready = jnp.concatenate([sum_f, sum_x[2 * half], sum_y[2 * half]], 0)
        late = jnp.concatenate(
            [
                jnp.concatenate([one[:half], one[half : 2 * half]], 1)
                for one in (sum_x, sum_y)
            ],
            0,
        )
        late = scatter(by_bits(late, 0, clip_count), 0, "clip", range(clip_bits)[::-1])
        ready = jnp.concatenate([ready, late], 0)
        ready_all = [ready] + to_peers([ready] * (tm_count - 1), "tm")
        small = small + swap(small)
        for axis, bits in (("tm", tm_bits), ("clip", clip_bits)):
            for bit in range(bits):
                small = small + across(small, axis, bit)
        grad_mine, grad_send = finish(z, info, own, received, *finish_args)

    here = lax.axis_index("clip")

    def shard(vector):
        count = vector.shape[0] // clip_count
        return lax.dynamic_slice_in_dim(vector, here * count, count, 0)

    if not z.tape:
        vectors = [shard(small[0:2].reshape(-1)), *[shard(small[i]) for i in range(2, 8)]]
        vectors.append(shard(small[8:12].reshape(-1)))
    input_bias_grad, gain_one_grad, shift_one_grad, output_bias_grad = vectors[:4]
    gain_two_grad, shift_two_grad, reduce_bias_grad, expand_bias_grad = vectors[4:]

    if z.tape:
        expand_weight_grad, reduce_weight_grad = feed_grads
    else:
        block = block_of(total)
        block_mine, block_send = block[: z.half], block[z.half :]
        grad_got, block_got = swap(grad_send), swap(block_send)
        patch_outs = (patches_of(block_mine, block_got), patches_of(grad_mine, grad_got))
        tapes = jnp.stack(ready_all)
        other_tapes = swap(tapes)
        both = in_order(tapes, [other_tapes], "freq")
        both = pick(jnp.stack([both[:, np.arange(tm_count) ^ t] for t in range(tm_count)]), 0, place)
        part_r, part_e = both[:, :, :count_f], both[:, :, count_f : 2 * count_f]
        rows_r, rows_e = ff // (2 * clip_count * tm_count), feat // (clip_count * split)
        part_r = part_r.reshape(2, tm_count, feat // 128, rows_r, 128).swapaxes(2, 3)
        reduce_weight_grad = part_r.reshape(ff // clip_count, feat).astype(f32)
        part_e = part_e.reshape(2, FF_PARTS // 2, split, size // 128, rows_e, 128)
        part_e = part_e.transpose(2, 4, 1, 0, 3, 5)
        if not paired:
            part_e = part_e.swapaxes(2, 3).reshape(feat // clip_count, 2, clip_count, -1)
            part_e = part_e.swapaxes(1, 2)
        expand_weight_grad = part_e.reshape(feat // clip_count, ff).astype(f32)
        lanes = z.width // 128
        part_a = both[:, :, 2 * count_f :].reshape(2, tm_count // lanes, lanes, 4, 3, -1, 128)
        part_a = part_a.transpose(0, 1, 5, 3, 4, 2, 6)
        part_a = part_a.reshape(feat // clip_count, 4, 3, z.width).astype(f32)
        output_weight_grad = part_a[:, 0].reshape(-1, feat)
        input_weight_grad = part_a[:, 1:].swapaxes(1, 2).reshape(-1, 3 * feat)

    def leads_of(sent, got):
        mine, theirs = sent[z.half : z.half + LEADS], got[z.half : z.half + LEADS]
        first = jnp.where(core == 0, mine, theirs)
        second = jnp.where(core == 0, theirs, mine)
        return jnp.stack([first, second], 0)

    return (
        patch_outs[0],
        leads_of(block_send, block_got),
        patch_outs[1],
        leads_of(grad_send, grad_got),
        input_weight_grad,
        input_bias_grad,
        output_weight_grad,
        output_bias_grad,
        gain_one_grad,
        shift_one_grad,
        gain_two_grad,
        shift_two_grad,
        expand_weight_grad,
        expand_bias_grad,
        reduce_weight_grad,
        reduce_bias_grad,
    )


def solution(mesh):
    rows = P("freq", "tm", "clip", None)
    lead = P("clip", None, None)
    in_specs = (rows, lead, P("clip")) + (P(),) * 12 + (rows, lead)
    matrix, vector = P("clip", None), P("clip")
    out_specs = (rows, lead, rows, lead) + (matrix, vector) * 2 + (vector,) * 4 + (matrix, vector) * 2
    return jax.shard_map(
        per_device, mesh=mesh, in_specs=in_specs, out_specs=out_specs, check_vma=False
    )
```
